32 devices in a mesh: dp: 8 (over y, x, core), mp: 4 (over z).
Axes of the slice: x: 2, y: 2, z: 4, core: 2. Of those that a mesh axis runs over, the one named last changes fastest.
Arguments:
- hidden_in: bfloat16 [8192, 2048], P(('dp', 'mp')), may hold values from -6 to 6
- cotangent: bfloat16 [8192, 2048], P(('dp', 'mp')), may hold values from -6 to 6
- doc_lengths: int32 [8, 4], P('dp'), may hold values from 1 to 640, 1024 in all within a row
- owner: int32 [8], replicated, may hold values from 0 to 7, each once
- projection_master_weight: float32 [2048, 4096], P('dp', 'mp'), may hold values from -0.125 to 0.125
- gateup_weight: float32 [2048, 12288], P('dp', 'mp'), may hold values from -0.125 to 0.125
- out_weight: float32 [2048, 2048], P(('mp', 'dp')), may hold values from -0.75 to 0.75
- down_weight: float32 [6144, 2048], P(('mp', 'dp')), may hold values from -0.078125 to 0.078125
- projection_first_moment: float32 [2048, 4096], P('dp', 'mp'), may hold values from -9.1552734e-05 to 9.1552734e-05
- gateup_first: float32 [2048, 12288], P('dp', 'mp'), may hold values from -9.1552734e-05 to 9.1552734e-05
- out_first: float32 [2048, 2048], P(('mp', 'dp')), may hold values from -3.0517578e-05 to 3.0517578e-05
- down_first: float32 [6144, 2048], P(('mp', 'dp')), may hold values from -9.1552734e-05 to 9.1552734e-05
- projection_second_moment: float32 [2048, 4096], P('dp', 'mp'), may hold values from 1.0529243e-09 to 4.1719646e-09
- gateup_second: float32 [2048, 12288], P('dp', 'mp'), may hold values from 1.0529243e-09 to 4.1719646e-09
- out_second: float32 [2048, 2048], P(('mp', 'dp')), may hold values from 1.5893198e-10 to 6.357279e-10
- down_second: float32 [6144, 2048], P(('mp', 'dp')), may hold values from 1.0529243e-09 to 4.1719646e-09
- gains: float32 [4352], replicated, may hold values from 0.3 to 1.5
- gain_first: float32 [4352], replicated, may hold values from -0.00024414062 to 0.00024414062
- gain_second: float32 [4352], replicated, may hold values from 9.337254e-09 to 3.7746343e-08
Outputs:
- output: bfloat16 [8192, 2048], P(('dp', 'mp'))
- input_grad: float32 [8192, 2048], P(('dp', 'mp'))
- qkv_new: float32 [2048, 4096], P('dp', 'mp')
- gateup_new: float32 [2048, 12288], P('dp', 'mp')
- out_new: float32 [2048, 2048], P(('mp', 'dp'))
- down_new: float32 [6144, 2048], P(('mp', 'dp'))
- qkv_first_new: float32 [2048, 4096], P('dp', 'mp')
- gateup_first_new: float32 [2048, 12288], P('dp', 'mp')
- out_first_new: float32 [2048, 2048], P(('mp', 'dp'))
- down_first_new: float32 [6144, 2048], P(('mp', 'dp'))
- qkv_second_new: float32 [2048, 4096], P('dp', 'mp')
- gateup_second_new: float32 [2048, 12288], P('dp', 'mp')
- out_second_new: float32 [2048, 2048], P(('mp', 'dp'))
- down_second_new: float32 [6144, 2048], P(('mp', 'dp'))
- gains_new: float32 [4352], replicated
- gain_first_new: float32 [4352], replicated
- gain_second_new: float32 [4352], replicated
- grad_norm: float32 [], replicated
The draws below stay inside these ranges and needn't reach their ends.
Inputs may be any that keep to these rules, and one draw needn't show every extreme that they name: `doc_lengths`: each row sums to 1024; its longest document has exactly 640 tokens. `owner`: a permutation: each stored block number once.
All inputs are finite; a program needn't handle non-finite values.
Results may differ from the reference program's by a relative error of at most 0.02.
Values may be sent and summed in bfloat16 or wider, within the bound.
A program may use at most 256 MiB of HBM per device.

```python
import math
import jax
import jax.numpy as jnp
import numpy as np
from jax import lax

MODEL_WIDTH = 2048
QUERY_HEADS = 16
KEY_VALUE_HEADS = 8
HEAD_SIZE = 128
FF = 6144
SEQUENCE_TOKENS = 1024
NDOC = 4
STEP = 10
SEQUENCE_COUNT = 8
TOKEN_COUNT = 8192
GAINS = 4352
TRAINED_ENTRIES = 50336000
N_DP = 8
N_MP = 4


def draw_gains(key, part):
    key = jax.random.fold_in(key, 7)
    first_key, second_key = jax.random.split(key, 2)
    ramp = jnp.arange(MODEL_WIDTH, dtype=jnp.float32) / MODEL_WIDTH
    low_end = 0.6
    rising = low_end + (1.1 - low_end) * ramp
    rough = jax.random.uniform(first_key, (2, MODEL_WIDTH), jnp.float32, 0.75, 1.3)
    head_gains = jax.random.uniform(second_key, (2 * HEAD_SIZE,), jnp.float32, 0.5, 1.5)
    return jnp.concatenate([(rough * rising[None, :]).reshape(-1), head_gains])


def shard_levels(key, dims, cuts, smallest, top_value):
    loudness, own = 1.0, jax.random.fold_in(key, 6)
    for axis_at, blocks in cuts:
        heights = jnp.exp(jax.random.uniform(jax.random.fold_in(own, axis_at), (blocks,), jnp.float32, smallest / len(cuts), top_value / len(cuts)))
        loudness = loudness * jnp.repeat(heights, dims[axis_at] // blocks).reshape([-1 if axis == axis_at else 1 for axis in range(len(dims))])
    return loudness


def length_profile(number_of, total, bound, skew):
    weights = [(1 << 20) // math.isqrt(standing ** skew) + 1 for standing in range(2, number_of + 1)]
    surplus, holding = total - bound - (number_of - 1), [1] * (number_of - 1)
    while surplus > 0:
        candidates = [i for i in range(number_of - 1) if holding[i] < bound]
        mass, remaining = sum([weights[i] for i in candidates]), surplus
        for i in candidates:
            more = min(bound - holding[i], max(1, remaining * weights[i] // mass), surplus)
            holding[i] = holding[i] + more
            surplus = surplus - more
    return np.array([bound] + holding)


def ragged_sizes(own_key, count, total, most, lean):
    if count == 2:
        one = jax.random.randint(own_key, (), max(1, total - most), min(most, total - 1) + 1)
        return jnp.stack([one, total - one])
    sizes = jnp.asarray(length_profile(count, total, most, lean), jnp.int32)
    pairs = (count - 1) // 2
    source_of, receiver = sizes[1:1 + 2 * pairs:2], sizes[2:2 + 2 * pairs:2]
    margin = jnp.minimum(source_of - 1, most - receiver)
    shifted = jax.random.randint(jax.random.fold_in(own_key, 1), (pairs,), 0, 1 << 20) % (margin + 1)
    sizes = sizes.at[1:1 + 2 * pairs:2].set(source_of - shifted).at[2:2 + 2 * pairs:2].set(receiver + shifted)
    return sizes[jax.random.permutation(jax.random.fold_in(own_key, 2), count)]


def scatter_about(stream_key, dims, width, limit, cuts=(), held_as=jnp.bfloat16):
    array = width * jax.random.normal(stream_key, dims, jnp.float32)
    if cuts:
        array = array * shard_levels(stream_key, dims, cuts, -0.22, 0.18)
    return jnp.clip(array, -limit, limit).astype(held_as)


def setup_inputs(seed: int = 0) -> dict:
    splits = jax.random.split(jax.random.key(seed), 20)
    hidden_in = scatter_about(splits[0], (TOKEN_COUNT, MODEL_WIDTH), 1.0, 6.0, ((0, 32),))
    cotangent = scatter_about(splits[1], (TOKEN_COUNT, MODEL_WIDTH), 1.0, 6.0, ((0, 32),))
    doc_lengths = jax.vmap(lambda own: ragged_sizes(own, NDOC, SEQUENCE_TOKENS, SEQUENCE_TOKENS * 5 // 8, 2))(jax.random.split(splits[2], SEQUENCE_COUNT)).reshape((SEQUENCE_COUNT, NDOC)).astype(jnp.int32)
    owner = jax.random.permutation(splits[3], SEQUENCE_COUNT).astype(jnp.int32)
    projection_master_weight = scatter_about(splits[4], (MODEL_WIDTH, (QUERY_HEADS + 2 * KEY_VALUE_HEADS) * HEAD_SIZE), MODEL_WIDTH ** -0.5, 0.125, ((0, 8), (1, 4)), jnp.float32)
    gateup_weight = scatter_about(splits[5], (MODEL_WIDTH, 2 * FF), MODEL_WIDTH ** -0.5, 0.125, ((0, 8), (1, 4)), jnp.float32)
    out_weight = scatter_about(splits[6], (QUERY_HEADS * HEAD_SIZE, MODEL_WIDTH), (QUERY_HEADS * HEAD_SIZE // 32) ** -0.5, 0.75, ((0, 32),), jnp.float32)
    down_weight = scatter_about(splits[7], (FF, MODEL_WIDTH), FF ** -0.5, 0.078125, ((0, 32),), jnp.float32)
    projection_first_moment = scatter_about(splits[8], (MODEL_WIDTH, (QUERY_HEADS + 2 * KEY_VALUE_HEADS) * HEAD_SIZE), (0.11 * TRAINED_ENTRIES ** -0.5), 9.1552734375e-05, ((0, 8), (1, 4)), jnp.float32)
    gateup_first = scatter_about(splits[9], (MODEL_WIDTH, 2 * FF), (0.11 * TRAINED_ENTRIES ** -0.5), 9.1552734375e-05, ((0, 8), (1, 4)), jnp.float32)
    out_first = scatter_about(splits[10], (QUERY_HEADS * HEAD_SIZE, MODEL_WIDTH), (0.04 * TRAINED_ENTRIES ** -0.5), 3.0517578125e-05, ((0, 32),), jnp.float32)
    down_first = scatter_about(splits[11], (FF, MODEL_WIDTH), (0.11 * TRAINED_ENTRIES ** -0.5), 9.1552734375e-05, ((0, 32),), jnp.float32)
    projection_second_moment = jnp.clip(jnp.exp(math.log(4.171964551602514e-09) - 1.3768157 * jax.random.uniform(splits[12], (MODEL_WIDTH, (QUERY_HEADS + 2 * KEY_VALUE_HEADS) * HEAD_SIZE), jnp.float32) ** shard_levels(splits[12], (MODEL_WIDTH, (QUERY_HEADS + 2 * KEY_VALUE_HEADS) * HEAD_SIZE), ((0, 8), (1, 4)), -0.2, 0.2)), 1.0529243033019497e-09, 4.171964551602514e-09)
    gateup_second = jnp.clip(jnp.exp(math.log(4.171964551602514e-09) - 1.3768157 * jax.random.uniform(splits[13], (MODEL_WIDTH, 2 * FF), jnp.float32) ** shard_levels(splits[13], (MODEL_WIDTH, 2 * FF), ((0, 8), (1, 4)), -0.2, 0.2)), 1.0529243033019497e-09, 4.171964551602514e-09)
    out_second = jnp.clip(jnp.exp(math.log(6.357279147550798e-10) - 1.3862944 * jax.random.uniform(splits[14], (QUERY_HEADS * HEAD_SIZE, MODEL_WIDTH), jnp.float32) ** shard_levels(splits[14], (QUERY_HEADS * HEAD_SIZE, MODEL_WIDTH), ((0, 32),), -0.2, 0.2)), 1.5893197868876996e-10, 6.357279147550798e-10)
    down_second = jnp.clip(jnp.exp(math.log(4.171964551602514e-09) - 1.3768157 * jax.random.uniform(splits[15], (FF, MODEL_WIDTH), jnp.float32) ** shard_levels(splits[15], (FF, MODEL_WIDTH), ((0, 32),), -0.2, 0.2)), 1.0529243033019497e-09, 4.171964551602514e-09)
    gains = draw_gains(jax.random.fold_in(splits[19], 71), 0)
    gain_first = scatter_about(splits[17], (GAINS,), (0.33 * TRAINED_ENTRIES ** -0.5), 0.00024414062, (), jnp.float32)
    gain_second = jnp.clip(jnp.exp(jax.random.uniform(splits[18], (GAINS,), jnp.float32, math.log(9.337253636942933e-09), math.log(3.774634294018142e-08))), 9.337253636942933e-09, 3.774634294018142e-08)
    return {"hidden_in": hidden_in, "cotangent": cotangent, "doc_lengths": doc_lengths, "owner": owner, "projection_master_weight": projection_master_weight, "gateup_weight": gateup_weight, "out_weight": out_weight, "down_weight": down_weight, "projection_first_moment": projection_first_moment, "gateup_first": gateup_first, "out_first": out_first, "down_first": down_first, "projection_second_moment": projection_second_moment, "gateup_second": gateup_second, "out_second": out_second, "down_second": down_second, "gains": gains, "gain_first": gain_first, "gain_second": gain_second}


EPS_NORM = 1e-06
THETA = 1000000.0
LEARN = 0.03
GAIN_LEARN = 0.5
FIRST_DECAY = 0.9
SECOND_DECAY = 0.95
ADAM_EPS = 1e-08
WEIGHT_DECAY = 0.1
CLIP_LIMIT = 1.0
MASKED = -1e+30

@jax.custom_vjp
def low(v):
    return lax.optimization_barrier(v.astype(jnp.bfloat16)).astype(jnp.float32)

@jax.custom_vjp
def low_back(v):
    return v

def low_keep(v):
    return (low(v), None)

def low_pass(kept, grad):
    return (grad,)

def back_keep(v):
    return (v, None)

def back_low(kept, grad):
    return (low(grad),)
low.defvjp(low_keep, low_pass)
low_back.defvjp(back_keep, back_low)

def dot32(left, right):
    return jnp.dot(left, right, precision=lax.Precision.HIGHEST, preferred_element_type=jnp.float32)

def rms_norm(value_rows, gain):
    return value_rows * lax.rsqrt(lax.optimization_barrier(jnp.mean(value_rows * value_rows, axis=-1, keepdims=True)) + EPS_NORM) * gain

def rotate(value_rows, cosine, sine):
    half = value_rows.shape[-1] // 2
    turned = jnp.concatenate([-value_rows[..., half:], value_rows[..., :half]], axis=-1)
    return value_rows * cosine + turned * sine

def layout(lengths):
    ends = jnp.cumsum(lengths).astype(jnp.int32)
    starts = ends - lengths
    places = jnp.arange(SEQUENCE_TOKENS, dtype=jnp.int32)
    doc_of = lax.optimization_barrier(jnp.sum((places[:, None] >= ends[None, :]).astype(jnp.int32), axis=1))
    chosen = doc_of[:, None] == jnp.arange(NDOC, dtype=jnp.int32)[None, :]
    begin = lax.optimization_barrier(jnp.sum(jnp.where(chosen, starts[None, :], 0), axis=1))
    offset = (places - begin).astype(jnp.float32)
    half = HEAD_SIZE // 2
    freq = THETA ** (-(2.0 * jnp.arange(half, dtype=jnp.float32)) / HEAD_SIZE)
    angle = offset[:, None] * freq[None, :]
    angle = jnp.concatenate([angle, angle], axis=-1)
    return (doc_of, jnp.cos(angle), jnp.sin(angle))

def arrange(stored, order, groups):
    rows = stored.shape[0] // (groups * N_DP)
    blocks = stored.reshape(groups, N_DP, rows, stored.shape[1])
    return jnp.take(blocks, order, axis=1).reshape(stored.shape)

def attend_heads(parts):
    query_rows, key_rows, value_rows, doc_of = parts
    places = jnp.arange(SEQUENCE_TOKENS, dtype=jnp.int32)
    allowed = (doc_of[:, None] == doc_of[None, :]) & (places[None, :] <= places[:, None])
    query_group = QUERY_HEADS // KEY_VALUE_HEADS
    grouped_queries = query_rows.reshape(SEQUENCE_TOKENS, KEY_VALUE_HEADS, query_group, HEAD_SIZE)
    score_matrix = jnp.einsum('tlwd,uld->lwtu', grouped_queries, key_rows, precision=lax.Precision.HIGHEST) * HEAD_SIZE ** (-0.5)
    score_matrix = low_back(score_matrix)
    score_matrix = jnp.where(allowed[None, None], score_matrix, MASKED)
    top = lax.optimization_barrier(jnp.max(score_matrix, axis=-1, keepdims=True))
    total = jnp.log(lax.optimization_barrier(jnp.sum(jnp.exp(score_matrix - top), axis=-1, keepdims=True))) + top
    probabilities = low(jnp.exp(score_matrix - total))
    attention_result = jnp.einsum('cpyx,xca->ycpa', probabilities, value_rows, precision=lax.Precision.HIGHEST)
    return attention_result.reshape(SEQUENCE_TOKENS, QUERY_HEADS * HEAD_SIZE)

def adam(weight, first, second, grad, factor, rate, decay):
    clipped = grad * factor
    first_new = FIRST_DECAY * first + (1.0 - FIRST_DECAY) * clipped
    second_new = SECOND_DECAY * second + (1.0 - SECOND_DECAY) * clipped * clipped
    first_hat = first_new / (1.0 - FIRST_DECAY ** STEP)
    second_hat = second_new / (1.0 - SECOND_DECAY ** STEP)
    weight_new = weight * (1.0 - rate * decay) - rate * first_hat / (jnp.sqrt(second_hat) + ADAM_EPS)
    return (weight_new, first_new, second_new)

def reference(hidden_in, cotangent, doc_lengths, owner, projection_master_weight, gateup_weight, out_weight, down_weight, projection_first_moment, gateup_first, out_first, down_first, projection_second_moment, gateup_second, out_second, down_second, gains, gain_first, gain_second):
    inverse = jnp.argsort(owner).astype(jnp.int32)
    document_ids, cos_all, sin_all = jax.vmap(layout)(doc_lengths)
    cosine = cos_all.reshape(TOKEN_COUNT, 1, HEAD_SIZE)
    sine = sin_all.reshape(TOKEN_COUNT, 1, HEAD_SIZE)
    query_width = QUERY_HEADS // N_MP * HEAD_SIZE
    key_width = KEY_VALUE_HEADS // N_MP * HEAD_SIZE
    units = FF // N_MP
    out_rate = float(QUERY_HEADS * HEAD_SIZE // 32) ** (-0.5)

    def forward(inputs, w_qkv, w_gateup, w_out, w_down, gain_all):
        ln_in = gain_all[:MODEL_WIDTH]
        ln_mid = gain_all[MODEL_WIDTH:2 * MODEL_WIDTH]
        q_gain = gain_all[2 * MODEL_WIDTH:2 * MODEL_WIDTH + HEAD_SIZE]
        k_gain = gain_all[2 * MODEL_WIDTH + HEAD_SIZE:]
        normed = low(rms_norm(inputs, ln_in))
        projected = low_back(dot32(normed, low(w_qkv)))
        grouped_queries = projected.reshape(TOKEN_COUNT, N_MP, query_width + 2 * key_width)
        query_raw = grouped_queries[:, :, :query_width].reshape(TOKEN_COUNT, QUERY_HEADS, HEAD_SIZE)
        unrotated_key = grouped_queries[:, :, query_width:query_width + key_width].reshape(TOKEN_COUNT, KEY_VALUE_HEADS, HEAD_SIZE)
        projected_value = grouped_queries[:, :, query_width + key_width:].reshape(TOKEN_COUNT, KEY_VALUE_HEADS, HEAD_SIZE)
        query_rows = low(rotate(rms_norm(query_raw, q_gain), cosine, sine))
        key_rows = low(rotate(rms_norm(unrotated_key, k_gain), cosine, sine))
        value_rows = low(projected_value)
        head_outputs = lax.map(jax.checkpoint(attend_heads), (query_rows.reshape(SEQUENCE_COUNT, SEQUENCE_TOKENS, QUERY_HEADS, HEAD_SIZE), key_rows.reshape(SEQUENCE_COUNT, SEQUENCE_TOKENS, KEY_VALUE_HEADS, HEAD_SIZE), value_rows.reshape(SEQUENCE_COUNT, SEQUENCE_TOKENS, KEY_VALUE_HEADS, HEAD_SIZE), document_ids))
        head_outputs = low(low_back(head_outputs.reshape(TOKEN_COUNT, QUERY_HEADS * HEAD_SIZE)))
        attn = low_back(dot32(head_outputs, low(w_out)))
        mixed = inputs + attn
        normed_mid = low(rms_norm(mixed, ln_mid))
        gateup = low_back(dot32(normed_mid, low(w_gateup)))
        paired = gateup.reshape(TOKEN_COUNT, N_MP, 2 * units)
        gate = paired[:, :, :units].reshape(TOKEN_COUNT, FF)
        upper = paired[:, :, units:].reshape(TOKEN_COUNT, FF)
        act = low(jax.nn.silu(gate) * upper)
        branch = low_back(dot32(act, low(w_down)))
        return mixed + branch
    primals = (hidden_in.astype(jnp.float32), arrange(projection_master_weight, owner, 1), arrange(gateup_weight, owner, 1), arrange(out_weight, owner, N_MP), arrange(down_weight, owner, N_MP), gains)
    attention_result, pull = jax.vjp(forward, primals[0], primals[1], primals[2], primals[3], primals[4], primals[5])
    d_input, d_qkv, d_gateup, d_out, d_down, d_gains = pull(cotangent.astype(jnp.float32))
    g_qkv = arrange(d_qkv, inverse, 1)
    g_gateup = arrange(d_gateup, inverse, 1)
    g_out = arrange(d_out, inverse, N_MP)
    g_down = arrange(d_down, inverse, N_MP)
    squares = jnp.sum(g_qkv * g_qkv) + jnp.sum(g_gateup * g_gateup) + jnp.sum(g_out * g_out)
    squares = squares + jnp.sum(g_down * g_down) + jnp.sum(d_gains * d_gains)
    grad_norm = jnp.sqrt(squares)
    factor = jnp.minimum(1.0, CLIP_LIMIT / (grad_norm + 1e-06))
    qkv_new, qkv_first_new, qkv_second_new = adam(projection_master_weight, projection_first_moment, projection_second_moment, g_qkv, factor, LEARN, WEIGHT_DECAY)
    gateup_new, gateup_first_new, gateup_second_new = adam(gateup_weight, gateup_first, gateup_second, g_gateup, factor, LEARN, WEIGHT_DECAY)
    out_new, out_first_new, out_second_new = adam(out_weight, out_first, out_second, g_out, factor, out_rate, WEIGHT_DECAY)
    down_new, down_first_new, down_second_new = adam(down_weight, down_first, down_second, g_down, factor, LEARN, WEIGHT_DECAY)
    gains_new, gain_first_new, gain_second_new = adam(gains, gain_first, gain_second, d_gains, factor, GAIN_LEARN, 0.0)
    return (attention_result.astype(jnp.bfloat16), d_input, qkv_new, gateup_new, out_new, down_new, qkv_first_new, gateup_first_new, out_first_new, down_first_new, qkv_second_new, gateup_second_new, out_second_new, down_second_new, gains_new, gain_first_new, gain_second_new, grad_norm)
```

```python
import jax
import jax.numpy as jnp
from jax import lax
from jax.sharding import PartitionSpec as P

MODEL_WIDTH = 2048
QUERY_HEADS = 16
KEY_VALUE_HEADS = 8
HEAD_SIZE = 128
FF = 6144
STEP = 10


EPS_NORM = 1e-06
THETA = 1000000.0
LEARN = 0.03
GAIN_LEARN = 0.5
FIRST_DECAY = 0.9
SECOND_DECAY = 0.95
ADAM_EPS = 1e-08
WEIGHT_DECAY = 0.1
CLIP_LIMIT = 1.0
MASKED = -1e30


def rms_norm(value_rows, gain):
    return (
        value_rows
        * lax.rsqrt(jnp.mean(value_rows * value_rows, axis=-1, keepdims=True) + EPS_NORM)
        * gain
    )


def norm_back(value_rows, gain, grad):
    score_scale = lax.rsqrt(jnp.mean(value_rows * value_rows, axis=-1, keepdims=True) + EPS_NORM)
    normed_input = value_rows * score_scale
    d_normal = grad * gain
    d_values = score_scale * (
        d_normal - normed_input * jnp.mean(d_normal * normed_input, axis=-1, keepdims=True)
    )
    d_gain = jnp.sum((grad * normed_input).reshape(-1, value_rows.shape[-1]), axis=0)
    return (d_values, d_gain)


def turned(value_rows):
    half = value_rows.shape[-1] // 2
    return jnp.concatenate([-value_rows[..., half:], value_rows[..., :half]], axis=-1)


def rotate(value_rows, cosine, sine):
    return value_rows * cosine + turned(value_rows) * sine


def rotate_back(grad, cosine, sine):
    return grad * cosine - turned(grad * sine)


def rope_tables(lengths, count):
    ends = jnp.cumsum(lengths)
    starts = ends - lengths
    places = jnp.arange(count, dtype=jnp.int32)
    doc_of = jnp.sum((places[:, None] >= ends[None, :]).astype(jnp.int32), axis=1)
    chosen = doc_of[:, None] == jnp.arange(lengths.shape[0], dtype=jnp.int32)[None, :]
    begin = jnp.sum(jnp.where(chosen, starts[None, :], 0), axis=1)
    offset = (places - begin).astype(jnp.float32)
    half = HEAD_SIZE // 2
    freq = THETA ** (-(2.0 * jnp.arange(half, dtype=jnp.float32)) / HEAD_SIZE)
    angle = offset[:, None] * freq[None, :]
    angle = jnp.concatenate([angle, angle], axis=-1)
    return (doc_of, jnp.cos(angle), jnp.sin(angle))


def arrange(gathered, order, blocks_count):
    blocks = gathered.reshape(blocks_count, gathered.shape[0] // blocks_count, gathered.shape[1])
    return jnp.take(blocks, order, axis=0).reshape(gathered.shape)


def fetch_weights(
    projection_master_weight, gateup_weight, out_weight, down_weight, owner, blocks_count
):
    gathered = (
        lax.all_gather(projection_master_weight.astype(jnp.bfloat16), "dp", axis=0, tiled=True),
        lax.all_gather(gateup_weight.astype(jnp.bfloat16), "dp", axis=0, tiled=True),
        lax.all_gather(out_weight.astype(jnp.bfloat16), "dp", axis=0, tiled=True),
        lax.all_gather(down_weight.astype(jnp.bfloat16), "dp", axis=0, tiled=True),
    )
    return tuple((arrange(piece, owner, blocks_count) for piece in gathered))


def fetch_again(
    projection_master_weight, gateup_weight, out_weight, down_weight, owner, blocks_count
):
    gathered = (
        lax.all_gather(projection_master_weight.astype(jnp.bfloat16), "dp", axis=0, tiled=True),
        lax.all_gather(gateup_weight.astype(jnp.bfloat16), "dp", axis=0, tiled=True),
        lax.all_gather(out_weight.astype(jnp.bfloat16), "dp", axis=0, tiled=True),
        lax.all_gather(down_weight.astype(jnp.bfloat16), "dp", axis=0, tiled=True),
    )
    return tuple((arrange(piece, owner, blocks_count) for piece in gathered))


def collect(rows):
    return lax.all_gather(rows, "mp", axis=0, tiled=True)


def collect_back(rows):
    return lax.all_gather(rows, "mp", axis=0, tiled=True)


def spread(operand, weight, rows):

    def term(start, count):
        return jnp.dot(operand, weight, preferred_element_type=jnp.float32)

    return lax.psum_scatter(
        term(jnp.int32(0), rows * lax.axis_size("mp")).astype(jnp.bfloat16),
        "mp",
        scatter_dimension=0,
        tiled=True,
    ).astype(jnp.float32)


def spread_back(operand, weight, rows):

    def term(start, count):
        return jnp.einsum("tc,dc->td", operand, weight, preferred_element_type=jnp.float32)

    return lax.psum_scatter(
        term(jnp.int32(0), rows * lax.axis_size("mp")).astype(jnp.bfloat16),
        "mp",
        scatter_dimension=0,
        tiled=True,
    ).astype(jnp.float32)


def adam(weight, first, second, grad, factor, rate, decay):
    clipped = grad * factor
    first_new = FIRST_DECAY * first + (1.0 - FIRST_DECAY) * clipped
    second_new = SECOND_DECAY * second + (1.0 - SECOND_DECAY) * clipped * clipped
    first_hat = first_new / (1.0 - FIRST_DECAY**STEP)
    second_hat = second_new / (1.0 - SECOND_DECAY**STEP)
    weight_new = weight * (1.0 - rate * decay) - rate * first_hat / (
        jnp.sqrt(second_hat) + ADAM_EPS
    )
    return (weight_new, first_new, second_new)


def shards_general(
    hidden_in,
    cotangent,
    doc_lengths,
    owner,
    projection_master_weight,
    gateup_weight,
    out_weight,
    down_weight,
    projection_first_moment,
    gateup_first,
    out_first,
    down_first,
    projection_second_moment,
    gateup_second,
    out_second,
    down_second,
    gains,
    gain_first,
    gain_second,
):
    total_width = lax.axis_size("mp")
    blocks_count = lax.axis_size("dp")
    heads = QUERY_HEADS // total_width
    key_value_heads = KEY_VALUE_HEADS // total_width
    query_group = heads // key_value_heads
    query_width = heads * HEAD_SIZE
    key_width = key_value_heads * HEAD_SIZE
    units = FF // total_width
    rows_here = hidden_in.shape[0]
    inverse = jnp.argsort(owner)
    out_rate = float(QUERY_HEADS * HEAD_SIZE // 32) ** (-0.5)
    w_qkv, w_gateup, w_out, w_down = fetch_weights(
        projection_master_weight, gateup_weight, out_weight, down_weight, owner, blocks_count
    )
    ln_in = gains[:MODEL_WIDTH]
    ln_mid = gains[MODEL_WIDTH : 2 * MODEL_WIDTH]
    q_gain = gains[2 * MODEL_WIDTH : 2 * MODEL_WIDTH + HEAD_SIZE]
    k_gain = gains[2 * MODEL_WIDTH + HEAD_SIZE :]
    x_rows = hidden_in.astype(jnp.float32)
    full_in = collect(rms_norm(x_rows, ln_in).astype(jnp.bfloat16))
    projected = jnp.dot(full_in, w_qkv, preferred_element_type=jnp.float32)
    count = projected.shape[0]
    doc_of, cosine, sine = rope_tables(doc_lengths[0], count)
    cosine = cosine[:, None, :]
    sine = sine[:, None, :]
    query_raw = projected[:, :query_width].reshape(count, heads, HEAD_SIZE)
    unrotated_key = projected[:, query_width : query_width + key_width].reshape(
        count, key_value_heads, HEAD_SIZE
    )
    projected_value = projected[:, query_width + key_width :].reshape(
        count, key_value_heads, HEAD_SIZE
    )
    query_rows = rotate(rms_norm(query_raw, q_gain), cosine, sine).astype(jnp.bfloat16)
    key_rows = rotate(rms_norm(unrotated_key, k_gain), cosine, sine).astype(jnp.bfloat16)
    value_rows = projected_value.astype(jnp.bfloat16)
    block = min(512, count)
    nblocks = count // block
    score_scale = HEAD_SIZE ** (-0.5)
    places = jnp.arange(count, dtype=jnp.int32)

    def scores_of(start):
        query_block = lax.dynamic_slice_in_dim(query_rows, start, block, 0).reshape(
            block, key_value_heads, query_group, HEAD_SIZE
        )
        raw = (
            jnp.einsum("tlwd,uld->lwtu", query_block, key_rows, preferred_element_type=jnp.float32)
            * score_scale
        )
        row_doc = lax.dynamic_slice_in_dim(doc_of, start, block, 0)
        row_place = start + jnp.arange(block, dtype=jnp.int32)
        allowed = (row_doc[:, None] == doc_of[None, :]) & (places[None, :] <= row_place[:, None])
        return (jnp.where(allowed[None, None], raw, MASKED), query_block)

    def forward_block(index):
        score_matrix, query_block = scores_of(index * block)
        top = jnp.max(score_matrix, axis=-1, keepdims=True)
        total = jnp.log(jnp.sum(jnp.exp(score_matrix - top), axis=-1, keepdims=True)) + top
        probabilities = jnp.exp(score_matrix - total).astype(jnp.bfloat16)
        attention_result = jnp.einsum(
            "cpyx,xca->ycpa", probabilities, value_rows, preferred_element_type=jnp.float32
        )
        return (attention_result.reshape(block, query_width), total)

    outs, totals = lax.map(forward_block, jnp.arange(nblocks, dtype=jnp.int32))
    attn_heads = outs.reshape(count, query_width).astype(jnp.bfloat16)
    attn_rows = spread(attn_heads, w_out, rows_here)
    mixed = x_rows + attn_rows
    full_mid = collect(rms_norm(mixed, ln_mid).astype(jnp.bfloat16))
    gateup = jnp.dot(full_mid, w_gateup, preferred_element_type=jnp.float32)
    gate = gateup[:, :units]
    upper = gateup[:, units:]
    sigma = jax.nn.sigmoid(gate)
    act = (gate * sigma * upper).astype(jnp.bfloat16)
    mlp_rows = spread(act, w_down, rows_here)
    result_rows = mixed + mlp_rows
    w_qkv, w_gateup, w_out, w_down = fetch_again(
        projection_master_weight, gateup_weight, out_weight, down_weight, owner, blocks_count
    )
    grad_out = cotangent.astype(jnp.float32)
    d_branch = collect_back(grad_out.astype(jnp.bfloat16))
    g_down = jnp.einsum("tf,td->fd", act, d_branch, preferred_element_type=jnp.float32)
    d_act = jnp.einsum("td,fd->tf", d_branch, w_down, preferred_element_type=jnp.float32)
    d_upper = d_act * gate * sigma
    d_gate = d_act * upper * sigma * (1.0 + gate * (1.0 - sigma))
    d_gateup = jnp.concatenate([d_gate, d_upper], axis=1).astype(jnp.bfloat16)
    g_gateup = jnp.einsum("td,tf->df", full_mid, d_gateup, preferred_element_type=jnp.float32)
    d_mid_rows = spread_back(d_gateup, w_gateup, rows_here)
    d_mixed, g_ln_mid = norm_back(mixed, ln_mid, d_mid_rows)
    d_mixed = d_mixed + grad_out
    d_attn = collect_back(d_mixed.astype(jnp.bfloat16))
    g_out = jnp.einsum("th,td->hd", attn_heads, d_attn, preferred_element_type=jnp.float32)
    d_heads = jnp.einsum("td,hd->th", d_attn, w_out, preferred_element_type=jnp.float32).astype(
        jnp.bfloat16
    )
    d_heads = d_heads.reshape(count, key_value_heads, query_group, HEAD_SIZE)

    def backward_block(carry, index):
        d_key_sum, d_value_sum = carry
        start = index * block
        score_matrix, query_block = scores_of(start)
        probabilities = jnp.exp(score_matrix - totals[index])
        block_gradient = lax.dynamic_slice_in_dim(d_heads, start, block, 0)
        probability_gradient = jnp.einsum(
            "tlwd,uld->lwtu", block_gradient, value_rows, preferred_element_type=jnp.float32
        )
        d_value_sum = d_value_sum + jnp.einsum(
            "zxrb,rzxd->bzd",
            probabilities.astype(jnp.bfloat16),
            block_gradient,
            preferred_element_type=jnp.float32,
        )
        score_gradient = (
            probabilities
            * (
                probability_gradient
                - jnp.sum(probabilities * probability_gradient, axis=-1, keepdims=True)
            )
        ).astype(jnp.bfloat16)
        d_query = (
            jnp.einsum(
                "cpyx,xca->ycpa", score_gradient, key_rows, preferred_element_type=jnp.float32
            )
            * score_scale
        )
        d_key_sum = (
            d_key_sum
            + jnp.einsum(
                "zxrb,rzxd->bzd", score_gradient, query_block, preferred_element_type=jnp.float32
            )
            * score_scale
        )
        return ((d_key_sum, d_value_sum), d_query.reshape(block, heads, HEAD_SIZE))

    empty = jnp.zeros((count, key_value_heads, HEAD_SIZE), jnp.float32)
    (d_keys, d_values), d_queries = lax.scan(
        backward_block, (empty, empty), jnp.arange(nblocks, dtype=jnp.int32)
    )
    d_queries = d_queries.reshape(count, heads, HEAD_SIZE)
    d_query_raw, g_q = norm_back(query_raw, q_gain, rotate_back(d_queries, cosine, sine))
    d_key_raw, g_k = norm_back(unrotated_key, k_gain, rotate_back(d_keys, cosine, sine))
    d_projected = jnp.concatenate(
        [
            d_query_raw.reshape(count, query_width),
            d_key_raw.reshape(count, key_width),
            d_values.reshape(count, key_width),
        ],
        axis=1,
    ).astype(jnp.bfloat16)
    g_qkv = jnp.einsum("td,tc->dc", full_in, d_projected, preferred_element_type=jnp.float32)
    d_in_rows = spread_back(d_projected, w_qkv, rows_here)
    d_input, g_ln_in = norm_back(x_rows, ln_in, d_in_rows)
    input_grad = d_input + d_mixed
    gain_terms = jnp.concatenate([g_ln_in, g_ln_mid, g_q, g_k])
    red_qkv, red_gateup, red_out, red_down = (
        lax.psum_scatter(
            arrange(g_qkv, inverse, blocks_count).astype(jnp.bfloat16),
            "dp",
            scatter_dimension=0,
            tiled=True,
        ).astype(jnp.float32),
        lax.psum_scatter(
            arrange(g_gateup, inverse, blocks_count).astype(jnp.bfloat16),
            "dp",
            scatter_dimension=0,
            tiled=True,
        ).astype(jnp.float32),
        lax.psum_scatter(
            arrange(g_out, inverse, blocks_count).astype(jnp.bfloat16),
            "dp",
            scatter_dimension=0,
            tiled=True,
        ).astype(jnp.float32),
        lax.psum_scatter(
            arrange(g_down, inverse, blocks_count).astype(jnp.bfloat16),
            "dp",
            scatter_dimension=0,
            tiled=True,
        ).astype(jnp.float32),
    )
    squares = jnp.sum(red_qkv * red_qkv) + jnp.sum(red_gateup * red_gateup)
    squares = squares + jnp.sum(red_out * red_out) + jnp.sum(red_down * red_down)
    total_squares, gain_grad = lax.psum((squares, gain_terms), ("dp", "mp"))
    grad_norm = jnp.sqrt(total_squares + jnp.sum(gain_grad * gain_grad))
    factor = jnp.minimum(1.0, CLIP_LIMIT / (grad_norm + 1e-06))
    qkv_new, qkv_first_new, qkv_second_new = adam(
        projection_master_weight,
        projection_first_moment,
        projection_second_moment,
        red_qkv,
        factor,
        LEARN,
        WEIGHT_DECAY,
    )
    gateup_new, gateup_first_new, gateup_second_new = adam(
        gateup_weight, gateup_first, gateup_second, red_gateup, factor, LEARN, WEIGHT_DECAY
    )
    out_new, out_first_new, out_second_new = adam(
        out_weight, out_first, out_second, red_out, factor, out_rate, WEIGHT_DECAY
    )
    down_new, down_first_new, down_second_new = adam(
        down_weight, down_first, down_second, red_down, factor, LEARN, WEIGHT_DECAY
    )
    gains_new, gain_first_new, gain_second_new = adam(
        gains, gain_first, gain_second, gain_grad, factor, GAIN_LEARN, 0.0
    )
    return (
        result_rows.astype(jnp.bfloat16),
        input_grad,
        qkv_new,
        gateup_new,
        out_new,
        down_new,
        qkv_first_new,
        gateup_first_new,
        out_first_new,
        down_first_new,
        qkv_second_new,
        gateup_second_new,
        out_second_new,
        down_second_new,
        gains_new,
        gain_first_new,
        gain_second_new,
        grad_norm,
    )


def steps(move):
    pairs = []
    for index in range(32):
        y, x, c, zh, zl = (index >> 4) & 1, (index >> 3) & 1, (index >> 2) & 1, (index >> 1) & 1, index & 1
        source = move(y, x, c, zh, zl)
        if source is not None:
            sy, sx, sc, sh, sl = source
            pairs.append(((sy << 4) | (sx << 3) | (sc << 2) | (sh << 1) | sl, index))
    return pairs


OVER_X = steps(lambda y, x, c, h, l: (y, 1 - x, c, h, l))
OVER_Y = steps(lambda y, x, c, h, l: (1 - y, x, c, h, l))
OVER_C = steps(lambda y, x, c, h, l: (y, x, 1 - c, h, l))
OVER_L = steps(lambda y, x, c, h, l: (y, x, c, h, 1 - l))
TO_GROUP = (
    steps(lambda y, x, c, h, l: (y, x, h, c, l)),
    steps(lambda y, x, c, h, l: (y, x, 1 - h, c, l)),
)
FROM_GROUP = tuple([(b, a) for a, b in pairs] for pairs in TO_GROUP)
UPWARD = steps(lambda y, x, c, h, l: (y, x, c, 0, l) if h == 1 else None)
DOWNWARD = steps(lambda y, x, c, h, l: (y, x, c, 1, l) if h == 0 else None)


def move(value, pairs):
    return lax.ppermute(value, ("dp", "mp"), pairs)


def after(value, *others):
    return lax.optimization_barrier((value, *others))[0]


def gather_weight(shard):
    a = move(shard, TO_GROUP[0])
    b = move(shard, TO_GROUP[1])
    ax, ay = move(a, OVER_X), move(a, OVER_Y)
    by, bx = move(b, OVER_Y), move(b, OVER_X)
    axy, bxy = move(ax, OVER_Y), move(by, OVER_X)
    return [a, b, ax, bx, ay, by, axy, bxy]


def reduce_weight(grads):
    def plus(left, right):
        return (left.astype(jnp.float32) + right.astype(jnp.float32)).astype(jnp.bfloat16)

    a = move(jnp.stack([grads[4], grads[6]]), OVER_Y)
    b = move(jnp.stack([grads[3], grads[7]]), OVER_X)
    a_far = plus(grads[2], a[1])
    b_far = plus(grads[5], b[1])
    a_far = move(a_far, OVER_X)
    b_far = move(b_far, OVER_Y)
    a_own = plus(plus(grads[0], a[0]), a_far)
    b_own = plus(plus(grads[1], b[0]), b_far)
    return move(a_own, FROM_GROUP[0]).astype(jnp.float32) + move(b_own, FROM_GROUP[1]).astype(
        jnp.float32
    )


def gather_rows(rows):
    pair = jnp.concatenate([rows, move(rows, OVER_L)], axis=0)
    return jnp.concatenate([pair, move(pair, OVER_C)], axis=0)


def sum_rows(partial):
    half = partial.shape[0] // 2
    quarter = half // 2
    near = move(partial[half:].astype(jnp.bfloat16), OVER_C).astype(jnp.float32)
    summed = partial[:half] + near
    return summed[:quarter] + move(summed[quarter:].astype(jnp.bfloat16), OVER_L).astype(
        jnp.float32
    )


def shards_paired(
    hidden_in,
    cotangent,
    doc_lengths,
    owner,
    projection_master_weight,
    gateup_weight,
    out_weight,
    down_weight,
    projection_first_moment,
    gateup_first,
    out_first,
    down_first,
    projection_second_moment,
    gateup_second,
    out_second,
    down_second,
    gains,
    gain_first,
    gain_second,
):
    dp, mp = lax.axis_index("dp"), lax.axis_index("mp")
    core, high, low = dp % 2, mp // 2, mp % 2
    plane = (dp // 2) * 2 + high
    groups = lax.axis_size("mp")
    heads = QUERY_HEADS // groups
    key_value_heads = KEY_VALUE_HEADS // groups
    query_group = heads // key_value_heads
    query_width = heads * HEAD_SIZE
    key_width = key_value_heads * HEAD_SIZE
    units = FF // groups
    rows_here = hidden_in.shape[0]
    count = 4 * rows_here
    half = count // 2
    width = hidden_in.shape[1]
    inverse = jnp.argsort(owner)
    logical_of = jnp.take(inverse, jnp.arange(8, dtype=jnp.int32) ^ plane)
    slot_of = owner ^ plane
    out_rate = float(QUERY_HEADS * HEAD_SIZE // 32) ** (-0.5)

    def to_slots(rows):
        return jnp.take(rows.reshape(rows.shape[0], 8, -1), logical_of, axis=1).reshape(rows.shape)

    def from_slots(rows):
        return jnp.take(rows.reshape(rows.shape[0], 8, -1), slot_of, axis=1).reshape(rows.shape)

    ln_in = gains[:MODEL_WIDTH]
    ln_mid = gains[MODEL_WIDTH : 2 * MODEL_WIDTH]
    q_gain = gains[2 * MODEL_WIDTH : 2 * MODEL_WIDTH + HEAD_SIZE]
    k_gain = gains[2 * MODEL_WIDTH + HEAD_SIZE :]
    x_rows = hidden_in.astype(jnp.float32)
    full_in = gather_rows(to_slots(rms_norm(x_rows, ln_in).astype(jnp.bfloat16)))

    qkv_blocks = gather_weight(projection_master_weight.astype(jnp.bfloat16))
    w_qkv = jnp.concatenate(qkv_blocks, axis=0)
    out_blocks = gather_weight(out_weight.astype(jnp.bfloat16))
    w_out = jnp.take(jnp.stack(out_blocks), slot_of, axis=0).reshape(-1, width)
    gateup_blocks = gather_weight(gateup_weight.astype(jnp.bfloat16))
    w_gateup = jnp.concatenate(gateup_blocks, axis=0)
    down_blocks = gather_weight(down_weight.astype(jnp.bfloat16))
    w_down = jnp.take(jnp.stack(down_blocks), slot_of, axis=0).reshape(-1, width)

    grad_out = cotangent.astype(jnp.float32)
    d_branch = gather_rows(cotangent)

    lengths = jnp.concatenate([doc_lengths, move(doc_lengths, OVER_C)], axis=0)
    ends = jnp.cumsum(lengths, axis=1)
    spot = jnp.arange(half, dtype=jnp.int32)
    chunk = spot // rows_here
    own_places = high * half + (low ^ chunk) * rows_here + spot % rows_here
    key_places = jnp.concatenate([own_places - half, own_places])

    def documents(places):
        return jnp.sum((places[None, :, None] >= ends[:, None, :]).astype(jnp.int32), axis=2)

    doc_of = documents(own_places)
    key_doc = jnp.where(key_places[None, :] >= 0, documents(key_places), -1)
    chosen = doc_of[:, :, None] == jnp.arange(lengths.shape[1], dtype=jnp.int32)[None, None, :]
    begin = jnp.sum(jnp.where(chosen, (ends - lengths)[:, None, :], 0), axis=2)
    offset = (own_places[None, :] - begin).astype(jnp.float32).reshape(count)
    freq = THETA ** (
        -(2.0 * jnp.arange(HEAD_SIZE // 2, dtype=jnp.float32)) / HEAD_SIZE
    )
    angle = offset[:, None] * freq[None, :]
    cosine, sine = jnp.cos(angle), jnp.sin(angle)
    cosine = jnp.concatenate([cosine, cosine], axis=-1)[:, None, :]
    sine = jnp.concatenate([sine, sine], axis=-1)[:, None, :]

    projected = jnp.dot(full_in, w_qkv, preferred_element_type=jnp.float32)
    query_raw = projected[:, :query_width].reshape(count, heads, HEAD_SIZE)
    unrotated_key = projected[:, query_width : query_width + key_width].reshape(
        count, key_value_heads, HEAD_SIZE
    )
    query_rows = rotate(rms_norm(query_raw, q_gain), cosine, sine).astype(jnp.bfloat16)
    key_rows = rotate(rms_norm(unrotated_key, k_gain), cosine, sine).astype(jnp.bfloat16)
    key_rows = key_rows.reshape(count, key_width)
    value_rows = projected[:, query_width + key_width :].astype(jnp.bfloat16)
    own_kv = jnp.concatenate([key_rows, value_rows], axis=1)
    lower_kv = move(own_kv, UPWARD)
    all_kv = jnp.concatenate(
        [lower_kv.reshape(2, half, 2 * key_width), own_kv.reshape(2, half, 2 * key_width)], axis=1
    )
    keys = all_kv[:, :, :key_width].reshape(2, count, key_value_heads, HEAD_SIZE)
    values = all_kv[:, :, key_width:].reshape(2, count, key_value_heads, HEAD_SIZE)
    queries = query_rows.reshape(2, half, key_value_heads, query_group, HEAD_SIZE)
    score_scale = HEAD_SIZE ** (-0.5)

    def scores_of(part):
        query_block, key_block, row_doc, col_doc = part
        raw = (
            jnp.einsum("tlwd,uld->lwtu", query_block, key_block, preferred_element_type=jnp.float32)
            * score_scale
        )
        allowed = (row_doc[:, None] == col_doc[None, :]) & (
            key_places[None, :] <= own_places[:, None]
        )
        return jnp.where(allowed[None, None], raw, MASKED)

    def forward_part(parts):
        query_block, key_block, value_block, row_doc, col_doc = parts
        score_matrix = scores_of((query_block, key_block, row_doc, col_doc))
        top = jnp.max(score_matrix, axis=-1, keepdims=True)
        total = jnp.log(jnp.sum(jnp.exp(score_matrix - top), axis=-1, keepdims=True)) + top
        probabilities = jnp.exp(score_matrix - total).astype(jnp.bfloat16)
        attention_result = jnp.einsum(
            "cpyx,xca->ycpa", probabilities, value_block, preferred_element_type=jnp.float32
        )
        return (attention_result.reshape(half, query_width).astype(jnp.bfloat16), total)

    outs, totals = lax.map(forward_part, (queries, keys, values, doc_of, key_doc))
    attn_heads = outs.reshape(count, query_width)
    mixed = x_rows + sum_rows(jnp.dot(attn_heads, w_out, preferred_element_type=jnp.float32))
    full_mid = gather_rows(to_slots(rms_norm(mixed, ln_mid).astype(jnp.bfloat16)))
    gateup = jnp.dot(full_mid, w_gateup, preferred_element_type=jnp.float32)
    gate = gateup[:, :units]
    upper = gateup[:, units:]
    sigma = jax.nn.sigmoid(gate)
    act = (gate * sigma * upper).astype(jnp.bfloat16)
    result_rows = mixed + sum_rows(jnp.dot(act, w_down, preferred_element_type=jnp.float32))

    g_down = jnp.einsum("tf,td->fd", act, d_branch, preferred_element_type=jnp.float32)
    g_down = jnp.take(g_down.astype(jnp.bfloat16).reshape(8, -1, width), logical_of, axis=0)
    red_down = reduce_weight(g_down)
    d_act = jnp.einsum("td,fd->tf", d_branch, w_down, preferred_element_type=jnp.float32)
    d_upper = d_act * gate * sigma
    d_gate = d_act * upper * sigma * (1.0 + gate * (1.0 - sigma))
    d_gateup = jnp.concatenate([d_gate, d_upper], axis=1).astype(jnp.bfloat16)
    g_gateup = jnp.einsum("td,tf->df", full_mid, d_gateup, preferred_element_type=jnp.float32)
    red_gateup = reduce_weight(g_gateup.astype(jnp.bfloat16).reshape(8, -1, 2 * units))
    d_mid_rows = from_slots(
        sum_rows(jnp.einsum("tc,dc->td", d_gateup, w_gateup, preferred_element_type=jnp.float32))
    )
    d_mixed, g_ln_mid = norm_back(mixed, ln_mid, d_mid_rows)
    d_mixed = d_mixed + grad_out
    d_attn = gather_rows(d_mixed.astype(jnp.bfloat16))
    g_out = jnp.einsum("th,td->hd", attn_heads, d_attn, preferred_element_type=jnp.float32)
    g_out = jnp.take(g_out.astype(jnp.bfloat16).reshape(8, -1, width), logical_of, axis=0)
    red_out = reduce_weight(g_out)
    d_heads = jnp.einsum("td,hd->th", d_attn, w_out, preferred_element_type=jnp.float32).astype(
        jnp.bfloat16
    )
    d_heads = d_heads.reshape(2, half, key_value_heads, query_group, HEAD_SIZE)

    def backward_part(parts):
        query_block, key_block, value_block, row_doc, col_doc, block_total, block_gradient = parts
        score_matrix = scores_of((query_block, key_block, row_doc, col_doc))
        probabilities = jnp.exp(score_matrix - block_total)
        probability_gradient = jnp.einsum(
            "tlwd,uld->lwtu", block_gradient, value_block, preferred_element_type=jnp.float32
        )
        d_value = jnp.einsum(
            "zxrb,rzxd->bzd",
            probabilities.astype(jnp.bfloat16),
            block_gradient,
            preferred_element_type=jnp.float32,
        )
        score_gradient = (
            probabilities
            * (
                probability_gradient
                - jnp.sum(probabilities * probability_gradient, axis=-1, keepdims=True)
            )
        ).astype(jnp.bfloat16)
        d_query = (
            jnp.einsum(
                "cpyx,xca->ycpa", score_gradient, key_block, preferred_element_type=jnp.float32
            )
            * score_scale
        )
        d_key = (
            jnp.einsum(
                "zxrb,rzxd->bzd", score_gradient, query_block, preferred_element_type=jnp.float32
            )
            * score_scale
        )
        d_kv = jnp.concatenate([d_key.reshape(count, key_width), d_value.reshape(count, key_width)], axis=1)
        return (d_query.reshape(half, query_width), d_kv)

    d_queries, d_kv = lax.map(
        backward_part, (queries, keys, values, doc_of, key_doc, totals, d_heads)
    )
    from_above = move(d_kv[:, :half].astype(jnp.bfloat16), DOWNWARD)
    d_kv = (d_kv[:, half:] + from_above.astype(jnp.float32)).reshape(count, 2 * key_width)
    d_queries = d_queries.reshape(count, heads, HEAD_SIZE)
    d_keys = d_kv[:, :key_width].reshape(count, key_value_heads, HEAD_SIZE)
    d_query_raw, g_q = norm_back(query_raw, q_gain, rotate_back(d_queries, cosine, sine))
    d_key_raw, g_k = norm_back(unrotated_key, k_gain, rotate_back(d_keys, cosine, sine))
    d_projected = jnp.concatenate(
        [
            d_query_raw.reshape(count, query_width),
            d_key_raw.reshape(count, key_width),
            d_kv[:, key_width:],
        ],
        axis=1,
    ).astype(jnp.bfloat16)
    g_qkv = jnp.einsum("td,tc->dc", full_in, d_projected, preferred_element_type=jnp.float32)
    red_qkv = reduce_weight(g_qkv.astype(jnp.bfloat16).reshape(8, width // 8, -1))
    d_in_rows = from_slots(
        sum_rows(jnp.einsum("tc,dc->td", d_projected, w_qkv, preferred_element_type=jnp.float32))
    )
    d_input, g_ln_in = norm_back(x_rows, ln_in, d_in_rows)
    input_grad = d_input + d_mixed
    gain_terms = jnp.concatenate([g_ln_in, g_ln_mid, g_q, g_k])
    squares = jnp.sum(red_qkv * red_qkv) + jnp.sum(red_gateup * red_gateup)
    squares = squares + jnp.sum(red_out * red_out) + jnp.sum(red_down * red_down)
    total_squares, gain_grad = lax.psum((squares, gain_terms), ("dp", "mp"))
    grad_norm = jnp.sqrt(total_squares + jnp.sum(gain_grad * gain_grad))
    factor = jnp.minimum(1.0, CLIP_LIMIT / (grad_norm + 1e-06))
    qkv_new, qkv_first_new, qkv_second_new = adam(
        projection_master_weight,
        projection_first_moment,
        projection_second_moment,
        red_qkv,
        factor,
        LEARN,
        WEIGHT_DECAY,
    )
    gateup_new, gateup_first_new, gateup_second_new = adam(
        gateup_weight, gateup_first, gateup_second, red_gateup, factor, LEARN, WEIGHT_DECAY
    )
    out_new, out_first_new, out_second_new = adam(
        out_weight, out_first, out_second, red_out, factor, out_rate, WEIGHT_DECAY
    )
    down_new, down_first_new, down_second_new = adam(
        down_weight, down_first, down_second, red_down, factor, LEARN, WEIGHT_DECAY
    )
    gains_new, gain_first_new, gain_second_new = adam(
        gains, gain_first, gain_second, gain_grad, factor, GAIN_LEARN, 0.0
    )
    return (
        result_rows.astype(jnp.bfloat16),
        input_grad,
        qkv_new,
        gateup_new,
        out_new,
        down_new,
        qkv_first_new,
        gateup_first_new,
        out_first_new,
        down_first_new,
        qkv_second_new,
        gateup_second_new,
        out_second_new,
        down_second_new,
        gains_new,
        gain_first_new,
        gain_second_new,
        grad_norm,
    )


def paired(mesh):
    return dict(mesh.shape) == {"dp": 8, "mp": 4}


def solution(mesh):
    placed = (
        P(("dp", "mp"), None),
        P(("dp", "mp"), None),
        P("dp", None),
        P(),
        P("dp", "mp"),
        P("dp", "mp"),
        P(("mp", "dp"), None),
        P(("mp", "dp"), None),
        P("dp", "mp"),
        P("dp", "mp"),
        P(("mp", "dp"), None),
        P(("mp", "dp"), None),
        P("dp", "mp"),
        P("dp", "mp"),
        P(("mp", "dp"), None),
        P(("mp", "dp"), None),
        P(),
        P(),
        P(),
    )
    return jax.shard_map(
        shards_paired if paired(mesh) else shards_general,
        mesh=mesh,
        in_specs=placed,
        out_specs=(
            P(("dp", "mp"), None),
            P(("dp", "mp"), None),
            P("dp", "mp"),
            P("dp", "mp"),
            P(("mp", "dp"), None),
            P(("mp", "dp"), None),
            P("dp", "mp"),
            P("dp", "mp"),
            P(("mp", "dp"), None),
            P(("mp", "dp"), None),
            P("dp", "mp"),
            P("dp", "mp"),
            P(("mp", "dp"), None),
            P(("mp", "dp"), None),
            P(),
            P(),
            P(),
            P(),
        ),
        check_vma=False,
    )
```

```python
import jax
import jax.numpy as jnp
from jax import lax
from jax.experimental import pallas as pl
from jax.experimental.pallas import tpu as pltpu
from jax.sharding import PartitionSpec as P

MODEL_WIDTH = 2048
QUERY_HEADS = 16
KEY_VALUE_HEADS = 8
HEAD_SIZE = 128
FF = 6144
STEP = 10


EPS_NORM = 1e-06
THETA = 1000000.0
LEARN = 0.03
GAIN_LEARN = 0.5
FIRST_DECAY = 0.9
SECOND_DECAY = 0.95
ADAM_EPS = 1e-08
WEIGHT_DECAY = 0.1
CLIP_LIMIT = 1.0
MASKED = -1e30


def rms_norm(value_rows, gain):
    return (
        value_rows
        * lax.rsqrt(jnp.mean(value_rows * value_rows, axis=-1, keepdims=True) + EPS_NORM)
        * gain
    )


def norm_back(value_rows, gain, grad):
    score_scale = lax.rsqrt(jnp.mean(value_rows * value_rows, axis=-1, keepdims=True) + EPS_NORM)
    normed_input = value_rows * score_scale
    d_normal = grad * gain
    d_values = score_scale * (
        d_normal - normed_input * jnp.mean(d_normal * normed_input, axis=-1, keepdims=True)
    )
    d_gain = jnp.sum((grad * normed_input).reshape(-1, value_rows.shape[-1]), axis=0)
    return (d_values, d_gain)


def turned(value_rows):
    half = value_rows.shape[-1] // 2
    return jnp.concatenate([-value_rows[..., half:], value_rows[..., :half]], axis=-1)


def rotate(value_rows, cosine, sine):
    return value_rows * cosine + turned(value_rows) * sine


def rotate_back(grad, cosine, sine):
    return grad * cosine - turned(grad * sine)


def rope_tables(lengths, count):
    ends = jnp.cumsum(lengths)
    starts = ends - lengths
    places = jnp.arange(count, dtype=jnp.int32)
    doc_of = jnp.sum((places[:, None] >= ends[None, :]).astype(jnp.int32), axis=1)
    chosen = doc_of[:, None] == jnp.arange(lengths.shape[0], dtype=jnp.int32)[None, :]
    begin = jnp.sum(jnp.where(chosen, starts[None, :], 0), axis=1)
    offset = (places - begin).astype(jnp.float32)
    half = HEAD_SIZE // 2
    freq = THETA ** (-(2.0 * jnp.arange(half, dtype=jnp.float32)) / HEAD_SIZE)
    angle = offset[:, None] * freq[None, :]
    angle = jnp.concatenate([angle, angle], axis=-1)
    return (doc_of, jnp.cos(angle), jnp.sin(angle))


def arrange(gathered, order, blocks_count):
    blocks = gathered.reshape(blocks_count, gathered.shape[0] // blocks_count, gathered.shape[1])
    return jnp.take(blocks, order, axis=0).reshape(gathered.shape)


def fetch_weights(
    projection_master_weight, gateup_weight, out_weight, down_weight, owner, blocks_count
):
    gathered = (
        lax.all_gather(projection_master_weight.astype(jnp.bfloat16), "dp", axis=0, tiled=True),
        lax.all_gather(gateup_weight.astype(jnp.bfloat16), "dp", axis=0, tiled=True),
        lax.all_gather(out_weight.astype(jnp.bfloat16), "dp", axis=0, tiled=True),
        lax.all_gather(down_weight.astype(jnp.bfloat16), "dp", axis=0, tiled=True),
    )
    return tuple((arrange(piece, owner, blocks_count) for piece in gathered))


def fetch_again(
    projection_master_weight, gateup_weight, out_weight, down_weight, owner, blocks_count
):
    gathered = (
        lax.all_gather(projection_master_weight.astype(jnp.bfloat16), "dp", axis=0, tiled=True),
        lax.all_gather(gateup_weight.astype(jnp.bfloat16), "dp", axis=0, tiled=True),
        lax.all_gather(out_weight.astype(jnp.bfloat16), "dp", axis=0, tiled=True),
        lax.all_gather(down_weight.astype(jnp.bfloat16), "dp", axis=0, tiled=True),
    )
    return tuple((arrange(piece, owner, blocks_count) for piece in gathered))


def collect(rows):
    return lax.all_gather(rows, "mp", axis=0, tiled=True)


def collect_back(rows):
    return lax.all_gather(rows, "mp", axis=0, tiled=True)


def spread(operand, weight, rows):

    def term(start, count):
        return jnp.dot(operand, weight, preferred_element_type=jnp.float32)

    return lax.psum_scatter(
        term(jnp.int32(0), rows * lax.axis_size("mp")).astype(jnp.bfloat16),
        "mp",
        scatter_dimension=0,
        tiled=True,
    ).astype(jnp.float32)


def spread_back(operand, weight, rows):

    def term(start, count):
        return jnp.einsum("tc,dc->td", operand, weight, preferred_element_type=jnp.float32)

    return lax.psum_scatter(
        term(jnp.int32(0), rows * lax.axis_size("mp")).astype(jnp.bfloat16),
        "mp",
        scatter_dimension=0,
        tiled=True,
    ).astype(jnp.float32)


def adam(weight, first, second, grad, factor, rate, decay):
    clipped = grad * factor
    first_new = FIRST_DECAY * first + (1.0 - FIRST_DECAY) * clipped
    second_new = SECOND_DECAY * second + (1.0 - SECOND_DECAY) * clipped * clipped
    first_hat = first_new / (1.0 - FIRST_DECAY**STEP)
    second_hat = second_new / (1.0 - SECOND_DECAY**STEP)
    weight_new = weight * (1.0 - rate * decay) - rate * first_hat / (
        jnp.sqrt(second_hat) + ADAM_EPS
    )
    return (weight_new, first_new, second_new)


def shards_general(
    hidden_in,
    cotangent,
    doc_lengths,
    owner,
    projection_master_weight,
    gateup_weight,
    out_weight,
    down_weight,
    projection_first_moment,
    gateup_first,
    out_first,
    down_first,
    projection_second_moment,
    gateup_second,
    out_second,
    down_second,
    gains,
    gain_first,
    gain_second,
):
    total_width = lax.axis_size("mp")
    blocks_count = lax.axis_size("dp")
    heads = QUERY_HEADS // total_width
    key_value_heads = KEY_VALUE_HEADS // total_width
    query_group = heads // key_value_heads
    query_width = heads * HEAD_SIZE
    key_width = key_value_heads * HEAD_SIZE
    units = FF // total_width
    rows_here = hidden_in.shape[0]
    inverse = jnp.argsort(owner)
    out_rate = float(QUERY_HEADS * HEAD_SIZE // 32) ** (-0.5)
    w_qkv, w_gateup, w_out, w_down = fetch_weights(
        projection_master_weight, gateup_weight, out_weight, down_weight, owner, blocks_count
    )
    ln_in = gains[:MODEL_WIDTH]
    ln_mid = gains[MODEL_WIDTH : 2 * MODEL_WIDTH]
    q_gain = gains[2 * MODEL_WIDTH : 2 * MODEL_WIDTH + HEAD_SIZE]
    k_gain = gains[2 * MODEL_WIDTH + HEAD_SIZE :]
    x_rows = hidden_in.astype(jnp.float32)
    full_in = collect(rms_norm(x_rows, ln_in).astype(jnp.bfloat16))
    projected = jnp.dot(full_in, w_qkv, preferred_element_type=jnp.float32)
    count = projected.shape[0]
    doc_of, cosine, sine = rope_tables(doc_lengths[0], count)
    cosine = cosine[:, None, :]
    sine = sine[:, None, :]
    query_raw = projected[:, :query_width].reshape(count, heads, HEAD_SIZE)
    unrotated_key = projected[:, query_width : query_width + key_width].reshape(
        count, key_value_heads, HEAD_SIZE
    )
    projected_value = projected[:, query_width + key_width :].reshape(
        count, key_value_heads, HEAD_SIZE
    )
    query_rows = rotate(rms_norm(query_raw, q_gain), cosine, sine).astype(jnp.bfloat16)
    key_rows = rotate(rms_norm(unrotated_key, k_gain), cosine, sine).astype(jnp.bfloat16)
    value_rows = projected_value.astype(jnp.bfloat16)
    block = min(512, count)
    nblocks = count // block
    score_scale = HEAD_SIZE ** (-0.5)
    places = jnp.arange(count, dtype=jnp.int32)

    def scores_of(start):
        query_block = lax.dynamic_slice_in_dim(query_rows, start, block, 0).reshape(
            block, key_value_heads, query_group, HEAD_SIZE
        )
        raw = (
            jnp.einsum("tlwd,uld->lwtu", query_block, key_rows, preferred_element_type=jnp.float32)
            * score_scale
        )
        row_doc = lax.dynamic_slice_in_dim(doc_of, start, block, 0)
        row_place = start + jnp.arange(block, dtype=jnp.int32)
        allowed = (row_doc[:, None] == doc_of[None, :]) & (places[None, :] <= row_place[:, None])
        return (jnp.where(allowed[None, None], raw, MASKED), query_block)

    def forward_block(index):
        score_matrix, query_block = scores_of(index * block)
        top = jnp.max(score_matrix, axis=-1, keepdims=True)
        total = jnp.log(jnp.sum(jnp.exp(score_matrix - top), axis=-1, keepdims=True)) + top
        probabilities = jnp.exp(score_matrix - total).astype(jnp.bfloat16)
        attention_result = jnp.einsum(
            "cpyx,xca->ycpa", probabilities, value_rows, preferred_element_type=jnp.float32
        )
        return (attention_result.reshape(block, query_width), total)

    outs, totals = lax.map(forward_block, jnp.arange(nblocks, dtype=jnp.int32))
    attn_heads = outs.reshape(count, query_width).astype(jnp.bfloat16)
    attn_rows = spread(attn_heads, w_out, rows_here)
    mixed = x_rows + attn_rows
    full_mid = collect(rms_norm(mixed, ln_mid).astype(jnp.bfloat16))
    gateup = jnp.dot(full_mid, w_gateup, preferred_element_type=jnp.float32)
    gate = gateup[:, :units]
    upper = gateup[:, units:]
    sigma = jax.nn.sigmoid(gate)
    act = (gate * sigma * upper).astype(jnp.bfloat16)
    mlp_rows = spread(act, w_down, rows_here)
    result_rows = mixed + mlp_rows
    w_qkv, w_gateup, w_out, w_down = fetch_again(
        projection_master_weight, gateup_weight, out_weight, down_weight, owner, blocks_count
    )
    grad_out = cotangent.astype(jnp.float32)
    d_branch = collect_back(grad_out.astype(jnp.bfloat16))
    g_down = jnp.einsum("tf,td->fd", act, d_branch, preferred_element_type=jnp.float32)
    d_act = jnp.einsum("td,fd->tf", d_branch, w_down, preferred_element_type=jnp.float32)
    d_upper = d_act * gate * sigma
    d_gate = d_act * upper * sigma * (1.0 + gate * (1.0 - sigma))
    d_gateup = jnp.concatenate([d_gate, d_upper], axis=1).astype(jnp.bfloat16)
    g_gateup = jnp.einsum("td,tf->df", full_mid, d_gateup, preferred_element_type=jnp.float32)
    d_mid_rows = spread_back(d_gateup, w_gateup, rows_here)
    d_mixed, g_ln_mid = norm_back(mixed, ln_mid, d_mid_rows)
    d_mixed = d_mixed + grad_out
    d_attn = collect_back(d_mixed.astype(jnp.bfloat16))
    g_out = jnp.einsum("th,td->hd", attn_heads, d_attn, preferred_element_type=jnp.float32)
    d_heads = jnp.einsum("td,hd->th", d_attn, w_out, preferred_element_type=jnp.float32).astype(
        jnp.bfloat16
    )
    d_heads = d_heads.reshape(count, key_value_heads, query_group, HEAD_SIZE)

    def backward_block(carry, index):
        d_key_sum, d_value_sum = carry
        start = index * block
        score_matrix, query_block = scores_of(start)
        probabilities = jnp.exp(score_matrix - totals[index])
        block_gradient = lax.dynamic_slice_in_dim(d_heads, start, block, 0)
        probability_gradient = jnp.einsum(
            "tlwd,uld->lwtu", block_gradient, value_rows, preferred_element_type=jnp.float32
        )
        d_value_sum = d_value_sum + jnp.einsum(
            "zxrb,rzxd->bzd",
            probabilities.astype(jnp.bfloat16),
            block_gradient,
            preferred_element_type=jnp.float32,
        )
        score_gradient = (
            probabilities
            * (
                probability_gradient
                - jnp.sum(probabilities * probability_gradient, axis=-1, keepdims=True)
            )
        ).astype(jnp.bfloat16)
        d_query = (
            jnp.einsum(
                "cpyx,xca->ycpa", score_gradient, key_rows, preferred_element_type=jnp.float32
            )
            * score_scale
        )
        d_key_sum = (
            d_key_sum
            + jnp.einsum(
                "zxrb,rzxd->bzd", score_gradient, query_block, preferred_element_type=jnp.float32
            )
            * score_scale
        )
        return ((d_key_sum, d_value_sum), d_query.reshape(block, heads, HEAD_SIZE))

    empty = jnp.zeros((count, key_value_heads, HEAD_SIZE), jnp.float32)
    (d_keys, d_values), d_queries = lax.scan(
        backward_block, (empty, empty), jnp.arange(nblocks, dtype=jnp.int32)
    )
    d_queries = d_queries.reshape(count, heads, HEAD_SIZE)
    d_query_raw, g_q = norm_back(query_raw, q_gain, rotate_back(d_queries, cosine, sine))
    d_key_raw, g_k = norm_back(unrotated_key, k_gain, rotate_back(d_keys, cosine, sine))
    d_projected = jnp.concatenate(
        [
            d_query_raw.reshape(count, query_width),
            d_key_raw.reshape(count, key_width),
            d_values.reshape(count, key_width),
        ],
        axis=1,
    ).astype(jnp.bfloat16)
    g_qkv = jnp.einsum("td,tc->dc", full_in, d_projected, preferred_element_type=jnp.float32)
    d_in_rows = spread_back(d_projected, w_qkv, rows_here)
    d_input, g_ln_in = norm_back(x_rows, ln_in, d_in_rows)
    input_grad = d_input + d_mixed
    gain_terms = jnp.concatenate([g_ln_in, g_ln_mid, g_q, g_k])
    red_qkv, red_gateup, red_out, red_down = (
        lax.psum_scatter(
            arrange(g_qkv, inverse, blocks_count).astype(jnp.bfloat16),
            "dp",
            scatter_dimension=0,
            tiled=True,
        ).astype(jnp.float32),
        lax.psum_scatter(
            arrange(g_gateup, inverse, blocks_count).astype(jnp.bfloat16),
            "dp",
            scatter_dimension=0,
            tiled=True,
        ).astype(jnp.float32),
        lax.psum_scatter(
            arrange(g_out, inverse, blocks_count).astype(jnp.bfloat16),
            "dp",
            scatter_dimension=0,
            tiled=True,
        ).astype(jnp.float32),
        lax.psum_scatter(
            arrange(g_down, inverse, blocks_count).astype(jnp.bfloat16),
            "dp",
            scatter_dimension=0,
            tiled=True,
        ).astype(jnp.float32),
    )
    squares = jnp.sum(red_qkv * red_qkv) + jnp.sum(red_gateup * red_gateup)
    squares = squares + jnp.sum(red_out * red_out) + jnp.sum(red_down * red_down)
    total_squares, gain_grad = lax.psum((squares, gain_terms), ("dp", "mp"))
    grad_norm = jnp.sqrt(total_squares + jnp.sum(gain_grad * gain_grad))
    factor = jnp.minimum(1.0, CLIP_LIMIT / (grad_norm + 1e-06))
    qkv_new, qkv_first_new, qkv_second_new = adam(
        projection_master_weight,
        projection_first_moment,
        projection_second_moment,
        red_qkv,
        factor,
        LEARN,
        WEIGHT_DECAY,
    )
    gateup_new, gateup_first_new, gateup_second_new = adam(
        gateup_weight, gateup_first, gateup_second, red_gateup, factor, LEARN, WEIGHT_DECAY
    )
    out_new, out_first_new, out_second_new = adam(
        out_weight, out_first, out_second, red_out, factor, out_rate, WEIGHT_DECAY
    )
    down_new, down_first_new, down_second_new = adam(
        down_weight, down_first, down_second, red_down, factor, LEARN, WEIGHT_DECAY
    )
    gains_new, gain_first_new, gain_second_new = adam(
        gains, gain_first, gain_second, gain_grad, factor, GAIN_LEARN, 0.0
    )
    return (
        result_rows.astype(jnp.bfloat16),
        input_grad,
        qkv_new,
        gateup_new,
        out_new,
        down_new,
        qkv_first_new,
        gateup_first_new,
        out_first_new,
        down_first_new,
        qkv_second_new,
        gateup_second_new,
        out_second_new,
        down_second_new,
        gains_new,
        gain_first_new,
        gain_second_new,
        grad_norm,
    )


def steps(move):
    pairs = []
    for index in range(32):
        y, x, c, zh, zl = (index >> 4) & 1, (index >> 3) & 1, (index >> 2) & 1, (index >> 1) & 1, index & 1
        source = move(y, x, c, zh, zl)
        if source is not None:
            sy, sx, sc, sh, sl = source
            pairs.append(((sy << 4) | (sx << 3) | (sc << 2) | (sh << 1) | sl, index))
    return pairs


OVER_X = steps(lambda y, x, c, h, l: (y, 1 - x, c, h, l))
OVER_Y = steps(lambda y, x, c, h, l: (1 - y, x, c, h, l))
OVER_C = steps(lambda y, x, c, h, l: (y, x, 1 - c, h, l))
OVER_L = steps(lambda y, x, c, h, l: (y, x, c, h, 1 - l))
TO_GROUP = (
    steps(lambda y, x, c, h, l: (y, x, h, c, l)),
    steps(lambda y, x, c, h, l: (y, x, 1 - h, c, l)),
)
FROM_GROUP = tuple([(b, a) for a, b in pairs] for pairs in TO_GROUP)
UPWARD = steps(lambda y, x, c, h, l: (y, x, c, 0, l) if h == 1 else None)
DOWNWARD = steps(lambda y, x, c, h, l: (y, x, c, 1, l) if h == 0 else None)


def move(value, pairs):
    return lax.ppermute(value, ("dp", "mp"), pairs)


def after(value, *others):
    return lax.optimization_barrier((value, *others))[0]


PLANES = [[(block * 2 + c) * 4 + z for block in range(4)] for c in range(2) for z in range(4)]


MESH = pl.DeviceIdType.MESH


class Place:
    def __init__(self):
        dp, mp = lax.axis_index("dp"), lax.axis_index("mp")
        self.y, self.x, self.c = dp // 4, (dp // 2) % 2, dp % 2
        self.h, self.l = mp // 2, mp % 2
        self.block = (dp // 2) * 2

    def at(self, y=None, x=None, c=None, h=None, l=None):
        y, x, c = (o if n is None else n for o, n in ((self.y, y), (self.x, x), (self.c, c)))
        h, l = (o if n is None else n for o, n in ((self.h, h), (self.l, l)))
        return ((y * 2 + x) * 2 + c, h * 2 + l)

    def partners(self):
        return [
            self.at(x=1 - self.x),
            self.at(y=1 - self.y),
            self.at(l=1 - self.l),
            self.at(c=1 - self.c),
            self.at(h=1 - self.h),
            self.at(c=1 - self.c, h=1 - self.h),
        ]


def far_copy(source, target, sems, index, device):
    return pltpu.make_async_remote_copy(
        src_ref=source,
        dst_ref=target,
        send_sem=sems[0].at[index],
        recv_sem=sems[1].at[index],
        device_id=device,
        device_id_type=MESH,
    )


class Swap:
    def __init__(self, place, source, target, sems, index, local_sem):
        self.same = place.c == place.h
        self.far = far_copy(source, target, sems, index, place.at(c=place.h, h=place.c))
        self.near = pltpu.make_async_copy(source, target, local_sem)

    def start(self):
        pl.when(self.same)(self.near.start)
        pl.when(~self.same)(self.far.start)

    def wait_recv(self):
        pl.when(self.same)(self.near.wait)
        pl.when(~self.same)(self.far.wait_recv)

    def wait_send(self):
        pl.when(~self.same)(self.far.wait_send)


class Task:
    copies = 1
    locals = 1
    work = ()

    def __init__(self, *inputs, phase=0):
        self.inputs, self.phase = inputs, phase

    def scratch(self):
        return [
            pltpu.SemaphoreType.DMA((self.copies,)),
            pltpu.SemaphoreType.DMA((self.copies,)),
            pltpu.SemaphoreType.DMA((self.locals,)),
            *self.work,
        ]


class Rows(Task):
    copies = 3

    def outs(self):
        rows = self.inputs[0]
        return [jax.ShapeDtypeStruct((4, *rows.shape), rows.dtype)]

    def steps(self, place, ins, outs, scratch):
        own, full = ins[0], outs[0]
        send, recv, local = scratch[:3]
        keep = pltpu.make_async_copy(own, full.at[0], local.at[0])
        over_z = far_copy(own, full.at[1], (send, recv), 0, place.at(l=1 - place.l))
        over_c = far_copy(own, full.at[2], (send, recv), 1, place.at(c=1 - place.c))
        relay = far_copy(full.at[1], full.at[3], (send, recv), 2, place.at(c=1 - place.c))

        def first():
            over_z.start()
            over_c.start()
            keep.start()

        def second():
            over_z.wait_recv()
            relay.start()

        def last():
            keep.wait()
            over_c.wait()
            over_z.wait_send()
            relay.wait()

        return [first, None, second, last]


class Sums(Task):
    copies = 3

    def __init__(self, *inputs, phase=0):
        super().__init__(*inputs, phase=phase)
        block = inputs[0].shape[1:]
        self.work = tuple(pltpu.VMEM(block, jnp.bfloat16) for _ in range(3))

    def outs(self):
        block = jax.ShapeDtypeStruct(self.inputs[0].shape[1:], jnp.bfloat16)
        return [block, block]

    def steps(self, place, ins, outs, scratch):
        partial, (from_c, from_z) = ins[0], outs
        send, recv, local, mine, theirs, total = scratch
        core = place.at(c=1 - place.c)
        load = pltpu.make_async_copy(partial.at[1], mine, local.at[0])
        far = far_copy(partial.at[3], theirs, (send, recv), 0, core)
        near = far_copy(partial.at[2], from_c, (send, recv), 1, core)
        over_z = far_copy(total, from_z, (send, recv), 2, place.at(l=1 - place.l))
        rows = 32

        def first():
            far.start()
            near.start()
            load.start()

        def second():
            load.wait()
            far.wait_recv()

            @pl.loop(0, mine.shape[0] // rows)
            def _(index):
                part = pl.ds(pl.multiple_of(index * rows, rows), rows)
                summed = mine[part, :].astype(jnp.float32) + theirs[part, :].astype(jnp.float32)
                total[part, :] = summed.astype(jnp.bfloat16)

            over_z.start()

        def last():
            far.wait_send()
            near.wait()
            over_z.wait()

        return [first, second, None, last]


class Near(Task):
    copies = 2

    def outs(self):
        shard = self.inputs[0]
        return [jax.ShapeDtypeStruct((2, *shard.shape), shard.dtype)]

    def copies_of(self, place, shard, first, second, scratch):
        send, recv, local = scratch[:3]
        return (
            Swap(place, shard, first, (send, recv), 0, local.at[0]),
            far_copy(shard, second, (send, recv), 1, place.at(c=place.h, h=1 - place.c)),
        )

    def steps(self, place, ins, outs, scratch):
        a, b = self.copies_of(place, ins[0], outs[0].at[0], outs[0].at[1], scratch)

        def first():
            a.start()
            b.start()

        def last():
            a.wait_recv()
            a.wait_send()
            b.wait()

        return [first, None, None, last]


class Planes(Near):
    copies = 8

    def outs(self):
        shard = self.inputs[0]
        return [jax.ShapeDtypeStruct((8, *shard.shape), shard.dtype)]

    def steps(self, place, ins, outs, scratch):
        full = outs[0]
        block = place.block
        a, b = self.copies_of(place, ins[0], full.at[block], full.at[block + 1], scratch)
        over_x, over_y = place.at(x=1 - place.x), place.at(y=1 - place.y)
        x_block = block + 2 - 4 * place.x
        y_block = block + 4 - 8 * place.y

        def pass_on(slot, index, device):
            return far_copy(full.at[slot], full.at[slot], scratch[:2], index, device)

        ax, ay = pass_on(block, 2, over_x), pass_on(block, 3, over_y)
        by, bx = pass_on(block + 1, 4, over_y), pass_on(block + 1, 5, over_x)
        axy = pass_on(x_block, 6, over_y)
        byx = pass_on(y_block + 1, 7, over_x)

        def first():
            a.start()
            b.start()

        def second():
            a.wait_recv()
            ax.start()
            b.wait_recv()
            by.start()
            ay.start()
            bx.start()

        def third():
            ax.wait_recv()
            axy.start()
            by.wait_recv()
            byx.start()

        def last():
            a.wait_send()
            b.wait_send()
            for copy in (ax, by):
                copy.wait_send()
            for copy in (ay, bx, axy, byx):
                copy.wait()

        return [first, second, third, last]


class Owners(Task):
    copies = 2

    def outs(self):
        near = self.inputs[0]
        return [jax.ShapeDtypeStruct(near.shape, near.dtype)]

    def steps(self, place, ins, outs, scratch):
        send, recv, local = scratch[:3]
        near, got = ins[0], outs[0]
        a = Swap(place, near.at[0], got.at[0], (send, recv), 0, local.at[0])
        b = far_copy(near.at[1], got.at[1], (send, recv), 1, place.at(c=1 - place.h, h=place.c))

        def first():
            a.start()
            b.start()

        def last():
            a.wait_recv()
            a.wait_send()
            b.wait()

        return [first, None, None, last]


class Halves(Task):
    def __init__(self, array, sender, phase=0):
        super().__init__(array, phase=phase)
        self.sender = sender

    def outs(self):
        return [jax.ShapeDtypeStruct(self.inputs[0].shape, self.inputs[0].dtype)]

    def steps(self, place, ins, outs, scratch):
        copy = far_copy(ins[0], outs[0], scratch[:2], 0, place.at(h=1 - place.h))
        sends = place.h == self.sender

        def first():
            pl.when(sends)(copy.start)

        def last():
            pl.when(sends)(copy.wait_send)
            pl.when(~sends)(copy.wait_recv)

        return [first, None, None, last]


def transfer(name, number, micros, *tasks):
    outs = [task.outs() for task in tasks]
    scratch = [task.scratch() for task in tasks]

    def kernel(*refs):
        refs = list(refs)

        def take(count):
            taken = refs[:count]
            del refs[:count]
            return taken

        ins_of = [take(len(task.inputs)) for task in tasks]
        outs_of = [take(len(out)) for out in outs]
        scratch_of = [take(len(one)) for one in scratch]
        place = Place()
        barrier = pltpu.get_barrier_semaphore()
        partners = place.partners()
        for partner in partners:
            pl.semaphore_signal(barrier, inc=1, device_id=partner, device_id_type=MESH)
        pl.semaphore_wait(barrier, len(partners))
        plans = [
            task.steps(place, ins_of[n], outs_of[n], scratch_of[n]) for n, task in enumerate(tasks)
        ]
        for phase in range(4):
            for task, plan in zip(tasks, plans):
                steps_now = [plan[phase]] if phase else []
                if phase == task.phase:
                    steps_now.insert(0, plan[0])
                for step in steps_now:
                    if step is not None:
                        step()

    results = pl.pallas_call(
        kernel,
        out_shape=[leaf for out in outs for leaf in out],
        in_specs=[pl.BlockSpec(memory_space=pl.ANY) for task in tasks for _ in task.inputs],
        out_specs=[pl.BlockSpec(memory_space=pl.ANY) for out in outs for _ in out],
        scratch_shapes=[one for part in scratch for one in part],
        compiler_params=pltpu.CompilerParams(collective_id=number, has_side_effects=True),
        cost_estimate=pl.CostEstimate(
            flops=0, bytes_accessed=micros * 3_300_000, transcendentals=0
        ),
        name=name,
    )(*[leaf for task in tasks for leaf in task.inputs])
    results = list(results)
    grouped = []
    for out in outs:
        grouped.append(results[: len(out)])
        del results[: len(out)]
    return grouped


def over_plane(near):
    return lax.all_gather(near, ("dp", "mp"), axis=0, tiled=True, axis_index_groups=PLANES)


def to_plane(grads):
    return lax.psum_scatter(
        grads, ("dp", "mp"), scatter_dimension=0, tiled=True, axis_index_groups=PLANES
    )


def both(pair):
    return pair[0].astype(jnp.float32) + pair[1].astype(jnp.float32)


def summed(partial, received):
    return both(received) + partial[0].astype(jnp.float32)


def sum_all_kernel(value, total, held, arrived, send_sem, recv_sem):
    dp, mp = lax.axis_index("dp"), lax.axis_index("mp")
    partners = [
        (dp + 1 - 2 * (dp % 2), mp),
        (dp + 2 - 4 * ((dp // 2) % 2), mp),
        (dp + 4 - 8 * (dp // 4), mp),
        (dp, mp + 1 - 2 * (mp % 2)),
        (dp, mp + 2 - 4 * (mp // 2)),
    ]
    barrier = pltpu.get_barrier_semaphore()
    for partner in partners:
        pl.semaphore_signal(
            barrier, inc=1, device_id=partner, device_id_type=pl.DeviceIdType.MESH
        )
    pl.semaphore_wait(barrier, len(partners))
    held[0] = value[...]
    for step, partner in enumerate(partners):
        copy = pltpu.make_async_remote_copy(
            src_ref=held.at[step],
            dst_ref=arrived.at[step],
            send_sem=send_sem.at[step],
            recv_sem=recv_sem.at[step],
            device_id=partner,
            device_id_type=pl.DeviceIdType.MESH,
        )
        copy.start()
        copy.wait()
        held[step + 1] = held[step] + arrived[step]
    total[...] = held[len(partners)]


def sum_all(vector):
    size = vector.shape[0]
    rows = -(-size // 1024) * 8
    block = jnp.pad(vector, (0, rows * 128 - size)).reshape(rows, 128)
    total = pl.pallas_call(
        sum_all_kernel,
        out_shape=jax.ShapeDtypeStruct((rows, 128), jnp.float32),
        in_specs=[pl.BlockSpec(memory_space=pltpu.VMEM)],
        out_specs=pl.BlockSpec(memory_space=pltpu.VMEM),
        scratch_shapes=[
            pltpu.VMEM((6, rows, 128), jnp.float32),
            pltpu.VMEM((5, rows, 128), jnp.float32),
            pltpu.SemaphoreType.DMA((5,)),
            pltpu.SemaphoreType.DMA((5,)),
        ],
        compiler_params=pltpu.CompilerParams(collective_id=0, has_side_effects=True),
        name="sum_all",
    )(block)
    return total.reshape(-1)[:size]


def shards_paired(
    hidden_in,
    cotangent,
    doc_lengths,
    owner,
    projection_master_weight,
    gateup_weight,
    out_weight,
    down_weight,
    projection_first_moment,
    gateup_first,
    out_first,
    down_first,
    projection_second_moment,
    gateup_second,
    out_second,
    down_second,
    gains,
    gain_first,
    gain_second,
):
    high, low = lax.axis_index("mp") // 2, lax.axis_index("mp") % 2
    plane = high
    groups = lax.axis_size("mp")
    heads = QUERY_HEADS // groups
    key_value_heads = KEY_VALUE_HEADS // groups
    query_group = heads // key_value_heads
    query_width = heads * HEAD_SIZE
    key_width = key_value_heads * HEAD_SIZE
    units = FF // groups
    rows_here = hidden_in.shape[0]
    count = 4 * rows_here
    half = count // 2
    width = hidden_in.shape[1]
    inverse = jnp.argsort(owner)
    logical_of = jnp.take(inverse, jnp.arange(8, dtype=jnp.int32) ^ plane, mode="clip")
    slot_of = owner ^ plane
    out_rate = float(QUERY_HEADS * HEAD_SIZE // 32) ** (-0.5)

    def to_slots(rows):
        return jnp.take(rows.reshape(rows.shape[0], 8, -1), logical_of, axis=1, mode="clip").reshape(rows.shape)

    def from_slots(rows):
        return jnp.take(rows.reshape(rows.shape[0], 8, -1), slot_of, axis=1, mode="clip").reshape(rows.shape)

    ln_in = gains[:MODEL_WIDTH]
    ln_mid = gains[MODEL_WIDTH : 2 * MODEL_WIDTH]
    q_gain = gains[2 * MODEL_WIDTH : 2 * MODEL_WIDTH + HEAD_SIZE]
    k_gain = gains[2 * MODEL_WIDTH + HEAD_SIZE :]
    x_rows = hidden_in.astype(jnp.float32)
    low_qkv = projection_master_weight.astype(jnp.bfloat16)
    low_out = out_weight.astype(jnp.bfloat16)
    low_first = jnp.concatenate([low_qkv, low_out.reshape(low_qkv.shape[0], -1)], axis=1)
    (first_blocks,), (full_in,), (near_gateup,) = transfer(
        "gather_first",
        1,
        108,
        Planes(low_first),
        Rows(to_slots(rms_norm(x_rows, ln_in).astype(jnp.bfloat16))),
        Near(gateup_weight.astype(jnp.bfloat16), phase=1),
    )
    full_in = full_in.reshape(count, width)
    w_qkv = first_blocks[:, :, : low_qkv.shape[1]].reshape(width, -1)
    w_out = first_blocks[:, :, low_qkv.shape[1] :].reshape(8, low_out.shape[0], width)
    w_out = jnp.take(w_out, slot_of, axis=0, mode="clip").reshape(-1, width)
    w_gateup = over_plane(near_gateup).reshape(width, -1)
    grad_out = cotangent.astype(jnp.float32)

    lengths = jnp.concatenate([doc_lengths, move(doc_lengths, OVER_C)], axis=0)
    ends = jnp.cumsum(lengths, axis=1)
    spot = jnp.arange(half, dtype=jnp.int32)
    chunk = spot // rows_here
    own_places = high * half + (low ^ chunk) * rows_here + spot % rows_here
    key_places = jnp.concatenate([own_places - half, own_places])

    def documents(places):
        return jnp.sum((places[None, :, None] >= ends[:, None, :]).astype(jnp.int32), axis=2)

    doc_of = documents(own_places)
    key_doc = jnp.where(key_places[None, :] >= 0, documents(key_places), -1)
    chosen = doc_of[:, :, None] == jnp.arange(lengths.shape[1], dtype=jnp.int32)[None, None, :]
    begin = jnp.sum(jnp.where(chosen, (ends - lengths)[:, None, :], 0), axis=2)
    offset = (own_places[None, :] - begin).astype(jnp.float32).reshape(count)
    freq = THETA ** (
        -(2.0 * jnp.arange(HEAD_SIZE // 2, dtype=jnp.float32)) / HEAD_SIZE
    )
    angle = offset[:, None] * freq[None, :]
    cosine, sine = jnp.cos(angle), jnp.sin(angle)
    cosine = jnp.concatenate([cosine, cosine], axis=-1)[:, None, :]
    sine = jnp.concatenate([sine, sine], axis=-1)[:, None, :]

    projected = jnp.dot(full_in, w_qkv, preferred_element_type=jnp.float32)
    query_raw = projected[:, :query_width].reshape(count, heads, HEAD_SIZE)
    unrotated_key = projected[:, query_width : query_width + key_width].reshape(
        count, key_value_heads, HEAD_SIZE
    )
    query_rows = rotate(rms_norm(query_raw, q_gain), cosine, sine).astype(jnp.bfloat16)
    key_rows = rotate(rms_norm(unrotated_key, k_gain), cosine, sine).astype(jnp.bfloat16)
    key_rows = key_rows.reshape(count, key_width)
    value_rows = projected[:, query_width + key_width :].astype(jnp.bfloat16)
    own_kv = jnp.concatenate([key_rows, value_rows], axis=1)
    (lower_kv,), (d_branch,) = transfer(
        "keys_up", 2, 47, Halves(own_kv, 0), Rows(cotangent)
    )
    lower_kv = jnp.where(high == 1, lower_kv, jnp.zeros_like(lower_kv))
    d_branch = d_branch.reshape(count, width)
    all_kv = jnp.concatenate(
        [lower_kv.reshape(2, half, 2 * key_width), own_kv.reshape(2, half, 2 * key_width)], axis=1
    )
    keys = all_kv[:, :, :key_width].reshape(2, count, key_value_heads, HEAD_SIZE)
    values = all_kv[:, :, key_width:].reshape(2, count, key_value_heads, HEAD_SIZE)
    queries = query_rows.reshape(2, half, key_value_heads, query_group, HEAD_SIZE)
    score_scale = HEAD_SIZE ** (-0.5)

    def scores_of(part):
        query_block, key_block, row_doc, col_doc = part
        raw = (
            jnp.einsum("tlwd,uld->lwtu", query_block, key_block, preferred_element_type=jnp.float32)
            * score_scale
        )
        allowed = (row_doc[:, None] == col_doc[None, :]) & (
            key_places[None, :] <= own_places[:, None]
        )
        return jnp.where(allowed[None, None], raw, MASKED)

    def forward_part(parts):
        query_block, key_block, value_block, row_doc, col_doc = parts
        score_matrix = scores_of((query_block, key_block, row_doc, col_doc))
        top = jnp.max(score_matrix, axis=-1, keepdims=True)
        total = jnp.log(jnp.sum(jnp.exp(score_matrix - top), axis=-1, keepdims=True)) + top
        probabilities = jnp.exp(score_matrix - total).astype(jnp.bfloat16)
        attention_result = jnp.einsum(
            "cpyx,xca->ycpa", probabilities, value_block, preferred_element_type=jnp.float32
        )
        return (attention_result.reshape(half, query_width).astype(jnp.bfloat16), total)

    outs, totals = lax.map(forward_part, (queries, keys, values, doc_of, key_doc))
    attn_heads = outs.reshape(count, query_width)

    def blocks(partial):
        return partial.astype(jnp.bfloat16).reshape(4, rows_here, width)

    partial = blocks(jnp.dot(attn_heads, w_out, preferred_element_type=jnp.float32))
    received, (near_down,) = transfer(
        "sum_attention", 3, 50, Sums(partial), Near(down_weight.astype(jnp.bfloat16))
    )
    down_blocks = over_plane(near_down)
    mixed = x_rows + summed(partial, received)
    ((full_mid,),) = transfer(
        "gather_mid", 4, 34, Rows(to_slots(rms_norm(mixed, ln_mid).astype(jnp.bfloat16)))
    )
    full_mid = full_mid.reshape(count, width)
    gateup = jnp.dot(full_mid, w_gateup, preferred_element_type=jnp.float32)
    down_blocks, gateup = lax.optimization_barrier((down_blocks, gateup))
    w_down = jnp.take(down_blocks, slot_of, axis=0, mode="clip").reshape(-1, width)
    gate = gateup[:, :units]
    upper = gateup[:, units:]
    sigma = jax.nn.sigmoid(gate)
    act = (gate * sigma * upper).astype(jnp.bfloat16)
    branch = blocks(jnp.dot(act, w_down, preferred_element_type=jnp.float32))

    g_down = jnp.einsum("tf,td->fd", act, d_branch, preferred_element_type=jnp.float32)
    g_down = jnp.take(g_down.astype(jnp.bfloat16).reshape(8, -1, width), logical_of, axis=0, mode="clip")
    d_act = jnp.einsum("td,fd->tf", d_branch, w_down, preferred_element_type=jnp.float32)
    d_upper = d_act * gate * sigma
    d_gate = d_act * upper * sigma * (1.0 + gate * (1.0 - sigma))
    d_gateup = jnp.concatenate([d_gate, d_upper], axis=1).astype(jnp.bfloat16)
    d_gateup, g_down = lax.optimization_barrier((d_gateup, g_down))
    near_g_down = to_plane(g_down)
    g_gateup = jnp.einsum("td,tf->df", full_mid, d_gateup, preferred_element_type=jnp.float32)
    g_gateup = g_gateup.astype(jnp.bfloat16).reshape(8, -1, 2 * units)
    partial = blocks(
        jnp.einsum("tc,dc->td", d_gateup, w_gateup, preferred_element_type=jnp.float32)
    )
    partial, g_gateup = lax.optimization_barrier((partial, g_gateup))
    near_g_gateup = to_plane(g_gateup)
    (received,) = transfer("sum_mid", 5, 32, Sums(partial))
    d_mid_rows = from_slots(summed(partial, received))
    d_mixed, g_ln_mid = norm_back(mixed, ln_mid, d_mid_rows)
    d_mixed = d_mixed + grad_out
    (d_attn,), (owned_down,) = transfer(
        "gather_attention", 6, 40, Rows(d_mixed.astype(jnp.bfloat16)), Owners(near_g_down)
    )
    d_attn = d_attn.reshape(count, width)
    red_down = both(owned_down)
    g_out = jnp.einsum("th,td->hd", attn_heads, d_attn, preferred_element_type=jnp.float32)
    g_out = jnp.take(g_out.astype(jnp.bfloat16).reshape(8, -1, width), logical_of, axis=0, mode="clip")
    near_g_out = to_plane(g_out)
    d_heads = jnp.einsum("td,hd->th", d_attn, w_out, preferred_element_type=jnp.float32).astype(
        jnp.bfloat16
    )
    d_heads = d_heads.reshape(2, half, key_value_heads, query_group, HEAD_SIZE)

    def backward_part(parts):
        query_block, key_block, value_block, row_doc, col_doc, block_total, block_gradient = parts
        score_matrix = scores_of((query_block, key_block, row_doc, col_doc))
        probabilities = jnp.exp(score_matrix - block_total)
        probability_gradient = jnp.einsum(
            "tlwd,uld->lwtu", block_gradient, value_block, preferred_element_type=jnp.float32
        )
        d_value = jnp.einsum(
            "zxrb,rzxd->bzd",
            probabilities.astype(jnp.bfloat16),
            block_gradient,
            preferred_element_type=jnp.float32,
        )
        score_gradient = (
            probabilities
            * (
                probability_gradient
                - jnp.sum(probabilities * probability_gradient, axis=-1, keepdims=True)
            )
        ).astype(jnp.bfloat16)
        d_query = (
            jnp.einsum(
                "cpyx,xca->ycpa", score_gradient, key_block, preferred_element_type=jnp.float32
            )
            * score_scale
        )
        d_key = (
            jnp.einsum(
                "zxrb,rzxd->bzd", score_gradient, query_block, preferred_element_type=jnp.float32
            )
            * score_scale
        )
        d_kv = jnp.concatenate([d_key.reshape(count, key_width), d_value.reshape(count, key_width)], axis=1)
        return (d_query.reshape(half, query_width), d_kv)

    d_queries, d_kv = lax.map(
        backward_part, (queries, keys, values, doc_of, key_doc, totals, d_heads)
    )
    (from_above,), received = transfer(
        "keys_down", 7, 53, Halves(d_kv[:, :half].astype(jnp.bfloat16), 1), Sums(branch)
    )
    result_rows = mixed + summed(branch, received)
    from_above = jnp.where(high == 0, from_above, jnp.zeros_like(from_above))
    d_kv = (d_kv[:, half:] + from_above.astype(jnp.float32)).reshape(count, 2 * key_width)
    d_queries = d_queries.reshape(count, heads, HEAD_SIZE)
    d_keys = d_kv[:, :key_width].reshape(count, key_value_heads, HEAD_SIZE)
    d_query_raw, g_q = norm_back(query_raw, q_gain, rotate_back(d_queries, cosine, sine))
    d_key_raw, g_k = norm_back(unrotated_key, k_gain, rotate_back(d_keys, cosine, sine))
    d_projected = jnp.concatenate(
        [
            d_query_raw.reshape(count, query_width),
            d_key_raw.reshape(count, key_width),
            d_kv[:, key_width:],
        ],
        axis=1,
    ).astype(jnp.bfloat16)
    g_qkv = jnp.einsum("td,tc->dc", full_in, d_projected, preferred_element_type=jnp.float32)
    near_g_qkv = to_plane(g_qkv.astype(jnp.bfloat16).reshape(8, width // 8, -1))
    partial = blocks(
        jnp.einsum("tc,dc->td", d_projected, w_qkv, preferred_element_type=jnp.float32)
    )
    received, (owned_gateup,) = transfer("sum_in", 8, 74, Sums(partial), Owners(near_g_gateup))
    red_gateup = both(owned_gateup)
    d_in_rows = from_slots(summed(partial, received))
    near_g_out, near_g_qkv, red_gateup = lax.optimization_barrier(
        (near_g_out, near_g_qkv, red_gateup)
    )
    (owned_out,), (owned_qkv,) = transfer(
        "last_owners", 9, 40, Owners(near_g_out), Owners(near_g_qkv)
    )
    red_out, red_qkv = both(owned_out), both(owned_qkv)
    d_input, g_ln_in = norm_back(x_rows, ln_in, d_in_rows)
    input_grad = d_input + d_mixed
    gain_terms = jnp.concatenate([g_ln_in, g_ln_mid, g_q, g_k])
    squares = jnp.sum(red_qkv * red_qkv) + jnp.sum(red_gateup * red_gateup)
    squares = squares + jnp.sum(red_out * red_out) + jnp.sum(red_down * red_down)
    totals_here = sum_all(jnp.concatenate([gain_terms, squares[None]]))
    gain_grad, total_squares = totals_here[:-1], totals_here[-1]
    grad_norm = jnp.sqrt(total_squares + jnp.sum(gain_grad * gain_grad))
    factor = jnp.minimum(1.0, CLIP_LIMIT / (grad_norm + 1e-06))
    qkv_new, qkv_first_new, qkv_second_new = adam(
        projection_master_weight,
        projection_first_moment,
        projection_second_moment,
        red_qkv,
        factor,
        LEARN,
        WEIGHT_DECAY,
    )
    gateup_new, gateup_first_new, gateup_second_new = adam(
        gateup_weight, gateup_first, gateup_second, red_gateup, factor, LEARN, WEIGHT_DECAY
    )
    out_new, out_first_new, out_second_new = adam(
        out_weight, out_first, out_second, red_out, factor, out_rate, WEIGHT_DECAY
    )
    down_new, down_first_new, down_second_new = adam(
        down_weight, down_first, down_second, red_down, factor, LEARN, WEIGHT_DECAY
    )
    gains_new, gain_first_new, gain_second_new = adam(
        gains, gain_first, gain_second, gain_grad, factor, GAIN_LEARN, 0.0
    )
    return (
        result_rows.astype(jnp.bfloat16),
        input_grad,
        qkv_new,
        gateup_new,
        out_new,
        down_new,
        qkv_first_new,
        gateup_first_new,
        out_first_new,
        down_first_new,
        qkv_second_new,
        gateup_second_new,
        out_second_new,
        down_second_new,
        gains_new,
        gain_first_new,
        gain_second_new,
        grad_norm,
    )


def paired(mesh):
    return dict(mesh.shape) == {"dp": 8, "mp": 4}


def solution(mesh):
    placed = (
        P(("dp", "mp"), None),
        P(("dp", "mp"), None),
        P("dp", None),
        P(),
        P("dp", "mp"),
        P("dp", "mp"),
        P(("mp", "dp"), None),
        P(("mp", "dp"), None),
        P("dp", "mp"),
        P("dp", "mp"),
        P(("mp", "dp"), None),
        P(("mp", "dp"), None),
        P("dp", "mp"),
        P("dp", "mp"),
        P(("mp", "dp"), None),
        P(("mp", "dp"), None),
        P(),
        P(),
        P(),
    )
    return jax.shard_map(
        shards_paired if paired(mesh) else shards_general,
        mesh=mesh,
        in_specs=placed,
        out_specs=(
            P(("dp", "mp"), None),
            P(("dp", "mp"), None),
            P("dp", "mp"),
            P("dp", "mp"),
            P(("mp", "dp"), None),
            P(("mp", "dp"), None),
            P("dp", "mp"),
            P("dp", "mp"),
            P(("mp", "dp"), None),
            P(("mp", "dp"), None),
            P("dp", "mp"),
            P("dp", "mp"),
            P(("mp", "dp"), None),
            P(("mp", "dp"), None),
            P(),
            P(),
            P(),
            P(),
        ),
        check_vma=False,
    )
```

```python
import jax
import jax.numpy as jnp
from jax import lax
from jax.experimental import pallas as pl
from jax.experimental.pallas import tpu as pltpu
from jax.sharding import PartitionSpec as P

MODEL_WIDTH = 2048
QUERY_HEADS = 16
KEY_VALUE_HEADS = 8
HEAD_SIZE = 128
FF = 6144
STEP = 10


EPS_NORM = 1e-06
THETA = 1000000.0
LEARN = 0.03
GAIN_LEARN = 0.5
FIRST_DECAY = 0.9
SECOND_DECAY = 0.95
ADAM_EPS = 1e-08
WEIGHT_DECAY = 0.1
CLIP_LIMIT = 1.0
MASKED = -1e30


def rms_norm(value_rows, gain):
    return (
        value_rows
        * lax.rsqrt(jnp.mean(value_rows * value_rows, axis=-1, keepdims=True) + EPS_NORM)
        * gain
    )


def norm_back(value_rows, gain, grad):
    score_scale = lax.rsqrt(jnp.mean(value_rows * value_rows, axis=-1, keepdims=True) + EPS_NORM)
    normed_input = value_rows * score_scale
    d_normal = grad * gain
    d_values = score_scale * (
        d_normal - normed_input * jnp.mean(d_normal * normed_input, axis=-1, keepdims=True)
    )
    d_gain = jnp.sum((grad * normed_input).reshape(-1, value_rows.shape[-1]), axis=0)
    return (d_values, d_gain)


def turned(value_rows):
    half = value_rows.shape[-1] // 2
    return jnp.concatenate([-value_rows[..., half:], value_rows[..., :half]], axis=-1)


def rotate(value_rows, cosine, sine):
    return value_rows * cosine + turned(value_rows) * sine


def rotate_back(grad, cosine, sine):
    return grad * cosine - turned(grad * sine)


def rope_tables(lengths, count):
    ends = jnp.cumsum(lengths)
    starts = ends - lengths
    places = jnp.arange(count, dtype=jnp.int32)
    doc_of = jnp.sum((places[:, None] >= ends[None, :]).astype(jnp.int32), axis=1)
    chosen = doc_of[:, None] == jnp.arange(lengths.shape[0], dtype=jnp.int32)[None, :]
    begin = jnp.sum(jnp.where(chosen, starts[None, :], 0), axis=1)
    offset = (places - begin).astype(jnp.float32)
    half = HEAD_SIZE // 2
    freq = THETA ** (-(2.0 * jnp.arange(half, dtype=jnp.float32)) / HEAD_SIZE)
    angle = offset[:, None] * freq[None, :]
    angle = jnp.concatenate([angle, angle], axis=-1)
    return (doc_of, jnp.cos(angle), jnp.sin(angle))


def arrange(gathered, order, blocks_count):
    blocks = gathered.reshape(blocks_count, gathered.shape[0] // blocks_count, gathered.shape[1])
    return jnp.take(blocks, order, axis=0).reshape(gathered.shape)


def fetch_weights(
    projection_master_weight, gateup_weight, out_weight, down_weight, owner, blocks_count
):
    gathered = (
        lax.all_gather(projection_master_weight.astype(jnp.bfloat16), "dp", axis=0, tiled=True),
        lax.all_gather(gateup_weight.astype(jnp.bfloat16), "dp", axis=0, tiled=True),
        lax.all_gather(out_weight.astype(jnp.bfloat16), "dp", axis=0, tiled=True),
        lax.all_gather(down_weight.astype(jnp.bfloat16), "dp", axis=0, tiled=True),
    )
    return tuple((arrange(piece, owner, blocks_count) for piece in gathered))


def fetch_again(
    projection_master_weight, gateup_weight, out_weight, down_weight, owner, blocks_count
):
    gathered = (
        lax.all_gather(projection_master_weight.astype(jnp.bfloat16), "dp", axis=0, tiled=True),
        lax.all_gather(gateup_weight.astype(jnp.bfloat16), "dp", axis=0, tiled=True),
        lax.all_gather(out_weight.astype(jnp.bfloat16), "dp", axis=0, tiled=True),
        lax.all_gather(down_weight.astype(jnp.bfloat16), "dp", axis=0, tiled=True),
    )
    return tuple((arrange(piece, owner, blocks_count) for piece in gathered))


def collect(rows):
    return lax.all_gather(rows, "mp", axis=0, tiled=True)


def collect_back(rows):
    return lax.all_gather(rows, "mp", axis=0, tiled=True)


def spread(operand, weight, rows):

    def term(start, count):
        return jnp.dot(operand, weight, preferred_element_type=jnp.float32)

    return lax.psum_scatter(
        term(jnp.int32(0), rows * lax.axis_size("mp")).astype(jnp.bfloat16),
        "mp",
        scatter_dimension=0,
        tiled=True,
    ).astype(jnp.float32)


def spread_back(operand, weight, rows):

    def term(start, count):
        return jnp.einsum("tc,dc->td", operand, weight, preferred_element_type=jnp.float32)

    return lax.psum_scatter(
        term(jnp.int32(0), rows * lax.axis_size("mp")).astype(jnp.bfloat16),
        "mp",
        scatter_dimension=0,
        tiled=True,
    ).astype(jnp.float32)


def adam(weight, first, second, grad, factor, rate, decay):
    clipped = grad * factor
    first_new = FIRST_DECAY * first + (1.0 - FIRST_DECAY) * clipped
    second_new = SECOND_DECAY * second + (1.0 - SECOND_DECAY) * clipped * clipped
    first_hat = first_new / (1.0 - FIRST_DECAY**STEP)
    second_hat = second_new / (1.0 - SECOND_DECAY**STEP)
    weight_new = weight * (1.0 - rate * decay) - rate * first_hat / (
        jnp.sqrt(second_hat) + ADAM_EPS
    )
    return (weight_new, first_new, second_new)


def shards_general(
    hidden_in,
    cotangent,
    doc_lengths,
    owner,
    projection_master_weight,
    gateup_weight,
    out_weight,
    down_weight,
    projection_first_moment,
    gateup_first,
    out_first,
    down_first,
    projection_second_moment,
    gateup_second,
    out_second,
    down_second,
    gains,
    gain_first,
    gain_second,
):
    total_width = lax.axis_size("mp")
    blocks_count = lax.axis_size("dp")
    heads = QUERY_HEADS // total_width
    key_value_heads = KEY_VALUE_HEADS // total_width
    query_group = heads // key_value_heads
    query_width = heads * HEAD_SIZE
    key_width = key_value_heads * HEAD_SIZE
    units = FF // total_width
    rows_here = hidden_in.shape[0]
    inverse = jnp.argsort(owner)
    out_rate = float(QUERY_HEADS * HEAD_SIZE // 32) ** (-0.5)
    w_qkv, w_gateup, w_out, w_down = fetch_weights(
        projection_master_weight, gateup_weight, out_weight, down_weight, owner, blocks_count
    )
    ln_in = gains[:MODEL_WIDTH]
    ln_mid = gains[MODEL_WIDTH : 2 * MODEL_WIDTH]
    q_gain = gains[2 * MODEL_WIDTH : 2 * MODEL_WIDTH + HEAD_SIZE]
    k_gain = gains[2 * MODEL_WIDTH + HEAD_SIZE :]
    x_rows = hidden_in.astype(jnp.float32)
    full_in = collect(rms_norm(x_rows, ln_in).astype(jnp.bfloat16))
    projected = jnp.dot(full_in, w_qkv, preferred_element_type=jnp.float32)
    count = projected.shape[0]
    doc_of, cosine, sine = rope_tables(doc_lengths[0], count)
    cosine = cosine[:, None, :]
    sine = sine[:, None, :]
    query_raw = projected[:, :query_width].reshape(count, heads, HEAD_SIZE)
    unrotated_key = projected[:, query_width : query_width + key_width].reshape(
        count, key_value_heads, HEAD_SIZE
    )
    projected_value = projected[:, query_width + key_width :].reshape(
        count, key_value_heads, HEAD_SIZE
    )
    query_rows = rotate(rms_norm(query_raw, q_gain), cosine, sine).astype(jnp.bfloat16)
    key_rows = rotate(rms_norm(unrotated_key, k_gain), cosine, sine).astype(jnp.bfloat16)
    value_rows = projected_value.astype(jnp.bfloat16)
    block = min(512, count)
    nblocks = count // block
    score_scale = HEAD_SIZE ** (-0.5)
    places = jnp.arange(count, dtype=jnp.int32)

    def scores_of(start):
        query_block = lax.dynamic_slice_in_dim(query_rows, start, block, 0).reshape(
            block, key_value_heads, query_group, HEAD_SIZE
        )
        raw = (
            jnp.einsum("tlwd,uld->lwtu", query_block, key_rows, preferred_element_type=jnp.float32)
            * score_scale
        )
        row_doc = lax.dynamic_slice_in_dim(doc_of, start, block, 0)
        row_place = start + jnp.arange(block, dtype=jnp.int32)
        allowed = (row_doc[:, None] == doc_of[None, :]) & (places[None, :] <= row_place[:, None])
        return (jnp.where(allowed[None, None], raw, MASKED), query_block)

    def forward_block(index):
        score_matrix, query_block = scores_of(index * block)
        top = jnp.max(score_matrix, axis=-1, keepdims=True)
        total = jnp.log(jnp.sum(jnp.exp(score_matrix - top), axis=-1, keepdims=True)) + top
        probabilities = jnp.exp(score_matrix - total).astype(jnp.bfloat16)
        attention_result = jnp.einsum(
            "cpyx,xca->ycpa", probabilities, value_rows, preferred_element_type=jnp.float32
        )
        return (attention_result.reshape(block, query_width), total)

    outs, totals = lax.map(forward_block, jnp.arange(nblocks, dtype=jnp.int32))
    attn_heads = outs.reshape(count, query_width).astype(jnp.bfloat16)
    attn_rows = spread(attn_heads, w_out, rows_here)
    mixed = x_rows + attn_rows
    full_mid = collect(rms_norm(mixed, ln_mid).astype(jnp.bfloat16))
    gateup = jnp.dot(full_mid, w_gateup, preferred_element_type=jnp.float32)
    gate = gateup[:, :units]
    upper = gateup[:, units:]
    sigma = jax.nn.sigmoid(gate)
    act = (gate * sigma * upper).astype(jnp.bfloat16)
    mlp_rows = spread(act, w_down, rows_here)
    result_rows = mixed + mlp_rows
    w_qkv, w_gateup, w_out, w_down = fetch_again(
        projection_master_weight, gateup_weight, out_weight, down_weight, owner, blocks_count
    )
    grad_out = cotangent.astype(jnp.float32)
    d_branch = collect_back(grad_out.astype(jnp.bfloat16))
    g_down = jnp.einsum("tf,td->fd", act, d_branch, preferred_element_type=jnp.float32)
    d_act = jnp.einsum("td,fd->tf", d_branch, w_down, preferred_element_type=jnp.float32)
    d_upper = d_act * gate * sigma
    d_gate = d_act * upper * sigma * (1.0 + gate * (1.0 - sigma))
    d_gateup = jnp.concatenate([d_gate, d_upper], axis=1).astype(jnp.bfloat16)
    g_gateup = jnp.einsum("td,tf->df", full_mid, d_gateup, preferred_element_type=jnp.float32)
    d_mid_rows = spread_back(d_gateup, w_gateup, rows_here)
    d_mixed, g_ln_mid = norm_back(mixed, ln_mid, d_mid_rows)
    d_mixed = d_mixed + grad_out
    d_attn = collect_back(d_mixed.astype(jnp.bfloat16))
    g_out = jnp.einsum("th,td->hd", attn_heads, d_attn, preferred_element_type=jnp.float32)
    d_heads = jnp.einsum("td,hd->th", d_attn, w_out, preferred_element_type=jnp.float32).astype(
        jnp.bfloat16
    )
    d_heads = d_heads.reshape(count, key_value_heads, query_group, HEAD_SIZE)

    def backward_block(carry, index):
        d_key_sum, d_value_sum = carry
        start = index * block
        score_matrix, query_block = scores_of(start)
        probabilities = jnp.exp(score_matrix - totals[index])
        block_gradient = lax.dynamic_slice_in_dim(d_heads, start, block, 0)
        probability_gradient = jnp.einsum(
            "tlwd,uld->lwtu", block_gradient, value_rows, preferred_element_type=jnp.float32
        )
        d_value_sum = d_value_sum + jnp.einsum(
            "zxrb,rzxd->bzd",
            probabilities.astype(jnp.bfloat16),
            block_gradient,
            preferred_element_type=jnp.float32,
        )
        score_gradient = (
            probabilities
            * (
                probability_gradient
                - jnp.sum(probabilities * probability_gradient, axis=-1, keepdims=True)
            )
        ).astype(jnp.bfloat16)
        d_query = (
            jnp.einsum(
                "cpyx,xca->ycpa", score_gradient, key_rows, preferred_element_type=jnp.float32
            )
            * score_scale
        )
        d_key_sum = (
            d_key_sum
            + jnp.einsum(
                "zxrb,rzxd->bzd", score_gradient, query_block, preferred_element_type=jnp.float32
            )
            * score_scale
        )
        return ((d_key_sum, d_value_sum), d_query.reshape(block, heads, HEAD_SIZE))

    empty = jnp.zeros((count, key_value_heads, HEAD_SIZE), jnp.float32)
    (d_keys, d_values), d_queries = lax.scan(
        backward_block, (empty, empty), jnp.arange(nblocks, dtype=jnp.int32)
    )
    d_queries = d_queries.reshape(count, heads, HEAD_SIZE)
    d_query_raw, g_q = norm_back(query_raw, q_gain, rotate_back(d_queries, cosine, sine))
    d_key_raw, g_k = norm_back(unrotated_key, k_gain, rotate_back(d_keys, cosine, sine))
    d_projected = jnp.concatenate(
        [
            d_query_raw.reshape(count, query_width),
            d_key_raw.reshape(count, key_width),
            d_values.reshape(count, key_width),
        ],
        axis=1,
    ).astype(jnp.bfloat16)
    g_qkv = jnp.einsum("td,tc->dc", full_in, d_projected, preferred_element_type=jnp.float32)
    d_in_rows = spread_back(d_projected, w_qkv, rows_here)
    d_input, g_ln_in = norm_back(x_rows, ln_in, d_in_rows)
    input_grad = d_input + d_mixed
    gain_terms = jnp.concatenate([g_ln_in, g_ln_mid, g_q, g_k])
    red_qkv, red_gateup, red_out, red_down = (
        lax.psum_scatter(
            arrange(g_qkv, inverse, blocks_count).astype(jnp.bfloat16),
            "dp",
            scatter_dimension=0,
            tiled=True,
        ).astype(jnp.float32),
        lax.psum_scatter(
            arrange(g_gateup, inverse, blocks_count).astype(jnp.bfloat16),
            "dp",
            scatter_dimension=0,
            tiled=True,
        ).astype(jnp.float32),
        lax.psum_scatter(
            arrange(g_out, inverse, blocks_count).astype(jnp.bfloat16),
            "dp",
            scatter_dimension=0,
            tiled=True,
        ).astype(jnp.float32),
        lax.psum_scatter(
            arrange(g_down, inverse, blocks_count).astype(jnp.bfloat16),
            "dp",
            scatter_dimension=0,
            tiled=True,
        ).astype(jnp.float32),
    )
    squares = jnp.sum(red_qkv * red_qkv) + jnp.sum(red_gateup * red_gateup)
    squares = squares + jnp.sum(red_out * red_out) + jnp.sum(red_down * red_down)
    total_squares, gain_grad = lax.psum((squares, gain_terms), ("dp", "mp"))
    grad_norm = jnp.sqrt(total_squares + jnp.sum(gain_grad * gain_grad))
    factor = jnp.minimum(1.0, CLIP_LIMIT / (grad_norm + 1e-06))
    qkv_new, qkv_first_new, qkv_second_new = adam(
        projection_master_weight,
        projection_first_moment,
        projection_second_moment,
        red_qkv,
        factor,
        LEARN,
        WEIGHT_DECAY,
    )
    gateup_new, gateup_first_new, gateup_second_new = adam(
        gateup_weight, gateup_first, gateup_second, red_gateup, factor, LEARN, WEIGHT_DECAY
    )
    out_new, out_first_new, out_second_new = adam(
        out_weight, out_first, out_second, red_out, factor, out_rate, WEIGHT_DECAY
    )
    down_new, down_first_new, down_second_new = adam(
        down_weight, down_first, down_second, red_down, factor, LEARN, WEIGHT_DECAY
    )
    gains_new, gain_first_new, gain_second_new = adam(
        gains, gain_first, gain_second, gain_grad, factor, GAIN_LEARN, 0.0
    )
    return (
        result_rows.astype(jnp.bfloat16),
        input_grad,
        qkv_new,
        gateup_new,
        out_new,
        down_new,
        qkv_first_new,
        gateup_first_new,
        out_first_new,
        down_first_new,
        qkv_second_new,
        gateup_second_new,
        out_second_new,
        down_second_new,
        gains_new,
        gain_first_new,
        gain_second_new,
        grad_norm,
    )


def steps(move):
    pairs = []
    for index in range(32):
        y, x, c, zh, zl = (index >> 4) & 1, (index >> 3) & 1, (index >> 2) & 1, (index >> 1) & 1, index & 1
        source = move(y, x, c, zh, zl)
        if source is not None:
            sy, sx, sc, sh, sl = source
            pairs.append(((sy << 4) | (sx << 3) | (sc << 2) | (sh << 1) | sl, index))
    return pairs


OVER_X = steps(lambda y, x, c, h, l: (y, 1 - x, c, h, l))
OVER_Y = steps(lambda y, x, c, h, l: (1 - y, x, c, h, l))
OVER_C = steps(lambda y, x, c, h, l: (y, x, 1 - c, h, l))
OVER_L = steps(lambda y, x, c, h, l: (y, x, c, h, 1 - l))
TO_GROUP = (
    steps(lambda y, x, c, h, l: (y, x, h, c, l)),
    steps(lambda y, x, c, h, l: (y, x, 1 - h, c, l)),
)
FROM_GROUP = tuple([(b, a) for a, b in pairs] for pairs in TO_GROUP)
UPWARD = steps(lambda y, x, c, h, l: (y, x, c, 0, l) if h == 1 else None)
DOWNWARD = steps(lambda y, x, c, h, l: (y, x, c, 1, l) if h == 0 else None)


def move(value, pairs):
    return lax.ppermute(value, ("dp", "mp"), pairs)


def after(value, *others):
    return lax.optimization_barrier((value, *others))[0]


PLANES = [[(block * 2 + c) * 4 + z for block in range(4)] for c in range(2) for z in range(4)]


MESH = pl.DeviceIdType.MESH


class Place:
    def __init__(self):
        dp, mp = lax.axis_index("dp"), lax.axis_index("mp")
        self.y, self.x, self.c = dp // 4, (dp // 2) % 2, dp % 2
        self.h, self.l = mp // 2, mp % 2
        self.block = (dp // 2) * 2

    def at(self, y=None, x=None, c=None, h=None, l=None):
        y, x, c = (o if n is None else n for o, n in ((self.y, y), (self.x, x), (self.c, c)))
        h, l = (o if n is None else n for o, n in ((self.h, h), (self.l, l)))
        return ((y * 2 + x) * 2 + c, h * 2 + l)

    def partners(self):
        return [
            self.at(x=1 - self.x),
            self.at(y=1 - self.y),
            self.at(l=1 - self.l),
            self.at(c=1 - self.c),
            self.at(h=1 - self.h),
            self.at(c=1 - self.c, h=1 - self.h),
        ]


def far_copy(source, target, sems, index, device):
    return pltpu.make_async_remote_copy(
        src_ref=source,
        dst_ref=target,
        send_sem=sems[0].at[index],
        recv_sem=sems[1].at[index],
        device_id=device,
        device_id_type=MESH,
    )


class Swap:
    def __init__(self, place, source, target, sems, index, local_sem):
        self.same = place.c == place.h
        self.far = far_copy(source, target, sems, index, place.at(c=place.h, h=place.c))
        self.near = pltpu.make_async_copy(source, target, local_sem)

    def start(self):
        pl.when(self.same)(self.near.start)
        pl.when(~self.same)(self.far.start)

    def wait_recv(self):
        pl.when(self.same)(self.near.wait)
        pl.when(~self.same)(self.far.wait_recv)

    def wait_send(self):
        pl.when(~self.same)(self.far.wait_send)


class Task:
    copies = 1
    locals = 1
    work = ()

    def __init__(self, *inputs, phase=0):
        self.inputs, self.phase = inputs, phase

    def scratch(self):
        return [
            pltpu.SemaphoreType.DMA((self.copies,)),
            pltpu.SemaphoreType.DMA((self.copies,)),
            pltpu.SemaphoreType.DMA((self.locals,)),
            *self.work,
        ]


class Rows(Task):
    copies = 3

    def outs(self):
        rows = self.inputs[0]
        return [jax.ShapeDtypeStruct((4, *rows.shape), rows.dtype)]

    def steps(self, place, ins, outs, scratch):
        own, full = ins[0], outs[0]
        send, recv, local = scratch[:3]
        keep = pltpu.make_async_copy(own, full.at[0], local.at[0])
        over_z = far_copy(own, full.at[1], (send, recv), 0, place.at(l=1 - place.l))
        over_c = far_copy(own, full.at[2], (send, recv), 1, place.at(c=1 - place.c))
        relay = far_copy(full.at[1], full.at[3], (send, recv), 2, place.at(c=1 - place.c))

        def first():
            over_z.start()
            over_c.start()
            keep.start()

        def second():
            over_z.wait_recv()
            relay.start()

        def last():
            keep.wait()
            over_c.wait()
            over_z.wait_send()
            relay.wait()

        return [first, None, second, last]


class Sums(Task):
    copies = 3

    def __init__(self, *inputs, phase=0):
        super().__init__(*inputs, phase=phase)
        block = inputs[0].shape[1:]
        self.work = tuple(pltpu.VMEM(block, jnp.bfloat16) for _ in range(3))

    def outs(self):
        block = jax.ShapeDtypeStruct(self.inputs[0].shape[1:], jnp.bfloat16)
        return [block, block]

    def steps(self, place, ins, outs, scratch):
        partial, (from_c, from_z) = ins[0], outs
        send, recv, local, mine, theirs, total = scratch
        core = place.at(c=1 - place.c)
        load = pltpu.make_async_copy(partial.at[1], mine, local.at[0])
        far = far_copy(partial.at[3], theirs, (send, recv), 0, core)
        near = far_copy(partial.at[2], from_c, (send, recv), 1, core)
        over_z = far_copy(total, from_z, (send, recv), 2, place.at(l=1 - place.l))
        rows = 32

        def first():
            far.start()
            near.start()
            load.start()

        def second():
            load.wait()
            far.wait_recv()

            @pl.loop(0, mine.shape[0] // rows)
            def _(index):
                part = pl.ds(pl.multiple_of(index * rows, rows), rows)
                summed = mine[part, :].astype(jnp.float32) + theirs[part, :].astype(jnp.float32)
                total[part, :] = summed.astype(jnp.bfloat16)

            over_z.start()

        def last():
            far.wait_send()
            near.wait()
            over_z.wait()

        return [first, second, None, last]


class Near(Task):
    copies = 2

    def outs(self):
        shard = self.inputs[0]
        return [jax.ShapeDtypeStruct((2, *shard.shape), shard.dtype)]

    def copies_of(self, place, shard, first, second, scratch):
        send, recv, local = scratch[:3]
        return (
            Swap(place, shard, first, (send, recv), 0, local.at[0]),
            far_copy(shard, second, (send, recv), 1, place.at(c=place.h, h=1 - place.c)),
        )

    def steps(self, place, ins, outs, scratch):
        a, b = self.copies_of(place, ins[0], outs[0].at[0], outs[0].at[1], scratch)

        def first():
            a.start()
            b.start()

        def last():
            a.wait_recv()
            a.wait_send()
            b.wait()

        return [first, None, None, last]


class Planes(Near):
    copies = 8

    def outs(self):
        shard = self.inputs[0]
        return [jax.ShapeDtypeStruct((8, *shard.shape), shard.dtype)]

    def steps(self, place, ins, outs, scratch):
        full = outs[0]
        block = place.block
        a, b = self.copies_of(place, ins[0], full.at[block], full.at[block + 1], scratch)
        over_x, over_y = place.at(x=1 - place.x), place.at(y=1 - place.y)
        x_block = block + 2 - 4 * place.x
        y_block = block + 4 - 8 * place.y

        def pass_on(slot, index, device):
            return far_copy(full.at[slot], full.at[slot], scratch[:2], index, device)

        ax, ay = pass_on(block, 2, over_x), pass_on(block, 3, over_y)
        by, bx = pass_on(block + 1, 4, over_y), pass_on(block + 1, 5, over_x)
        axy = pass_on(x_block, 6, over_y)
        byx = pass_on(y_block + 1, 7, over_x)

        def first():
            a.start()
            b.start()

        def second():
            a.wait_recv()
            ax.start()
            b.wait_recv()
            by.start()
            ay.start()
            bx.start()

        def third():
            ax.wait_recv()
            axy.start()
            by.wait_recv()
            byx.start()

        def last():
            a.wait_send()
            b.wait_send()
            for copy in (ax, by):
                copy.wait_send()
            for copy in (ay, bx, axy, byx):
                copy.wait()

        return [first, second, third, last]


class Owners(Task):
    copies = 2

    def outs(self):
        near = self.inputs[0]
        return [jax.ShapeDtypeStruct(near.shape, near.dtype)]

    def steps(self, place, ins, outs, scratch):
        send, recv, local = scratch[:3]
        near, got = ins[0], outs[0]
        a = Swap(place, near.at[0], got.at[0], (send, recv), 0, local.at[0])
        b = far_copy(near.at[1], got.at[1], (send, recv), 1, place.at(c=1 - place.h, h=place.c))

        def first():
            a.start()
            b.start()

        def last():
            a.wait_recv()
            a.wait_send()
            b.wait()

        return [first, None, None, last]


class Halves(Task):
    def __init__(self, array, sender, phase=0):
        super().__init__(array, phase=phase)
        self.sender = sender

    def outs(self):
        return [jax.ShapeDtypeStruct(self.inputs[0].shape, self.inputs[0].dtype)]

    def steps(self, place, ins, outs, scratch):
        copy = far_copy(ins[0], outs[0], scratch[:2], 0, place.at(h=1 - place.h))
        sends = place.h == self.sender

        def first():
            pl.when(sends)(copy.start)

        def last():
            pl.when(sends)(copy.wait_send)
            pl.when(~sends)(copy.wait_recv)

        return [first, None, None, last]


def transfer(name, number, micros, *tasks):
    outs = [task.outs() for task in tasks]
    scratch = [task.scratch() for task in tasks]

    def kernel(*refs):
        refs = list(refs)

        def take(count):
            taken = refs[:count]
            del refs[:count]
            return taken

        ins_of = [take(len(task.inputs)) for task in tasks]
        outs_of = [take(len(out)) for out in outs]
        scratch_of = [take(len(one)) for one in scratch]
        place = Place()
        barrier = pltpu.get_barrier_semaphore()
        partners = place.partners()
        for partner in partners:
            pl.semaphore_signal(barrier, inc=1, device_id=partner, device_id_type=MESH)
        pl.semaphore_wait(barrier, len(partners))
        plans = [
            task.steps(place, ins_of[n], outs_of[n], scratch_of[n]) for n, task in enumerate(tasks)
        ]
        for phase in range(4):
            for task, plan in zip(tasks, plans):
                steps_now = [plan[phase]] if phase else []
                if phase == task.phase:
                    steps_now.insert(0, plan[0])
                for step in steps_now:
                    if step is not None:
                        step()

    results = pl.pallas_call(
        kernel,
        out_shape=[leaf for out in outs for leaf in out],
        in_specs=[pl.BlockSpec(memory_space=pl.ANY) for task in tasks for _ in task.inputs],
        out_specs=[pl.BlockSpec(memory_space=pl.ANY) for out in outs for _ in out],
        scratch_shapes=[one for part in scratch for one in part],
        compiler_params=pltpu.CompilerParams(
            collective_id=number, has_side_effects=True, vmem_limit_bytes=48 * 2**20
        ),
        cost_estimate=pl.CostEstimate(
            flops=0, bytes_accessed=micros * 3_300_000, transcendentals=0
        ),
        name=name,
    )(*[leaf for task in tasks for leaf in task.inputs])
    results = list(results)
    grouped = []
    for out in outs:
        grouped.append(results[: len(out)])
        del results[: len(out)]
    return grouped


def to_group(shard):
    return jnp.stack([move(shard, TO_GROUP[0]), move(shard, TO_GROUP[1])])


def to_owner(near):
    return [move(near[0], FROM_GROUP[0]), move(near[1], FROM_GROUP[1])]


def over_plane(near):
    return lax.all_gather(near, ("dp", "mp"), axis=0, tiled=True, axis_index_groups=PLANES)


def to_plane(grads):
    return lax.psum_scatter(
        grads, ("dp", "mp"), scatter_dimension=0, tiled=True, axis_index_groups=PLANES
    )


def both(pair):
    return pair[0].astype(jnp.float32) + pair[1].astype(jnp.float32)


def summed(partial, received):
    return both(received) + partial[0].astype(jnp.float32)


def sum_all_kernel(value, total, held, arrived, send_sem, recv_sem):
    dp, mp = lax.axis_index("dp"), lax.axis_index("mp")
    partners = [
        (dp + 1 - 2 * (dp % 2), mp),
        (dp + 2 - 4 * ((dp // 2) % 2), mp),
        (dp + 4 - 8 * (dp // 4), mp),
        (dp, mp + 1 - 2 * (mp % 2)),
        (dp, mp + 2 - 4 * (mp // 2)),
    ]
    barrier = pltpu.get_barrier_semaphore()
    for partner in partners:
        pl.semaphore_signal(
            barrier, inc=1, device_id=partner, device_id_type=pl.DeviceIdType.MESH
        )
    pl.semaphore_wait(barrier, len(partners))
    held[0] = value[...]
    for step, partner in enumerate(partners):
        copy = pltpu.make_async_remote_copy(
            src_ref=held.at[step],
            dst_ref=arrived.at[step],
            send_sem=send_sem.at[step],
            recv_sem=recv_sem.at[step],
            device_id=partner,
            device_id_type=pl.DeviceIdType.MESH,
        )
        copy.start()
        copy.wait()
        held[step + 1] = held[step] + arrived[step]
    total[...] = held[len(partners)]


def sum_all(vector):
    size = vector.shape[0]
    rows = -(-size // 1024) * 8
    block = jnp.pad(vector, (0, rows * 128 - size)).reshape(rows, 128)
    total = pl.pallas_call(
        sum_all_kernel,
        out_shape=jax.ShapeDtypeStruct((rows, 128), jnp.float32),
        in_specs=[pl.BlockSpec(memory_space=pltpu.VMEM)],
        out_specs=pl.BlockSpec(memory_space=pltpu.VMEM),
        scratch_shapes=[
            pltpu.VMEM((6, rows, 128), jnp.float32),
            pltpu.VMEM((5, rows, 128), jnp.float32),
            pltpu.SemaphoreType.DMA((5,)),
            pltpu.SemaphoreType.DMA((5,)),
        ],
        compiler_params=pltpu.CompilerParams(collective_id=0, has_side_effects=True),
        name="sum_all",
    )(block)
    return total.reshape(-1)[:size]


def column_places(index, high, low, rows):
    chunk = index // rows
    return high * 2 * rows + (low + chunk - 2 * low * chunk) * rows + index - chunk * rows


def project_kernel(rows_ref, weight_ref, cos_ref, sin_ref, gain_ref, raw_ref, query_ref, kv_ref):
    width = rows_ref.shape[1]
    weight = weight_ref[...].reshape(width, weight_ref.shape[2])
    projected = jnp.dot(rows_ref[...], weight, preferred_element_type=jnp.float32)
    query_width, key_width = query_ref.shape[1], kv_ref.shape[1] // 2
    turned_width = query_width + key_width
    raw_ref[...] = projected[:, :turned_width]
    cosine, sine = cos_ref[...], sin_ref[...]
    for start in range(0, turned_width, HEAD_SIZE):
        raw = projected[:, start : start + HEAD_SIZE]
        gain = gain_ref[0:1, :] if start < query_width else gain_ref[1:2, :]
        normed = raw * lax.rsqrt(jnp.mean(raw * raw, axis=1, keepdims=True) + EPS_NORM) * gain
        turned = normed * cosine + pltpu.roll(normed, HEAD_SIZE // 2, 1) * sine
        if start < query_width:
            query_ref[:, start : start + HEAD_SIZE] = turned.astype(jnp.bfloat16)
        else:
            place = start - query_width
            kv_ref[:, place : place + HEAD_SIZE] = turned.astype(jnp.bfloat16)
    kv_ref[:, key_width:] = projected[:, turned_width:].astype(jnp.bfloat16)


def project(rows, blocks, cosine, sine, head_gains, query_width, key_width):
    count, width = rows.shape
    tile = 256
    total = query_width + 2 * key_width
    by_rows = lambda columns: pl.BlockSpec((tile, columns), lambda i: (i, 0))
    return pl.pallas_call(
        project_kernel,
        grid=(count // tile,),
        in_specs=[
            by_rows(width),
            pl.BlockSpec((8, width // 8, total), lambda i: (0, 0, 0)),
            by_rows(HEAD_SIZE),
            by_rows(HEAD_SIZE),
            pl.BlockSpec((2, HEAD_SIZE), lambda i: (0, 0)),
        ],
        out_specs=[by_rows(query_width + key_width), by_rows(query_width), by_rows(2 * key_width)],
        out_shape=[
            jax.ShapeDtypeStruct((count, query_width + key_width), jnp.float32),
            jax.ShapeDtypeStruct((count, query_width), jnp.bfloat16),
            jax.ShapeDtypeStruct((count, 2 * key_width), jnp.bfloat16),
        ],
        compiler_params=pltpu.CompilerParams(vmem_limit_bytes=48 * 2**20),
        cost_estimate=pl.CostEstimate(
            flops=2 * count * width * total, bytes_accessed=16 * 2**20, transcendentals=0
        ),
        name="project",
    )(rows, blocks, cosine, sine, head_gains)


def unproject_kernel(
    place_ref, dq_ref, own_ref, above_ref, raw_ref, cos_ref, sin_ref, gain_ref, out_ref, gq_ref, gk_ref
):
    query_width, key_width = dq_ref.shape[1], own_ref.shape[1] // 2
    turned_width = query_width + key_width
    lower = place_ref[0] == 0
    cosine, sine = cos_ref[...], sin_ref[...]

    @pl.when(pl.program_id(0) == 0)
    def _():
        gq_ref[...] = jnp.zeros_like(gq_ref)
        gk_ref[...] = jnp.zeros_like(gk_ref)

    def with_above(columns):
        above = jnp.where(lower, above_ref[:, columns].astype(jnp.float32), 0.0)
        return own_ref[:, columns] + above

    for start in range(0, turned_width, HEAD_SIZE):
        columns = slice(start, start + HEAD_SIZE)
        if start < query_width:
            grad, gain, gain_sum = dq_ref[:, columns], gain_ref[0:1, :], gq_ref
        else:
            grad = with_above(slice(start - query_width, start - query_width + HEAD_SIZE))
            gain, gain_sum = gain_ref[1:2, :], gk_ref
        grad = grad * cosine - pltpu.roll(grad, HEAD_SIZE // 2, 1) * sine
        raw = raw_ref[:, columns]
        scale = lax.rsqrt(jnp.mean(raw * raw, axis=1, keepdims=True) + EPS_NORM)
        normed = raw * scale
        gain_sum[...] += jnp.sum((grad * normed).reshape(-1, 8, HEAD_SIZE), axis=0)
        d_normal = grad * gain
        value = scale * (d_normal - normed * jnp.mean(d_normal * normed, axis=1, keepdims=True))
        out_ref[:, columns] = value.astype(jnp.bfloat16)
    out_ref[:, turned_width:] = with_above(slice(key_width, 2 * key_width)).astype(jnp.bfloat16)


def unproject(place, d_queries, d_own, above, raw, cosine, sine, head_gains):
    count, query_width = d_queries.shape
    key_width = d_own.shape[1] // 2
    tile = 256
    total = query_width + 2 * key_width
    by_rows = lambda columns: pl.BlockSpec((tile, columns), lambda i, p: (i, 0))
    fixed = lambda rows: pl.BlockSpec((rows, HEAD_SIZE), lambda i, p: (0, 0))
    return pl.pallas_call(
        unproject_kernel,
        grid_spec=pltpu.PrefetchScalarGridSpec(
            num_scalar_prefetch=1,
            grid=(count // tile,),
            in_specs=[
                by_rows(query_width),
                by_rows(2 * key_width),
                by_rows(2 * key_width),
                by_rows(query_width + key_width),
                by_rows(HEAD_SIZE),
                by_rows(HEAD_SIZE),
                fixed(2),
            ],
            out_specs=[by_rows(total), fixed(8), fixed(8)],
        ),
        out_shape=[
            jax.ShapeDtypeStruct((count, total), jnp.bfloat16),
            jax.ShapeDtypeStruct((8, HEAD_SIZE), jnp.float32),
            jax.ShapeDtypeStruct((8, HEAD_SIZE), jnp.float32),
        ],
        compiler_params=pltpu.CompilerParams(vmem_limit_bytes=32 * 2**20),
        cost_estimate=pl.CostEstimate(flops=0, bytes_accessed=16 * 2**20, transcendentals=0),
        name="unproject",
    )(place, d_queries, d_own, above, raw, cosine, sine, head_gains)


def dot_t(left, right):
    return lax.dot_general(
        left, right, (((1,), (1,)), ((), ())), preferred_element_type=jnp.float32
    )


def t_dot(left, right):
    return lax.dot_general(
        left, right, (((0,), (0,)), ((), ())), preferred_element_type=jnp.float32
    )


def exps_of(place_ref, time_ref, begin_ref, rows, query, key_low, key_own):
    high, low = place_ref[0], place_ref[1]
    keys = key_own.shape[0]
    scale = HEAD_SIZE ** (-0.5)
    column = lax.broadcasted_iota(jnp.int32, (rows.size, keys), 1)
    time, begin = time_ref[rows, :], begin_ref[rows, :]
    own_place = column_places(column, high, low, keys // 2)
    low_place = column_places(column, 0, low, keys // 2)
    own_seen = (own_place <= time) & (own_place >= begin)
    low_seen = (low_place >= begin) & (low_place < high * keys)
    own = jnp.where(own_seen, dot_t(query, key_own) * scale, MASKED)
    lower = jnp.where(low_seen, dot_t(query, key_low) * scale, MASKED)
    top = jnp.maximum(
        jnp.max(own, axis=1, keepdims=True), jnp.max(lower, axis=1, keepdims=True)
    )
    own, lower = jnp.exp(own - top), jnp.exp(lower - top)
    total = jnp.sum(own, axis=1, keepdims=True) + jnp.sum(lower, axis=1, keepdims=True)
    return lower, own, 1.0 / total


def attend_kernel(place_ref, time_ref, begin_ref, query_ref, low_ref, own_ref, out_ref):
    half, query_width = query_ref.shape
    key_width = own_ref.shape[1] // 2
    group = query_width // key_width
    size = half // 2
    upper = place_ref[0] == 1
    for kv in range(key_width // HEAD_SIZE):
        key_at = slice(kv * HEAD_SIZE, (kv + 1) * HEAD_SIZE)
        value_at = slice(key_width + kv * HEAD_SIZE, key_width + (kv + 1) * HEAD_SIZE)
        key_low, key_own, value_own = low_ref[:, key_at], own_ref[:, key_at], own_ref[:, value_at]
        value_low = jnp.where(upper, low_ref[:, value_at], jnp.zeros_like(value_own))
        for part in range(2):
            rows = pl.ds(part * size, size)
            for head in range(kv * group, (kv + 1) * group):
                query_at = slice(head * HEAD_SIZE, (head + 1) * HEAD_SIZE)
                lower, own, inverse = exps_of(
                    place_ref, time_ref, begin_ref, rows, query_ref[rows, query_at], key_low, key_own
                )
                result = jnp.dot(
                    lower.astype(jnp.bfloat16), value_low, preferred_element_type=jnp.float32
                ) + jnp.dot(own.astype(jnp.bfloat16), value_own, preferred_element_type=jnp.float32)
                out_ref[rows, query_at] = (result * inverse).astype(jnp.bfloat16)


def attend_back_kernel(
    place_ref, time_ref, begin_ref, query_ref, low_ref, own_ref, grad_ref, dq_ref, dlow_ref, down_ref
):
    half, query_width = query_ref.shape
    key_width = own_ref.shape[1] // 2
    group = query_width // key_width
    size = half // 2
    scale = HEAD_SIZE ** (-0.5)
    upper = place_ref[0] == 1
    for kv in range(key_width // HEAD_SIZE):
        key_at = slice(kv * HEAD_SIZE, (kv + 1) * HEAD_SIZE)
        value_at = slice(key_width + kv * HEAD_SIZE, key_width + (kv + 1) * HEAD_SIZE)
        key_own, value_own = own_ref[:, key_at], own_ref[:, value_at]
        key_low = jnp.where(upper, low_ref[:, key_at], jnp.zeros_like(key_own))
        value_low = jnp.where(upper, low_ref[:, value_at], jnp.zeros_like(value_own))
        dk_low = dk_own = dv_low = dv_own = None
        for part in range(2):
            rows = pl.ds(part * size, size)
            for head in range(kv * group, (kv + 1) * group):
                query_at = slice(head * HEAD_SIZE, (head + 1) * HEAD_SIZE)
                query, grad = query_ref[rows, query_at], grad_ref[rows, query_at]
                lower, own, inverse = exps_of(
                    place_ref, time_ref, begin_ref, rows, query, key_low, key_own
                )
                lower, own = lower * inverse, own * inverse
                g_low, g_own = dot_t(grad, value_low), dot_t(grad, value_own)
                mean = jnp.sum(lower * g_low, axis=1, keepdims=True) + jnp.sum(
                    own * g_own, axis=1, keepdims=True
                )
                s_low = (lower * (g_low - mean)).astype(jnp.bfloat16)
                s_own = (own * (g_own - mean)).astype(jnp.bfloat16)
                dq_ref[rows, query_at] = scale * (
                    jnp.dot(s_low, key_low, preferred_element_type=jnp.float32)
                    + jnp.dot(s_own, key_own, preferred_element_type=jnp.float32)
                )
                terms = (
                    t_dot(s_low, query),
                    t_dot(s_own, query),
                    t_dot(lower.astype(jnp.bfloat16), grad),
                    t_dot(own.astype(jnp.bfloat16), grad),
                )
                if dk_low is None:
                    dk_low, dk_own, dv_low, dv_own = terms
                else:
                    dk_low, dk_own = dk_low + terms[0], dk_own + terms[1]
                    dv_low, dv_own = dv_low + terms[2], dv_own + terms[3]
        dlow_ref[:, key_at] = (dk_low * scale).astype(jnp.bfloat16)
        dlow_ref[:, value_at] = dv_low.astype(jnp.bfloat16)
        down_ref[:, key_at] = dk_own * scale
        down_ref[:, value_at] = dv_own


def attention_call(kernel, name, place, arrays, outs, flops):
    count = arrays[0].shape[0]
    half = count // 2
    spec = lambda leaf: pl.BlockSpec((half, leaf.shape[1]), lambda i, p: (i, 0))
    return pl.pallas_call(
        kernel,
        grid_spec=pltpu.PrefetchScalarGridSpec(
            num_scalar_prefetch=1,
            grid=(2,),
            in_specs=[spec(leaf) for leaf in arrays],
            out_specs=[spec(leaf) for leaf in outs],
        ),
        out_shape=outs,
        compiler_params=pltpu.CompilerParams(vmem_limit_bytes=56 * 2**20),
        cost_estimate=pl.CostEstimate(flops=flops, bytes_accessed=16 * 2**20, transcendentals=0),
        name=name,
    )(place, *arrays)


def scaled(values):
    return values * lax.rsqrt(jnp.mean(values * values, axis=1, keepdims=True) + EPS_NORM)


def three(parts, columns=slice(None)):
    own, from_c, from_z = parts
    return (
        own[0, :, columns].astype(jnp.float32)
        + from_c[:, columns].astype(jnp.float32)
        + from_z[:, columns].astype(jnp.float32)
    )


def slot_columns(slot_ref, index, block):
    return pl.ds(pl.multiple_of(slot_ref[index] * block, block), block)


def store_slots(slot_ref, out_ref, values):
    block = out_ref.shape[1] // 8
    for index in range(8):
        out_ref[:, slot_columns(slot_ref, index, block)] = values[
            :, index * block : (index + 1) * block
        ]


def norm_kernel(slot_ref, x_ref, gain_ref, out_ref):
    x = x_ref[...].astype(jnp.float32)
    store_slots(slot_ref, out_ref, (scaled(x) * gain_ref[...]).astype(jnp.bfloat16))


def mix_kernel(slot_ref, x_ref, own_ref, c_ref, z_ref, gain_ref, mixed_ref, out_ref):
    mixed = x_ref[...].astype(jnp.float32) + three((own_ref, c_ref, z_ref))
    mixed_ref[...] = mixed
    store_slots(slot_ref, out_ref, (scaled(mixed) * gain_ref[...]).astype(jnp.bfloat16))


def norm_back_of(slot_ref, value_ref, parts, gain_ref, sum_ref, grad_ref):
    width = value_ref.shape[1]
    block = width // 8
    for index in range(8):
        grad_ref[:, index * block : (index + 1) * block] = three(
            parts, slot_columns(slot_ref, index, block)
        )
    value, grad = value_ref[...].astype(jnp.float32), grad_ref[...]
    scale = lax.rsqrt(jnp.mean(value * value, axis=1, keepdims=True) + EPS_NORM)
    normed = value * scale

    @pl.when(pl.program_id(0) == 0)
    def _():
        sum_ref[...] = jnp.zeros_like(sum_ref)

    sum_ref[...] += jnp.sum((grad * normed).reshape(-1, 8, width), axis=0)
    d_normal = grad * gain_ref[...]
    return scale * (d_normal - normed * jnp.mean(d_normal * normed, axis=1, keepdims=True))


def mix_back_kernel(
    slot_ref, mixed_ref, own_ref, c_ref, z_ref, gain_ref, cot_ref, d_ref, low_ref, sum_ref, grad_ref
):
    value = norm_back_of(slot_ref, mixed_ref, (own_ref, c_ref, z_ref), gain_ref, sum_ref, grad_ref)
    value = value + cot_ref[...].astype(jnp.float32)
    d_ref[...] = value
    low_ref[...] = value.astype(jnp.bfloat16)


def in_back_kernel(
    slot_ref, x_ref, own_ref, c_ref, z_ref, gain_ref, d_ref, out_ref, sum_ref, grad_ref
):
    value = norm_back_of(slot_ref, x_ref, (own_ref, c_ref, z_ref), gain_ref, sum_ref, grad_ref)
    out_ref[...] = value + d_ref[...]


def by_row_tiles(kernel, name, slot_of, inputs, outs, scratch=False):
    rows, width = 64, inputs[0].shape[1]
    steps = inputs[0].shape[0] // rows

    def spec(leaf):
        if len(leaf.shape) == 3:
            return pl.BlockSpec((1, rows, width), lambda i, p: (0, i, 0))
        if leaf.shape[0] in (1, 8):
            return pl.BlockSpec(leaf.shape, lambda i, p: (0, 0))
        return pl.BlockSpec((rows, width), lambda i, p: (i, 0))

    return pl.pallas_call(
        kernel,
        grid_spec=pltpu.PrefetchScalarGridSpec(
            num_scalar_prefetch=1,
            grid=(steps,),
            in_specs=[spec(leaf) for leaf in inputs],
            out_specs=[spec(leaf) for leaf in outs],
            scratch_shapes=[pltpu.VMEM((rows, width), jnp.float32)] if scratch else [],
        ),
        out_shape=outs,
        compiler_params=pltpu.CompilerParams(vmem_limit_bytes=24 * 2**20),
        cost_estimate=pl.CostEstimate(flops=0, bytes_accessed=8 * 2**20, transcendentals=0),
        name=name,
    )(slot_of, *inputs)


def mlp_back_kernel(
    slot_ref, dy_ref, gate_ref, up_ref, down_ref, act_ref, dgate_ref, dup_ref, branch_ref, weight_ref
):
    block = down_ref.shape[1]

    @pl.when(pl.program_id(0) == 0)
    def _():
        for index in range(8):
            weight_ref[index * block : (index + 1) * block, :] = down_ref[slot_ref[index]]

    units, step = gate_ref.shape[1], 512
    dy = dy_ref[...]
    total = None
    for start in range(0, units, step):
        columns = slice(start, start + step)
        weight = weight_ref[columns, :]
        gate, upper = gate_ref[:, columns], up_ref[:, columns]
        d_act = dot_t(dy, weight)
        sigma = 1.0 / (1.0 + jnp.exp(-gate))
        silu = gate * sigma
        act = (silu * upper).astype(jnp.bfloat16)
        act_ref[:, columns] = act
        dup_ref[:, columns] = (d_act * silu).astype(jnp.bfloat16)
        d_gate = d_act * upper * sigma * (1.0 + gate * (1.0 - sigma))
        dgate_ref[:, columns] = d_gate.astype(jnp.bfloat16)
        term = jnp.dot(act, weight, preferred_element_type=jnp.float32)
        total = term if total is None else total + term
    branch_ref[0] = total.astype(jnp.bfloat16)


def mlp_back(slot_of, d_branch, gate, upper, down_blocks):
    count, units = gate.shape
    width = d_branch.shape[1]
    rows = 256
    by_rows = lambda columns: pl.BlockSpec((rows, columns), lambda i, p: (i, 0))
    wide = jax.ShapeDtypeStruct((count, units), jnp.bfloat16)
    return pl.pallas_call(
        mlp_back_kernel,
        grid_spec=pltpu.PrefetchScalarGridSpec(
            num_scalar_prefetch=1,
            grid=(count // rows,),
            in_specs=[
                by_rows(width),
                by_rows(units),
                by_rows(units),
                pl.BlockSpec(down_blocks.shape, lambda i, p: (0, 0, 0)),
            ],
            out_specs=[by_rows(units)] * 3
            + [pl.BlockSpec((1, rows, width), lambda i, p: (i, 0, 0))],
            scratch_shapes=[pltpu.VMEM((units, width), jnp.bfloat16)],
        ),
        out_shape=[
            wide,
            wide,
            wide,
            jax.ShapeDtypeStruct((count // rows, rows, width), jnp.bfloat16),
        ],
        compiler_params=pltpu.CompilerParams(vmem_limit_bytes=56 * 2**20),
        cost_estimate=pl.CostEstimate(
            flops=4 * count * units * width, bytes_accessed=32 * 2**20, transcendentals=0
        ),
        name="mlp_back",
    )(slot_of, d_branch, gate, upper, down_blocks)


def slot_grad_kernel(slot_ref, left_ref, right_ref, out_ref):
    block = out_ref.shape[1]
    grad = t_dot(left_ref[...], right_ref[...]).astype(jnp.bfloat16)
    for index in range(8):
        out_ref[slot_ref[index]] = grad[index * block : (index + 1) * block, :]


def slot_grad(slot_of, left, right):
    count, rows = left.shape
    width = right.shape[1]
    columns = 512
    return pl.pallas_call(
        slot_grad_kernel,
        grid_spec=pltpu.PrefetchScalarGridSpec(
            num_scalar_prefetch=1,
            grid=(width // columns,),
            in_specs=[
                pl.BlockSpec((count, rows), lambda i, p: (0, 0)),
                pl.BlockSpec((count, columns), lambda i, p: (0, i)),
            ],
            out_specs=pl.BlockSpec((8, rows // 8, columns), lambda i, p: (0, 0, i)),
        ),
        out_shape=jax.ShapeDtypeStruct((8, rows // 8, width), jnp.bfloat16),
        compiler_params=pltpu.CompilerParams(vmem_limit_bytes=48 * 2**20),
        cost_estimate=pl.CostEstimate(
            flops=2 * count * rows * width, bytes_accessed=16 * 2**20, transcendentals=0
        ),
        name="slot_grad",
    )(slot_of, left, right)


class Grads(Task):
    copies = 1

    def outs(self):
        rows, left, right = self.inputs
        block = rows.shape[1] // 8
        return [jax.ShapeDtypeStruct((8, block, one.shape[1]), jnp.bfloat16) for one in (left, right)]

    def scratch(self):
        return []

    def steps(self, place, ins, outs, scratch):
        count, width = self.inputs[0].shape
        block = width // 8

        def body(rows_ref, left_ref, right_ref, left_out, right_out):
            rows = rows_ref[...]
            left_out[0] = t_dot(rows, left_ref[...]).astype(jnp.bfloat16)
            right_out[0] = t_dot(rows, right_ref[...]).astype(jnp.bfloat16)

        def whole(one):
            return pl.BlockSpec((count, one.shape[1]), lambda i: (0, 0))

        def out(one):
            return pl.BlockSpec((1, block, one.shape[1]), lambda i: (i, 0, 0))

        run = pltpu.emit_pipeline(
            body,
            grid=(8,),
            in_specs=[
                pl.BlockSpec((count, block), lambda i: (0, i)),
                whole(self.inputs[1]),
                whole(self.inputs[2]),
            ],
            out_specs=[out(self.inputs[1]), out(self.inputs[2])],
        )
        return [lambda: None, None, lambda: run(*ins, *outs), None]


def shards_paired(
    hidden_in,
    cotangent,
    doc_lengths,
    owner,
    projection_master_weight,
    gateup_weight,
    out_weight,
    down_weight,
    projection_first_moment,
    gateup_first,
    out_first,
    down_first,
    projection_second_moment,
    gateup_second,
    out_second,
    down_second,
    gains,
    gain_first,
    gain_second,
):
    high, low = lax.axis_index("mp") // 2, lax.axis_index("mp") % 2
    plane = high
    groups = lax.axis_size("mp")
    query_width = QUERY_HEADS // groups * HEAD_SIZE
    key_width = KEY_VALUE_HEADS // groups * HEAD_SIZE
    units = FF // groups
    rows_here = hidden_in.shape[0]
    count = 4 * rows_here
    half = count // 2
    width = hidden_in.shape[1]
    slot_of = (owner ^ plane).astype(jnp.int32)
    out_rate = float(QUERY_HEADS * HEAD_SIZE // 32) ** (-0.5)

    ln_in = gains[:MODEL_WIDTH]
    ln_mid = gains[MODEL_WIDTH : 2 * MODEL_WIDTH]
    q_gain = gains[2 * MODEL_WIDTH : 2 * MODEL_WIDTH + HEAD_SIZE]
    k_gain = gains[2 * MODEL_WIDTH + HEAD_SIZE :]
    low_gateup = gateup_weight.astype(jnp.bfloat16)
    own_in = by_row_tiles(
        norm_kernel,
        "norm_in",
        slot_of,
        [hidden_in, ln_in[None]],
        [jax.ShapeDtypeStruct(hidden_in.shape, jnp.bfloat16)],
    )
    (qkv_blocks,), (out_blocks,), (full_in,), (near_gate,) = transfer(
        "gather_first",
        1,
        75,
        Planes(projection_master_weight.astype(jnp.bfloat16)),
        Planes(out_weight.astype(jnp.bfloat16)),
        Rows(own_in[0]),
        Near(low_gateup[:, :units], phase=1),
    )
    full_in = full_in.reshape(count, width)
    w_qkv = qkv_blocks.reshape(width, -1)
    w_out = jnp.take(out_blocks, slot_of, axis=0, mode="clip").reshape(-1, width)
    gate_blocks = over_plane(near_gate)
    near_up = to_group(after(low_gateup[:, units:], full_in))

    lengths = jnp.concatenate([doc_lengths, move(doc_lengths, OVER_C)], axis=0)
    ends = jnp.cumsum(lengths, axis=1)
    spot = jnp.arange(half, dtype=jnp.int32)
    chunk = spot // rows_here
    own_places = high * half + (low ^ chunk) * rows_here + spot % rows_here
    later = own_places[None, :, None] >= ends[:, None, :]
    begin = jnp.max(jnp.where(later, ends[:, None, :], 0), axis=2).reshape(count, 1)
    time = jnp.concatenate([own_places, own_places]).reshape(count, 1)
    freq = THETA ** (-(2.0 * jnp.arange(HEAD_SIZE // 2, dtype=jnp.float32)) / HEAD_SIZE)
    angle = (time - begin).astype(jnp.float32) * freq[None, :]
    cosine, sine = jnp.cos(angle), jnp.sin(angle)
    cosine = jnp.concatenate([cosine, cosine], axis=-1)
    sine = jnp.concatenate([-sine, sine], axis=-1)
    head_gains = jnp.stack([q_gain, k_gain])
    place = jnp.stack([high, low]).astype(jnp.int32)

    raw, queries, own_kv = project(
        full_in, qkv_blocks, cosine, sine, head_gains, query_width, key_width
    )
    (lower_kv,), (d_branch,) = transfer("keys_up", 2, 47, Halves(own_kv, 0), Rows(cotangent))
    d_branch = d_branch.reshape(count, width)
    lower_kv, near_up = lax.optimization_barrier((lower_kv, near_up))
    up_blocks = over_plane(near_up)
    score_flops = 2 * count * count * query_width
    (attn_heads,) = attention_call(
        attend_kernel,
        "attend",
        place,
        [time, begin, queries, lower_kv, own_kv],
        [jax.ShapeDtypeStruct((count, query_width), jnp.bfloat16)],
        2 * score_flops,
    )

    def blocks(partial):
        return partial.astype(jnp.bfloat16).reshape(4, rows_here, width)

    partial = blocks(jnp.dot(attn_heads, w_out, preferred_element_type=jnp.float32))
    received, (near_down,) = transfer(
        "sum_attention", 3, 50, Sums(partial), Near(down_weight.astype(jnp.bfloat16))
    )
    down_blocks = over_plane(near_down)
    row = jax.ShapeDtypeStruct((rows_here, width), jnp.float32)
    low_row = jax.ShapeDtypeStruct((rows_here, width), jnp.bfloat16)
    gain_row = jax.ShapeDtypeStruct((8, width), jnp.float32)
    mixed, own_mid = by_row_tiles(
        mix_kernel, "mix", slot_of, [hidden_in, partial, *received, ln_mid[None]], [row, low_row]
    )
    ((full_mid,),) = transfer("gather_mid", 4, 34, Rows(own_mid))
    full_mid = full_mid.reshape(count, width)
    w_gate = gate_blocks.reshape(width, units)
    gate = jnp.dot(full_mid, w_gate, preferred_element_type=jnp.float32)
    up_blocks, gate = lax.optimization_barrier((up_blocks, gate))
    w_up = up_blocks.reshape(width, units)
    upper = jnp.dot(full_mid, w_up, preferred_element_type=jnp.float32)
    down_blocks, upper = lax.optimization_barrier((down_blocks, upper))
    act, d_gate, d_upper, branch = mlp_back(slot_of, d_branch, gate, upper, down_blocks)
    g_down = slot_grad(slot_of, act, d_branch)
    d_gate, d_upper, g_down = lax.optimization_barrier((d_gate, d_upper, g_down))
    near_g_down = to_plane(g_down)
    partial = blocks(
        jnp.einsum("tc,dc->td", d_gate, w_gate, preferred_element_type=jnp.float32)
        + jnp.einsum("tc,dc->td", d_upper, w_up, preferred_element_type=jnp.float32)
    )
    received, (g_gate, g_up) = transfer(
        "sum_mid", 5, 33, Sums(partial), Grads(full_mid, d_gate, d_upper)
    )
    near_g_gate, near_g_up = to_plane(g_gate), to_plane(g_up)
    d_mixed, low_d_mixed, mid_gain = by_row_tiles(
        mix_back_kernel,
        "mix_back",
        slot_of,
        [mixed, partial, *received, ln_mid[None], cotangent],
        [row, low_row, gain_row],
        scratch=True,
    )
    g_ln_mid = jnp.sum(mid_gain, axis=0)
    (d_attn,), (owned_down,) = transfer(
        "gather_attention", 6, 40, Rows(low_d_mixed), Owners(near_g_down)
    )
    d_attn = d_attn.reshape(count, width)
    red_down = both(owned_down)
    g_out = slot_grad(slot_of, attn_heads, d_attn)
    d_heads = jnp.einsum("td,hd->th", d_attn, w_out, preferred_element_type=jnp.float32).astype(
        jnp.bfloat16
    )
    d_heads, near_g_gate, g_out = lax.optimization_barrier((d_heads, near_g_gate, g_out))
    near_g_out = to_plane(g_out)
    owned_gate = to_owner(near_g_gate)
    d_queries, d_low, d_own = attention_call(
        attend_back_kernel,
        "attend_back",
        place,
        [time, begin, queries, lower_kv, own_kv, d_heads],
        [
            jax.ShapeDtypeStruct((count, query_width), jnp.float32),
            jax.ShapeDtypeStruct((count, 2 * key_width), jnp.bfloat16),
            jax.ShapeDtypeStruct((count, 2 * key_width), jnp.float32),
        ],
        5 * score_flops,
    )
    d_low, *owned_gate = lax.optimization_barrier((d_low, *owned_gate))
    red_gate = both(owned_gate)
    (from_above,), received = transfer("keys_down", 7, 53, Halves(d_low, 1), Sums(branch))
    result_rows = mixed + summed(branch, received)
    near_g_up, from_above = lax.optimization_barrier((near_g_up, from_above))
    d_projected, g_q, g_k = unproject(
        place, d_queries, d_own, from_above, raw, cosine, sine, head_gains
    )
    g_q, g_k = jnp.sum(g_q, axis=0), jnp.sum(g_k, axis=0)
    g_qkv = jnp.einsum("td,tc->dc", full_in, d_projected, preferred_element_type=jnp.float32)
    near_g_qkv = to_plane(g_qkv.astype(jnp.bfloat16).reshape(8, width // 8, -1))
    partial = blocks(
        jnp.einsum("tc,dc->td", d_projected, w_qkv, preferred_element_type=jnp.float32)
    )
    received, (owned_up,) = transfer("sum_in", 8, 40, Sums(partial), Owners(near_g_up))
    red_gateup = jnp.concatenate([red_gate, both(owned_up)], axis=1)
    near_g_out, near_g_qkv, *received = lax.optimization_barrier((near_g_out, near_g_qkv, *received))
    red_out, red_qkv = both(to_owner(near_g_out)), both(to_owner(near_g_qkv))
    input_grad, in_gain = by_row_tiles(
        in_back_kernel,
        "in_back",
        slot_of,
        [hidden_in, partial, *received, ln_in[None], d_mixed],
        [row, gain_row],
        scratch=True,
    )
    g_ln_in = jnp.sum(in_gain, axis=0)
    gain_terms = jnp.concatenate([g_ln_in, g_ln_mid, g_q, g_k])
    squares = jnp.sum(red_qkv * red_qkv) + jnp.sum(red_gateup * red_gateup)
    squares = squares + jnp.sum(red_out * red_out) + jnp.sum(red_down * red_down)
    totals_here = sum_all(jnp.concatenate([gain_terms, squares[None]]))
    gain_grad, total_squares = totals_here[:-1], totals_here[-1]
    grad_norm = jnp.sqrt(total_squares + jnp.sum(gain_grad * gain_grad))
    factor = jnp.minimum(1.0, CLIP_LIMIT / (grad_norm + 1e-06))
    qkv_new, qkv_first_new, qkv_second_new = adam(
        projection_master_weight,
        projection_first_moment,
        projection_second_moment,
        red_qkv,
        factor,
        LEARN,
        WEIGHT_DECAY,
    )
    gateup_new, gateup_first_new, gateup_second_new = adam(
        gateup_weight, gateup_first, gateup_second, red_gateup, factor, LEARN, WEIGHT_DECAY
    )
    out_new, out_first_new, out_second_new = adam(
        out_weight, out_first, out_second, red_out, factor, out_rate, WEIGHT_DECAY
    )
    down_new, down_first_new, down_second_new = adam(
        down_weight, down_first, down_second, red_down, factor, LEARN, WEIGHT_DECAY
    )
    gains_new, gain_first_new, gain_second_new = adam(
        gains, gain_first, gain_second, gain_grad, factor, GAIN_LEARN, 0.0
    )
    return (
        result_rows.astype(jnp.bfloat16),
        input_grad,
        qkv_new,
        gateup_new,
        out_new,
        down_new,
        qkv_first_new,
        gateup_first_new,
        out_first_new,
        down_first_new,
        qkv_second_new,
        gateup_second_new,
        out_second_new,
        down_second_new,
        gains_new,
        gain_first_new,
        gain_second_new,
        grad_norm,
    )


def paired(mesh):
    return dict(mesh.shape) == {"dp": 8, "mp": 4}


def solution(mesh):
    placed = (
        P(("dp", "mp"), None),
        P(("dp", "mp"), None),
        P("dp", None),
        P(),
        P("dp", "mp"),
        P("dp", "mp"),
        P(("mp", "dp"), None),
        P(("mp", "dp"), None),
        P("dp", "mp"),
        P("dp", "mp"),
        P(("mp", "dp"), None),
        P(("mp", "dp"), None),
        P("dp", "mp"),
        P("dp", "mp"),
        P(("mp", "dp"), None),
        P(("mp", "dp"), None),
        P(),
        P(),
        P(),
    )
    return jax.shard_map(
        shards_paired if paired(mesh) else shards_general,
        mesh=mesh,
        in_specs=placed,
        out_specs=(
            P(("dp", "mp"), None),
            P(("dp", "mp"), None),
            P("dp", "mp"),
            P("dp", "mp"),
            P(("mp", "dp"), None),
            P(("mp", "dp"), None),
            P("dp", "mp"),
            P("dp", "mp"),
            P(("mp", "dp"), None),
            P(("mp", "dp"), None),
            P("dp", "mp"),
            P("dp", "mp"),
            P(("mp", "dp"), None),
            P(("mp", "dp"), None),
            P(),
            P(),
            P(),
            P(),
        ),
        check_vma=False,
    )
```

```python
import jax
import jax.numpy as jnp
from jax import lax
from jax.experimental import pallas as pl
from jax.experimental.pallas import tpu as pltpu
from jax.sharding import PartitionSpec as P

MODEL_WIDTH = 2048
QUERY_HEADS = 16
KEY_VALUE_HEADS = 8
HEAD_SIZE = 128
FF = 6144
STEP = 10


EPS_NORM = 1e-06
THETA = 1000000.0
LEARN = 0.03
GAIN_LEARN = 0.5
FIRST_DECAY = 0.9
SECOND_DECAY = 0.95
ADAM_EPS = 1e-08
WEIGHT_DECAY = 0.1
CLIP_LIMIT = 1.0
MASKED = -1e30


def rms_norm(value_rows, gain):
    return (
        value_rows
        * lax.rsqrt(jnp.mean(value_rows * value_rows, axis=-1, keepdims=True) + EPS_NORM)
        * gain
    )


def norm_back(value_rows, gain, grad):
    score_scale = lax.rsqrt(jnp.mean(value_rows * value_rows, axis=-1, keepdims=True) + EPS_NORM)
    normed_input = value_rows * score_scale
    d_normal = grad * gain
    d_values = score_scale * (
        d_normal - normed_input * jnp.mean(d_normal * normed_input, axis=-1, keepdims=True)
    )
    d_gain = jnp.sum((grad * normed_input).reshape(-1, value_rows.shape[-1]), axis=0)
    return (d_values, d_gain)


def turned(value_rows):
    half = value_rows.shape[-1] // 2
    return jnp.concatenate([-value_rows[..., half:], value_rows[..., :half]], axis=-1)


def rotate(value_rows, cosine, sine):
    return value_rows * cosine + turned(value_rows) * sine


def rotate_back(grad, cosine, sine):
    return grad * cosine - turned(grad * sine)


def rope_tables(lengths, count):
    ends = jnp.cumsum(lengths)
    starts = ends - lengths
    places = jnp.arange(count, dtype=jnp.int32)
    doc_of = jnp.sum((places[:, None] >= ends[None, :]).astype(jnp.int32), axis=1)
    chosen = doc_of[:, None] == jnp.arange(lengths.shape[0], dtype=jnp.int32)[None, :]
    begin = jnp.sum(jnp.where(chosen, starts[None, :], 0), axis=1)
    offset = (places - begin).astype(jnp.float32)
    half = HEAD_SIZE // 2
    freq = THETA ** (-(2.0 * jnp.arange(half, dtype=jnp.float32)) / HEAD_SIZE)
    angle = offset[:, None] * freq[None, :]
    angle = jnp.concatenate([angle, angle], axis=-1)
    return (doc_of, jnp.cos(angle), jnp.sin(angle))


def arrange(gathered, order, blocks_count):
    blocks = gathered.reshape(blocks_count, gathered.shape[0] // blocks_count, gathered.shape[1])
    return jnp.take(blocks, order, axis=0).reshape(gathered.shape)


def fetch_weights(
    projection_master_weight, gateup_weight, out_weight, down_weight, owner, blocks_count
):
    gathered = (
        lax.all_gather(projection_master_weight.astype(jnp.bfloat16), "dp", axis=0, tiled=True),
        lax.all_gather(gateup_weight.astype(jnp.bfloat16), "dp", axis=0, tiled=True),
        lax.all_gather(out_weight.astype(jnp.bfloat16), "dp", axis=0, tiled=True),
        lax.all_gather(down_weight.astype(jnp.bfloat16), "dp", axis=0, tiled=True),
    )
    return tuple((arrange(piece, owner, blocks_count) for piece in gathered))


def fetch_again(
    projection_master_weight, gateup_weight, out_weight, down_weight, owner, blocks_count
):
    gathered = (
        lax.all_gather(projection_master_weight.astype(jnp.bfloat16), "dp", axis=0, tiled=True),
        lax.all_gather(gateup_weight.astype(jnp.bfloat16), "dp", axis=0, tiled=True),
        lax.all_gather(out_weight.astype(jnp.bfloat16), "dp", axis=0, tiled=True),
        lax.all_gather(down_weight.astype(jnp.bfloat16), "dp", axis=0, tiled=True),
    )
    return tuple((arrange(piece, owner, blocks_count) for piece in gathered))


def collect(rows):
    return lax.all_gather(rows, "mp", axis=0, tiled=True)


def collect_back(rows):
    return lax.all_gather(rows, "mp", axis=0, tiled=True)


def spread(operand, weight, rows):

    def term(start, count):
        return jnp.dot(operand, weight, preferred_element_type=jnp.float32)

    return lax.psum_scatter(
        term(jnp.int32(0), rows * lax.axis_size("mp")).astype(jnp.bfloat16),
        "mp",
        scatter_dimension=0,
        tiled=True,
    ).astype(jnp.float32)


def spread_back(operand, weight, rows):

    def term(start, count):
        return jnp.einsum("tc,dc->td", operand, weight, preferred_element_type=jnp.float32)

    return lax.psum_scatter(
        term(jnp.int32(0), rows * lax.axis_size("mp")).astype(jnp.bfloat16),
        "mp",
        scatter_dimension=0,
        tiled=True,
    ).astype(jnp.float32)


def adam(weight, first, second, grad, factor, rate, decay):
    clipped = grad * factor
    first_new = FIRST_DECAY * first + (1.0 - FIRST_DECAY) * clipped
    second_new = SECOND_DECAY * second + (1.0 - SECOND_DECAY) * clipped * clipped
    first_hat = first_new / (1.0 - FIRST_DECAY**STEP)
    second_hat = second_new / (1.0 - SECOND_DECAY**STEP)
    weight_new = weight * (1.0 - rate * decay) - rate * first_hat / (
        jnp.sqrt(second_hat) + ADAM_EPS
    )
    return (weight_new, first_new, second_new)


def shards_general(
    hidden_in,
    cotangent,
    doc_lengths,
    owner,
    projection_master_weight,
    gateup_weight,
    out_weight,
    down_weight,
    projection_first_moment,
    gateup_first,
    out_first,
    down_first,
    projection_second_moment,
    gateup_second,
    out_second,
    down_second,
    gains,
    gain_first,
    gain_second,
):
    total_width = lax.axis_size("mp")
    blocks_count = lax.axis_size("dp")
    heads = QUERY_HEADS // total_width
    key_value_heads = KEY_VALUE_HEADS // total_width
    query_group = heads // key_value_heads
    query_width = heads * HEAD_SIZE
    key_width = key_value_heads * HEAD_SIZE
    units = FF // total_width
    rows_here = hidden_in.shape[0]
    inverse = jnp.argsort(owner)
    out_rate = float(QUERY_HEADS * HEAD_SIZE // 32) ** (-0.5)
    w_qkv, w_gateup, w_out, w_down = fetch_weights(
        projection_master_weight, gateup_weight, out_weight, down_weight, owner, blocks_count
    )
    ln_in = gains[:MODEL_WIDTH]
    ln_mid = gains[MODEL_WIDTH : 2 * MODEL_WIDTH]
    q_gain = gains[2 * MODEL_WIDTH : 2 * MODEL_WIDTH + HEAD_SIZE]
    k_gain = gains[2 * MODEL_WIDTH + HEAD_SIZE :]
    x_rows = hidden_in.astype(jnp.float32)
    full_in = collect(rms_norm(x_rows, ln_in).astype(jnp.bfloat16))
    projected = jnp.dot(full_in, w_qkv, preferred_element_type=jnp.float32)
    count = projected.shape[0]
    doc_of, cosine, sine = rope_tables(doc_lengths[0], count)
    cosine = cosine[:, None, :]
    sine = sine[:, None, :]
    query_raw = projected[:, :query_width].reshape(count, heads, HEAD_SIZE)
    unrotated_key = projected[:, query_width : query_width + key_width].reshape(
        count, key_value_heads, HEAD_SIZE
    )
    projected_value = projected[:, query_width + key_width :].reshape(
        count, key_value_heads, HEAD_SIZE
    )
    query_rows = rotate(rms_norm(query_raw, q_gain), cosine, sine).astype(jnp.bfloat16)
    key_rows = rotate(rms_norm(unrotated_key, k_gain), cosine, sine).astype(jnp.bfloat16)
    value_rows = projected_value.astype(jnp.bfloat16)
    block = min(512, count)
    nblocks = count // block
    score_scale = HEAD_SIZE ** (-0.5)
    places = jnp.arange(count, dtype=jnp.int32)

    def scores_of(start):
        query_block = lax.dynamic_slice_in_dim(query_rows, start, block, 0).reshape(
            block, key_value_heads, query_group, HEAD_SIZE
        )
        raw = (
            jnp.einsum("tlwd,uld->lwtu", query_block, key_rows, preferred_element_type=jnp.float32)
            * score_scale
        )
        row_doc = lax.dynamic_slice_in_dim(doc_of, start, block, 0)
        row_place = start + jnp.arange(block, dtype=jnp.int32)
        allowed = (row_doc[:, None] == doc_of[None, :]) & (places[None, :] <= row_place[:, None])
        return (jnp.where(allowed[None, None], raw, MASKED), query_block)

    def forward_block(index):
        score_matrix, query_block = scores_of(index * block)
        top = jnp.max(score_matrix, axis=-1, keepdims=True)
        total = jnp.log(jnp.sum(jnp.exp(score_matrix - top), axis=-1, keepdims=True)) + top
        probabilities = jnp.exp(score_matrix - total).astype(jnp.bfloat16)
        attention_result = jnp.einsum(
            "cpyx,xca->ycpa", probabilities, value_rows, preferred_element_type=jnp.float32
        )
        return (attention_result.reshape(block, query_width), total)

    outs, totals = lax.map(forward_block, jnp.arange(nblocks, dtype=jnp.int32))
    attn_heads = outs.reshape(count, query_width).astype(jnp.bfloat16)
    attn_rows = spread(attn_heads, w_out, rows_here)
    mixed = x_rows + attn_rows
    full_mid = collect(rms_norm(mixed, ln_mid).astype(jnp.bfloat16))
    gateup = jnp.dot(full_mid, w_gateup, preferred_element_type=jnp.float32)
    gate = gateup[:, :units]
    upper = gateup[:, units:]
    sigma = jax.nn.sigmoid(gate)
    act = (gate * sigma * upper).astype(jnp.bfloat16)
    mlp_rows = spread(act, w_down, rows_here)
    result_rows = mixed + mlp_rows
    w_qkv, w_gateup, w_out, w_down = fetch_again(
        projection_master_weight, gateup_weight, out_weight, down_weight, owner, blocks_count
    )
    grad_out = cotangent.astype(jnp.float32)
    d_branch = collect_back(grad_out.astype(jnp.bfloat16))
    g_down = jnp.einsum("tf,td->fd", act, d_branch, preferred_element_type=jnp.float32)
    d_act = jnp.einsum("td,fd->tf", d_branch, w_down, preferred_element_type=jnp.float32)
    d_upper = d_act * gate * sigma
    d_gate = d_act * upper * sigma * (1.0 + gate * (1.0 - sigma))
    d_gateup = jnp.concatenate([d_gate, d_upper], axis=1).astype(jnp.bfloat16)
    g_gateup = jnp.einsum("td,tf->df", full_mid, d_gateup, preferred_element_type=jnp.float32)
    d_mid_rows = spread_back(d_gateup, w_gateup, rows_here)
    d_mixed, g_ln_mid = norm_back(mixed, ln_mid, d_mid_rows)
    d_mixed = d_mixed + grad_out
    d_attn = collect_back(d_mixed.astype(jnp.bfloat16))
    g_out = jnp.einsum("th,td->hd", attn_heads, d_attn, preferred_element_type=jnp.float32)
    d_heads = jnp.einsum("td,hd->th", d_attn, w_out, preferred_element_type=jnp.float32).astype(
        jnp.bfloat16
    )
    d_heads = d_heads.reshape(count, key_value_heads, query_group, HEAD_SIZE)

    def backward_block(carry, index):
        d_key_sum, d_value_sum = carry
        start = index * block
        score_matrix, query_block = scores_of(start)
        probabilities = jnp.exp(score_matrix - totals[index])
        block_gradient = lax.dynamic_slice_in_dim(d_heads, start, block, 0)
        probability_gradient = jnp.einsum(
            "tlwd,uld->lwtu", block_gradient, value_rows, preferred_element_type=jnp.float32
        )
        d_value_sum = d_value_sum + jnp.einsum(
            "zxrb,rzxd->bzd",
            probabilities.astype(jnp.bfloat16),
            block_gradient,
            preferred_element_type=jnp.float32,
        )
        score_gradient = (
            probabilities
            * (
                probability_gradient
                - jnp.sum(probabilities * probability_gradient, axis=-1, keepdims=True)
            )
        ).astype(jnp.bfloat16)
        d_query = (
            jnp.einsum(
                "cpyx,xca->ycpa", score_gradient, key_rows, preferred_element_type=jnp.float32
            )
            * score_scale
        )
        d_key_sum = (
            d_key_sum
            + jnp.einsum(
                "zxrb,rzxd->bzd", score_gradient, query_block, preferred_element_type=jnp.float32
            )
            * score_scale
        )
        return ((d_key_sum, d_value_sum), d_query.reshape(block, heads, HEAD_SIZE))

    empty = jnp.zeros((count, key_value_heads, HEAD_SIZE), jnp.float32)
    (d_keys, d_values), d_queries = lax.scan(
        backward_block, (empty, empty), jnp.arange(nblocks, dtype=jnp.int32)
    )
    d_queries = d_queries.reshape(count, heads, HEAD_SIZE)
    d_query_raw, g_q = norm_back(query_raw, q_gain, rotate_back(d_queries, cosine, sine))
    d_key_raw, g_k = norm_back(unrotated_key, k_gain, rotate_back(d_keys, cosine, sine))
    d_projected = jnp.concatenate(
        [
            d_query_raw.reshape(count, query_width),
            d_key_raw.reshape(count, key_width),
            d_values.reshape(count, key_width),
        ],
        axis=1,
    ).astype(jnp.bfloat16)
    g_qkv = jnp.einsum("td,tc->dc", full_in, d_projected, preferred_element_type=jnp.float32)
    d_in_rows = spread_back(d_projected, w_qkv, rows_here)
    d_input, g_ln_in = norm_back(x_rows, ln_in, d_in_rows)
    input_grad = d_input + d_mixed
    gain_terms = jnp.concatenate([g_ln_in, g_ln_mid, g_q, g_k])
    red_qkv, red_gateup, red_out, red_down = (
        lax.psum_scatter(
            arrange(g_qkv, inverse, blocks_count).astype(jnp.bfloat16),
            "dp",
            scatter_dimension=0,
            tiled=True,
        ).astype(jnp.float32),
        lax.psum_scatter(
            arrange(g_gateup, inverse, blocks_count).astype(jnp.bfloat16),
            "dp",
            scatter_dimension=0,
            tiled=True,
        ).astype(jnp.float32),
        lax.psum_scatter(
            arrange(g_out, inverse, blocks_count).astype(jnp.bfloat16),
            "dp",
            scatter_dimension=0,
            tiled=True,
        ).astype(jnp.float32),
        lax.psum_scatter(
            arrange(g_down, inverse, blocks_count).astype(jnp.bfloat16),
            "dp",
            scatter_dimension=0,
            tiled=True,
        ).astype(jnp.float32),
    )
    squares = jnp.sum(red_qkv * red_qkv) + jnp.sum(red_gateup * red_gateup)
    squares = squares + jnp.sum(red_out * red_out) + jnp.sum(red_down * red_down)
    total_squares, gain_grad = lax.psum((squares, gain_terms), ("dp", "mp"))
    grad_norm = jnp.sqrt(total_squares + jnp.sum(gain_grad * gain_grad))
    factor = jnp.minimum(1.0, CLIP_LIMIT / (grad_norm + 1e-06))
    qkv_new, qkv_first_new, qkv_second_new = adam(
        projection_master_weight,
        projection_first_moment,
        projection_second_moment,
        red_qkv,
        factor,
        LEARN,
        WEIGHT_DECAY,
    )
    gateup_new, gateup_first_new, gateup_second_new = adam(
        gateup_weight, gateup_first, gateup_second, red_gateup, factor, LEARN, WEIGHT_DECAY
    )
    out_new, out_first_new, out_second_new = adam(
        out_weight, out_first, out_second, red_out, factor, out_rate, WEIGHT_DECAY
    )
    down_new, down_first_new, down_second_new = adam(
        down_weight, down_first, down_second, red_down, factor, LEARN, WEIGHT_DECAY
    )
    gains_new, gain_first_new, gain_second_new = adam(
        gains, gain_first, gain_second, gain_grad, factor, GAIN_LEARN, 0.0
    )
    return (
        result_rows.astype(jnp.bfloat16),
        input_grad,
        qkv_new,
        gateup_new,
        out_new,
        down_new,
        qkv_first_new,
        gateup_first_new,
        out_first_new,
        down_first_new,
        qkv_second_new,
        gateup_second_new,
        out_second_new,
        down_second_new,
        gains_new,
        gain_first_new,
        gain_second_new,
        grad_norm,
    )


def steps(move):
    pairs = []
    for index in range(32):
        y, x, c, zh, zl = (index >> 4) & 1, (index >> 3) & 1, (index >> 2) & 1, (index >> 1) & 1, index & 1
        source = move(y, x, c, zh, zl)
        if source is not None:
            sy, sx, sc, sh, sl = source
            pairs.append(((sy << 4) | (sx << 3) | (sc << 2) | (sh << 1) | sl, index))
    return pairs


OVER_X = steps(lambda y, x, c, h, l: (y, 1 - x, c, h, l))
OVER_Y = steps(lambda y, x, c, h, l: (1 - y, x, c, h, l))
OVER_C = steps(lambda y, x, c, h, l: (y, x, 1 - c, h, l))
OVER_L = steps(lambda y, x, c, h, l: (y, x, c, h, 1 - l))
TO_GROUP = (
    steps(lambda y, x, c, h, l: (y, x, h, c, l)),
    steps(lambda y, x, c, h, l: (y, x, 1 - h, c, l)),
)
FROM_GROUP = tuple([(b, a) for a, b in pairs] for pairs in TO_GROUP)
UPWARD = steps(lambda y, x, c, h, l: (y, x, c, 0, l) if h == 1 else None)
DOWNWARD = steps(lambda y, x, c, h, l: (y, x, c, 1, l) if h == 0 else None)


def move(value, pairs):
    return lax.ppermute(value, ("dp", "mp"), pairs)


def after(value, *others):
    return lax.optimization_barrier((value, *others))[0]


PLANES = [[(block * 2 + c) * 4 + z for block in range(4)] for c in range(2) for z in range(4)]


MESH = pl.DeviceIdType.MESH


class Place:
    def __init__(self):
        dp, mp = lax.axis_index("dp"), lax.axis_index("mp")
        self.y, self.x, self.c = dp // 4, (dp // 2) % 2, dp % 2
        self.h, self.l = mp // 2, mp % 2
        self.block = (dp // 2) * 2

    def at(self, y=None, x=None, c=None, h=None, l=None):
        y, x, c = (o if n is None else n for o, n in ((self.y, y), (self.x, x), (self.c, c)))
        h, l = (o if n is None else n for o, n in ((self.h, h), (self.l, l)))
        return ((y * 2 + x) * 2 + c, h * 2 + l)

    def partners(self):
        return [
            self.at(x=1 - self.x),
            self.at(y=1 - self.y),
            self.at(l=1 - self.l),
            self.at(c=1 - self.c),
            self.at(h=1 - self.h),
            self.at(c=1 - self.c, h=1 - self.h),
        ]


def far_copy(source, target, sems, index, device):
    return pltpu.make_async_remote_copy(
        src_ref=source,
        dst_ref=target,
        send_sem=sems[0].at[index],
        recv_sem=sems[1].at[index],
        device_id=device,
        device_id_type=MESH,
    )


class Swap:
    def __init__(self, place, source, target, sems, index, local_sem):
        self.same = place.c == place.h
        self.far = far_copy(source, target, sems, index, place.at(c=place.h, h=place.c))
        self.near = pltpu.make_async_copy(source, target, local_sem)

    def start(self):
        pl.when(self.same)(self.near.start)
        pl.when(~self.same)(self.far.start)

    def wait_recv(self):
        pl.when(self.same)(self.near.wait)
        pl.when(~self.same)(self.far.wait_recv)

    def wait_send(self):
        pl.when(~self.same)(self.far.wait_send)


class Task:
    copies = 1
    locals = 1
    work = ()

    def __init__(self, *inputs, phase=0):
        self.inputs, self.phase = inputs, phase

    def scratch(self):
        return [
            pltpu.SemaphoreType.DMA((self.copies,)),
            pltpu.SemaphoreType.DMA((self.copies,)),
            pltpu.SemaphoreType.DMA((self.locals,)),
            *self.work,
        ]


class Rows(Task):
    copies = 3

    def outs(self):
        rows = self.inputs[0]
        return [jax.ShapeDtypeStruct((4, *rows.shape), rows.dtype)]

    def steps(self, place, ins, outs, scratch):
        own, full = ins[0], outs[0]
        send, recv, local = scratch[:3]
        keep = pltpu.make_async_copy(own, full.at[0], local.at[0])
        over_z = far_copy(own, full.at[1], (send, recv), 0, place.at(l=1 - place.l))
        over_c = far_copy(own, full.at[2], (send, recv), 1, place.at(c=1 - place.c))
        relay = far_copy(full.at[1], full.at[3], (send, recv), 2, place.at(c=1 - place.c))

        def first():
            over_z.start()
            over_c.start()
            keep.start()

        def second():
            over_z.wait_recv()
            relay.start()

        def last():
            keep.wait()
            over_c.wait()
            over_z.wait_send()
            relay.wait()

        return [first, None, second, last]


class Sums(Task):
    copies = 3

    def __init__(self, *inputs, phase=0):
        super().__init__(*inputs, phase=phase)
        block = inputs[0].shape[1:]
        self.work = tuple(pltpu.VMEM(block, jnp.bfloat16) for _ in range(3))

    def outs(self):
        block = jax.ShapeDtypeStruct(self.inputs[0].shape[1:], jnp.bfloat16)
        return [block, block]

    def steps(self, place, ins, outs, scratch):
        partial, (from_c, from_z) = ins[0], outs
        send, recv, local, mine, theirs, total = scratch
        core = place.at(c=1 - place.c)
        load = pltpu.make_async_copy(partial.at[1], mine, local.at[0])
        far = far_copy(partial.at[3], theirs, (send, recv), 0, core)
        near = far_copy(partial.at[2], from_c, (send, recv), 1, core)
        over_z = far_copy(total, from_z, (send, recv), 2, place.at(l=1 - place.l))
        rows = 32

        def first():
            far.start()
            near.start()
            load.start()

        def second():
            load.wait()
            far.wait_recv()

            @pl.loop(0, mine.shape[0] // rows)
            def _(index):
                part = pl.ds(pl.multiple_of(index * rows, rows), rows)
                summed = mine[part, :].astype(jnp.float32) + theirs[part, :].astype(jnp.float32)
                total[part, :] = summed.astype(jnp.bfloat16)

            over_z.start()

        def last():
            far.wait_send()
            near.wait()
            over_z.wait()

        return [first, second, None, last]


class Near(Task):
    copies = 2

    def outs(self):
        shard = self.inputs[0]
        return [jax.ShapeDtypeStruct((2, *shard.shape), shard.dtype)]

    def copies_of(self, place, shard, first, second, scratch):
        send, recv, local = scratch[:3]
        return (
            Swap(place, shard, first, (send, recv), 0, local.at[0]),
            far_copy(shard, second, (send, recv), 1, place.at(c=place.h, h=1 - place.c)),
        )

    def steps(self, place, ins, outs, scratch):
        a, b = self.copies_of(place, ins[0], outs[0].at[0], outs[0].at[1], scratch)

        def first():
            a.start()
            b.start()

        def last():
            a.wait_recv()
            a.wait_send()
            b.wait()

        return [first, None, None, last]


class Planes(Near):
    copies = 8

    def outs(self):
        shard = self.inputs[0]
        return [jax.ShapeDtypeStruct((8, *shard.shape), shard.dtype)]

    def steps(self, place, ins, outs, scratch):
        full = outs[0]
        block = place.block
        a, b = self.copies_of(place, ins[0], full.at[block], full.at[block + 1], scratch)
        over_x, over_y = place.at(x=1 - place.x), place.at(y=1 - place.y)
        x_block = block + 2 - 4 * place.x
        y_block = block + 4 - 8 * place.y

        def pass_on(slot, index, device):
            return far_copy(full.at[slot], full.at[slot], scratch[:2], index, device)

        ax, ay = pass_on(block, 2, over_x), pass_on(block, 3, over_y)
        by, bx = pass_on(block + 1, 4, over_y), pass_on(block + 1, 5, over_x)
        axy = pass_on(x_block, 6, over_y)
        byx = pass_on(y_block + 1, 7, over_x)

        def first():
            a.start()
            b.start()

        def second():
            a.wait_recv()
            ax.start()
            b.wait_recv()
            by.start()
            ay.start()
            bx.start()

        def third():
            ax.wait_recv()
            axy.start()
            by.wait_recv()
            byx.start()

        def last():
            a.wait_send()
            b.wait_send()
            for copy in (ax, by):
                copy.wait_send()
            for copy in (ay, bx, axy, byx):
                copy.wait()

        return [first, second, third, last]


class Owners(Task):
    copies = 2

    def outs(self):
        near = self.inputs[0]
        return [jax.ShapeDtypeStruct(near.shape, near.dtype)]

    def steps(self, place, ins, outs, scratch):
        send, recv, local = scratch[:3]
        near, got = ins[0], outs[0]
        a = Swap(place, near.at[0], got.at[0], (send, recv), 0, local.at[0])
        b = far_copy(near.at[1], got.at[1], (send, recv), 1, place.at(c=1 - place.h, h=place.c))

        def first():
            a.start()
            b.start()

        def last():
            a.wait_recv()
            a.wait_send()
            b.wait()

        return [first, None, None, last]


class Halves(Task):
    def __init__(self, array, sender, phase=0):
        super().__init__(array, phase=phase)
        self.sender = sender

    def outs(self):
        return [jax.ShapeDtypeStruct(self.inputs[0].shape, self.inputs[0].dtype)]

    def steps(self, place, ins, outs, scratch):
        copy = far_copy(ins[0], outs[0], scratch[:2], 0, place.at(h=1 - place.h))
        sends = place.h == self.sender

        def first():
            pl.when(sends)(copy.start)

        def last():
            pl.when(sends)(copy.wait_send)
            pl.when(~sends)(copy.wait_recv)

        return [first, None, None, last]


def transfer(name, number, micros, *tasks, scoped=12):
    outs = [task.outs() for task in tasks]
    scratch = [task.scratch() for task in tasks]

    def kernel(*refs):
        refs = list(refs)

        def take(count):
            taken = refs[:count]
            del refs[:count]
            return taken

        ins_of = [take(len(task.inputs)) for task in tasks]
        outs_of = [take(len(out)) for out in outs]
        scratch_of = [take(len(one)) for one in scratch]
        place = Place()
        barrier = pltpu.get_barrier_semaphore()
        partners = place.partners()
        for partner in partners:
            pl.semaphore_signal(barrier, inc=1, device_id=partner, device_id_type=MESH)
        pl.semaphore_wait(barrier, len(partners))
        plans = [
            task.steps(place, ins_of[n], outs_of[n], scratch_of[n]) for n, task in enumerate(tasks)
        ]
        for phase in range(4):
            for task, plan in zip(tasks, plans):
                steps_now = [plan[phase]] if phase else []
                if phase == task.phase:
                    steps_now.insert(0, plan[0])
                for step in steps_now:
                    if step is not None:
                        step()

    results = pl.pallas_call(
        kernel,
        out_shape=[leaf for out in outs for leaf in out],
        in_specs=[pl.BlockSpec(memory_space=pl.ANY) for task in tasks for _ in task.inputs],
        out_specs=[pl.BlockSpec(memory_space=pl.ANY) for out in outs for _ in out],
        scratch_shapes=[one for part in scratch for one in part],
        compiler_params=pltpu.CompilerParams(
            collective_id=number, has_side_effects=True, vmem_limit_bytes=scoped * 2**20
        ),
        cost_estimate=pl.CostEstimate(
            flops=0, bytes_accessed=micros * 3_300_000, transcendentals=0
        ),
        name=name,
    )(*[leaf for task in tasks for leaf in task.inputs])
    results = list(results)
    grouped = []
    for out in outs:
        grouped.append(results[: len(out)])
        del results[: len(out)]
    return grouped


def to_group(shard):
    return jnp.stack([move(shard, TO_GROUP[0]), move(shard, TO_GROUP[1])])


def to_owner(near):
    return [move(near[0], FROM_GROUP[0]), move(near[1], FROM_GROUP[1])]


def over_plane(near):
    return lax.all_gather(near, ("dp", "mp"), axis=0, tiled=True, axis_index_groups=PLANES)


def to_plane(grads):
    return lax.psum_scatter(
        grads, ("dp", "mp"), scatter_dimension=0, tiled=True, axis_index_groups=PLANES
    )


def both(pair):
    return pair[0].astype(jnp.float32) + pair[1].astype(jnp.float32)


def summed(partial, received):
    return both(received) + partial[0].astype(jnp.float32)


def sum_all_kernel(value, total, by_mp, by_dp, send_sem, recv_sem):
    dp, mp = lax.axis_index("dp"), lax.axis_index("mp")
    over_mp = [(dp, (mp + step) % 4) for step in range(1, 4)]
    over_dp = [((dp + step) % 8, mp) for step in range(1, 8)]
    barrier = pltpu.get_barrier_semaphore()
    for partner in over_mp + over_dp:
        pl.semaphore_signal(
            barrier, inc=1, device_id=partner, device_id_type=pl.DeviceIdType.MESH
        )
    pl.semaphore_wait(barrier, len(over_mp) + len(over_dp))

    def share(table, place, partners, first):
        copies = [
            pltpu.make_async_remote_copy(
                src_ref=table.at[place],
                dst_ref=table.at[place],
                send_sem=send_sem.at[first + step],
                recv_sem=recv_sem.at[first + step],
                device_id=partner,
                device_id_type=pl.DeviceIdType.MESH,
            )
            for step, partner in enumerate(partners)
        ]
        for copy in copies:
            copy.start()
        for copy in copies:
            copy.wait()

    by_mp[mp] = value[...]
    share(by_mp, mp, over_mp, 0)
    by_dp[dp] = (by_mp[0] + by_mp[1]) + (by_mp[2] + by_mp[3])
    share(by_dp, dp, over_dp, 3)
    result = by_dp[0]
    for place in range(1, 8):
        result = result + by_dp[place]
    total[...] = result


def sum_all(vector):
    size = vector.shape[0]
    rows = -(-size // 1024) * 8
    block = jnp.pad(vector, (0, rows * 128 - size)).reshape(rows, 128)
    total = pl.pallas_call(
        sum_all_kernel,
        out_shape=jax.ShapeDtypeStruct((rows, 128), jnp.float32),
        in_specs=[pl.BlockSpec(memory_space=pltpu.VMEM)],
        out_specs=pl.BlockSpec(memory_space=pltpu.VMEM),
        scratch_shapes=[
            pltpu.VMEM((4, rows, 128), jnp.float32),
            pltpu.VMEM((8, rows, 128), jnp.float32),
            pltpu.SemaphoreType.DMA((10,)),
            pltpu.SemaphoreType.DMA((10,)),
        ],
        compiler_params=pltpu.CompilerParams(collective_id=0, has_side_effects=True),
        name="sum_all",
    )(block)
    return total.reshape(-1)[:size]


def column_places(index, high, low, rows):
    chunk = index // rows
    return high * 2 * rows + (low + chunk - 2 * low * chunk) * rows + index - chunk * rows


def project_kernel(rows_ref, weight_ref, cos_ref, sin_ref, gain_ref, raw_ref, query_ref, kv_ref):
    width = rows_ref.shape[1]
    weight = weight_ref[...].reshape(width, weight_ref.shape[2])
    projected = jnp.dot(rows_ref[...], weight, preferred_element_type=jnp.float32)
    query_width, key_width = query_ref.shape[1], kv_ref.shape[1] // 2
    turned_width = query_width + key_width
    raw_ref[...] = projected[:, :turned_width]
    cosine, sine = cos_ref[...], sin_ref[...]
    for start in range(0, turned_width, HEAD_SIZE):
        raw = projected[:, start : start + HEAD_SIZE]
        gain = gain_ref[0:1, :] if start < query_width else gain_ref[1:2, :]
        normed = raw * lax.rsqrt(jnp.mean(raw * raw, axis=1, keepdims=True) + EPS_NORM) * gain
        turned = normed * cosine + pltpu.roll(normed, HEAD_SIZE // 2, 1) * sine
        if start < query_width:
            query_ref[:, start : start + HEAD_SIZE] = turned.astype(jnp.bfloat16)
        else:
            place = start - query_width
            kv_ref[:, place : place + HEAD_SIZE] = turned.astype(jnp.bfloat16)
    kv_ref[:, key_width:] = projected[:, turned_width:].astype(jnp.bfloat16)


def project(rows, blocks, cosine, sine, head_gains, query_width, key_width):
    count, width = rows.shape
    tile = 256
    total = query_width + 2 * key_width
    by_rows = lambda columns: pl.BlockSpec((tile, columns), lambda i: (i, 0))
    return pl.pallas_call(
        project_kernel,
        grid=(count // tile,),
        in_specs=[
            by_rows(width),
            pl.BlockSpec((8, width // 8, total), lambda i: (0, 0, 0)),
            by_rows(HEAD_SIZE),
            by_rows(HEAD_SIZE),
            pl.BlockSpec((2, HEAD_SIZE), lambda i: (0, 0)),
        ],
        out_specs=[by_rows(query_width + key_width), by_rows(query_width), by_rows(2 * key_width)],
        out_shape=[
            jax.ShapeDtypeStruct((count, query_width + key_width), jnp.float32),
            jax.ShapeDtypeStruct((count, query_width), jnp.bfloat16),
            jax.ShapeDtypeStruct((count, 2 * key_width), jnp.bfloat16),
        ],
        compiler_params=pltpu.CompilerParams(vmem_limit_bytes=48 * 2**20),
        cost_estimate=pl.CostEstimate(
            flops=2 * count * width * total, bytes_accessed=16 * 2**20, transcendentals=0
        ),
        name="project",
    )(rows, blocks, cosine, sine, head_gains)


def unproject_kernel(
    place_ref, dq_ref, own_ref, above_ref, raw_ref, cos_ref, sin_ref, gain_ref, out_ref, gq_ref, gk_ref
):
    query_width, key_width = dq_ref.shape[1], own_ref.shape[1] // 2
    turned_width = query_width + key_width
    lower = place_ref[0] == 0
    cosine, sine = cos_ref[...], sin_ref[...]

    @pl.when(pl.program_id(0) == 0)
    def _():
        gq_ref[...] = jnp.zeros_like(gq_ref)
        gk_ref[...] = jnp.zeros_like(gk_ref)

    def with_above(columns):
        above = jnp.where(lower, above_ref[:, columns].astype(jnp.float32), 0.0)
        return own_ref[:, columns] + above

    for start in range(0, turned_width, HEAD_SIZE):
        columns = slice(start, start + HEAD_SIZE)
        if start < query_width:
            grad, gain, gain_sum = dq_ref[:, columns], gain_ref[0:1, :], gq_ref
        else:
            grad = with_above(slice(start - query_width, start - query_width + HEAD_SIZE))
            gain, gain_sum = gain_ref[1:2, :], gk_ref
        grad = grad * cosine - pltpu.roll(grad, HEAD_SIZE // 2, 1) * sine
        raw = raw_ref[:, columns]
        scale = lax.rsqrt(jnp.mean(raw * raw, axis=1, keepdims=True) + EPS_NORM)
        normed = raw * scale
        gain_sum[...] += jnp.sum((grad * normed).reshape(-1, 8, HEAD_SIZE), axis=0)
        d_normal = grad * gain
        value = scale * (d_normal - normed * jnp.mean(d_normal * normed, axis=1, keepdims=True))
        out_ref[:, columns] = value.astype(jnp.bfloat16)
    out_ref[:, turned_width:] = with_above(slice(key_width, 2 * key_width)).astype(jnp.bfloat16)


def unproject(place, d_queries, d_own, above, raw, cosine, sine, head_gains):
    count, query_width = d_queries.shape
    key_width = d_own.shape[1] // 2
    tile = 256
    total = query_width + 2 * key_width
    by_rows = lambda columns: pl.BlockSpec((tile, columns), lambda i, p: (i, 0))
    fixed = lambda rows: pl.BlockSpec((rows, HEAD_SIZE), lambda i, p: (0, 0))
    return pl.pallas_call(
        unproject_kernel,
        grid_spec=pltpu.PrefetchScalarGridSpec(
            num_scalar_prefetch=1,
            grid=(count // tile,),
            in_specs=[
                by_rows(query_width),
                by_rows(2 * key_width),
                by_rows(2 * key_width),
                by_rows(query_width + key_width),
                by_rows(HEAD_SIZE),
                by_rows(HEAD_SIZE),
                fixed(2),
            ],
            out_specs=[by_rows(total), fixed(8), fixed(8)],
        ),
        out_shape=[
            jax.ShapeDtypeStruct((count, total), jnp.bfloat16),
            jax.ShapeDtypeStruct((8, HEAD_SIZE), jnp.float32),
            jax.ShapeDtypeStruct((8, HEAD_SIZE), jnp.float32),
        ],
        compiler_params=pltpu.CompilerParams(vmem_limit_bytes=32 * 2**20),
        cost_estimate=pl.CostEstimate(flops=0, bytes_accessed=2 * 2**20, transcendentals=0),
        name="unproject",
    )(place, d_queries, d_own, above, raw, cosine, sine, head_gains)


def dot_t(left, right):
    return lax.dot_general(
        left, right, (((1,), (1,)), ((), ())), preferred_element_type=jnp.float32
    )


def t_dot(left, right):
    return lax.dot_general(
        left, right, (((0,), (0,)), ((), ())), preferred_element_type=jnp.float32
    )


def exps_of(place_ref, time_ref, begin_ref, rows, query, key_low, key_own):
    high, low = place_ref[0], place_ref[1]
    keys = key_own.shape[0]
    scale = HEAD_SIZE ** (-0.5)
    column = lax.broadcasted_iota(jnp.int32, (rows.size, keys), 1)
    time, begin = time_ref[rows, :], begin_ref[rows, :]
    own_place = column_places(column, high, low, keys // 2)
    low_place = column_places(column, 0, low, keys // 2)
    own_seen = (own_place <= time) & (own_place >= begin)
    low_seen = (low_place >= begin) & (low_place < high * keys)
    own = jnp.where(own_seen, dot_t(query, key_own) * scale, MASKED)
    lower = jnp.where(low_seen, dot_t(query, key_low) * scale, MASKED)
    top = jnp.maximum(
        jnp.max(own, axis=1, keepdims=True), jnp.max(lower, axis=1, keepdims=True)
    )
    own, lower = jnp.exp(own - top), jnp.exp(lower - top)
    total = jnp.sum(own, axis=1, keepdims=True) + jnp.sum(lower, axis=1, keepdims=True)
    return lower, own, 1.0 / total


def attend_kernel(place_ref, time_ref, begin_ref, query_ref, low_ref, own_ref, out_ref):
    half, query_width = query_ref.shape
    key_width = own_ref.shape[1] // 2
    group = query_width // key_width
    size = half // 2
    upper = place_ref[0] == 1
    for kv in range(key_width // HEAD_SIZE):
        key_at = slice(kv * HEAD_SIZE, (kv + 1) * HEAD_SIZE)
        value_at = slice(key_width + kv * HEAD_SIZE, key_width + (kv + 1) * HEAD_SIZE)
        key_low, key_own, value_own = low_ref[:, key_at], own_ref[:, key_at], own_ref[:, value_at]
        value_low = jnp.where(upper, low_ref[:, value_at], jnp.zeros_like(value_own))
        for part in range(2):
            rows = pl.ds(part * size, size)
            for head in range(kv * group, (kv + 1) * group):
                query_at = slice(head * HEAD_SIZE, (head + 1) * HEAD_SIZE)
                lower, own, inverse = exps_of(
                    place_ref, time_ref, begin_ref, rows, query_ref[rows, query_at], key_low, key_own
                )
                result = jnp.dot(
                    lower.astype(jnp.bfloat16), value_low, preferred_element_type=jnp.float32
                ) + jnp.dot(own.astype(jnp.bfloat16), value_own, preferred_element_type=jnp.float32)
                out_ref[rows, query_at] = (result * inverse).astype(jnp.bfloat16)


def attend_back_kernel(
    place_ref, time_ref, begin_ref, query_ref, low_ref, own_ref, grad_ref, dq_ref, dlow_ref, down_ref
):
    half, query_width = query_ref.shape
    key_width = own_ref.shape[1] // 2
    group = query_width // key_width
    size = half // 2
    scale = HEAD_SIZE ** (-0.5)
    upper = place_ref[0] == 1
    for kv in range(key_width // HEAD_SIZE):
        key_at = slice(kv * HEAD_SIZE, (kv + 1) * HEAD_SIZE)
        value_at = slice(key_width + kv * HEAD_SIZE, key_width + (kv + 1) * HEAD_SIZE)
        key_own, value_own = own_ref[:, key_at], own_ref[:, value_at]
        key_low = jnp.where(upper, low_ref[:, key_at], jnp.zeros_like(key_own))
        value_low = jnp.where(upper, low_ref[:, value_at], jnp.zeros_like(value_own))
        dk_low = dk_own = dv_low = dv_own = None
        for part in range(2):
            rows = pl.ds(part * size, size)
            for head in range(kv * group, (kv + 1) * group):
                query_at = slice(head * HEAD_SIZE, (head + 1) * HEAD_SIZE)
                query, grad = query_ref[rows, query_at], grad_ref[rows, query_at]
                lower, own, inverse = exps_of(
                    place_ref, time_ref, begin_ref, rows, query, key_low, key_own
                )
                lower, own = lower * inverse, own * inverse
                g_low, g_own = dot_t(grad, value_low), dot_t(grad, value_own)
                mean = jnp.sum(lower * g_low, axis=1, keepdims=True) + jnp.sum(
                    own * g_own, axis=1, keepdims=True
                )
                s_low = (lower * (g_low - mean)).astype(jnp.bfloat16)
                s_own = (own * (g_own - mean)).astype(jnp.bfloat16)
                dq_ref[rows, query_at] = scale * (
                    jnp.dot(s_low, key_low, preferred_element_type=jnp.float32)
                    + jnp.dot(s_own, key_own, preferred_element_type=jnp.float32)
                )
                terms = (
                    t_dot(s_low, query),
                    t_dot(s_own, query),
                    t_dot(lower.astype(jnp.bfloat16), grad),
                    t_dot(own.astype(jnp.bfloat16), grad),
                )
                if dk_low is None:
                    dk_low, dk_own, dv_low, dv_own = terms
                else:
                    dk_low, dk_own = dk_low + terms[0], dk_own + terms[1]
                    dv_low, dv_own = dv_low + terms[2], dv_own + terms[3]
        dlow_ref[:, key_at] = (dk_low * scale).astype(jnp.bfloat16)
        dlow_ref[:, value_at] = dv_low.astype(jnp.bfloat16)
        down_ref[:, key_at] = dk_own * scale
        down_ref[:, value_at] = dv_own


def attention_call(kernel, name, place, arrays, outs, flops):
    count = arrays[0].shape[0]
    half = count // 2
    spec = lambda leaf: pl.BlockSpec((half, leaf.shape[1]), lambda i, p: (i, 0))
    return pl.pallas_call(
        kernel,
        grid_spec=pltpu.PrefetchScalarGridSpec(
            num_scalar_prefetch=1,
            grid=(2,),
            in_specs=[spec(leaf) for leaf in arrays],
            out_specs=[spec(leaf) for leaf in outs],
        ),
        out_shape=outs,
        compiler_params=pltpu.CompilerParams(vmem_limit_bytes=56 * 2**20),
        cost_estimate=pl.CostEstimate(flops=flops, bytes_accessed=16 * 2**20, transcendentals=0),
        name=name,
    )(place, *arrays)


def scaled(values):
    return values * lax.rsqrt(jnp.mean(values * values, axis=1, keepdims=True) + EPS_NORM)


def three(parts, columns=slice(None)):
    own, from_c, from_z = parts
    return (
        own[0, :, columns].astype(jnp.float32)
        + from_c[:, columns].astype(jnp.float32)
        + from_z[:, columns].astype(jnp.float32)
    )


def slot_columns(slot_ref, index, block):
    return pl.ds(pl.multiple_of(slot_ref[index] * block, block), block)


def store_slots(slot_ref, out_ref, values):
    block = out_ref.shape[1] // 8
    for index in range(8):
        out_ref[:, slot_columns(slot_ref, index, block)] = values[
            :, index * block : (index + 1) * block
        ]


def norm_kernel(slot_ref, x_ref, gain_ref, out_ref):
    x = x_ref[...].astype(jnp.float32)
    store_slots(slot_ref, out_ref, (scaled(x) * gain_ref[...]).astype(jnp.bfloat16))


def mix_kernel(slot_ref, x_ref, own_ref, c_ref, z_ref, gain_ref, mixed_ref, out_ref):
    mixed = x_ref[...].astype(jnp.float32) + three((own_ref, c_ref, z_ref))
    mixed_ref[...] = mixed
    store_slots(slot_ref, out_ref, (scaled(mixed) * gain_ref[...]).astype(jnp.bfloat16))


def norm_back_of(slot_ref, value_ref, parts, gain_ref, sum_ref, grad_ref):
    width = value_ref.shape[1]
    block = width // 8
    for index in range(8):
        grad_ref[:, index * block : (index + 1) * block] = three(
            parts, slot_columns(slot_ref, index, block)
        )
    value, grad = value_ref[...].astype(jnp.float32), grad_ref[...]
    scale = lax.rsqrt(jnp.mean(value * value, axis=1, keepdims=True) + EPS_NORM)
    normed = value * scale

    @pl.when(pl.program_id(0) == 0)
    def _():
        sum_ref[...] = jnp.zeros_like(sum_ref)

    sum_ref[...] += jnp.sum((grad * normed).reshape(-1, 8, width), axis=0)
    d_normal = grad * gain_ref[...]
    return scale * (d_normal - normed * jnp.mean(d_normal * normed, axis=1, keepdims=True))


def mix_back_kernel(
    slot_ref, mixed_ref, own_ref, c_ref, z_ref, gain_ref, cot_ref, d_ref, low_ref, sum_ref, grad_ref
):
    value = norm_back_of(slot_ref, mixed_ref, (own_ref, c_ref, z_ref), gain_ref, sum_ref, grad_ref)
    value = value + cot_ref[...].astype(jnp.float32)
    d_ref[...] = value
    low_ref[...] = value.astype(jnp.bfloat16)


def in_back_kernel(
    slot_ref, x_ref, own_ref, c_ref, z_ref, gain_ref, d_ref, out_ref, sum_ref, grad_ref
):
    value = norm_back_of(slot_ref, x_ref, (own_ref, c_ref, z_ref), gain_ref, sum_ref, grad_ref)
    out_ref[...] = value + d_ref[...]


def by_row_tiles(kernel, name, slot_of, inputs, outs, scratch=False, micros=3):
    rows, width = 64, inputs[0].shape[1]
    steps = inputs[0].shape[0] // rows

    def spec(leaf):
        if len(leaf.shape) == 3:
            return pl.BlockSpec((1, rows, width), lambda i, p: (0, i, 0))
        if leaf.shape[0] in (1, 8):
            return pl.BlockSpec(leaf.shape, lambda i, p: (0, 0))
        return pl.BlockSpec((rows, width), lambda i, p: (i, 0))

    return pl.pallas_call(
        kernel,
        grid_spec=pltpu.PrefetchScalarGridSpec(
            num_scalar_prefetch=1,
            grid=(steps,),
            in_specs=[spec(leaf) for leaf in inputs],
            out_specs=[spec(leaf) for leaf in outs],
            scratch_shapes=[pltpu.VMEM((rows, width), jnp.float32)] if scratch else [],
        ),
        out_shape=outs,
        compiler_params=pltpu.CompilerParams(vmem_limit_bytes=(60 if scratch else 24) * 2**20),
        cost_estimate=pl.CostEstimate(flops=0, bytes_accessed=micros * 3_300_000, transcendentals=0),
        name=name,
    )(slot_of, *inputs)


def mlp_front_kernel(rows_ref, gate_ref, up_ref, gate_out, up_out, act_out):
    width = rows_ref.shape[1]
    rows = rows_ref[...]
    gate = jnp.dot(rows, gate_ref[...].reshape(width, -1), preferred_element_type=jnp.float32)
    upper = jnp.dot(rows, up_ref[...].reshape(width, -1), preferred_element_type=jnp.float32)
    gate_out[...] = gate
    up_out[...] = upper
    act_out[...] = (gate * upper / (1.0 + jnp.exp(-gate))).astype(jnp.bfloat16)


def mlp_front(rows, gate_blocks, up_blocks):
    count, width = rows.shape
    units = gate_blocks.shape[2]
    columns = 256
    weight = pl.BlockSpec((8, width // 8, columns), lambda i: (0, 0, i))
    out = pl.BlockSpec((count, columns), lambda i: (0, i))
    return pl.pallas_call(
        mlp_front_kernel,
        grid=(units // columns,),
        in_specs=[pl.BlockSpec((count, width), lambda i: (0, 0)), weight, weight],
        out_specs=[out, out, out],
        out_shape=[
            jax.ShapeDtypeStruct((count, units), jnp.float32),
            jax.ShapeDtypeStruct((count, units), jnp.float32),
            jax.ShapeDtypeStruct((count, units), jnp.bfloat16),
        ],
        compiler_params=pltpu.CompilerParams(vmem_limit_bytes=32 * 2**20),
        cost_estimate=pl.CostEstimate(
            flops=4 * count * units * width, bytes_accessed=32 * 2**20, transcendentals=0
        ),
        name="mlp_front",
    )(rows, gate_blocks, up_blocks)


def mlp_back_kernel(
    slot_ref, dy_ref, gate_ref, up_ref, act_ref, down_ref, dgate_ref, dup_ref, branch_ref, weight_ref
):
    block = down_ref.shape[1]

    @pl.when(pl.program_id(0) == 0)
    def _():
        for index in range(8):
            weight_ref[index * block : (index + 1) * block, :] = down_ref[slot_ref[index]]

    units, step = gate_ref.shape[1], 512
    dy = dy_ref[...]
    total = None
    for start in range(0, units, step):
        columns = slice(start, start + step)
        weight = weight_ref[columns, :]
        gate, upper = gate_ref[:, columns], up_ref[:, columns]
        d_act = dot_t(dy, weight)
        sigma = 1.0 / (1.0 + jnp.exp(-gate))
        dup_ref[:, columns] = (d_act * gate * sigma).astype(jnp.bfloat16)
        d_gate = d_act * upper * sigma * (1.0 + gate * (1.0 - sigma))
        dgate_ref[:, columns] = d_gate.astype(jnp.bfloat16)
        term = jnp.dot(act_ref[:, columns], weight, preferred_element_type=jnp.float32)
        total = term if total is None else total + term
    branch_ref[0] = total.astype(jnp.bfloat16)


def mlp_back(slot_of, d_branch, gate, upper, act, down_blocks):
    count, units = gate.shape
    width = d_branch.shape[1]
    rows = 256
    by_rows = lambda columns: pl.BlockSpec((rows, columns), lambda i, p: (i, 0))
    wide = jax.ShapeDtypeStruct((count, units), jnp.bfloat16)
    return pl.pallas_call(
        mlp_back_kernel,
        grid_spec=pltpu.PrefetchScalarGridSpec(
            num_scalar_prefetch=1,
            grid=(count // rows,),
            in_specs=[
                by_rows(width),
                by_rows(units),
                by_rows(units),
                by_rows(units),
                pl.BlockSpec(down_blocks.shape, lambda i, p: (0, 0, 0)),
            ],
            out_specs=[by_rows(units)] * 2
            + [pl.BlockSpec((1, rows, width), lambda i, p: (i, 0, 0))],
            scratch_shapes=[pltpu.VMEM((units, width), jnp.bfloat16)],
        ),
        out_shape=[
            wide,
            wide,
            jax.ShapeDtypeStruct((count // rows, rows, width), jnp.bfloat16),
        ],
        compiler_params=pltpu.CompilerParams(vmem_limit_bytes=48 * 2**20),
        cost_estimate=pl.CostEstimate(
            flops=4 * count * units * width, bytes_accessed=32 * 2**20, transcendentals=0
        ),
        name="mlp_back",
    )(slot_of, d_branch, gate, upper, act, down_blocks)


def rows_back_kernel(*refs):
    *pairs, out_ref = refs
    total = None
    for grad_ref, weight_ref in zip(pairs[::2], pairs[1::2]):
        term = dot_t(grad_ref[...], weight_ref[0])
        total = term if total is None else total + term
    out_ref[...] = total.astype(jnp.bfloat16).reshape(out_ref.shape)


def rows_back(name, *pairs):
    count = pairs[0].shape[0]
    block = pairs[1].shape[1]
    specs = []
    for grad, weight in zip(pairs[::2], pairs[1::2]):
        specs.append(pl.BlockSpec(grad.shape, lambda i: (0, 0)))
        specs.append(pl.BlockSpec((1, *weight.shape[1:]), lambda i: (i, 0, 0)))
    return pl.pallas_call(
        rows_back_kernel,
        grid=(8,),
        in_specs=specs,
        out_specs=pl.BlockSpec((4, count // 4, block), lambda i: (0, 0, i)),
        out_shape=jax.ShapeDtypeStruct((4, count // 4, 8 * block), jnp.bfloat16),
        compiler_params=pltpu.CompilerParams(vmem_limit_bytes=28 * 2**20),
        cost_estimate=pl.CostEstimate(
            flops=sum(count * w.size for w in pairs[1::2]) // 4,
            bytes_accessed=2 * 2**20,
            transcendentals=0,
        ),
        name=name,
    )(*pairs)


def adam_kernel(factor_ref, *refs, rates):
    factor = factor_ref[0]
    ins, outs = refs[: len(refs) - 3 * len(rates)], refs[len(refs) - 3 * len(rates) :]
    at = 0
    for place, (rate, pieces) in enumerate(rates):
        weight_ref, first_ref, second_ref, *grads = ins[at : at + 3 + pieces]
        at += 3 + pieces
        start = 0
        for grad_ref in grads:
            columns = slice(start, start + grad_ref.shape[1])
            start += grad_ref.shape[1]
            results = adam(
                weight_ref[:, columns],
                first_ref[:, columns],
                second_ref[:, columns],
                grad_ref[...],
                factor,
                rate,
                WEIGHT_DECAY,
            )
            for out_ref, result in zip(outs[3 * place : 3 * place + 3], results):
                out_ref[:, columns] = result


def adam_all(factor, weights):
    steps = 8
    rates = tuple((rate, len(grads)) for rate, *_, grads in weights)
    arrays, outs = [], []
    for _, master, first, second, grads in weights:
        arrays += [master, first, second, *grads]
        outs += [jax.ShapeDtypeStruct(master.shape, jnp.float32)] * 3

    def spec(leaf):
        return pl.BlockSpec((leaf.shape[0] // steps, leaf.shape[1]), lambda i, p: (i, 0))

    results = pl.pallas_call(
        lambda *refs: adam_kernel(*refs, rates=rates),
        grid_spec=pltpu.PrefetchScalarGridSpec(
            num_scalar_prefetch=1,
            grid=(steps,),
            in_specs=[spec(leaf) for leaf in arrays],
            out_specs=[spec(leaf) for leaf in outs],
        ),
        out_shape=outs,
        compiler_params=pltpu.CompilerParams(vmem_limit_bytes=60 * 2**20),
        cost_estimate=pl.CostEstimate(flops=0, bytes_accessed=48 * 2**20, transcendentals=0),
        name="adam_all",
    )(factor[None], *arrays)
    return [results[n : n + 3] for n in range(0, len(results), 3)]


def slot_grad_kernel(slot_ref, left_ref, right_ref, out_ref):
    block = out_ref.shape[1]
    grad = t_dot(left_ref[...], right_ref[...]).astype(jnp.bfloat16)
    for index in range(8):
        out_ref[slot_ref[index]] = grad[index * block : (index + 1) * block, :]


def slot_grad(slot_of, left, right):
    count, rows = left.shape
    width = right.shape[1]
    columns = 512
    return pl.pallas_call(
        slot_grad_kernel,
        grid_spec=pltpu.PrefetchScalarGridSpec(
            num_scalar_prefetch=1,
            grid=(width // columns,),
            in_specs=[
                pl.BlockSpec((count, rows), lambda i, p: (0, 0)),
                pl.BlockSpec((count, columns), lambda i, p: (0, i)),
            ],
            out_specs=pl.BlockSpec((8, rows // 8, columns), lambda i, p: (0, 0, i)),
        ),
        out_shape=jax.ShapeDtypeStruct((8, rows // 8, width), jnp.bfloat16),
        compiler_params=pltpu.CompilerParams(vmem_limit_bytes=48 * 2**20),
        cost_estimate=pl.CostEstimate(
            flops=2 * count * rows * width, bytes_accessed=16 * 2**20, transcendentals=0
        ),
        name="slot_grad",
    )(slot_of, left, right)


class Grads(Task):
    def outs(self):
        rows, left, right = self.inputs
        columns = left.shape[1] + right.shape[1]
        return [jax.ShapeDtypeStruct((8, rows.shape[1] // 8, columns), jnp.bfloat16)]

    def scratch(self):
        return []

    def steps(self, place, ins, outs, scratch):
        count, width = self.inputs[0].shape
        block = width // 8
        columns = self.inputs[1].shape[1]

        def body(rows_ref, left_ref, right_ref, out_ref):
            rows = rows_ref[...]
            out_ref[0, :, :columns] = t_dot(rows, left_ref[...]).astype(jnp.bfloat16)
            out_ref[0, :, columns:] = t_dot(rows, right_ref[...]).astype(jnp.bfloat16)

        def whole(one):
            return pl.BlockSpec((count, one.shape[1]), lambda i: (0, 0))

        run = pltpu.emit_pipeline(
            body,
            grid=(8,),
            in_specs=[
                pl.BlockSpec((count, block), lambda i: (0, i)),
                whole(self.inputs[1]),
                whole(self.inputs[2]),
            ],
            out_specs=[pl.BlockSpec((1, block, 2 * columns), lambda i: (i, 0, 0))],
        )
        return [lambda: None, None, lambda: run(*ins, *outs), None]


def shards_paired(
    hidden_in,
    cotangent,
    doc_lengths,
    owner,
    projection_master_weight,
    gateup_weight,
    out_weight,
    down_weight,
    projection_first_moment,
    gateup_first,
    out_first,
    down_first,
    projection_second_moment,
    gateup_second,
    out_second,
    down_second,
    gains,
    gain_first,
    gain_second,
):
    high, low = lax.axis_index("mp") // 2, lax.axis_index("mp") % 2
    plane = high
    groups = lax.axis_size("mp")
    query_width = QUERY_HEADS // groups * HEAD_SIZE
    key_width = KEY_VALUE_HEADS // groups * HEAD_SIZE
    units = FF // groups
    rows_here = hidden_in.shape[0]
    count = 4 * rows_here
    half = count // 2
    width = hidden_in.shape[1]
    slot_of = (owner ^ plane).astype(jnp.int32)
    out_rate = float(QUERY_HEADS * HEAD_SIZE // 32) ** (-0.5)

    ln_in = gains[:MODEL_WIDTH]
    ln_mid = gains[MODEL_WIDTH : 2 * MODEL_WIDTH]
    q_gain = gains[2 * MODEL_WIDTH : 2 * MODEL_WIDTH + HEAD_SIZE]
    k_gain = gains[2 * MODEL_WIDTH + HEAD_SIZE :]
    low_gateup = gateup_weight.astype(jnp.bfloat16)
    own_in = by_row_tiles(
        norm_kernel,
        "norm_in",
        slot_of,
        [hidden_in, ln_in[None]],
        [jax.ShapeDtypeStruct(hidden_in.shape, jnp.bfloat16)],
    )
    (qkv_blocks,), (out_blocks,), (full_in,), (near_gate,) = transfer(
        "gather_first",
        1,
        75,
        Planes(projection_master_weight.astype(jnp.bfloat16)),
        Planes(out_weight.astype(jnp.bfloat16)),
        Rows(own_in[0]),
        Near(low_gateup[:, :units], phase=1),
    )
    full_in = full_in.reshape(count, width)
    w_out = jnp.take(out_blocks, slot_of, axis=0, mode="clip").reshape(-1, width)
    gate_blocks = over_plane(near_gate)
    near_up = to_group(after(low_gateup[:, units:], full_in))

    lengths = jnp.concatenate([doc_lengths, move(doc_lengths, OVER_C)], axis=0)
    ends = jnp.cumsum(lengths, axis=1)
    spot = jnp.arange(half, dtype=jnp.int32)
    chunk = spot // rows_here
    own_places = high * half + (low ^ chunk) * rows_here + spot % rows_here
    later = own_places[None, :, None] >= ends[:, None, :]
    begin = jnp.max(jnp.where(later, ends[:, None, :], 0), axis=2).reshape(count, 1)
    time = jnp.concatenate([own_places, own_places]).reshape(count, 1)
    freq = THETA ** (-(2.0 * jnp.arange(HEAD_SIZE // 2, dtype=jnp.float32)) / HEAD_SIZE)
    angle = (time - begin).astype(jnp.float32) * freq[None, :]
    cosine, sine = jnp.cos(angle), jnp.sin(angle)
    cosine = jnp.concatenate([cosine, cosine], axis=-1)
    sine = jnp.concatenate([-sine, sine], axis=-1)
    head_gains = jnp.stack([q_gain, k_gain])
    place = jnp.stack([high, low]).astype(jnp.int32)

    raw, queries, own_kv = project(
        full_in, qkv_blocks, cosine, sine, head_gains, query_width, key_width
    )
    (lower_kv,), (d_branch,) = transfer("keys_up", 2, 47, Halves(own_kv, 0), Rows(cotangent))
    d_branch = d_branch.reshape(count, width)
    lower_kv, near_up = lax.optimization_barrier((lower_kv, near_up))
    up_blocks = over_plane(near_up)
    score_flops = 2 * count * count * query_width
    (attn_heads,) = attention_call(
        attend_kernel,
        "attend",
        place,
        [time, begin, queries, lower_kv, own_kv],
        [jax.ShapeDtypeStruct((count, query_width), jnp.bfloat16)],
        2 * score_flops,
    )

    def blocks(partial):
        return partial.astype(jnp.bfloat16).reshape(4, rows_here, width)

    partial = blocks(jnp.dot(attn_heads, w_out, preferred_element_type=jnp.float32))
    received, (near_down,) = transfer(
        "sum_attention", 3, 50, Sums(partial), Near(down_weight.astype(jnp.bfloat16))
    )
    down_blocks = over_plane(near_down)
    row = jax.ShapeDtypeStruct((rows_here, width), jnp.float32)
    low_row = jax.ShapeDtypeStruct((rows_here, width), jnp.bfloat16)
    gain_row = jax.ShapeDtypeStruct((8, width), jnp.float32)
    mixed, own_mid = by_row_tiles(
        mix_kernel, "mix", slot_of, [hidden_in, partial, *received, ln_mid[None]], [row, low_row]
    )
    ((full_mid,),) = transfer("gather_mid", 4, 34, Rows(own_mid))
    full_mid = full_mid.reshape(count, width)
    gate, upper, act = mlp_front(full_mid, gate_blocks, up_blocks)
    g_down = slot_grad(slot_of, act, d_branch)
    down_blocks, g_down = lax.optimization_barrier((down_blocks, g_down))
    near_g_down = to_plane(g_down)
    d_gate, d_upper, branch = mlp_back(slot_of, d_branch, gate, upper, act, down_blocks)
    partial = rows_back("mid_rows", d_gate, gate_blocks, d_upper, up_blocks)
    received, (g_gateup,) = transfer(
        "sum_mid", 5, 33, Sums(partial), Grads(full_mid, d_gate, d_upper), scoped=40
    )
    near_g_gateup = to_plane(g_gateup)
    d_mixed, low_d_mixed, mid_gain = by_row_tiles(
        mix_back_kernel,
        "mix_back",
        slot_of,
        [mixed, partial, *received, ln_mid[None], cotangent],
        [row, low_row, gain_row],
        scratch=True,
    )
    g_ln_mid = jnp.sum(mid_gain, axis=0)
    ((d_attn,),) = transfer("gather_attention", 6, 29, Rows(low_d_mixed))
    d_attn = d_attn.reshape(count, width)
    owned_down = to_owner(after(near_g_down, d_attn))
    g_out = slot_grad(slot_of, attn_heads, d_attn)
    d_heads = jnp.einsum("td,hd->th", d_attn, w_out, preferred_element_type=jnp.float32).astype(
        jnp.bfloat16
    )
    d_queries, d_low, d_own = attention_call(
        attend_back_kernel,
        "attend_back",
        place,
        [time, begin, queries, lower_kv, own_kv, d_heads],
        [
            jax.ShapeDtypeStruct((count, query_width), jnp.float32),
            jax.ShapeDtypeStruct((count, 2 * key_width), jnp.bfloat16),
            jax.ShapeDtypeStruct((count, 2 * key_width), jnp.float32),
        ],
        5 * score_flops,
    )
    d_low, g_out, *owned_down = lax.optimization_barrier((d_low, g_out, *owned_down))
    red_down = both(owned_down)
    near_g_out = to_plane(g_out)
    (from_above,), received = transfer("keys_down", 7, 53, Halves(d_low, 1), Sums(branch))
    result_rows = mixed + summed(branch, received)
    d_projected, g_q, g_k = unproject(
        place, d_queries, d_own, from_above, raw, cosine, sine, head_gains
    )
    g_q, g_k = jnp.sum(g_q, axis=0), jnp.sum(g_k, axis=0)
    g_qkv = jnp.einsum("td,tc->dc", full_in, d_projected, preferred_element_type=jnp.float32)
    near_g_qkv = to_plane(g_qkv.astype(jnp.bfloat16).reshape(8, width // 8, -1))
    partial = rows_back("in_rows", d_projected, qkv_blocks)
    received, (owned_gateup,) = transfer("sum_in", 8, 74, Sums(partial), Owners(near_g_gateup))
    near_g_out, near_g_qkv, *received = lax.optimization_barrier(
        (near_g_out, near_g_qkv, *received)
    )
    owned_out = to_owner(near_g_out)
    received, owned_out = lax.optimization_barrier((received, owned_out))
    red_gateup = both(owned_gateup)
    red_out, red_qkv = both(owned_out), both(to_owner(near_g_qkv))
    input_grad, in_gain = by_row_tiles(
        in_back_kernel,
        "in_back",
        slot_of,
        [hidden_in, partial, *received, ln_in[None], d_mixed],
        [row, gain_row],
        scratch=True,
        micros=40,
    )
    g_ln_in = jnp.sum(in_gain, axis=0)
    gain_terms = jnp.concatenate([g_ln_in, g_ln_mid, g_q, g_k])
    squares = sum(jnp.sum(red * red) for red in (red_qkv, red_gateup, red_out, red_down))
    totals_here = sum_all(jnp.concatenate([gain_terms, squares[None]]))
    gain_grad, total_squares = totals_here[:-1], totals_here[-1]
    grad_norm = jnp.sqrt(total_squares + jnp.sum(gain_grad * gain_grad))
    factor = jnp.minimum(1.0, CLIP_LIMIT / (grad_norm + 1e-06))
    (
        (qkv_new, qkv_first_new, qkv_second_new),
        (gateup_new, gateup_first_new, gateup_second_new),
        (out_new, out_first_new, out_second_new),
        (down_new, down_first_new, down_second_new),
    ) = adam_all(
        factor,
        [
            (
                LEARN,
                projection_master_weight,
                projection_first_moment,
                projection_second_moment,
                [red_qkv],
            ),
            (LEARN, gateup_weight, gateup_first, gateup_second, [red_gateup]),
            (out_rate, out_weight, out_first, out_second, [red_out]),
            (LEARN, down_weight, down_first, down_second, [red_down]),
        ],
    )
    gains_new, gain_first_new, gain_second_new = adam(
        gains, gain_first, gain_second, gain_grad, factor, GAIN_LEARN, 0.0
    )
    return (
        result_rows.astype(jnp.bfloat16),
        input_grad,
        qkv_new,
        gateup_new,
        out_new,
        down_new,
        qkv_first_new,
        gateup_first_new,
        out_first_new,
        down_first_new,
        qkv_second_new,
        gateup_second_new,
        out_second_new,
        down_second_new,
        gains_new,
        gain_first_new,
        gain_second_new,
        grad_norm,
    )


def paired(mesh):
    return dict(mesh.shape) == {"dp": 8, "mp": 4}


def solution(mesh):
    placed = (
        P(("dp", "mp"), None),
        P(("dp", "mp"), None),
        P("dp", None),
        P(),
        P("dp", "mp"),
        P("dp", "mp"),
        P(("mp", "dp"), None),
        P(("mp", "dp"), None),
        P("dp", "mp"),
        P("dp", "mp"),
        P(("mp", "dp"), None),
        P(("mp", "dp"), None),
        P("dp", "mp"),
        P("dp", "mp"),
        P(("mp", "dp"), None),
        P(("mp", "dp"), None),
        P(),
        P(),
        P(),
    )
    return jax.shard_map(
        shards_paired if paired(mesh) else shards_general,
        mesh=mesh,
        in_specs=placed,
        out_specs=(
            P(("dp", "mp"), None),
            P(("dp", "mp"), None),
            P("dp", "mp"),
            P("dp", "mp"),
            P(("mp", "dp"), None),
            P(("mp", "dp"), None),
            P("dp", "mp"),
            P("dp", "mp"),
            P(("mp", "dp"), None),
            P(("mp", "dp"), None),
            P("dp", "mp"),
            P("dp", "mp"),
            P(("mp", "dp"), None),
            P(("mp", "dp"), None),
            P(),
            P(),
            P(),
            P(),
        ),
        check_vma=False,
    )
```

```python
import jax
import jax.numpy as jnp
from jax import lax
from jax.experimental import pallas as pl
from jax.experimental.pallas import tpu as pltpu
from jax.sharding import PartitionSpec as P

MODEL_WIDTH = 2048
QUERY_HEADS = 16
KEY_VALUE_HEADS = 8
HEAD_SIZE = 128
FF = 6144
STEP = 10


EPS_NORM = 1e-06
THETA = 1000000.0
LEARN = 0.03
GAIN_LEARN = 0.5
FIRST_DECAY = 0.9
SECOND_DECAY = 0.95
ADAM_EPS = 1e-08
WEIGHT_DECAY = 0.1
CLIP_LIMIT = 1.0
MASKED = -1e30


def rms_norm(value_rows, gain):
    return (
        value_rows
        * lax.rsqrt(jnp.mean(value_rows * value_rows, axis=-1, keepdims=True) + EPS_NORM)
        * gain
    )


def norm_back(value_rows, gain, grad):
    score_scale = lax.rsqrt(jnp.mean(value_rows * value_rows, axis=-1, keepdims=True) + EPS_NORM)
    normed_input = value_rows * score_scale
    d_normal = grad * gain
    d_values = score_scale * (
        d_normal - normed_input * jnp.mean(d_normal * normed_input, axis=-1, keepdims=True)
    )
    d_gain = jnp.sum((grad * normed_input).reshape(-1, value_rows.shape[-1]), axis=0)
    return (d_values, d_gain)


def turned(value_rows):
    half = value_rows.shape[-1] // 2
    return jnp.concatenate([-value_rows[..., half:], value_rows[..., :half]], axis=-1)


def rotate(value_rows, cosine, sine):
    return value_rows * cosine + turned(value_rows) * sine


def rotate_back(grad, cosine, sine):
    return grad * cosine - turned(grad * sine)


def rope_tables(lengths, count):
    ends = jnp.cumsum(lengths)
    starts = ends - lengths
    places = jnp.arange(count, dtype=jnp.int32)
    doc_of = jnp.sum((places[:, None] >= ends[None, :]).astype(jnp.int32), axis=1)
    chosen = doc_of[:, None] == jnp.arange(lengths.shape[0], dtype=jnp.int32)[None, :]
    begin = jnp.sum(jnp.where(chosen, starts[None, :], 0), axis=1)
    offset = (places - begin).astype(jnp.float32)
    half = HEAD_SIZE // 2
    freq = THETA ** (-(2.0 * jnp.arange(half, dtype=jnp.float32)) / HEAD_SIZE)
    angle = offset[:, None] * freq[None, :]
    angle = jnp.concatenate([angle, angle], axis=-1)
    return (doc_of, jnp.cos(angle), jnp.sin(angle))


def arrange(gathered, order, blocks_count):
    blocks = gathered.reshape(blocks_count, gathered.shape[0] // blocks_count, gathered.shape[1])
    return jnp.take(blocks, order, axis=0).reshape(gathered.shape)


def fetch_weights(
    projection_master_weight, gateup_weight, out_weight, down_weight, owner, blocks_count
):
    gathered = (
        lax.all_gather(projection_master_weight.astype(jnp.bfloat16), "dp", axis=0, tiled=True),
        lax.all_gather(gateup_weight.astype(jnp.bfloat16), "dp", axis=0, tiled=True),
        lax.all_gather(out_weight.astype(jnp.bfloat16), "dp", axis=0, tiled=True),
        lax.all_gather(down_weight.astype(jnp.bfloat16), "dp", axis=0, tiled=True),
    )
    return tuple((arrange(piece, owner, blocks_count) for piece in gathered))


def fetch_again(
    projection_master_weight, gateup_weight, out_weight, down_weight, owner, blocks_count
):
    gathered = (
        lax.all_gather(projection_master_weight.astype(jnp.bfloat16), "dp", axis=0, tiled=True),
        lax.all_gather(gateup_weight.astype(jnp.bfloat16), "dp", axis=0, tiled=True),
        lax.all_gather(out_weight.astype(jnp.bfloat16), "dp", axis=0, tiled=True),
        lax.all_gather(down_weight.astype(jnp.bfloat16), "dp", axis=0, tiled=True),
    )
    return tuple((arrange(piece, owner, blocks_count) for piece in gathered))


def collect(rows):
    return lax.all_gather(rows, "mp", axis=0, tiled=True)


def collect_back(rows):
    return lax.all_gather(rows, "mp", axis=0, tiled=True)


def spread(operand, weight, rows):

    def term(start, count):
        return jnp.dot(operand, weight, preferred_element_type=jnp.float32)

    return lax.psum_scatter(
        term(jnp.int32(0), rows * lax.axis_size("mp")).astype(jnp.bfloat16),
        "mp",
        scatter_dimension=0,
        tiled=True,
    ).astype(jnp.float32)


def spread_back(operand, weight, rows):

    def term(start, count):
        return jnp.einsum("tc,dc->td", operand, weight, preferred_element_type=jnp.float32)

    return lax.psum_scatter(
        term(jnp.int32(0), rows * lax.axis_size("mp")).astype(jnp.bfloat16),
        "mp",
        scatter_dimension=0,
        tiled=True,
    ).astype(jnp.float32)


def adam(weight, first, second, grad, factor, rate, decay):
    clipped = grad * factor
    first_new = FIRST_DECAY * first + (1.0 - FIRST_DECAY) * clipped
    second_new = SECOND_DECAY * second + (1.0 - SECOND_DECAY) * clipped * clipped
    first_hat = first_new / (1.0 - FIRST_DECAY**STEP)
    second_hat = second_new / (1.0 - SECOND_DECAY**STEP)
    weight_new = weight * (1.0 - rate * decay) - rate * first_hat / (
        jnp.sqrt(second_hat) + ADAM_EPS
    )
    return (weight_new, first_new, second_new)


def shards_general(
    hidden_in,
    cotangent,
    doc_lengths,
    owner,
    projection_master_weight,
    gateup_weight,
    out_weight,
    down_weight,
    projection_first_moment,
    gateup_first,
    out_first,
    down_first,
    projection_second_moment,
    gateup_second,
    out_second,
    down_second,
    gains,
    gain_first,
    gain_second,
):
    total_width = lax.axis_size("mp")
    blocks_count = lax.axis_size("dp")
    heads = QUERY_HEADS // total_width
    key_value_heads = KEY_VALUE_HEADS // total_width
    query_group = heads // key_value_heads
    query_width = heads * HEAD_SIZE
    key_width = key_value_heads * HEAD_SIZE
    units = FF // total_width
    rows_here = hidden_in.shape[0]
    inverse = jnp.argsort(owner)
    out_rate = float(QUERY_HEADS * HEAD_SIZE // 32) ** (-0.5)
    w_qkv, w_gateup, w_out, w_down = fetch_weights(
        projection_master_weight, gateup_weight, out_weight, down_weight, owner, blocks_count
    )
    ln_in = gains[:MODEL_WIDTH]
    ln_mid = gains[MODEL_WIDTH : 2 * MODEL_WIDTH]
    q_gain = gains[2 * MODEL_WIDTH : 2 * MODEL_WIDTH + HEAD_SIZE]
    k_gain = gains[2 * MODEL_WIDTH + HEAD_SIZE :]
    x_rows = hidden_in.astype(jnp.float32)
    full_in = collect(rms_norm(x_rows, ln_in).astype(jnp.bfloat16))
    projected = jnp.dot(full_in, w_qkv, preferred_element_type=jnp.float32)
    count = projected.shape[0]
    doc_of, cosine, sine = rope_tables(doc_lengths[0], count)
    cosine = cosine[:, None, :]
    sine = sine[:, None, :]
    query_raw = projected[:, :query_width].reshape(count, heads, HEAD_SIZE)
    unrotated_key = projected[:, query_width : query_width + key_width].reshape(
        count, key_value_heads, HEAD_SIZE
    )
    projected_value = projected[:, query_width + key_width :].reshape(
        count, key_value_heads, HEAD_SIZE
    )
    query_rows = rotate(rms_norm(query_raw, q_gain), cosine, sine).astype(jnp.bfloat16)
    key_rows = rotate(rms_norm(unrotated_key, k_gain), cosine, sine).astype(jnp.bfloat16)
    value_rows = projected_value.astype(jnp.bfloat16)
    block = min(512, count)
    nblocks = count // block
    score_scale = HEAD_SIZE ** (-0.5)
    places = jnp.arange(count, dtype=jnp.int32)

    def scores_of(start):
        query_block = lax.dynamic_slice_in_dim(query_rows, start, block, 0).reshape(
            block, key_value_heads, query_group, HEAD_SIZE
        )
        raw = (
            jnp.einsum("tlwd,uld->lwtu", query_block, key_rows, preferred_element_type=jnp.float32)
            * score_scale
        )
        row_doc = lax.dynamic_slice_in_dim(doc_of, start, block, 0)
        row_place = start + jnp.arange(block, dtype=jnp.int32)
        allowed = (row_doc[:, None] == doc_of[None, :]) & (places[None, :] <= row_place[:, None])
        return (jnp.where(allowed[None, None], raw, MASKED), query_block)

    def forward_block(index):
        score_matrix, query_block = scores_of(index * block)
        top = jnp.max(score_matrix, axis=-1, keepdims=True)
        total = jnp.log(jnp.sum(jnp.exp(score_matrix - top), axis=-1, keepdims=True)) + top
        probabilities = jnp.exp(score_matrix - total).astype(jnp.bfloat16)
        attention_result = jnp.einsum(
            "cpyx,xca->ycpa", probabilities, value_rows, preferred_element_type=jnp.float32
        )
        return (attention_result.reshape(block, query_width), total)

    outs, totals = lax.map(forward_block, jnp.arange(nblocks, dtype=jnp.int32))
    attn_heads = outs.reshape(count, query_width).astype(jnp.bfloat16)
    attn_rows = spread(attn_heads, w_out, rows_here)
    mixed = x_rows + attn_rows
    full_mid = collect(rms_norm(mixed, ln_mid).astype(jnp.bfloat16))
    gateup = jnp.dot(full_mid, w_gateup, preferred_element_type=jnp.float32)
    gate = gateup[:, :units]
    upper = gateup[:, units:]
    sigma = jax.nn.sigmoid(gate)
    act = (gate * sigma * upper).astype(jnp.bfloat16)
    mlp_rows = spread(act, w_down, rows_here)
    result_rows = mixed + mlp_rows
    w_qkv, w_gateup, w_out, w_down = fetch_again(
        projection_master_weight, gateup_weight, out_weight, down_weight, owner, blocks_count
    )
    grad_out = cotangent.astype(jnp.float32)
    d_branch = collect_back(grad_out.astype(jnp.bfloat16))
    g_down = jnp.einsum("tf,td->fd", act, d_branch, preferred_element_type=jnp.float32)
    d_act = jnp.einsum("td,fd->tf", d_branch, w_down, preferred_element_type=jnp.float32)
    d_upper = d_act * gate * sigma
    d_gate = d_act * upper * sigma * (1.0 + gate * (1.0 - sigma))
    d_gateup = jnp.concatenate([d_gate, d_upper], axis=1).astype(jnp.bfloat16)
    g_gateup = jnp.einsum("td,tf->df", full_mid, d_gateup, preferred_element_type=jnp.float32)
    d_mid_rows = spread_back(d_gateup, w_gateup, rows_here)
    d_mixed, g_ln_mid = norm_back(mixed, ln_mid, d_mid_rows)
    d_mixed = d_mixed + grad_out
    d_attn = collect_back(d_mixed.astype(jnp.bfloat16))
    g_out = jnp.einsum("th,td->hd", attn_heads, d_attn, preferred_element_type=jnp.float32)
    d_heads = jnp.einsum("td,hd->th", d_attn, w_out, preferred_element_type=jnp.float32).astype(
        jnp.bfloat16
    )
    d_heads = d_heads.reshape(count, key_value_heads, query_group, HEAD_SIZE)

    def backward_block(carry, index):
        d_key_sum, d_value_sum = carry
        start = index * block
        score_matrix, query_block = scores_of(start)
        probabilities = jnp.exp(score_matrix - totals[index])
        block_gradient = lax.dynamic_slice_in_dim(d_heads, start, block, 0)
        probability_gradient = jnp.einsum(
            "tlwd,uld->lwtu", block_gradient, value_rows, preferred_element_type=jnp.float32
        )
        d_value_sum = d_value_sum + jnp.einsum(
            "zxrb,rzxd->bzd",
            probabilities.astype(jnp.bfloat16),
            block_gradient,
            preferred_element_type=jnp.float32,
        )
        score_gradient = (
            probabilities
            * (
                probability_gradient
                - jnp.sum(probabilities * probability_gradient, axis=-1, keepdims=True)
            )
        ).astype(jnp.bfloat16)
        d_query = (
            jnp.einsum(
                "cpyx,xca->ycpa", score_gradient, key_rows, preferred_element_type=jnp.float32
            )
            * score_scale
        )
        d_key_sum = (
            d_key_sum
            + jnp.einsum(
                "zxrb,rzxd->bzd", score_gradient, query_block, preferred_element_type=jnp.float32
            )
            * score_scale
        )
        return ((d_key_sum, d_value_sum), d_query.reshape(block, heads, HEAD_SIZE))

    empty = jnp.zeros((count, key_value_heads, HEAD_SIZE), jnp.float32)
    (d_keys, d_values), d_queries = lax.scan(
        backward_block, (empty, empty), jnp.arange(nblocks, dtype=jnp.int32)
    )
    d_queries = d_queries.reshape(count, heads, HEAD_SIZE)
    d_query_raw, g_q = norm_back(query_raw, q_gain, rotate_back(d_queries, cosine, sine))
    d_key_raw, g_k = norm_back(unrotated_key, k_gain, rotate_back(d_keys, cosine, sine))
    d_projected = jnp.concatenate(
        [
            d_query_raw.reshape(count, query_width),
            d_key_raw.reshape(count, key_width),
            d_values.reshape(count, key_width),
        ],
        axis=1,
    ).astype(jnp.bfloat16)
    g_qkv = jnp.einsum("td,tc->dc", full_in, d_projected, preferred_element_type=jnp.float32)
    d_in_rows = spread_back(d_projected, w_qkv, rows_here)
    d_input, g_ln_in = norm_back(x_rows, ln_in, d_in_rows)
    input_grad = d_input + d_mixed
    gain_terms = jnp.concatenate([g_ln_in, g_ln_mid, g_q, g_k])
    red_qkv, red_gateup, red_out, red_down = (
        lax.psum_scatter(
            arrange(g_qkv, inverse, blocks_count).astype(jnp.bfloat16),
            "dp",
            scatter_dimension=0,
            tiled=True,
        ).astype(jnp.float32),
        lax.psum_scatter(
            arrange(g_gateup, inverse, blocks_count).astype(jnp.bfloat16),
            "dp",
            scatter_dimension=0,
            tiled=True,
        ).astype(jnp.float32),
        lax.psum_scatter(
            arrange(g_out, inverse, blocks_count).astype(jnp.bfloat16),
            "dp",
            scatter_dimension=0,
            tiled=True,
        ).astype(jnp.float32),
        lax.psum_scatter(
            arrange(g_down, inverse, blocks_count).astype(jnp.bfloat16),
            "dp",
            scatter_dimension=0,
            tiled=True,
        ).astype(jnp.float32),
    )
    squares = jnp.sum(red_qkv * red_qkv) + jnp.sum(red_gateup * red_gateup)
    squares = squares + jnp.sum(red_out * red_out) + jnp.sum(red_down * red_down)
    total_squares, gain_grad = lax.psum((squares, gain_terms), ("dp", "mp"))
    grad_norm = jnp.sqrt(total_squares + jnp.sum(gain_grad * gain_grad))
    factor = jnp.minimum(1.0, CLIP_LIMIT / (grad_norm + 1e-06))
    qkv_new, qkv_first_new, qkv_second_new = adam(
        projection_master_weight,
        projection_first_moment,
        projection_second_moment,
        red_qkv,
        factor,
        LEARN,
        WEIGHT_DECAY,
    )
    gateup_new, gateup_first_new, gateup_second_new = adam(
        gateup_weight, gateup_first, gateup_second, red_gateup, factor, LEARN, WEIGHT_DECAY
    )
    out_new, out_first_new, out_second_new = adam(
        out_weight, out_first, out_second, red_out, factor, out_rate, WEIGHT_DECAY
    )
    down_new, down_first_new, down_second_new = adam(
        down_weight, down_first, down_second, red_down, factor, LEARN, WEIGHT_DECAY
    )
    gains_new, gain_first_new, gain_second_new = adam(
        gains, gain_first, gain_second, gain_grad, factor, GAIN_LEARN, 0.0
    )
    return (
        result_rows.astype(jnp.bfloat16),
        input_grad,
        qkv_new,
        gateup_new,
        out_new,
        down_new,
        qkv_first_new,
        gateup_first_new,
        out_first_new,
        down_first_new,
        qkv_second_new,
        gateup_second_new,
        out_second_new,
        down_second_new,
        gains_new,
        gain_first_new,
        gain_second_new,
        grad_norm,
    )


def steps(move):
    pairs = []
    for index in range(32):
        y, x, c, zh, zl = (index >> 4) & 1, (index >> 3) & 1, (index >> 2) & 1, (index >> 1) & 1, index & 1
        source = move(y, x, c, zh, zl)
        if source is not None:
            sy, sx, sc, sh, sl = source
            pairs.append(((sy << 4) | (sx << 3) | (sc << 2) | (sh << 1) | sl, index))
    return pairs


OVER_X = steps(lambda y, x, c, h, l: (y, 1 - x, c, h, l))
OVER_Y = steps(lambda y, x, c, h, l: (1 - y, x, c, h, l))
OVER_C = steps(lambda y, x, c, h, l: (y, x, 1 - c, h, l))
OVER_L = steps(lambda y, x, c, h, l: (y, x, c, h, 1 - l))
TO_GROUP = (
    steps(lambda y, x, c, h, l: (y, x, h, c, l)),
    steps(lambda y, x, c, h, l: (y, x, 1 - h, c, l)),
)
FROM_GROUP = tuple([(b, a) for a, b in pairs] for pairs in TO_GROUP)
UPWARD = steps(lambda y, x, c, h, l: (y, x, c, 0, l) if h == 1 else None)
DOWNWARD = steps(lambda y, x, c, h, l: (y, x, c, 1, l) if h == 0 else None)


def move(value, pairs):
    return lax.ppermute(value, ("dp", "mp"), pairs)


def after(value, *others):
    return lax.optimization_barrier((value, *others))[0]


PLANES = [[(block * 2 + c) * 4 + z for block in range(4)] for c in range(2) for z in range(4)]


MESH = pl.DeviceIdType.MESH


class Place:
    def __init__(self):
        dp, mp = lax.axis_index("dp"), lax.axis_index("mp")
        self.y, self.x, self.c = dp // 4, (dp // 2) % 2, dp % 2
        self.h, self.l = mp // 2, mp % 2
        self.block = (dp // 2) * 2

    def at(self, y=None, x=None, c=None, h=None, l=None):
        y, x, c = (o if n is None else n for o, n in ((self.y, y), (self.x, x), (self.c, c)))
        h, l = (o if n is None else n for o, n in ((self.h, h), (self.l, l)))
        return ((y * 2 + x) * 2 + c, h * 2 + l)

    def partners(self):
        return [
            self.at(x=1 - self.x),
            self.at(y=1 - self.y),
            self.at(l=1 - self.l),
            self.at(c=1 - self.c),
            self.at(h=1 - self.h),
            self.at(c=1 - self.c, h=1 - self.h),
        ]


def far_copy(source, target, sems, index, device):
    return pltpu.make_async_remote_copy(
        src_ref=source,
        dst_ref=target,
        send_sem=sems[0].at[index],
        recv_sem=sems[1].at[index],
        device_id=device,
        device_id_type=MESH,
    )


class Swap:
    def __init__(self, place, source, target, sems, index, local_sem):
        self.same = place.c == place.h
        self.far = far_copy(source, target, sems, index, place.at(c=place.h, h=place.c))
        self.near = pltpu.make_async_copy(source, target, local_sem)

    def start(self):
        pl.when(self.same)(self.near.start)
        pl.when(~self.same)(self.far.start)

    def wait_recv(self):
        pl.when(self.same)(self.near.wait)
        pl.when(~self.same)(self.far.wait_recv)

    def wait_send(self):
        pl.when(~self.same)(self.far.wait_send)


class Task:
    copies = 1
    locals = 1
    work = ()

    def __init__(self, *inputs, phase=0):
        self.inputs, self.phase = inputs, phase

    def scratch(self):
        return [
            pltpu.SemaphoreType.DMA((self.copies,)),
            pltpu.SemaphoreType.DMA((self.copies,)),
            pltpu.SemaphoreType.DMA((self.locals,)),
            *self.work,
        ]


class Rows(Task):
    copies = 3

    def outs(self):
        rows = self.inputs[0]
        return [jax.ShapeDtypeStruct((4, *rows.shape), rows.dtype)]

    def steps(self, place, ins, outs, scratch):
        own, full = ins[0], outs[0]
        send, recv, local = scratch[:3]
        keep = pltpu.make_async_copy(own, full.at[0], local.at[0])
        over_z = far_copy(own, full.at[1], (send, recv), 0, place.at(l=1 - place.l))
        over_c = far_copy(own, full.at[2], (send, recv), 1, place.at(c=1 - place.c))
        relay = far_copy(full.at[1], full.at[3], (send, recv), 2, place.at(c=1 - place.c))

        def first():
            over_z.start()
            over_c.start()
            keep.start()

        def second():
            over_z.wait_recv()
            relay.start()

        def last():
            keep.wait()
            over_c.wait()
            over_z.wait_send()
            relay.wait()

        return [first, None, second, last]


class Cores(Task):
    copies = 2
    locals = 2

    def outs(self):
        rows = self.inputs[0]
        return [jax.ShapeDtypeStruct((4, *rows.shape), rows.dtype)]

    def steps(self, place, ins, outs, scratch):
        send, recv, local = scratch[:3]
        full = outs[0]
        core = place.at(c=1 - place.c)
        keeps = [pltpu.make_async_copy(ins[n], full.at[n], local.at[n]) for n in range(2)]
        fars = [far_copy(ins[n], full.at[2 + n], (send, recv), n, core) for n in range(2)]

        def first():
            for copy in (*fars, *keeps):
                copy.start()

        def last():
            for copy in (*keeps, *fars):
                copy.wait()

        return [first, None, None, last]


class Sums(Task):
    copies = 3

    def __init__(self, *inputs, phase=0):
        super().__init__(*inputs, phase=phase)
        block = inputs[0].shape[1:]
        self.work = tuple(pltpu.VMEM(block, jnp.bfloat16) for _ in range(3))

    def outs(self):
        block = jax.ShapeDtypeStruct(self.inputs[0].shape[1:], jnp.bfloat16)
        return [block, block]

    def steps(self, place, ins, outs, scratch):
        partial, (from_c, from_z) = ins[0], outs
        send, recv, local, mine, theirs, total = scratch
        core = place.at(c=1 - place.c)
        load = pltpu.make_async_copy(partial.at[1], mine, local.at[0])
        far = far_copy(partial.at[3], theirs, (send, recv), 0, core)
        near = far_copy(partial.at[2], from_c, (send, recv), 1, core)
        over_z = far_copy(total, from_z, (send, recv), 2, place.at(l=1 - place.l))
        rows = 32

        def first():
            far.start()
            near.start()
            load.start()

        def second():
            load.wait()
            far.wait_recv()

            @pl.loop(0, mine.shape[0] // rows)
            def _(index):
                part = pl.ds(pl.multiple_of(index * rows, rows), rows)
                summed = mine[part, :].astype(jnp.float32) + theirs[part, :].astype(jnp.float32)
                total[part, :] = summed.astype(jnp.bfloat16)

            over_z.start()

        def last():
            far.wait_send()
            near.wait()
            over_z.wait()

        return [first, second, None, last]


class Near(Task):
    copies = 2

    def outs(self):
        shard = self.inputs[0]
        return [jax.ShapeDtypeStruct((2, *shard.shape), shard.dtype)]

    def copies_of(self, place, shard, first, second, scratch):
        send, recv, local = scratch[:3]
        return (
            Swap(place, shard, first, (send, recv), 0, local.at[0]),
            far_copy(shard, second, (send, recv), 1, place.at(c=place.h, h=1 - place.c)),
        )

    def steps(self, place, ins, outs, scratch):
        a, b = self.copies_of(place, ins[0], outs[0].at[0], outs[0].at[1], scratch)

        def first():
            a.start()
            b.start()

        def last():
            a.wait_recv()
            a.wait_send()
            b.wait()

        return [first, None, None, last]


class Planes(Near):
    copies = 8

    def outs(self):
        shard = self.inputs[0]
        return [jax.ShapeDtypeStruct((8, *shard.shape), shard.dtype)]

    def steps(self, place, ins, outs, scratch):
        full = outs[0]
        block = place.block
        a, b = self.copies_of(place, ins[0], full.at[block], full.at[block + 1], scratch)
        over_x, over_y = place.at(x=1 - place.x), place.at(y=1 - place.y)
        x_block = block + 2 - 4 * place.x
        y_block = block + 4 - 8 * place.y

        def pass_on(slot, index, device):
            return far_copy(full.at[slot], full.at[slot], scratch[:2], index, device)

        ax, ay = pass_on(block, 2, over_x), pass_on(block, 3, over_y)
        by, bx = pass_on(block + 1, 4, over_y), pass_on(block + 1, 5, over_x)
        axy = pass_on(x_block, 6, over_y)
        byx = pass_on(y_block + 1, 7, over_x)

        def first():
            a.start()
            b.start()

        def second():
            a.wait_recv()
            ax.start()
            b.wait_recv()
            by.start()
            ay.start()
            bx.start()

        def third():
            ax.wait_recv()
            axy.start()
            by.wait_recv()
            byx.start()

        def last():
            a.wait_send()
            b.wait_send()
            for copy in (ax, by):
                copy.wait_send()
            for copy in (ay, bx, axy, byx):
                copy.wait()

        return [first, second, third, last]


class Owners(Task):
    copies = 2

    def outs(self):
        near = self.inputs[0]
        return [jax.ShapeDtypeStruct(near.shape, near.dtype)]

    def steps(self, place, ins, outs, scratch):
        send, recv, local = scratch[:3]
        near, got = ins[0], outs[0]
        a = Swap(place, near.at[0], got.at[0], (send, recv), 0, local.at[0])
        b = far_copy(near.at[1], got.at[1], (send, recv), 1, place.at(c=1 - place.h, h=place.c))

        def first():
            a.start()
            b.start()

        def last():
            a.wait_recv()
            a.wait_send()
            b.wait()

        return [first, None, None, last]


class Halves(Task):
    def __init__(self, array, sender, phase=0):
        super().__init__(array, phase=phase)
        self.sender = sender

    def outs(self):
        return [jax.ShapeDtypeStruct(self.inputs[0].shape, self.inputs[0].dtype)]

    def steps(self, place, ins, outs, scratch):
        copy = far_copy(ins[0], outs[0], scratch[:2], 0, place.at(h=1 - place.h))
        sends = place.h == self.sender

        def first():
            pl.when(sends)(copy.start)

        def last():
            pl.when(sends)(copy.wait_send)
            pl.when(~sends)(copy.wait_recv)

        return [first, None, None, last]


def transfer(name, number, micros, *tasks, scoped=12):
    outs = [task.outs() for task in tasks]
    scratch = [task.scratch() for task in tasks]

    def kernel(*refs):
        refs = list(refs)

        def take(count):
            taken = refs[:count]
            del refs[:count]
            return taken

        ins_of = [take(len(task.inputs)) for task in tasks]
        outs_of = [take(len(out)) for out in outs]
        scratch_of = [take(len(one)) for one in scratch]
        place = Place()
        barrier = pltpu.get_barrier_semaphore()
        partners = place.partners()
        for partner in partners:
            pl.semaphore_signal(barrier, inc=1, device_id=partner, device_id_type=MESH)
        pl.semaphore_wait(barrier, len(partners))
        plans = [
            task.steps(place, ins_of[n], outs_of[n], scratch_of[n]) for n, task in enumerate(tasks)
        ]
        for phase in range(4):
            for task, plan in zip(tasks, plans):
                steps_now = [plan[phase]] if phase else []
                if phase == task.phase:
                    steps_now.insert(0, plan[0])
                for step in steps_now:
                    if step is not None:
                        step()

    results = pl.pallas_call(
        kernel,
        out_shape=[leaf for out in outs for leaf in out],
        in_specs=[pl.BlockSpec(memory_space=pl.ANY) for task in tasks for _ in task.inputs],
        out_specs=[pl.BlockSpec(memory_space=pl.ANY) for out in outs for _ in out],
        scratch_shapes=[one for part in scratch for one in part],
        compiler_params=pltpu.CompilerParams(
            collective_id=number, has_side_effects=True, vmem_limit_bytes=scoped * 2**20
        ),
        cost_estimate=pl.CostEstimate(
            flops=0, bytes_accessed=micros * 3_300_000, transcendentals=0
        ),
        name=name,
    )(*[leaf for task in tasks for leaf in task.inputs])
    results = list(results)
    grouped = []
    for out in outs:
        grouped.append(results[: len(out)])
        del results[: len(out)]
    return grouped


def to_group(shard):
    return jnp.stack([move(shard, TO_GROUP[0]), move(shard, TO_GROUP[1])])


def to_owner(near):
    return [move(near[0], FROM_GROUP[0]), move(near[1], FROM_GROUP[1])]


def over_plane(near):
    return lax.all_gather(near, ("dp", "mp"), axis=0, tiled=True, axis_index_groups=PLANES)


def to_plane(grads):
    return lax.psum_scatter(
        grads, ("dp", "mp"), scatter_dimension=0, tiled=True, axis_index_groups=PLANES
    )


def both(pair):
    return pair[0].astype(jnp.float32) + pair[1].astype(jnp.float32)


def summed(partial, received):
    return both(received) + partial[0].astype(jnp.float32)


def sum_all_kernel(value, total, by_mp, by_dp, send_sem, recv_sem):
    dp, mp = lax.axis_index("dp"), lax.axis_index("mp")
    over_mp = [(dp, (mp + step) % 4) for step in range(1, 4)]
    over_dp = [((dp + step) % 8, mp) for step in range(1, 8)]
    barrier = pltpu.get_barrier_semaphore()
    for partner in over_mp + over_dp:
        pl.semaphore_signal(
            barrier, inc=1, device_id=partner, device_id_type=pl.DeviceIdType.MESH
        )
    pl.semaphore_wait(barrier, len(over_mp) + len(over_dp))

    def share(table, place, partners, first):
        copies = [
            pltpu.make_async_remote_copy(
                src_ref=table.at[place],
                dst_ref=table.at[place],
                send_sem=send_sem.at[first + step],
                recv_sem=recv_sem.at[first + step],
                device_id=partner,
                device_id_type=pl.DeviceIdType.MESH,
            )
            for step, partner in enumerate(partners)
        ]
        for copy in copies:
            copy.start()
        for copy in copies:
            copy.wait()

    by_mp[mp] = value[...]
    share(by_mp, mp, over_mp, 0)
    by_dp[dp] = (by_mp[0] + by_mp[1]) + (by_mp[2] + by_mp[3])
    share(by_dp, dp, over_dp, 3)
    result = by_dp[0]
    for place in range(1, 8):
        result = result + by_dp[place]
    total[...] = result


def sum_all(vector):
    size = vector.shape[0]
    rows = -(-size // 1024) * 8
    block = jnp.pad(vector, (0, rows * 128 - size)).reshape(rows, 128)
    total = pl.pallas_call(
        sum_all_kernel,
        out_shape=jax.ShapeDtypeStruct((rows, 128), jnp.float32),
        in_specs=[pl.BlockSpec(memory_space=pltpu.VMEM)],
        out_specs=pl.BlockSpec(memory_space=pltpu.VMEM),
        scratch_shapes=[
            pltpu.VMEM((4, rows, 128), jnp.float32),
            pltpu.VMEM((8, rows, 128), jnp.float32),
            pltpu.SemaphoreType.DMA((10,)),
            pltpu.SemaphoreType.DMA((10,)),
        ],
        compiler_params=pltpu.CompilerParams(collective_id=0, has_side_effects=True),
        name="sum_all",
    )(block)
    return total.reshape(-1)[:size]


def column_places(index, high, low, rows):
    chunk = index // rows
    return high * 2 * rows + (low + chunk - 2 * low * chunk) * rows + index - chunk * rows


def project_kernel(rows_ref, weight_ref, cos_ref, sin_ref, gain_ref, raw_ref, query_ref, kv_ref):
    width = rows_ref.shape[1]
    weight = weight_ref[...].reshape(width, weight_ref.shape[2])
    projected = jnp.dot(rows_ref[...], weight, preferred_element_type=jnp.float32)
    query_width, key_width = query_ref.shape[1], kv_ref.shape[1] // 2
    turned_width = query_width + key_width
    raw_ref[...] = projected[:, :turned_width]
    cosine, sine = cos_ref[...], sin_ref[...]
    for start in range(0, turned_width, HEAD_SIZE):
        raw = projected[:, start : start + HEAD_SIZE]
        gain = gain_ref[0:1, :] if start < query_width else gain_ref[1:2, :]
        normed = raw * lax.rsqrt(jnp.mean(raw * raw, axis=1, keepdims=True) + EPS_NORM) * gain
        turned = normed * cosine + pltpu.roll(normed, HEAD_SIZE // 2, 1) * sine
        if start < query_width:
            query_ref[:, start : start + HEAD_SIZE] = turned.astype(jnp.bfloat16)
        else:
            place = start - query_width
            kv_ref[:, place : place + HEAD_SIZE] = turned.astype(jnp.bfloat16)
    kv_ref[:, key_width:] = projected[:, turned_width:].astype(jnp.bfloat16)


def project(rows, blocks, cosine, sine, head_gains, query_width, key_width):
    count, width = rows.shape
    tile = 256
    total = query_width + 2 * key_width
    by_rows = lambda columns: pl.BlockSpec((tile, columns), lambda i: (i, 0))
    return pl.pallas_call(
        project_kernel,
        grid=(count // tile,),
        in_specs=[
            by_rows(width),
            pl.BlockSpec((8, width // 8, total), lambda i: (0, 0, 0)),
            by_rows(HEAD_SIZE),
            by_rows(HEAD_SIZE),
            pl.BlockSpec((2, HEAD_SIZE), lambda i: (0, 0)),
        ],
        out_specs=[by_rows(query_width + key_width), by_rows(query_width), by_rows(2 * key_width)],
        out_shape=[
            jax.ShapeDtypeStruct((count, query_width + key_width), jnp.float32),
            jax.ShapeDtypeStruct((count, query_width), jnp.bfloat16),
            jax.ShapeDtypeStruct((count, 2 * key_width), jnp.bfloat16),
        ],
        compiler_params=pltpu.CompilerParams(vmem_limit_bytes=48 * 2**20),
        cost_estimate=pl.CostEstimate(
            flops=2 * count * width * total, bytes_accessed=16 * 2**20, transcendentals=0
        ),
        name="project",
    )(rows, blocks, cosine, sine, head_gains)


def unproject_kernel(
    place_ref, dq_ref, own_ref, above_ref, raw_ref, cos_ref, sin_ref, gain_ref, out_ref, gq_ref, gk_ref
):
    query_width, key_width = dq_ref.shape[1], own_ref.shape[1] // 2
    turned_width = query_width + key_width
    lower = place_ref[0] == 0
    cosine, sine = cos_ref[...], sin_ref[...]

    @pl.when(pl.program_id(0) == 0)
    def _():
        gq_ref[...] = jnp.zeros_like(gq_ref)
        gk_ref[...] = jnp.zeros_like(gk_ref)

    def with_above(columns):
        above = jnp.where(lower, above_ref[:, columns].astype(jnp.float32), 0.0)
        return own_ref[:, columns] + above

    for start in range(0, turned_width, HEAD_SIZE):
        columns = slice(start, start + HEAD_SIZE)
        if start < query_width:
            grad, gain, gain_sum = dq_ref[:, columns], gain_ref[0:1, :], gq_ref
        else:
            grad = with_above(slice(start - query_width, start - query_width + HEAD_SIZE))
            gain, gain_sum = gain_ref[1:2, :], gk_ref
        grad = grad * cosine - pltpu.roll(grad, HEAD_SIZE // 2, 1) * sine
        raw = raw_ref[:, columns]
        scale = lax.rsqrt(jnp.mean(raw * raw, axis=1, keepdims=True) + EPS_NORM)
        normed = raw * scale
        gain_sum[...] += jnp.sum((grad * normed).reshape(-1, 8, HEAD_SIZE), axis=0)
        d_normal = grad * gain
        value = scale * (d_normal - normed * jnp.mean(d_normal * normed, axis=1, keepdims=True))
        out_ref[:, columns] = value.astype(jnp.bfloat16)
    out_ref[:, turned_width:] = with_above(slice(key_width, 2 * key_width)).astype(jnp.bfloat16)


def unproject(place, d_queries, d_own, above, raw, cosine, sine, head_gains):
    count, query_width = d_queries.shape
    key_width = d_own.shape[1] // 2
    tile = 256
    total = query_width + 2 * key_width
    by_rows = lambda columns: pl.BlockSpec((tile, columns), lambda i, p: (i, 0))
    fixed = lambda rows: pl.BlockSpec((rows, HEAD_SIZE), lambda i, p: (0, 0))
    return pl.pallas_call(
        unproject_kernel,
        grid_spec=pltpu.PrefetchScalarGridSpec(
            num_scalar_prefetch=1,
            grid=(count // tile,),
            in_specs=[
                by_rows(query_width),
                by_rows(2 * key_width),
                by_rows(2 * key_width),
                by_rows(query_width + key_width),
                by_rows(HEAD_SIZE),
                by_rows(HEAD_SIZE),
                fixed(2),
            ],
            out_specs=[by_rows(total), fixed(8), fixed(8)],
        ),
        out_shape=[
            jax.ShapeDtypeStruct((count, total), jnp.bfloat16),
            jax.ShapeDtypeStruct((8, HEAD_SIZE), jnp.float32),
            jax.ShapeDtypeStruct((8, HEAD_SIZE), jnp.float32),
        ],
        compiler_params=pltpu.CompilerParams(vmem_limit_bytes=32 * 2**20),
        cost_estimate=pl.CostEstimate(flops=0, bytes_accessed=2 * 2**20, transcendentals=0),
        name="unproject",
    )(place, d_queries, d_own, above, raw, cosine, sine, head_gains)


def dot_t(left, right):
    return lax.dot_general(
        left, right, (((1,), (1,)), ((), ())), preferred_element_type=jnp.float32
    )


def t_dot(left, right):
    return lax.dot_general(
        left, right, (((0,), (0,)), ((), ())), preferred_element_type=jnp.float32
    )


def exps_of(place_ref, time_ref, begin_ref, rows, query, key_low, key_own):
    high, low = place_ref[0], place_ref[1]
    keys = key_own.shape[0]
    scale = HEAD_SIZE ** (-0.5)
    column = lax.broadcasted_iota(jnp.int32, (rows.size, keys), 1)
    time, begin = time_ref[rows, :], begin_ref[rows, :]
    own_place = column_places(column, high, low, keys // 2)
    low_place = column_places(column, 0, low, keys // 2)
    own_seen = (own_place <= time) & (own_place >= begin)
    low_seen = (low_place >= begin) & (low_place < high * keys)
    own = jnp.where(own_seen, dot_t(query, key_own) * scale, MASKED)
    lower = jnp.where(low_seen, dot_t(query, key_low) * scale, MASKED)
    top = jnp.maximum(
        jnp.max(own, axis=1, keepdims=True), jnp.max(lower, axis=1, keepdims=True)
    )
    own, lower = jnp.exp(own - top), jnp.exp(lower - top)
    total = jnp.sum(own, axis=1, keepdims=True) + jnp.sum(lower, axis=1, keepdims=True)
    return lower, own, 1.0 / total


def attend_kernel(place_ref, time_ref, begin_ref, query_ref, low_ref, own_ref, out_ref):
    half, query_width = query_ref.shape
    key_width = own_ref.shape[1] // 2
    group = query_width // key_width
    size = half // 2
    upper = place_ref[0] == 1
    for kv in range(key_width // HEAD_SIZE):
        key_at = slice(kv * HEAD_SIZE, (kv + 1) * HEAD_SIZE)
        value_at = slice(key_width + kv * HEAD_SIZE, key_width + (kv + 1) * HEAD_SIZE)
        key_low, key_own, value_own = low_ref[:, key_at], own_ref[:, key_at], own_ref[:, value_at]
        value_low = jnp.where(upper, low_ref[:, value_at], jnp.zeros_like(value_own))
        for part in range(2):
            rows = pl.ds(part * size, size)
            for head in range(kv * group, (kv + 1) * group):
                query_at = slice(head * HEAD_SIZE, (head + 1) * HEAD_SIZE)
                lower, own, inverse = exps_of(
                    place_ref, time_ref, begin_ref, rows, query_ref[rows, query_at], key_low, key_own
                )
                result = jnp.dot(
                    lower.astype(jnp.bfloat16), value_low, preferred_element_type=jnp.float32
                ) + jnp.dot(own.astype(jnp.bfloat16), value_own, preferred_element_type=jnp.float32)
                out_ref[rows, query_at] = (result * inverse).astype(jnp.bfloat16)


def attend_back_kernel(
    place_ref, time_ref, begin_ref, query_ref, low_ref, own_ref, grad_ref, dq_ref, dlow_ref, down_ref
):
    half, query_width = query_ref.shape
    key_width = own_ref.shape[1] // 2
    group = query_width // key_width
    size = half // 2
    scale = HEAD_SIZE ** (-0.5)
    upper = place_ref[0] == 1
    for kv in range(key_width // HEAD_SIZE):
        key_at = slice(kv * HEAD_SIZE, (kv + 1) * HEAD_SIZE)
        value_at = slice(key_width + kv * HEAD_SIZE, key_width + (kv + 1) * HEAD_SIZE)
        key_own, value_own = own_ref[:, key_at], own_ref[:, value_at]
        key_low = jnp.where(upper, low_ref[:, key_at], jnp.zeros_like(key_own))
        value_low = jnp.where(upper, low_ref[:, value_at], jnp.zeros_like(value_own))
        dk_low = dk_own = dv_low = dv_own = None
        for part in range(2):
            rows = pl.ds(part * size, size)
            for head in range(kv * group, (kv + 1) * group):
                query_at = slice(head * HEAD_SIZE, (head + 1) * HEAD_SIZE)
                query, grad = query_ref[rows, query_at], grad_ref[rows, query_at]
                lower, own, inverse = exps_of(
                    place_ref, time_ref, begin_ref, rows, query, key_low, key_own
                )
                lower, own = lower * inverse, own * inverse
                g_low, g_own = dot_t(grad, value_low), dot_t(grad, value_own)
                mean = jnp.sum(lower * g_low, axis=1, keepdims=True) + jnp.sum(
                    own * g_own, axis=1, keepdims=True
                )
                s_low = (lower * (g_low - mean)).astype(jnp.bfloat16)
                s_own = (own * (g_own - mean)).astype(jnp.bfloat16)
                dq_ref[rows, query_at] = scale * (
                    jnp.dot(s_low, key_low, preferred_element_type=jnp.float32)
                    + jnp.dot(s_own, key_own, preferred_element_type=jnp.float32)
                )
                terms = (
                    t_dot(s_low, query),
                    t_dot(s_own, query),
                    t_dot(lower.astype(jnp.bfloat16), grad),
                    t_dot(own.astype(jnp.bfloat16), grad),
                )
                if dk_low is None:
                    dk_low, dk_own, dv_low, dv_own = terms
                else:
                    dk_low, dk_own = dk_low + terms[0], dk_own + terms[1]
                    dv_low, dv_own = dv_low + terms[2], dv_own + terms[3]
        dlow_ref[:, key_at] = (dk_low * scale).astype(jnp.bfloat16)
        dlow_ref[:, value_at] = dv_low.astype(jnp.bfloat16)
        down_ref[:, key_at] = dk_own * scale
        down_ref[:, value_at] = dv_own


def attention_call(kernel, name, place, arrays, outs, flops):
    count = arrays[0].shape[0]
    half = count // 2
    spec = lambda leaf: pl.BlockSpec((half, leaf.shape[1]), lambda i, p: (i, 0))
    return pl.pallas_call(
        kernel,
        grid_spec=pltpu.PrefetchScalarGridSpec(
            num_scalar_prefetch=1,
            grid=(2,),
            in_specs=[spec(leaf) for leaf in arrays],
            out_specs=[spec(leaf) for leaf in outs],
        ),
        out_shape=outs,
        compiler_params=pltpu.CompilerParams(vmem_limit_bytes=56 * 2**20),
        cost_estimate=pl.CostEstimate(flops=flops, bytes_accessed=16 * 2**20, transcendentals=0),
        name=name,
    )(place, *arrays)


def scaled(values):
    return values * lax.rsqrt(jnp.mean(values * values, axis=1, keepdims=True) + EPS_NORM)


def three(parts, columns=slice(None)):
    own, from_c, from_z = parts
    return (
        own[0, :, columns].astype(jnp.float32)
        + from_c[:, columns].astype(jnp.float32)
        + from_z[:, columns].astype(jnp.float32)
    )


def slot_columns(slot_ref, index, block):
    return pl.ds(pl.multiple_of(slot_ref[index] * block, block), block)


def store_slots(slot_ref, out_ref, values):
    block = out_ref.shape[1] // 8
    for index in range(8):
        out_ref[:, slot_columns(slot_ref, index, block)] = values[
            :, index * block : (index + 1) * block
        ]


def norm_kernel(slot_ref, x_ref, gain_ref, out_ref):
    x = x_ref[...].astype(jnp.float32)
    store_slots(slot_ref, out_ref, (scaled(x) * gain_ref[...]).astype(jnp.bfloat16))


def mix_kernel(slot_ref, x_ref, own_ref, c_ref, z_ref, gain_ref, mixed_ref, out_ref):
    mixed = x_ref[...].astype(jnp.float32) + three((own_ref, c_ref, z_ref))
    mixed_ref[...] = mixed
    store_slots(slot_ref, out_ref, (scaled(mixed) * gain_ref[...]).astype(jnp.bfloat16))


def norm_back_of(slot_ref, value_ref, parts, gain_ref, sum_ref, grad_ref):
    width = value_ref.shape[1]
    block = width // 8
    for index in range(8):
        grad_ref[:, index * block : (index + 1) * block] = three(
            parts, slot_columns(slot_ref, index, block)
        )
    value, grad = value_ref[...].astype(jnp.float32), grad_ref[...]
    scale = lax.rsqrt(jnp.mean(value * value, axis=1, keepdims=True) + EPS_NORM)
    normed = value * scale

    @pl.when(pl.program_id(0) == 0)
    def _():
        sum_ref[...] = jnp.zeros_like(sum_ref)

    sum_ref[...] += jnp.sum((grad * normed).reshape(-1, 8, width), axis=0)
    d_normal = grad * gain_ref[...]
    return scale * (d_normal - normed * jnp.mean(d_normal * normed, axis=1, keepdims=True))


def mix_back_kernel(
    slot_ref, mixed_ref, own_ref, c_ref, z_ref, gain_ref, cot_ref, d_ref, low_ref, sum_ref, grad_ref
):
    value = norm_back_of(slot_ref, mixed_ref, (own_ref, c_ref, z_ref), gain_ref, sum_ref, grad_ref)
    value = value + cot_ref[...].astype(jnp.float32)
    d_ref[...] = value
    low_ref[...] = value.astype(jnp.bfloat16)


def in_back_kernel(
    slot_ref, x_ref, own_ref, c_ref, z_ref, gain_ref, d_ref, out_ref, sum_ref, grad_ref
):
    value = norm_back_of(slot_ref, x_ref, (own_ref, c_ref, z_ref), gain_ref, sum_ref, grad_ref)
    out_ref[...] = value + d_ref[...]


def by_row_tiles(kernel, name, slot_of, inputs, outs, scratch=False, micros=3):
    rows, width = 64, inputs[0].shape[1]
    steps = inputs[0].shape[0] // rows

    def spec(leaf):
        if len(leaf.shape) == 3:
            return pl.BlockSpec((1, rows, width), lambda i, p: (0, i, 0))
        if leaf.shape[0] in (1, 8):
            return pl.BlockSpec(leaf.shape, lambda i, p: (0, 0))
        return pl.BlockSpec((rows, width), lambda i, p: (i, 0))

    return pl.pallas_call(
        kernel,
        grid_spec=pltpu.PrefetchScalarGridSpec(
            num_scalar_prefetch=1,
            grid=(steps,),
            in_specs=[spec(leaf) for leaf in inputs],
            out_specs=[spec(leaf) for leaf in outs],
            scratch_shapes=[pltpu.VMEM((rows, width), jnp.float32)] if scratch else [],
        ),
        out_shape=outs,
        compiler_params=pltpu.CompilerParams(vmem_limit_bytes=(60 if scratch else 24) * 2**20),
        cost_estimate=pl.CostEstimate(flops=0, bytes_accessed=micros * 3_300_000, transcendentals=0),
        name=name,
    )(slot_of, *inputs)


def mlp_front_kernel(rows_ref, gate_ref, up_ref, gate_out, up_out, act_out):
    width = rows_ref.shape[1]
    rows = rows_ref[...]
    gate = jnp.dot(rows, gate_ref[...].reshape(width, -1), preferred_element_type=jnp.float32)
    upper = jnp.dot(rows, up_ref[...].reshape(width, -1), preferred_element_type=jnp.float32)
    gate_out[...] = gate
    up_out[...] = upper
    act_out[...] = (gate * upper / (1.0 + jnp.exp(-gate))).astype(jnp.bfloat16)


def mlp_front(rows, gate_blocks, up_blocks):
    count, width = rows.shape
    units = gate_blocks.shape[2]
    columns = 256
    weight = pl.BlockSpec((8, width // 8, columns), lambda i: (0, 0, i))
    out = pl.BlockSpec((count, columns), lambda i: (0, i))
    return pl.pallas_call(
        mlp_front_kernel,
        grid=(units // columns,),
        in_specs=[pl.BlockSpec((count, width), lambda i: (0, 0)), weight, weight],
        out_specs=[out, out, out],
        out_shape=[
            jax.ShapeDtypeStruct((count, units), jnp.float32),
            jax.ShapeDtypeStruct((count, units), jnp.float32),
            jax.ShapeDtypeStruct((count, units), jnp.bfloat16),
        ],
        compiler_params=pltpu.CompilerParams(vmem_limit_bytes=60 * 2**20),
        cost_estimate=pl.CostEstimate(
            flops=4 * count * units * width, bytes_accessed=32 * 2**20, transcendentals=0
        ),
        name="mlp_front",
    )(rows, gate_blocks, up_blocks)


def mlp_back_kernel(
    slot_ref, dy_ref, gate_ref, up_ref, act_ref, down_ref, dgate_ref, dup_ref, branch_ref, weight_ref
):
    block = down_ref.shape[1]

    @pl.when(pl.program_id(0) == 0)
    def _():
        for index in range(8):
            weight_ref[index * block : (index + 1) * block, :] = down_ref[slot_ref[index]]

    units, step = gate_ref.shape[1], 512
    dy = dy_ref[...]
    total = None
    for start in range(0, units, step):
        columns = slice(start, start + step)
        weight = weight_ref[columns, :]
        gate, upper = gate_ref[:, columns], up_ref[:, columns]
        d_act = dot_t(dy, weight)
        sigma = 1.0 / (1.0 + jnp.exp(-gate))
        dup_ref[:, columns] = (d_act * gate * sigma).astype(jnp.bfloat16)
        d_gate = d_act * upper * sigma * (1.0 + gate * (1.0 - sigma))
        dgate_ref[:, columns] = d_gate.astype(jnp.bfloat16)
        term = jnp.dot(act_ref[:, columns], weight, preferred_element_type=jnp.float32)
        total = term if total is None else total + term
    branch_ref[0] = total.astype(jnp.bfloat16)


def mlp_back(slot_of, d_branch, gate, upper, act, down_blocks):
    count, units = gate.shape
    width = d_branch.shape[1]
    rows = 256
    by_rows = lambda columns: pl.BlockSpec((rows, columns), lambda i, p: (i, 0))
    wide = jax.ShapeDtypeStruct((count, units), jnp.bfloat16)
    return pl.pallas_call(
        mlp_back_kernel,
        grid_spec=pltpu.PrefetchScalarGridSpec(
            num_scalar_prefetch=1,
            grid=(count // rows,),
            in_specs=[
                by_rows(width),
                by_rows(units),
                by_rows(units),
                by_rows(units),
                pl.BlockSpec(down_blocks.shape, lambda i, p: (0, 0, 0)),
            ],
            out_specs=[by_rows(units)] * 2
            + [pl.BlockSpec((1, rows, width), lambda i, p: (i, 0, 0))],
            scratch_shapes=[pltpu.VMEM((units, width), jnp.bfloat16)],
        ),
        out_shape=[
            wide,
            wide,
            jax.ShapeDtypeStruct((count // rows, rows, width), jnp.bfloat16),
        ],
        compiler_params=pltpu.CompilerParams(vmem_limit_bytes=48 * 2**20),
        cost_estimate=pl.CostEstimate(
            flops=4 * count * units * width, bytes_accessed=32 * 2**20, transcendentals=0
        ),
        name="mlp_back",
    )(slot_of, d_branch, gate, upper, act, down_blocks)


def rows_back_kernel(*refs):
    *pairs, out_ref = refs
    total = None
    for grad_ref, weight_ref in zip(pairs[::2], pairs[1::2]):
        term = dot_t(grad_ref[...], weight_ref[0])
        total = term if total is None else total + term
    out_ref[...] = total.astype(jnp.bfloat16).reshape(out_ref.shape)


def rows_back(name, *pairs):
    count = pairs[0].shape[0]
    block = pairs[1].shape[1]
    specs = []
    for grad, weight in zip(pairs[::2], pairs[1::2]):
        specs.append(pl.BlockSpec(grad.shape, lambda i: (0, 0)))
        specs.append(pl.BlockSpec((1, *weight.shape[1:]), lambda i: (i, 0, 0)))
    return pl.pallas_call(
        rows_back_kernel,
        grid=(8,),
        in_specs=specs,
        out_specs=pl.BlockSpec((4, count // 4, block), lambda i: (0, 0, i)),
        out_shape=jax.ShapeDtypeStruct((4, count // 4, 8 * block), jnp.bfloat16),
        compiler_params=pltpu.CompilerParams(vmem_limit_bytes=28 * 2**20),
        cost_estimate=pl.CostEstimate(
            flops=sum(count * w.size for w in pairs[1::2]) // 4,
            bytes_accessed=2 * 2**20,
            transcendentals=0,
        ),
        name=name,
    )(*pairs)


def adam_kernel(factor_ref, *refs, rates):
    factor = factor_ref[0]
    ins, outs = refs[: len(refs) - 3 * len(rates)], refs[len(refs) - 3 * len(rates) :]
    at = 0
    for place, (rate, pieces) in enumerate(rates):
        weight_ref, first_ref, second_ref, *grads = ins[at : at + 3 + pieces]
        at += 3 + pieces
        start = 0
        for grad_ref in grads:
            columns = slice(start, start + grad_ref.shape[1])
            start += grad_ref.shape[1]
            results = adam(
                weight_ref[:, columns],
                first_ref[:, columns],
                second_ref[:, columns],
                grad_ref[...],
                factor,
                rate,
                WEIGHT_DECAY,
            )
            for out_ref, result in zip(outs[3 * place : 3 * place + 3], results):
                out_ref[:, columns] = result


def adam_all(factor, weights):
    steps = 8
    rates = tuple((rate, len(grads)) for rate, *_, grads in weights)
    arrays, outs = [], []
    for _, master, first, second, grads in weights:
        arrays += [master, first, second, *grads]
        outs += [jax.ShapeDtypeStruct(master.shape, jnp.float32)] * 3

    def spec(leaf):
        return pl.BlockSpec((leaf.shape[0] // steps, leaf.shape[1]), lambda i, p: (i, 0))

    results = pl.pallas_call(
        lambda *refs: adam_kernel(*refs, rates=rates),
        grid_spec=pltpu.PrefetchScalarGridSpec(
            num_scalar_prefetch=1,
            grid=(steps,),
            in_specs=[spec(leaf) for leaf in arrays],
            out_specs=[spec(leaf) for leaf in outs],
        ),
        out_shape=outs,
        compiler_params=pltpu.CompilerParams(vmem_limit_bytes=60 * 2**20),
        cost_estimate=pl.CostEstimate(flops=0, bytes_accessed=48 * 2**20, transcendentals=0),
        name="adam_all",
    )(factor[None], *arrays)
    return [results[n : n + 3] for n in range(0, len(results), 3)]


def slot_grad_kernel(slot_ref, left_ref, right_ref, out_ref):
    block = out_ref.shape[1]
    grad = t_dot(left_ref[...], right_ref[...]).astype(jnp.bfloat16)
    for index in range(8):
        out_ref[slot_ref[index]] = grad[index * block : (index + 1) * block, :]


def slot_grad(slot_of, left, right):
    count, rows = left.shape
    width = right.shape[1]
    columns = 512
    return pl.pallas_call(
        slot_grad_kernel,
        grid_spec=pltpu.PrefetchScalarGridSpec(
            num_scalar_prefetch=1,
            grid=(width // columns,),
            in_specs=[
                pl.BlockSpec((count, rows), lambda i, p: (0, 0)),
                pl.BlockSpec((count, columns), lambda i, p: (0, i)),
            ],
            out_specs=pl.BlockSpec((8, rows // 8, columns), lambda i, p: (0, 0, i)),
        ),
        out_shape=jax.ShapeDtypeStruct((8, rows // 8, width), jnp.bfloat16),
        compiler_params=pltpu.CompilerParams(vmem_limit_bytes=48 * 2**20),
        cost_estimate=pl.CostEstimate(
            flops=2 * count * rows * width, bytes_accessed=16 * 2**20, transcendentals=0
        ),
        name="slot_grad",
    )(slot_of, left, right)


class Grads(Task):
    def outs(self):
        rows, left, right = self.inputs
        columns = left.shape[1] + right.shape[1]
        return [jax.ShapeDtypeStruct((8, rows.shape[1] // 8, columns), jnp.bfloat16)]

    def scratch(self):
        return []

    def steps(self, place, ins, outs, scratch):
        count, width = self.inputs[0].shape
        block = width // 8
        columns = self.inputs[1].shape[1]

        def body(rows_ref, left_ref, right_ref, out_ref):
            rows = rows_ref[...]
            out_ref[0, :, :columns] = t_dot(rows, left_ref[...]).astype(jnp.bfloat16)
            out_ref[0, :, columns:] = t_dot(rows, right_ref[...]).astype(jnp.bfloat16)

        def whole(one):
            return pl.BlockSpec((count, one.shape[1]), lambda i: (0, 0))

        run = pltpu.emit_pipeline(
            body,
            grid=(8,),
            in_specs=[
                pl.BlockSpec((count, block), lambda i: (0, i)),
                whole(self.inputs[1]),
                whole(self.inputs[2]),
            ],
            out_specs=[pl.BlockSpec((1, block, 2 * columns), lambda i: (i, 0, 0))],
        )
        return [lambda: None, None, lambda: run(*ins, *outs), None]


def shards_paired(
    hidden_in,
    cotangent,
    doc_lengths,
    owner,
    projection_master_weight,
    gateup_weight,
    out_weight,
    down_weight,
    projection_first_moment,
    gateup_first,
    out_first,
    down_first,
    projection_second_moment,
    gateup_second,
    out_second,
    down_second,
    gains,
    gain_first,
    gain_second,
):
    high, low = lax.axis_index("mp") // 2, lax.axis_index("mp") % 2
    plane = high
    groups = lax.axis_size("mp")
    query_width = QUERY_HEADS // groups * HEAD_SIZE
    key_width = KEY_VALUE_HEADS // groups * HEAD_SIZE
    units = FF // groups
    rows_here = hidden_in.shape[0]
    count = 4 * rows_here
    half = count // 2
    width = hidden_in.shape[1]
    slot_of = (owner ^ plane).astype(jnp.int32)
    out_rate = float(QUERY_HEADS * HEAD_SIZE // 32) ** (-0.5)

    ln_in = gains[:MODEL_WIDTH]
    ln_mid = gains[MODEL_WIDTH : 2 * MODEL_WIDTH]
    q_gain = gains[2 * MODEL_WIDTH : 2 * MODEL_WIDTH + HEAD_SIZE]
    k_gain = gains[2 * MODEL_WIDTH + HEAD_SIZE :]
    low_gateup = gateup_weight.astype(jnp.bfloat16)
    own_in = by_row_tiles(
        norm_kernel,
        "norm_in",
        slot_of,
        [hidden_in, ln_in[None]],
        [jax.ShapeDtypeStruct(hidden_in.shape, jnp.bfloat16)],
    )
    (qkv_blocks,), (out_blocks,), (full_in,), (near_gate,) = transfer(
        "gather_first",
        1,
        75,
        Planes(projection_master_weight.astype(jnp.bfloat16)),
        Planes(out_weight.astype(jnp.bfloat16)),
        Rows(own_in[0]),
        Near(low_gateup[:, :units], phase=1),
    )
    full_in = full_in.reshape(count, width)
    w_out = jnp.take(out_blocks, slot_of, axis=0, mode="clip").reshape(-1, width)
    gate_blocks = over_plane(near_gate)
    near_up = to_group(after(low_gateup[:, units:], full_in))

    lengths = jnp.concatenate([doc_lengths, move(doc_lengths, OVER_C)], axis=0)
    ends = jnp.cumsum(lengths, axis=1)
    spot = jnp.arange(half, dtype=jnp.int32)
    chunk = spot // rows_here
    own_places = high * half + (low ^ chunk) * rows_here + spot % rows_here
    later = own_places[None, :, None] >= ends[:, None, :]
    begin = jnp.max(jnp.where(later, ends[:, None, :], 0), axis=2).reshape(count, 1)
    time = jnp.concatenate([own_places, own_places]).reshape(count, 1)
    freq = THETA ** (-(2.0 * jnp.arange(HEAD_SIZE // 2, dtype=jnp.float32)) / HEAD_SIZE)
    angle = (time - begin).astype(jnp.float32) * freq[None, :]
    cosine, sine = jnp.cos(angle), jnp.sin(angle)
    cosine = jnp.concatenate([cosine, cosine], axis=-1)
    sine = jnp.concatenate([-sine, sine], axis=-1)
    head_gains = jnp.stack([q_gain, k_gain])
    place = jnp.stack([high, low]).astype(jnp.int32)

    raw, queries, own_kv = project(
        full_in, qkv_blocks, cosine, sine, head_gains, query_width, key_width
    )
    ((lower_kv,),) = transfer("keys_up", 2, 40, Halves(own_kv, 0))
    lower_kv, near_up = lax.optimization_barrier((lower_kv, near_up))
    near_cotangent = move(after(cotangent, lower_kv), OVER_L)
    up_blocks = over_plane(near_up)
    score_flops = 2 * count * count * query_width
    (attn_heads,) = attention_call(
        attend_kernel,
        "attend",
        place,
        [time, begin, queries, lower_kv, own_kv],
        [jax.ShapeDtypeStruct((count, query_width), jnp.bfloat16)],
        2 * score_flops,
    )

    def blocks(partial):
        return partial.astype(jnp.bfloat16).reshape(4, rows_here, width)

    partial = blocks(jnp.dot(attn_heads, w_out, preferred_element_type=jnp.float32))
    partial, near_cotangent = lax.optimization_barrier((partial, near_cotangent))
    received, (near_down,) = transfer(
        "sum_attention", 3, 50, Sums(partial), Near(down_weight.astype(jnp.bfloat16))
    )
    down_blocks = over_plane(near_down)
    row = jax.ShapeDtypeStruct((rows_here, width), jnp.float32)
    low_row = jax.ShapeDtypeStruct((rows_here, width), jnp.bfloat16)
    gain_row = jax.ShapeDtypeStruct((8, width), jnp.float32)
    mixed, own_mid = by_row_tiles(
        mix_kernel, "mix", slot_of, [hidden_in, partial, *received, ln_mid[None]], [row, low_row]
    )
    (full_mid,), (d_branch,) = transfer(
        "gather_mid", 4, 34, Rows(own_mid), Cores(cotangent, near_cotangent)
    )
    d_branch = d_branch.reshape(count, width)
    full_mid = full_mid.reshape(count, width)
    gate, upper, act = mlp_front(full_mid, gate_blocks, up_blocks)
    g_down = slot_grad(slot_of, act, d_branch)
    down_blocks, g_down = lax.optimization_barrier((down_blocks, g_down))
    near_g_down = to_plane(g_down)
    d_gate, d_upper, branch = mlp_back(slot_of, d_branch, gate, upper, act, down_blocks)
    partial = rows_back("mid_rows", d_gate, gate_blocks, d_upper, up_blocks)
    received, (g_gateup,) = transfer(
        "sum_mid", 5, 33, Sums(partial), Grads(full_mid, d_gate, d_upper), scoped=40
    )
    near_g_gateup = to_plane(g_gateup)
    d_mixed, low_d_mixed, mid_gain = by_row_tiles(
        mix_back_kernel,
        "mix_back",
        slot_of,
        [mixed, partial, *received, ln_mid[None], cotangent],
        [row, low_row, gain_row],
        scratch=True,
    )
    g_ln_mid = jnp.sum(mid_gain, axis=0)
    ((d_attn,),) = transfer("gather_attention", 6, 29, Rows(low_d_mixed))
    d_attn = d_attn.reshape(count, width)
    owned_down = to_owner(after(near_g_down, d_attn))
    g_out = slot_grad(slot_of, attn_heads, d_attn)
    d_heads = jnp.einsum("td,hd->th", d_attn, w_out, preferred_element_type=jnp.float32).astype(
        jnp.bfloat16
    )
    d_queries, d_low, d_own = attention_call(
        attend_back_kernel,
        "attend_back",
        place,
        [time, begin, queries, lower_kv, own_kv, d_heads],
        [
            jax.ShapeDtypeStruct((count, query_width), jnp.float32),
            jax.ShapeDtypeStruct((count, 2 * key_width), jnp.bfloat16),
            jax.ShapeDtypeStruct((count, 2 * key_width), jnp.float32),
        ],
        5 * score_flops,
    )
    d_low, g_out, *owned_down = lax.optimization_barrier((d_low, g_out, *owned_down))
    near_g_out = to_plane(g_out)
    (from_above,), branch_received = transfer("keys_down", 7, 53, Halves(d_low, 1), Sums(branch))
    d_projected, g_q, g_k = unproject(
        place, d_queries, d_own, from_above, raw, cosine, sine, head_gains
    )
    g_q, g_k = jnp.sum(g_q, axis=0), jnp.sum(g_k, axis=0)
    g_qkv = jnp.einsum("td,tc->dc", full_in, d_projected, preferred_element_type=jnp.float32)
    near_g_qkv = to_plane(g_qkv.astype(jnp.bfloat16).reshape(8, width // 8, -1))
    partial = rows_back("in_rows", d_projected, qkv_blocks)
    received, (owned_gateup,) = transfer("sum_in", 8, 74, Sums(partial), Owners(near_g_gateup))
    near_g_out, near_g_qkv, branch_received, owned_down, received = lax.optimization_barrier(
        (near_g_out, near_g_qkv, branch_received, owned_down, received)
    )
    red_down = both(owned_down)
    result_rows = mixed + summed(branch, branch_received)
    owned_out = to_owner(near_g_out)
    received, owned_out = lax.optimization_barrier((received, owned_out))
    red_gateup = both(owned_gateup)
    red_out, red_qkv = both(owned_out), both(to_owner(near_g_qkv))
    input_grad, in_gain = by_row_tiles(
        in_back_kernel,
        "in_back",
        slot_of,
        [hidden_in, partial, *received, ln_in[None], d_mixed],
        [row, gain_row],
        scratch=True,
        micros=40,
    )
    g_ln_in = jnp.sum(in_gain, axis=0)
    gain_terms = jnp.concatenate([g_ln_in, g_ln_mid, g_q, g_k])
    squares = sum(jnp.sum(red * red) for red in (red_qkv, red_gateup, red_out, red_down))
    totals_here = sum_all(jnp.concatenate([gain_terms, squares[None]]))
    gain_grad, total_squares = totals_here[:-1], totals_here[-1]
    grad_norm = jnp.sqrt(total_squares + jnp.sum(gain_grad * gain_grad))
    factor = jnp.minimum(1.0, CLIP_LIMIT / (grad_norm + 1e-06))
    (
        (qkv_new, qkv_first_new, qkv_second_new),
        (gateup_new, gateup_first_new, gateup_second_new),
        (out_new, out_first_new, out_second_new),
        (down_new, down_first_new, down_second_new),
    ) = adam_all(
        factor,
        [
            (
                LEARN,
                projection_master_weight,
                projection_first_moment,
                projection_second_moment,
                [red_qkv],
            ),
            (LEARN, gateup_weight, gateup_first, gateup_second, [red_gateup]),
            (out_rate, out_weight, out_first, out_second, [red_out]),
            (LEARN, down_weight, down_first, down_second, [red_down]),
        ],
    )
    gains_new, gain_first_new, gain_second_new = adam(
        gains, gain_first, gain_second, gain_grad, factor, GAIN_LEARN, 0.0
    )
    return (
        result_rows.astype(jnp.bfloat16),
        input_grad,
        qkv_new,
        gateup_new,
        out_new,
        down_new,
        qkv_first_new,
        gateup_first_new,
        out_first_new,
        down_first_new,
        qkv_second_new,
        gateup_second_new,
        out_second_new,
        down_second_new,
        gains_new,
        gain_first_new,
        gain_second_new,
        grad_norm,
    )


def paired(mesh):
    return dict(mesh.shape) == {"dp": 8, "mp": 4}


def solution(mesh):
    placed = (
        P(("dp", "mp"), None),
        P(("dp", "mp"), None),
        P("dp", None),
        P(),
        P("dp", "mp"),
        P("dp", "mp"),
        P(("mp", "dp"), None),
        P(("mp", "dp"), None),
        P("dp", "mp"),
        P("dp", "mp"),
        P(("mp", "dp"), None),
        P(("mp", "dp"), None),
        P("dp", "mp"),
        P("dp", "mp"),
        P(("mp", "dp"), None),
        P(("mp", "dp"), None),
        P(),
        P(),
        P(),
    )
    return jax.shard_map(
        shards_paired if paired(mesh) else shards_general,
        mesh=mesh,
        in_specs=placed,
        out_specs=(
            P(("dp", "mp"), None),
            P(("dp", "mp"), None),
            P("dp", "mp"),
            P("dp", "mp"),
            P(("mp", "dp"), None),
            P(("mp", "dp"), None),
            P("dp", "mp"),
            P("dp", "mp"),
            P(("mp", "dp"), None),
            P(("mp", "dp"), None),
            P("dp", "mp"),
            P("dp", "mp"),
            P(("mp", "dp"), None),
            P(("mp", "dp"), None),
            P(),
            P(),
            P(),
            P(),
        ),
        check_vma=False,
    )
```

```python
import jax
import jax.numpy as jnp
from jax import lax
from jax.experimental import pallas as pl
from jax.experimental.pallas import tpu as pltpu
from jax.sharding import PartitionSpec as P

MODEL_WIDTH = 2048
QUERY_HEADS = 16
KEY_VALUE_HEADS = 8
HEAD_SIZE = 128
FF = 6144
STEP = 10


EPS_NORM = 1e-06
THETA = 1000000.0
LEARN = 0.03
GAIN_LEARN = 0.5
FIRST_DECAY = 0.9
SECOND_DECAY = 0.95
ADAM_EPS = 1e-08
WEIGHT_DECAY = 0.1
CLIP_LIMIT = 1.0
MASKED = -1e30


def rms_norm(value_rows, gain):
    return (
        value_rows
        * lax.rsqrt(jnp.mean(value_rows * value_rows, axis=-1, keepdims=True) + EPS_NORM)
        * gain
    )


def norm_back(value_rows, gain, grad):
    score_scale = lax.rsqrt(jnp.mean(value_rows * value_rows, axis=-1, keepdims=True) + EPS_NORM)
    normed_input = value_rows * score_scale
    d_normal = grad * gain
    d_values = score_scale * (
        d_normal - normed_input * jnp.mean(d_normal * normed_input, axis=-1, keepdims=True)
    )
    d_gain = jnp.sum((grad * normed_input).reshape(-1, value_rows.shape[-1]), axis=0)
    return (d_values, d_gain)


def turned(value_rows):
    half = value_rows.shape[-1] // 2
    return jnp.concatenate([-value_rows[..., half:], value_rows[..., :half]], axis=-1)


def rotate(value_rows, cosine, sine):
    return value_rows * cosine + turned(value_rows) * sine


def rotate_back(grad, cosine, sine):
    return grad * cosine - turned(grad * sine)


def rope_tables(lengths, count):
    ends = jnp.cumsum(lengths)
    starts = ends - lengths
    places = jnp.arange(count, dtype=jnp.int32)
    doc_of = jnp.sum((places[:, None] >= ends[None, :]).astype(jnp.int32), axis=1)
    chosen = doc_of[:, None] == jnp.arange(lengths.shape[0], dtype=jnp.int32)[None, :]
    begin = jnp.sum(jnp.where(chosen, starts[None, :], 0), axis=1)
    offset = (places - begin).astype(jnp.float32)
    half = HEAD_SIZE // 2
    freq = THETA ** (-(2.0 * jnp.arange(half, dtype=jnp.float32)) / HEAD_SIZE)
    angle = offset[:, None] * freq[None, :]
    angle = jnp.concatenate([angle, angle], axis=-1)
    return (doc_of, jnp.cos(angle), jnp.sin(angle))


def arrange(gathered, order, blocks_count):
    blocks = gathered.reshape(blocks_count, gathered.shape[0] // blocks_count, gathered.shape[1])
    return jnp.take(blocks, order, axis=0).reshape(gathered.shape)


def fetch_weights(
    projection_master_weight, gateup_weight, out_weight, down_weight, owner, blocks_count
):
    gathered = (
        lax.all_gather(projection_master_weight.astype(jnp.bfloat16), "dp", axis=0, tiled=True),
        lax.all_gather(gateup_weight.astype(jnp.bfloat16), "dp", axis=0, tiled=True),
        lax.all_gather(out_weight.astype(jnp.bfloat16), "dp", axis=0, tiled=True),
        lax.all_gather(down_weight.astype(jnp.bfloat16), "dp", axis=0, tiled=True),
    )
    return tuple((arrange(piece, owner, blocks_count) for piece in gathered))


def fetch_again(
    projection_master_weight, gateup_weight, out_weight, down_weight, owner, blocks_count
):
    gathered = (
        lax.all_gather(projection_master_weight.astype(jnp.bfloat16), "dp", axis=0, tiled=True),
        lax.all_gather(gateup_weight.astype(jnp.bfloat16), "dp", axis=0, tiled=True),
        lax.all_gather(out_weight.astype(jnp.bfloat16), "dp", axis=0, tiled=True),
        lax.all_gather(down_weight.astype(jnp.bfloat16), "dp", axis=0, tiled=True),
    )
    return tuple((arrange(piece, owner, blocks_count) for piece in gathered))


def collect(rows):
    return lax.all_gather(rows, "mp", axis=0, tiled=True)


def collect_back(rows):
    return lax.all_gather(rows, "mp", axis=0, tiled=True)


def spread(operand, weight, rows):

    def term(start, count):
        return jnp.dot(operand, weight, preferred_element_type=jnp.float32)

    return lax.psum_scatter(
        term(jnp.int32(0), rows * lax.axis_size("mp")).astype(jnp.bfloat16),
        "mp",
        scatter_dimension=0,
        tiled=True,
    ).astype(jnp.float32)


def spread_back(operand, weight, rows):

    def term(start, count):
        return jnp.einsum("tc,dc->td", operand, weight, preferred_element_type=jnp.float32)

    return lax.psum_scatter(
        term(jnp.int32(0), rows * lax.axis_size("mp")).astype(jnp.bfloat16),
        "mp",
        scatter_dimension=0,
        tiled=True,
    ).astype(jnp.float32)


def adam(weight, first, second, grad, factor, rate, decay):
    clipped = grad * factor
    first_new = FIRST_DECAY * first + (1.0 - FIRST_DECAY) * clipped
    second_new = SECOND_DECAY * second + (1.0 - SECOND_DECAY) * clipped * clipped
    first_hat = first_new / (1.0 - FIRST_DECAY**STEP)
    second_hat = second_new / (1.0 - SECOND_DECAY**STEP)
    weight_new = weight * (1.0 - rate * decay) - rate * first_hat / (
        jnp.sqrt(second_hat) + ADAM_EPS
    )
    return (weight_new, first_new, second_new)


def shards_general(
    hidden_in,
    cotangent,
    doc_lengths,
    owner,
    projection_master_weight,
    gateup_weight,
    out_weight,
    down_weight,
    projection_first_moment,
    gateup_first,
    out_first,
    down_first,
    projection_second_moment,
    gateup_second,
    out_second,
    down_second,
    gains,
    gain_first,
    gain_second,
):
    total_width = lax.axis_size("mp")
    blocks_count = lax.axis_size("dp")
    heads = QUERY_HEADS // total_width
    key_value_heads = KEY_VALUE_HEADS // total_width
    query_group = heads // key_value_heads
    query_width = heads * HEAD_SIZE
    key_width = key_value_heads * HEAD_SIZE
    units = FF // total_width
    rows_here = hidden_in.shape[0]
    inverse = jnp.argsort(owner)
    out_rate = float(QUERY_HEADS * HEAD_SIZE // 32) ** (-0.5)
    w_qkv, w_gateup, w_out, w_down = fetch_weights(
        projection_master_weight, gateup_weight, out_weight, down_weight, owner, blocks_count
    )
    ln_in = gains[:MODEL_WIDTH]
    ln_mid = gains[MODEL_WIDTH : 2 * MODEL_WIDTH]
    q_gain = gains[2 * MODEL_WIDTH : 2 * MODEL_WIDTH + HEAD_SIZE]
    k_gain = gains[2 * MODEL_WIDTH + HEAD_SIZE :]
    x_rows = hidden_in.astype(jnp.float32)
    full_in = collect(rms_norm(x_rows, ln_in).astype(jnp.bfloat16))
    projected = jnp.dot(full_in, w_qkv, preferred_element_type=jnp.float32)
    count = projected.shape[0]
    doc_of, cosine, sine = rope_tables(doc_lengths[0], count)
    cosine = cosine[:, None, :]
    sine = sine[:, None, :]
    query_raw = projected[:, :query_width].reshape(count, heads, HEAD_SIZE)
    unrotated_key = projected[:, query_width : query_width + key_width].reshape(
        count, key_value_heads, HEAD_SIZE
    )
    projected_value = projected[:, query_width + key_width :].reshape(
        count, key_value_heads, HEAD_SIZE
    )
    query_rows = rotate(rms_norm(query_raw, q_gain), cosine, sine).astype(jnp.bfloat16)
    key_rows = rotate(rms_norm(unrotated_key, k_gain), cosine, sine).astype(jnp.bfloat16)
    value_rows = projected_value.astype(jnp.bfloat16)
    block = min(512, count)
    nblocks = count // block
    score_scale = HEAD_SIZE ** (-0.5)
    places = jnp.arange(count, dtype=jnp.int32)

    def scores_of(start):
        query_block = lax.dynamic_slice_in_dim(query_rows, start, block, 0).reshape(
            block, key_value_heads, query_group, HEAD_SIZE
        )
        raw = (
            jnp.einsum("tlwd,uld->lwtu", query_block, key_rows, preferred_element_type=jnp.float32)
            * score_scale
        )
        row_doc = lax.dynamic_slice_in_dim(doc_of, start, block, 0)
        row_place = start + jnp.arange(block, dtype=jnp.int32)
        allowed = (row_doc[:, None] == doc_of[None, :]) & (places[None, :] <= row_place[:, None])
        return (jnp.where(allowed[None, None], raw, MASKED), query_block)

    def forward_block(index):
        score_matrix, query_block = scores_of(index * block)
        top = jnp.max(score_matrix, axis=-1, keepdims=True)
        total = jnp.log(jnp.sum(jnp.exp(score_matrix - top), axis=-1, keepdims=True)) + top
        probabilities = jnp.exp(score_matrix - total).astype(jnp.bfloat16)
        attention_result = jnp.einsum(
            "cpyx,xca->ycpa", probabilities, value_rows, preferred_element_type=jnp.float32
        )
        return (attention_result.reshape(block, query_width), total)

    outs, totals = lax.map(forward_block, jnp.arange(nblocks, dtype=jnp.int32))
    attn_heads = outs.reshape(count, query_width).astype(jnp.bfloat16)
    attn_rows = spread(attn_heads, w_out, rows_here)
    mixed = x_rows + attn_rows
    full_mid = collect(rms_norm(mixed, ln_mid).astype(jnp.bfloat16))
    gateup = jnp.dot(full_mid, w_gateup, preferred_element_type=jnp.float32)
    gate = gateup[:, :units]
    upper = gateup[:, units:]
    sigma = jax.nn.sigmoid(gate)
    act = (gate * sigma * upper).astype(jnp.bfloat16)
    mlp_rows = spread(act, w_down, rows_here)
    result_rows = mixed + mlp_rows
    w_qkv, w_gateup, w_out, w_down = fetch_again(
        projection_master_weight, gateup_weight, out_weight, down_weight, owner, blocks_count
    )
    grad_out = cotangent.astype(jnp.float32)
    d_branch = collect_back(grad_out.astype(jnp.bfloat16))
    g_down = jnp.einsum("tf,td->fd", act, d_branch, preferred_element_type=jnp.float32)
    d_act = jnp.einsum("td,fd->tf", d_branch, w_down, preferred_element_type=jnp.float32)
    d_upper = d_act * gate * sigma
    d_gate = d_act * upper * sigma * (1.0 + gate * (1.0 - sigma))
    d_gateup = jnp.concatenate([d_gate, d_upper], axis=1).astype(jnp.bfloat16)
    g_gateup = jnp.einsum("td,tf->df", full_mid, d_gateup, preferred_element_type=jnp.float32)
    d_mid_rows = spread_back(d_gateup, w_gateup, rows_here)
    d_mixed, g_ln_mid = norm_back(mixed, ln_mid, d_mid_rows)
    d_mixed = d_mixed + grad_out
    d_attn = collect_back(d_mixed.astype(jnp.bfloat16))
    g_out = jnp.einsum("th,td->hd", attn_heads, d_attn, preferred_element_type=jnp.float32)
    d_heads = jnp.einsum("td,hd->th", d_attn, w_out, preferred_element_type=jnp.float32).astype(
        jnp.bfloat16
    )
    d_heads = d_heads.reshape(count, key_value_heads, query_group, HEAD_SIZE)

    def backward_block(carry, index):
        d_key_sum, d_value_sum = carry
        start = index * block
        score_matrix, query_block = scores_of(start)
        probabilities = jnp.exp(score_matrix - totals[index])
        block_gradient = lax.dynamic_slice_in_dim(d_heads, start, block, 0)
        probability_gradient = jnp.einsum(
            "tlwd,uld->lwtu", block_gradient, value_rows, preferred_element_type=jnp.float32
        )
        d_value_sum = d_value_sum + jnp.einsum(
            "zxrb,rzxd->bzd",
            probabilities.astype(jnp.bfloat16),
            block_gradient,
            preferred_element_type=jnp.float32,
        )
        score_gradient = (
            probabilities
            * (
                probability_gradient
                - jnp.sum(probabilities * probability_gradient, axis=-1, keepdims=True)
            )
        ).astype(jnp.bfloat16)
        d_query = (
            jnp.einsum(
                "cpyx,xca->ycpa", score_gradient, key_rows, preferred_element_type=jnp.float32
            )
            * score_scale
        )
        d_key_sum = (
            d_key_sum
            + jnp.einsum(
                "zxrb,rzxd->bzd", score_gradient, query_block, preferred_element_type=jnp.float32
            )
            * score_scale
        )
        return ((d_key_sum, d_value_sum), d_query.reshape(block, heads, HEAD_SIZE))

    empty = jnp.zeros((count, key_value_heads, HEAD_SIZE), jnp.float32)
    (d_keys, d_values), d_queries = lax.scan(
        backward_block, (empty, empty), jnp.arange(nblocks, dtype=jnp.int32)
    )
    d_queries = d_queries.reshape(count, heads, HEAD_SIZE)
    d_query_raw, g_q = norm_back(query_raw, q_gain, rotate_back(d_queries, cosine, sine))
    d_key_raw, g_k = norm_back(unrotated_key, k_gain, rotate_back(d_keys, cosine, sine))
    d_projected = jnp.concatenate(
        [
            d_query_raw.reshape(count, query_width),
            d_key_raw.reshape(count, key_width),
            d_values.reshape(count, key_width),
        ],
        axis=1,
    ).astype(jnp.bfloat16)
    g_qkv = jnp.einsum("td,tc->dc", full_in, d_projected, preferred_element_type=jnp.float32)
    d_in_rows = spread_back(d_projected, w_qkv, rows_here)
    d_input, g_ln_in = norm_back(x_rows, ln_in, d_in_rows)
    input_grad = d_input + d_mixed
    gain_terms = jnp.concatenate([g_ln_in, g_ln_mid, g_q, g_k])
    red_qkv, red_gateup, red_out, red_down = (
        lax.psum_scatter(
            arrange(g_qkv, inverse, blocks_count).astype(jnp.bfloat16),
            "dp",
            scatter_dimension=0,
            tiled=True,
        ).astype(jnp.float32),
        lax.psum_scatter(
            arrange(g_gateup, inverse, blocks_count).astype(jnp.bfloat16),
            "dp",
            scatter_dimension=0,
            tiled=True,
        ).astype(jnp.float32),
        lax.psum_scatter(
            arrange(g_out, inverse, blocks_count).astype(jnp.bfloat16),
            "dp",
            scatter_dimension=0,
            tiled=True,
        ).astype(jnp.float32),
        lax.psum_scatter(
            arrange(g_down, inverse, blocks_count).astype(jnp.bfloat16),
            "dp",
            scatter_dimension=0,
            tiled=True,
        ).astype(jnp.float32),
    )
    squares = jnp.sum(red_qkv * red_qkv) + jnp.sum(red_gateup * red_gateup)
    squares = squares + jnp.sum(red_out * red_out) + jnp.sum(red_down * red_down)
    total_squares, gain_grad = lax.psum((squares, gain_terms), ("dp", "mp"))
    grad_norm = jnp.sqrt(total_squares + jnp.sum(gain_grad * gain_grad))
    factor = jnp.minimum(1.0, CLIP_LIMIT / (grad_norm + 1e-06))
    qkv_new, qkv_first_new, qkv_second_new = adam(
        projection_master_weight,
        projection_first_moment,
        projection_second_moment,
        red_qkv,
        factor,
        LEARN,
        WEIGHT_DECAY,
    )
    gateup_new, gateup_first_new, gateup_second_new = adam(
        gateup_weight, gateup_first, gateup_second, red_gateup, factor, LEARN, WEIGHT_DECAY
    )
    out_new, out_first_new, out_second_new = adam(
        out_weight, out_first, out_second, red_out, factor, out_rate, WEIGHT_DECAY
    )
    down_new, down_first_new, down_second_new = adam(
        down_weight, down_first, down_second, red_down, factor, LEARN, WEIGHT_DECAY
    )
    gains_new, gain_first_new, gain_second_new = adam(
        gains, gain_first, gain_second, gain_grad, factor, GAIN_LEARN, 0.0
    )
    return (
        result_rows.astype(jnp.bfloat16),
        input_grad,
        qkv_new,
        gateup_new,
        out_new,
        down_new,
        qkv_first_new,
        gateup_first_new,
        out_first_new,
        down_first_new,
        qkv_second_new,
        gateup_second_new,
        out_second_new,
        down_second_new,
        gains_new,
        gain_first_new,
        gain_second_new,
        grad_norm,
    )


def steps(move):
    pairs = []
    for index in range(32):
        y, x, c, zh, zl = (index >> 4) & 1, (index >> 3) & 1, (index >> 2) & 1, (index >> 1) & 1, index & 1
        source = move(y, x, c, zh, zl)
        if source is not None:
            sy, sx, sc, sh, sl = source
            pairs.append(((sy << 4) | (sx << 3) | (sc << 2) | (sh << 1) | sl, index))
    return pairs


OVER_X = steps(lambda y, x, c, h, l: (y, 1 - x, c, h, l))
OVER_Y = steps(lambda y, x, c, h, l: (1 - y, x, c, h, l))
OVER_C = steps(lambda y, x, c, h, l: (y, x, 1 - c, h, l))
OVER_L = steps(lambda y, x, c, h, l: (y, x, c, h, 1 - l))
TO_GROUP = (
    steps(lambda y, x, c, h, l: (y, x, h, c, l)),
    steps(lambda y, x, c, h, l: (y, x, 1 - h, c, l)),
)
FROM_GROUP = tuple([(b, a) for a, b in pairs] for pairs in TO_GROUP)
UPWARD = steps(lambda y, x, c, h, l: (y, x, c, 0, l) if h == 1 else None)
DOWNWARD = steps(lambda y, x, c, h, l: (y, x, c, 1, l) if h == 0 else None)


def move(value, pairs):
    return lax.ppermute(value, ("dp", "mp"), pairs)


def after(value, *others):
    return lax.optimization_barrier((value, *others))[0]


PLANES = [[(block * 2 + c) * 4 + z for block in range(4)] for c in range(2) for z in range(4)]


MESH = pl.DeviceIdType.MESH


class Place:
    def __init__(self):
        dp, mp = lax.axis_index("dp"), lax.axis_index("mp")
        self.y, self.x, self.c = dp // 4, (dp // 2) % 2, dp % 2
        self.h, self.l = mp // 2, mp % 2
        self.block = (dp // 2) * 2

    def at(self, y=None, x=None, c=None, h=None, l=None):
        y, x, c = (o if n is None else n for o, n in ((self.y, y), (self.x, x), (self.c, c)))
        h, l = (o if n is None else n for o, n in ((self.h, h), (self.l, l)))
        return ((y * 2 + x) * 2 + c, h * 2 + l)

    def partners(self):
        return [
            self.at(x=1 - self.x),
            self.at(y=1 - self.y),
            self.at(l=1 - self.l),
            self.at(c=1 - self.c),
            self.at(h=1 - self.h),
            self.at(c=1 - self.c, h=1 - self.h),
        ]


def far_copy(source, target, sems, index, device):
    return pltpu.make_async_remote_copy(
        src_ref=source,
        dst_ref=target,
        send_sem=sems[0].at[index],
        recv_sem=sems[1].at[index],
        device_id=device,
        device_id_type=MESH,
    )


class Swap:
    def __init__(self, place, source, target, sems, index, local_sem):
        self.same = place.c == place.h
        self.far = far_copy(source, target, sems, index, place.at(c=place.h, h=place.c))
        self.near = pltpu.make_async_copy(source, target, local_sem)

    def start(self):
        pl.when(self.same)(self.near.start)
        pl.when(~self.same)(self.far.start)

    def wait_recv(self):
        pl.when(self.same)(self.near.wait)
        pl.when(~self.same)(self.far.wait_recv)

    def wait_send(self):
        pl.when(~self.same)(self.far.wait_send)


class Task:
    copies = 1
    locals = 1
    work = ()

    def __init__(self, *inputs, phase=0):
        self.inputs, self.phase = inputs, phase

    def scratch(self):
        return [
            pltpu.SemaphoreType.DMA((self.copies,)),
            pltpu.SemaphoreType.DMA((self.copies,)),
            pltpu.SemaphoreType.DMA((self.locals,)),
            *self.work,
        ]


class Rows(Task):
    copies = 3

    def outs(self):
        rows = self.inputs[0]
        return [jax.ShapeDtypeStruct((4, *rows.shape), rows.dtype)]

    def steps(self, place, ins, outs, scratch):
        own, full = ins[0], outs[0]
        send, recv, local = scratch[:3]
        keep = pltpu.make_async_copy(own, full.at[0], local.at[0])
        over_z = far_copy(own, full.at[1], (send, recv), 0, place.at(l=1 - place.l))
        over_c = far_copy(own, full.at[2], (send, recv), 1, place.at(c=1 - place.c))
        relay = far_copy(full.at[1], full.at[3], (send, recv), 2, place.at(c=1 - place.c))

        def first():
            over_z.start()
            over_c.start()
            keep.start()

        def second():
            over_z.wait_recv()
            relay.start()

        def last():
            keep.wait()
            over_c.wait()
            over_z.wait_send()
            relay.wait()

        return [first, None, second, last]


class Cores(Task):
    copies = 2
    locals = 2

    def outs(self):
        rows = self.inputs[0]
        return [jax.ShapeDtypeStruct((4, *rows.shape), rows.dtype)]

    def steps(self, place, ins, outs, scratch):
        send, recv, local = scratch[:3]
        full = outs[0]
        core = place.at(c=1 - place.c)
        keeps = [pltpu.make_async_copy(ins[n], full.at[n], local.at[n]) for n in range(2)]
        fars = [far_copy(ins[n], full.at[2 + n], (send, recv), n, core) for n in range(2)]

        def first():
            for copy in (*fars, *keeps):
                copy.start()

        def last():
            for copy in (*keeps, *fars):
                copy.wait()

        return [first, None, None, last]


class Sums(Task):
    copies = 3

    def __init__(self, *inputs, phase=0):
        super().__init__(*inputs, phase=phase)
        block = inputs[0].shape[1:]
        self.work = tuple(pltpu.VMEM(block, jnp.bfloat16) for _ in range(3))

    def outs(self):
        block = jax.ShapeDtypeStruct(self.inputs[0].shape[1:], jnp.bfloat16)
        return [block, block]

    def steps(self, place, ins, outs, scratch):
        partial, (from_c, from_z) = ins[0], outs
        send, recv, local, mine, theirs, total = scratch
        core = place.at(c=1 - place.c)
        load = pltpu.make_async_copy(partial.at[1], mine, local.at[0])
        far = far_copy(partial.at[3], theirs, (send, recv), 0, core)
        near = far_copy(partial.at[2], from_c, (send, recv), 1, core)
        over_z = far_copy(total, from_z, (send, recv), 2, place.at(l=1 - place.l))
        rows = 32

        def first():
            far.start()
            near.start()
            load.start()

        def second():
            load.wait()
            far.wait_recv()

            @pl.loop(0, mine.shape[0] // rows)
            def _(index):
                part = pl.ds(pl.multiple_of(index * rows, rows), rows)
                summed = mine[part, :].astype(jnp.float32) + theirs[part, :].astype(jnp.float32)
                total[part, :] = summed.astype(jnp.bfloat16)

            over_z.start()

        def last():
            far.wait_send()
            near.wait()
            over_z.wait()

        return [first, second, None, last]


class Near(Task):
    copies = 2

    def outs(self):
        shard = self.inputs[0]
        return [jax.ShapeDtypeStruct((2, *shard.shape), shard.dtype)]

    def copies_of(self, place, shard, first, second, scratch):
        send, recv, local = scratch[:3]
        return (
            Swap(place, shard, first, (send, recv), 0, local.at[0]),
            far_copy(shard, second, (send, recv), 1, place.at(c=place.h, h=1 - place.c)),
        )

    def steps(self, place, ins, outs, scratch):
        a, b = self.copies_of(place, ins[0], outs[0].at[0], outs[0].at[1], scratch)

        def first():
            a.start()
            b.start()

        def last():
            a.wait_recv()
            a.wait_send()
            b.wait()

        return [first, None, None, last]


class Planes(Near):
    copies = 8

    def outs(self):
        shard = self.inputs[0]
        return [jax.ShapeDtypeStruct((8, *shard.shape), shard.dtype)]

    def steps(self, place, ins, outs, scratch):
        full = outs[0]
        block = place.block
        a, b = self.copies_of(place, ins[0], full.at[block], full.at[block + 1], scratch)
        over_x, over_y = place.at(x=1 - place.x), place.at(y=1 - place.y)
        x_block = block + 2 - 4 * place.x
        y_block = block + 4 - 8 * place.y

        def pass_on(slot, index, device):
            return far_copy(full.at[slot], full.at[slot], scratch[:2], index, device)

        ax, ay = pass_on(block, 2, over_x), pass_on(block, 3, over_y)
        by, bx = pass_on(block + 1, 4, over_y), pass_on(block + 1, 5, over_x)
        axy = pass_on(x_block, 6, over_y)
        byx = pass_on(y_block + 1, 7, over_x)

        def first():
            a.start()
            b.start()

        def second():
            a.wait_recv()
            ax.start()
            b.wait_recv()
            by.start()
            ay.start()
            bx.start()

        def third():
            ax.wait_recv()
            axy.start()
            by.wait_recv()
            byx.start()

        def last():
            a.wait_send()
            b.wait_send()
            for copy in (ax, by):
                copy.wait_send()
            for copy in (ay, bx, axy, byx):
                copy.wait()

        return [first, second, third, last]


class Owners(Task):
    copies = 2

    def outs(self):
        near = self.inputs[0]
        return [jax.ShapeDtypeStruct(near.shape, near.dtype)]

    def steps(self, place, ins, outs, scratch):
        send, recv, local = scratch[:3]
        near, got = ins[0], outs[0]
        a = Swap(place, near.at[0], got.at[0], (send, recv), 0, local.at[0])
        b = far_copy(near.at[1], got.at[1], (send, recv), 1, place.at(c=1 - place.h, h=place.c))

        def first():
            a.start()
            b.start()

        def last():
            a.wait_recv()
            a.wait_send()
            b.wait()

        return [first, None, None, last]


class Halves(Task):
    def __init__(self, array, sender, phase=0):
        super().__init__(array, phase=phase)
        self.sender = sender

    def outs(self):
        return [jax.ShapeDtypeStruct(self.inputs[0].shape, self.inputs[0].dtype)]

    def steps(self, place, ins, outs, scratch):
        copy = far_copy(ins[0], outs[0], scratch[:2], 0, place.at(h=1 - place.h))
        sends = place.h == self.sender

        def first():
            pl.when(sends)(copy.start)

        def last():
            pl.when(sends)(copy.wait_send)
            pl.when(~sends)(copy.wait_recv)

        return [first, None, None, last]


def transfer(name, number, micros, *tasks, scoped=12):
    outs = [task.outs() for task in tasks]
    scratch = [task.scratch() for task in tasks]

    def kernel(*refs):
        refs = list(refs)

        def take(count):
            taken = refs[:count]
            del refs[:count]
            return taken

        ins_of = [take(len(task.inputs)) for task in tasks]
        outs_of = [take(len(out)) for out in outs]
        scratch_of = [take(len(one)) for one in scratch]
        place = Place()
        barrier = pltpu.get_barrier_semaphore()
        partners = place.partners()
        for partner in partners:
            pl.semaphore_signal(barrier, inc=1, device_id=partner, device_id_type=MESH)
        pl.semaphore_wait(barrier, len(partners))
        plans = [
            task.steps(place, ins_of[n], outs_of[n], scratch_of[n]) for n, task in enumerate(tasks)
        ]
        for phase in range(4):
            for task, plan in zip(tasks, plans):
                steps_now = [plan[phase]] if phase else []
                if phase == task.phase:
                    steps_now.insert(0, plan[0])
                for step in steps_now:
                    if step is not None:
                        step()

    results = pl.pallas_call(
        kernel,
        out_shape=[leaf for out in outs for leaf in out],
        in_specs=[pl.BlockSpec(memory_space=pl.ANY) for task in tasks for _ in task.inputs],
        out_specs=[pl.BlockSpec(memory_space=pl.ANY) for out in outs for _ in out],
        scratch_shapes=[one for part in scratch for one in part],
        compiler_params=pltpu.CompilerParams(
            collective_id=number, has_side_effects=True, vmem_limit_bytes=scoped * 2**20
        ),
        cost_estimate=pl.CostEstimate(
            flops=0, bytes_accessed=micros * 3_300_000, transcendentals=0
        ),
        name=name,
    )(*[leaf for task in tasks for leaf in task.inputs])
    results = list(results)
    grouped = []
    for out in outs:
        grouped.append(results[: len(out)])
        del results[: len(out)]
    return grouped


def to_group(shard):
    return jnp.stack([move(shard, TO_GROUP[0]), move(shard, TO_GROUP[1])])


def to_owner(near):
    return [move(near[0], FROM_GROUP[0]), move(near[1], FROM_GROUP[1])]


def over_plane(near):
    return lax.all_gather(near, ("dp", "mp"), axis=0, tiled=True, axis_index_groups=PLANES)


def to_plane(grads):
    return lax.psum_scatter(
        grads, ("dp", "mp"), scatter_dimension=0, tiled=True, axis_index_groups=PLANES
    )


def both(pair):
    return pair[0].astype(jnp.float32) + pair[1].astype(jnp.float32)


def summed(partial, received):
    return both(received) + partial[0].astype(jnp.float32)


def sum_all_kernel(value, total, by_mp, by_dp, send_sem, recv_sem):
    dp, mp = lax.axis_index("dp"), lax.axis_index("mp")
    over_mp = [(dp, (mp + step) % 4) for step in range(1, 4)]
    over_dp = [((dp + step) % 8, mp) for step in range(1, 8)]
    barrier = pltpu.get_barrier_semaphore()
    for partner in over_mp + over_dp:
        pl.semaphore_signal(
            barrier, inc=1, device_id=partner, device_id_type=pl.DeviceIdType.MESH
        )
    pl.semaphore_wait(barrier, len(over_mp) + len(over_dp))

    def share(table, place, partners, first):
        copies = [
            pltpu.make_async_remote_copy(
                src_ref=table.at[place],
                dst_ref=table.at[place],
                send_sem=send_sem.at[first + step],
                recv_sem=recv_sem.at[first + step],
                device_id=partner,
                device_id_type=pl.DeviceIdType.MESH,
            )
            for step, partner in enumerate(partners)
        ]
        for copy in copies:
            copy.start()
        for copy in copies:
            copy.wait()

    by_mp[mp] = value[...]
    share(by_mp, mp, over_mp, 0)
    by_dp[dp] = (by_mp[0] + by_mp[1]) + (by_mp[2] + by_mp[3])
    share(by_dp, dp, over_dp, 3)
    result = by_dp[0]
    for place in range(1, 8):
        result = result + by_dp[place]
    total[...] = result


def sum_all(vector):
    size = vector.shape[0]
    rows = -(-size // 1024) * 8
    block = jnp.pad(vector, (0, rows * 128 - size)).reshape(rows, 128)
    total = pl.pallas_call(
        sum_all_kernel,
        out_shape=jax.ShapeDtypeStruct((rows, 128), jnp.float32),
        in_specs=[pl.BlockSpec(memory_space=pltpu.VMEM)],
        out_specs=pl.BlockSpec(memory_space=pltpu.VMEM),
        scratch_shapes=[
            pltpu.VMEM((4, rows, 128), jnp.float32),
            pltpu.VMEM((8, rows, 128), jnp.float32),
            pltpu.SemaphoreType.DMA((10,)),
            pltpu.SemaphoreType.DMA((10,)),
        ],
        compiler_params=pltpu.CompilerParams(collective_id=0, has_side_effects=True),
        name="sum_all",
    )(block)
    return total.reshape(-1)[:size]


def column_places(index, high, low, rows):
    chunk = index // rows
    return high * 2 * rows + (low + chunk - 2 * low * chunk) * rows + index - chunk * rows


def project_kernel(rows_ref, weight_ref, cos_ref, sin_ref, gain_ref, raw_ref, query_ref, kv_ref):
    width = rows_ref.shape[1]
    weight = weight_ref[...].reshape(width, weight_ref.shape[2])
    projected = jnp.dot(rows_ref[...], weight, preferred_element_type=jnp.float32)
    query_width, key_width = query_ref.shape[1], kv_ref.shape[1] // 2
    turned_width = query_width + key_width
    raw_ref[...] = projected[:, :turned_width]
    cosine, sine = cos_ref[...], sin_ref[...]
    for start in range(0, turned_width, HEAD_SIZE):
        raw = projected[:, start : start + HEAD_SIZE]
        gain = gain_ref[0:1, :] if start < query_width else gain_ref[1:2, :]
        normed = raw * lax.rsqrt(jnp.mean(raw * raw, axis=1, keepdims=True) + EPS_NORM) * gain
        turned = normed * cosine + pltpu.roll(normed, HEAD_SIZE // 2, 1) * sine
        if start < query_width:
            query_ref[:, start : start + HEAD_SIZE] = turned.astype(jnp.bfloat16)
        else:
            place = start - query_width
            kv_ref[:, place : place + HEAD_SIZE] = turned.astype(jnp.bfloat16)
    kv_ref[:, key_width:] = projected[:, turned_width:].astype(jnp.bfloat16)


def project(rows, blocks, cosine, sine, head_gains, query_width, key_width):
    count, width = rows.shape
    tile = 256
    total = query_width + 2 * key_width
    by_rows = lambda columns: pl.BlockSpec((tile, columns), lambda i: (i, 0))
    return pl.pallas_call(
        project_kernel,
        grid=(count // tile,),
        in_specs=[
            by_rows(width),
            pl.BlockSpec((8, width // 8, total), lambda i: (0, 0, 0)),
            by_rows(HEAD_SIZE),
            by_rows(HEAD_SIZE),
            pl.BlockSpec((2, HEAD_SIZE), lambda i: (0, 0)),
        ],
        out_specs=[by_rows(query_width + key_width), by_rows(query_width), by_rows(2 * key_width)],
        out_shape=[
            jax.ShapeDtypeStruct((count, query_width + key_width), jnp.float32),
            jax.ShapeDtypeStruct((count, query_width), jnp.bfloat16),
            jax.ShapeDtypeStruct((count, 2 * key_width), jnp.bfloat16),
        ],
        compiler_params=pltpu.CompilerParams(vmem_limit_bytes=48 * 2**20),
        cost_estimate=pl.CostEstimate(
            flops=2 * count * width * total, bytes_accessed=16 * 2**20, transcendentals=0
        ),
        name="project",
    )(rows, blocks, cosine, sine, head_gains)


def unproject_kernel(
    place_ref, dq_ref, own_ref, above_ref, raw_ref, cos_ref, sin_ref, gain_ref, out_ref, gq_ref, gk_ref
):
    query_width, key_width = dq_ref.shape[1], own_ref.shape[1] // 2
    turned_width = query_width + key_width
    lower = place_ref[0] == 0
    cosine, sine = cos_ref[...], sin_ref[...]

    @pl.when(pl.program_id(0) == 0)
    def _():
        gq_ref[...] = jnp.zeros_like(gq_ref)
        gk_ref[...] = jnp.zeros_like(gk_ref)

    def with_above(columns):
        above = jnp.where(lower, above_ref[:, columns].astype(jnp.float32), 0.0)
        return own_ref[:, columns] + above

    for start in range(0, turned_width, HEAD_SIZE):
        columns = slice(start, start + HEAD_SIZE)
        if start < query_width:
            grad, gain, gain_sum = dq_ref[:, columns], gain_ref[0:1, :], gq_ref
        else:
            grad = with_above(slice(start - query_width, start - query_width + HEAD_SIZE))
            gain, gain_sum = gain_ref[1:2, :], gk_ref
        grad = grad * cosine - pltpu.roll(grad, HEAD_SIZE // 2, 1) * sine
        raw = raw_ref[:, columns]
        scale = lax.rsqrt(jnp.mean(raw * raw, axis=1, keepdims=True) + EPS_NORM)
        normed = raw * scale
        gain_sum[...] += jnp.sum((grad * normed).reshape(-1, 8, HEAD_SIZE), axis=0)
        d_normal = grad * gain
        value = scale * (d_normal - normed * jnp.mean(d_normal * normed, axis=1, keepdims=True))
        out_ref[:, columns] = value.astype(jnp.bfloat16)
    out_ref[:, turned_width:] = with_above(slice(key_width, 2 * key_width)).astype(jnp.bfloat16)


def unproject(place, d_queries, d_own, above, raw, cosine, sine, head_gains):
    count, query_width = d_queries.shape
    key_width = d_own.shape[1] // 2
    tile = 256
    total = query_width + 2 * key_width
    by_rows = lambda columns: pl.BlockSpec((tile, columns), lambda i, p: (i, 0))
    fixed = lambda rows: pl.BlockSpec((rows, HEAD_SIZE), lambda i, p: (0, 0))
    return pl.pallas_call(
        unproject_kernel,
        grid_spec=pltpu.PrefetchScalarGridSpec(
            num_scalar_prefetch=1,
            grid=(count // tile,),
            in_specs=[
                by_rows(query_width),
                by_rows(2 * key_width),
                by_rows(2 * key_width),
                by_rows(query_width + key_width),
                by_rows(HEAD_SIZE),
                by_rows(HEAD_SIZE),
                fixed(2),
            ],
            out_specs=[by_rows(total), fixed(8), fixed(8)],
        ),
        out_shape=[
            jax.ShapeDtypeStruct((count, total), jnp.bfloat16),
            jax.ShapeDtypeStruct((8, HEAD_SIZE), jnp.float32),
            jax.ShapeDtypeStruct((8, HEAD_SIZE), jnp.float32),
        ],
        compiler_params=pltpu.CompilerParams(vmem_limit_bytes=32 * 2**20),
        cost_estimate=pl.CostEstimate(flops=0, bytes_accessed=2 * 2**20, transcendentals=0),
        name="unproject",
    )(place, d_queries, d_own, above, raw, cosine, sine, head_gains)


def dot_t(left, right):
    return lax.dot_general(
        left, right, (((1,), (1,)), ((), ())), preferred_element_type=jnp.float32
    )


def t_dot(left, right):
    return lax.dot_general(
        left, right, (((0,), (0,)), ((), ())), preferred_element_type=jnp.float32
    )


def exps_of(place_ref, time_ref, begin_ref, rows, query, key_low, key_own):
    high, low = place_ref[0], place_ref[1]
    keys = key_own.shape[0]
    scale = HEAD_SIZE ** (-0.5)
    column = lax.broadcasted_iota(jnp.int32, (rows.size, keys), 1)
    time, begin = time_ref[rows, :], begin_ref[rows, :]
    own_place = column_places(column, high, low, keys // 2)
    low_place = column_places(column, 0, low, keys // 2)
    own_seen = (own_place <= time) & (own_place >= begin)
    low_seen = (low_place >= begin) & (low_place < high * keys)
    own = jnp.where(own_seen, dot_t(query, key_own) * scale, MASKED)
    lower = jnp.where(low_seen, dot_t(query, key_low) * scale, MASKED)
    top = jnp.maximum(
        jnp.max(own, axis=1, keepdims=True), jnp.max(lower, axis=1, keepdims=True)
    )
    own, lower = jnp.exp(own - top), jnp.exp(lower - top)
    total = jnp.sum(own, axis=1, keepdims=True) + jnp.sum(lower, axis=1, keepdims=True)
    return lower, own, 1.0 / total


def attend_kernel(place_ref, time_ref, begin_ref, query_ref, low_ref, own_ref, out_ref):
    half, query_width = query_ref.shape
    key_width = own_ref.shape[1] // 2
    group = query_width // key_width
    size = half // 2
    upper = place_ref[0] == 1
    for kv in range(key_width // HEAD_SIZE):
        key_at = slice(kv * HEAD_SIZE, (kv + 1) * HEAD_SIZE)
        value_at = slice(key_width + kv * HEAD_SIZE, key_width + (kv + 1) * HEAD_SIZE)
        key_low, key_own, value_own = low_ref[:, key_at], own_ref[:, key_at], own_ref[:, value_at]
        value_low = jnp.where(upper, low_ref[:, value_at], jnp.zeros_like(value_own))
        for part in range(2):
            rows = pl.ds(part * size, size)
            for head in range(kv * group, (kv + 1) * group):
                query_at = slice(head * HEAD_SIZE, (head + 1) * HEAD_SIZE)
                lower, own, inverse = exps_of(
                    place_ref, time_ref, begin_ref, rows, query_ref[rows, query_at], key_low, key_own
                )
                result = jnp.dot(
                    lower.astype(jnp.bfloat16), value_low, preferred_element_type=jnp.float32
                ) + jnp.dot(own.astype(jnp.bfloat16), value_own, preferred_element_type=jnp.float32)
                out_ref[rows, query_at] = (result * inverse).astype(jnp.bfloat16)


def attend_back_kernel(
    place_ref, time_ref, begin_ref, query_ref, low_ref, own_ref, grad_ref, dq_ref, dlow_ref, down_ref
):
    half, query_width = query_ref.shape
    key_width = own_ref.shape[1] // 2
    group = query_width // key_width
    size = half // 2
    scale = HEAD_SIZE ** (-0.5)
    upper = place_ref[0] == 1
    for kv in range(key_width // HEAD_SIZE):
        key_at = slice(kv * HEAD_SIZE, (kv + 1) * HEAD_SIZE)
        value_at = slice(key_width + kv * HEAD_SIZE, key_width + (kv + 1) * HEAD_SIZE)
        key_own, value_own = own_ref[:, key_at], own_ref[:, value_at]
        key_low = jnp.where(upper, low_ref[:, key_at], jnp.zeros_like(key_own))
        value_low = jnp.where(upper, low_ref[:, value_at], jnp.zeros_like(value_own))
        dk_low = dk_own = dv_low = dv_own = None
        for part in range(2):
            rows = pl.ds(part * size, size)
            for head in range(kv * group, (kv + 1) * group):
                query_at = slice(head * HEAD_SIZE, (head + 1) * HEAD_SIZE)
                query, grad = query_ref[rows, query_at], grad_ref[rows, query_at]
                lower, own, inverse = exps_of(
                    place_ref, time_ref, begin_ref, rows, query, key_low, key_own
                )
                lower, own = lower * inverse, own * inverse
                g_low, g_own = dot_t(grad, value_low), dot_t(grad, value_own)
                mean = jnp.sum(lower * g_low, axis=1, keepdims=True) + jnp.sum(
                    own * g_own, axis=1, keepdims=True
                )
                s_low = (lower * (g_low - mean)).astype(jnp.bfloat16)
                s_own = (own * (g_own - mean)).astype(jnp.bfloat16)
                dq_ref[rows, query_at] = scale * (
                    jnp.dot(s_low, key_low, preferred_element_type=jnp.float32)
                    + jnp.dot(s_own, key_own, preferred_element_type=jnp.float32)
                )
                terms = (
                    t_dot(s_low, query),
                    t_dot(s_own, query),
                    t_dot(lower.astype(jnp.bfloat16), grad),
                    t_dot(own.astype(jnp.bfloat16), grad),
                )
                if dk_low is None:
                    dk_low, dk_own, dv_low, dv_own = terms
                else:
                    dk_low, dk_own = dk_low + terms[0], dk_own + terms[1]
                    dv_low, dv_own = dv_low + terms[2], dv_own + terms[3]
        dlow_ref[:, key_at] = (dk_low * scale).astype(jnp.bfloat16)
        dlow_ref[:, value_at] = dv_low.astype(jnp.bfloat16)
        down_ref[:, key_at] = dk_own * scale
        down_ref[:, value_at] = dv_own


def attention_call(kernel, name, place, arrays, outs, flops):
    count = arrays[0].shape[0]
    half = count // 2
    spec = lambda leaf: pl.BlockSpec((half, leaf.shape[1]), lambda i, p: (i, 0))
    return pl.pallas_call(
        kernel,
        grid_spec=pltpu.PrefetchScalarGridSpec(
            num_scalar_prefetch=1,
            grid=(2,),
            in_specs=[spec(leaf) for leaf in arrays],
            out_specs=[spec(leaf) for leaf in outs],
        ),
        out_shape=outs,
        compiler_params=pltpu.CompilerParams(vmem_limit_bytes=56 * 2**20),
        cost_estimate=pl.CostEstimate(flops=flops, bytes_accessed=16 * 2**20, transcendentals=0),
        name=name,
    )(place, *arrays)


def scaled(values):
    return values * lax.rsqrt(jnp.mean(values * values, axis=1, keepdims=True) + EPS_NORM)


def three(parts, columns=slice(None)):
    own, from_c, from_z = parts
    return (
        own[0, :, columns].astype(jnp.float32)
        + from_c[:, columns].astype(jnp.float32)
        + from_z[:, columns].astype(jnp.float32)
    )


def slot_columns(slot_ref, index, block):
    return pl.ds(pl.multiple_of(slot_ref[index] * block, block), block)


def store_slots(slot_ref, out_ref, values):
    block = out_ref.shape[1] // 8
    for index in range(8):
        out_ref[:, slot_columns(slot_ref, index, block)] = values[
            :, index * block : (index + 1) * block
        ]


def norm_kernel(slot_ref, x_ref, gain_ref, out_ref):
    x = x_ref[...].astype(jnp.float32)
    store_slots(slot_ref, out_ref, (scaled(x) * gain_ref[...]).astype(jnp.bfloat16))


def mix_kernel(slot_ref, x_ref, own_ref, c_ref, z_ref, gain_ref, mixed_ref, out_ref):
    mixed = x_ref[...].astype(jnp.float32) + three((own_ref, c_ref, z_ref))
    mixed_ref[...] = mixed
    store_slots(slot_ref, out_ref, (scaled(mixed) * gain_ref[...]).astype(jnp.bfloat16))


def norm_back_of(slot_ref, value_ref, parts, gain_ref, sum_ref, grad_ref):
    width = value_ref.shape[1]
    block = width // 8
    for index in range(8):
        grad_ref[:, index * block : (index + 1) * block] = three(
            parts, slot_columns(slot_ref, index, block)
        )
    value, grad = value_ref[...].astype(jnp.float32), grad_ref[...]
    scale = lax.rsqrt(jnp.mean(value * value, axis=1, keepdims=True) + EPS_NORM)
    normed = value * scale

    @pl.when(pl.program_id(0) == 0)
    def _():
        sum_ref[...] = jnp.zeros_like(sum_ref)

    sum_ref[...] += jnp.sum((grad * normed).reshape(-1, 8, width), axis=0)
    d_normal = grad * gain_ref[...]
    return scale * (d_normal - normed * jnp.mean(d_normal * normed, axis=1, keepdims=True))


def mix_back_kernel(
    slot_ref, mixed_ref, own_ref, c_ref, z_ref, gain_ref, cot_ref, d_ref, low_ref, sum_ref, grad_ref
):
    value = norm_back_of(slot_ref, mixed_ref, (own_ref, c_ref, z_ref), gain_ref, sum_ref, grad_ref)
    value = value + cot_ref[...].astype(jnp.float32)
    d_ref[...] = value
    low_ref[...] = value.astype(jnp.bfloat16)


def in_back_kernel(
    slot_ref, x_ref, own_ref, c_ref, z_ref, gain_ref, d_ref, out_ref, sum_ref, grad_ref
):
    value = norm_back_of(slot_ref, x_ref, (own_ref, c_ref, z_ref), gain_ref, sum_ref, grad_ref)
    out_ref[...] = value + d_ref[...]


def by_row_tiles(kernel, name, slot_of, inputs, outs, scratch=False, micros=3):
    rows, width = 128 if scratch else 64, inputs[0].shape[1]
    steps = inputs[0].shape[0] // rows

    def spec(leaf):
        if len(leaf.shape) == 3:
            return pl.BlockSpec((1, rows, width), lambda i, p: (0, i, 0))
        if leaf.shape[0] in (1, 8):
            return pl.BlockSpec(leaf.shape, lambda i, p: (0, 0))
        return pl.BlockSpec((rows, width), lambda i, p: (i, 0))

    return pl.pallas_call(
        kernel,
        grid_spec=pltpu.PrefetchScalarGridSpec(
            num_scalar_prefetch=1,
            grid=(steps,),
            in_specs=[spec(leaf) for leaf in inputs],
            out_specs=[spec(leaf) for leaf in outs],
            scratch_shapes=[pltpu.VMEM((rows, width), jnp.float32)] if scratch else [],
        ),
        out_shape=outs,
        compiler_params=pltpu.CompilerParams(vmem_limit_bytes=(60 if scratch else 24) * 2**20),
        cost_estimate=pl.CostEstimate(flops=0, bytes_accessed=micros * 3_300_000, transcendentals=0),
        name=name,
    )(slot_of, *inputs)


def mlp_front_kernel(rows_ref, gate_ref, up_ref, gate_out, up_out, act_out):
    width = rows_ref.shape[1]
    rows = rows_ref[...]
    gate = jnp.dot(rows, gate_ref[...].reshape(width, -1), preferred_element_type=jnp.float32)
    upper = jnp.dot(rows, up_ref[...].reshape(width, -1), preferred_element_type=jnp.float32)
    gate_out[...] = gate
    up_out[...] = upper
    act_out[...] = (gate * upper / (1.0 + jnp.exp(-gate))).astype(jnp.bfloat16)


def mlp_front(rows, gate_blocks, up_blocks):
    count, width = rows.shape
    units = gate_blocks.shape[2]
    columns = 256
    weight = pl.BlockSpec((8, width // 8, columns), lambda i: (0, 0, i))
    out = pl.BlockSpec((count, columns), lambda i: (0, i))
    return pl.pallas_call(
        mlp_front_kernel,
        grid=(units // columns,),
        in_specs=[pl.BlockSpec((count, width), lambda i: (0, 0)), weight, weight],
        out_specs=[out, out, out],
        out_shape=[
            jax.ShapeDtypeStruct((count, units), jnp.float32),
            jax.ShapeDtypeStruct((count, units), jnp.float32),
            jax.ShapeDtypeStruct((count, units), jnp.bfloat16),
        ],
        compiler_params=pltpu.CompilerParams(vmem_limit_bytes=60 * 2**20),
        cost_estimate=pl.CostEstimate(
            flops=4 * count * units * width, bytes_accessed=32 * 2**20, transcendentals=0
        ),
        name="mlp_front",
    )(rows, gate_blocks, up_blocks)


def mlp_back_kernel(
    slot_ref, dy_ref, gate_ref, up_ref, act_ref, down_ref, dgate_ref, dup_ref, branch_ref, weight_ref
):
    block = down_ref.shape[1]

    @pl.when(pl.program_id(0) == 0)
    def _():
        for index in range(8):
            weight_ref[index * block : (index + 1) * block, :] = down_ref[slot_ref[index]]

    units, step = gate_ref.shape[1], 512
    dy = dy_ref[...]
    total = None
    for start in range(0, units, step):
        columns = slice(start, start + step)
        weight = weight_ref[columns, :]
        gate, upper = gate_ref[:, columns], up_ref[:, columns]
        d_act = dot_t(dy, weight)
        sigma = 1.0 / (1.0 + jnp.exp(-gate))
        dup_ref[:, columns] = (d_act * gate * sigma).astype(jnp.bfloat16)
        d_gate = d_act * upper * sigma * (1.0 + gate * (1.0 - sigma))
        dgate_ref[:, columns] = d_gate.astype(jnp.bfloat16)
        term = jnp.dot(act_ref[:, columns], weight, preferred_element_type=jnp.float32)
        total = term if total is None else total + term
    branch_ref[0] = total.astype(jnp.bfloat16)


def mlp_back(slot_of, d_branch, gate, upper, act, down_blocks):
    count, units = gate.shape
    width = d_branch.shape[1]
    rows = 256
    by_rows = lambda columns: pl.BlockSpec((rows, columns), lambda i, p: (i, 0))
    wide = jax.ShapeDtypeStruct((count, units), jnp.bfloat16)
    return pl.pallas_call(
        mlp_back_kernel,
        grid_spec=pltpu.PrefetchScalarGridSpec(
            num_scalar_prefetch=1,
            grid=(count // rows,),
            in_specs=[
                by_rows(width),
                by_rows(units),
                by_rows(units),
                by_rows(units),
                pl.BlockSpec(down_blocks.shape, lambda i, p: (0, 0, 0)),
            ],
            out_specs=[by_rows(units)] * 2
            + [pl.BlockSpec((1, rows, width), lambda i, p: (i, 0, 0))],
            scratch_shapes=[pltpu.VMEM((units, width), jnp.bfloat16)],
        ),
        out_shape=[
            wide,
            wide,
            jax.ShapeDtypeStruct((count // rows, rows, width), jnp.bfloat16),
        ],
        compiler_params=pltpu.CompilerParams(vmem_limit_bytes=48 * 2**20),
        cost_estimate=pl.CostEstimate(
            flops=4 * count * units * width, bytes_accessed=32 * 2**20, transcendentals=0
        ),
        name="mlp_back",
    )(slot_of, d_branch, gate, upper, act, down_blocks)


def rows_back_kernel(*refs):
    *pairs, out_ref = refs
    total = None
    for grad_ref, weight_ref in zip(pairs[::2], pairs[1::2]):
        term = dot_t(grad_ref[...], weight_ref[0])
        total = term if total is None else total + term
    out_ref[...] = total.astype(jnp.bfloat16).reshape(out_ref.shape)


def rows_back(name, *pairs):
    count = pairs[0].shape[0]
    block = pairs[1].shape[1]
    specs = []
    for grad, weight in zip(pairs[::2], pairs[1::2]):
        specs.append(pl.BlockSpec(grad.shape, lambda i: (0, 0)))
        specs.append(pl.BlockSpec((1, *weight.shape[1:]), lambda i: (i, 0, 0)))
    return pl.pallas_call(
        rows_back_kernel,
        grid=(8,),
        in_specs=specs,
        out_specs=pl.BlockSpec((4, count // 4, block), lambda i: (0, 0, i)),
        out_shape=jax.ShapeDtypeStruct((4, count // 4, 8 * block), jnp.bfloat16),
        compiler_params=pltpu.CompilerParams(vmem_limit_bytes=28 * 2**20),
        cost_estimate=pl.CostEstimate(
            flops=sum(count * w.size for w in pairs[1::2]) // 4,
            bytes_accessed=2 * 2**20,
            transcendentals=0,
        ),
        name=name,
    )(*pairs)


def adam_kernel(factor_ref, *refs, rates):
    factor = factor_ref[0]
    ins, outs = refs[: len(refs) - 3 * len(rates)], refs[len(refs) - 3 * len(rates) :]
    at = 0
    for place, (rate, pieces) in enumerate(rates):
        weight_ref, first_ref, second_ref, *grads = ins[at : at + 3 + pieces]
        at += 3 + pieces
        start = 0
        for grad_ref in grads:
            columns = slice(start, start + grad_ref.shape[1])
            start += grad_ref.shape[1]
            results = adam(
                weight_ref[:, columns],
                first_ref[:, columns],
                second_ref[:, columns],
                grad_ref[...],
                factor,
                rate,
                WEIGHT_DECAY,
            )
            for out_ref, result in zip(outs[3 * place : 3 * place + 3], results):
                out_ref[:, columns] = result


def adam_all(factor, weights):
    steps = 8
    rates = tuple((rate, len(grads)) for rate, *_, grads in weights)
    arrays, outs = [], []
    for _, master, first, second, grads in weights:
        arrays += [master, first, second, *grads]
        outs += [jax.ShapeDtypeStruct(master.shape, jnp.float32)] * 3

    def spec(leaf):
        return pl.BlockSpec((leaf.shape[0] // steps, leaf.shape[1]), lambda i, p: (i, 0))

    results = pl.pallas_call(
        lambda *refs: adam_kernel(*refs, rates=rates),
        grid_spec=pltpu.PrefetchScalarGridSpec(
            num_scalar_prefetch=1,
            grid=(steps,),
            in_specs=[spec(leaf) for leaf in arrays],
            out_specs=[spec(leaf) for leaf in outs],
        ),
        out_shape=outs,
        compiler_params=pltpu.CompilerParams(vmem_limit_bytes=60 * 2**20),
        cost_estimate=pl.CostEstimate(flops=0, bytes_accessed=48 * 2**20, transcendentals=0),
        name="adam_all",
    )(factor[None], *arrays)
    return [results[n : n + 3] for n in range(0, len(results), 3)]


def slot_grad_kernel(slot_ref, left_ref, right_ref, out_ref):
    block = out_ref.shape[1]
    grad = t_dot(left_ref[...], right_ref[...]).astype(jnp.bfloat16)
    for index in range(8):
        out_ref[slot_ref[index]] = grad[index * block : (index + 1) * block, :]


def slot_grad(slot_of, left, right):
    count, rows = left.shape
    width = right.shape[1]
    columns = 512
    return pl.pallas_call(
        slot_grad_kernel,
        grid_spec=pltpu.PrefetchScalarGridSpec(
            num_scalar_prefetch=1,
            grid=(width // columns,),
            in_specs=[
                pl.BlockSpec((count, rows), lambda i, p: (0, 0)),
                pl.BlockSpec((count, columns), lambda i, p: (0, i)),
            ],
            out_specs=pl.BlockSpec((8, rows // 8, columns), lambda i, p: (0, 0, i)),
        ),
        out_shape=jax.ShapeDtypeStruct((8, rows // 8, width), jnp.bfloat16),
        compiler_params=pltpu.CompilerParams(vmem_limit_bytes=48 * 2**20),
        cost_estimate=pl.CostEstimate(
            flops=2 * count * rows * width, bytes_accessed=16 * 2**20, transcendentals=0
        ),
        name="slot_grad",
    )(slot_of, left, right)


class Grads(Task):
    def outs(self):
        rows, left, right = self.inputs
        columns = left.shape[1] + right.shape[1]
        return [jax.ShapeDtypeStruct((8, rows.shape[1] // 8, columns), jnp.bfloat16)]

    def scratch(self):
        return []

    def steps(self, place, ins, outs, scratch):
        count, width = self.inputs[0].shape
        block = width // 8
        columns = self.inputs[1].shape[1]

        def body(rows_ref, left_ref, right_ref, out_ref):
            rows = rows_ref[...]
            out_ref[0, :, :columns] = t_dot(rows, left_ref[...]).astype(jnp.bfloat16)
            out_ref[0, :, columns:] = t_dot(rows, right_ref[...]).astype(jnp.bfloat16)

        def whole(one):
            return pl.BlockSpec((count, one.shape[1]), lambda i: (0, 0))

        run = pltpu.emit_pipeline(
            body,
            grid=(8,),
            in_specs=[
                pl.BlockSpec((count, block), lambda i: (0, i)),
                whole(self.inputs[1]),
                whole(self.inputs[2]),
            ],
            out_specs=[pl.BlockSpec((1, block, 2 * columns), lambda i: (i, 0, 0))],
        )
        return [lambda: None, None, lambda: run(*ins, *outs), None]


def shards_paired(
    hidden_in,
    cotangent,
    doc_lengths,
    owner,
    projection_master_weight,
    gateup_weight,
    out_weight,
    down_weight,
    projection_first_moment,
    gateup_first,
    out_first,
    down_first,
    projection_second_moment,
    gateup_second,
    out_second,
    down_second,
    gains,
    gain_first,
    gain_second,
):
    high, low = lax.axis_index("mp") // 2, lax.axis_index("mp") % 2
    plane = high
    groups = lax.axis_size("mp")
    query_width = QUERY_HEADS // groups * HEAD_SIZE
    key_width = KEY_VALUE_HEADS // groups * HEAD_SIZE
    units = FF // groups
    rows_here = hidden_in.shape[0]
    count = 4 * rows_here
    half = count // 2
    width = hidden_in.shape[1]
    slot_of = (owner ^ plane).astype(jnp.int32)
    out_rate = float(QUERY_HEADS * HEAD_SIZE // 32) ** (-0.5)

    ln_in = gains[:MODEL_WIDTH]
    ln_mid = gains[MODEL_WIDTH : 2 * MODEL_WIDTH]
    q_gain = gains[2 * MODEL_WIDTH : 2 * MODEL_WIDTH + HEAD_SIZE]
    k_gain = gains[2 * MODEL_WIDTH + HEAD_SIZE :]
    low_gateup = gateup_weight.astype(jnp.bfloat16)
    own_in = by_row_tiles(
        norm_kernel,
        "norm_in",
        slot_of,
        [hidden_in, ln_in[None]],
        [jax.ShapeDtypeStruct(hidden_in.shape, jnp.bfloat16)],
    )
    (qkv_blocks,), (out_blocks,), (full_in,), (near_gate,) = transfer(
        "gather_first",
        1,
        75,
        Planes(projection_master_weight.astype(jnp.bfloat16)),
        Planes(out_weight.astype(jnp.bfloat16)),
        Rows(own_in[0]),
        Near(low_gateup[:, :units], phase=1),
    )
    full_in = full_in.reshape(count, width)
    w_out = jnp.take(out_blocks, slot_of, axis=0, mode="clip").reshape(-1, width)
    gate_blocks = over_plane(near_gate)
    near_up = to_group(after(low_gateup[:, units:], full_in))

    lengths = jnp.concatenate([doc_lengths, move(doc_lengths, OVER_C)], axis=0)
    ends = jnp.cumsum(lengths, axis=1)
    spot = jnp.arange(half, dtype=jnp.int32)
    chunk = spot // rows_here
    own_places = high * half + (low ^ chunk) * rows_here + spot % rows_here
    later = own_places[None, :, None] >= ends[:, None, :]
    begin = jnp.max(jnp.where(later, ends[:, None, :], 0), axis=2).reshape(count, 1)
    time = jnp.concatenate([own_places, own_places]).reshape(count, 1)
    freq = THETA ** (-(2.0 * jnp.arange(HEAD_SIZE // 2, dtype=jnp.float32)) / HEAD_SIZE)
    angle = (time - begin).astype(jnp.float32) * freq[None, :]
    cosine, sine = jnp.cos(angle), jnp.sin(angle)
    cosine = jnp.concatenate([cosine, cosine], axis=-1)
    sine = jnp.concatenate([-sine, sine], axis=-1)
    head_gains = jnp.stack([q_gain, k_gain])
    place = jnp.stack([high, low]).astype(jnp.int32)

    raw, queries, own_kv = project(
        full_in, qkv_blocks, cosine, sine, head_gains, query_width, key_width
    )
    low_down = down_weight.astype(jnp.bfloat16)
    own_kv, w_out, low_down = lax.optimization_barrier((own_kv, w_out, low_down))
    ((lower_kv,),) = transfer("keys_up", 2, 40, Halves(own_kv, 0))
    lower_kv, near_up = lax.optimization_barrier((lower_kv, near_up))
    near_cotangent = move(after(cotangent, lower_kv), OVER_L)
    up_blocks = over_plane(near_up)
    score_flops = 2 * count * count * query_width
    (attn_heads,) = attention_call(
        attend_kernel,
        "attend",
        place,
        [time, begin, queries, lower_kv, own_kv],
        [jax.ShapeDtypeStruct((count, query_width), jnp.bfloat16)],
        2 * score_flops,
    )

    def blocks(partial):
        return partial.astype(jnp.bfloat16).reshape(4, rows_here, width)

    partial = blocks(jnp.dot(attn_heads, w_out, preferred_element_type=jnp.float32))
    partial, near_cotangent = lax.optimization_barrier((partial, near_cotangent))
    received, (near_down,) = transfer(
        "sum_attention", 3, 50, Sums(partial), Near(low_down)
    )
    down_blocks = over_plane(near_down)
    row = jax.ShapeDtypeStruct((rows_here, width), jnp.float32)
    low_row = jax.ShapeDtypeStruct((rows_here, width), jnp.bfloat16)
    gain_row = jax.ShapeDtypeStruct((8, width), jnp.float32)
    mixed, own_mid = by_row_tiles(
        mix_kernel, "mix", slot_of, [hidden_in, partial, *received, ln_mid[None]], [row, low_row]
    )
    (full_mid,), (d_branch,) = transfer(
        "gather_mid", 4, 34, Rows(own_mid), Cores(cotangent, near_cotangent)
    )
    d_branch = d_branch.reshape(count, width)
    full_mid = full_mid.reshape(count, width)
    gate, upper, act = mlp_front(full_mid, gate_blocks, up_blocks)
    g_down = slot_grad(slot_of, act, d_branch)
    down_blocks, g_down = lax.optimization_barrier((down_blocks, g_down))
    near_g_down = to_plane(g_down)
    d_gate, d_upper, branch = mlp_back(slot_of, d_branch, gate, upper, act, down_blocks)
    partial = rows_back("mid_rows", d_gate, gate_blocks, d_upper, up_blocks)
    received, (g_gateup,) = transfer(
        "sum_mid", 5, 33, Sums(partial), Grads(full_mid, d_gate, d_upper), scoped=40
    )
    near_g_gateup = to_plane(g_gateup)
    d_mixed, low_d_mixed, mid_gain = by_row_tiles(
        mix_back_kernel,
        "mix_back",
        slot_of,
        [mixed, partial, *received, ln_mid[None], cotangent],
        [row, low_row, gain_row],
        scratch=True,
    )
    g_ln_mid = jnp.sum(mid_gain, axis=0)
    ((d_attn,),) = transfer("gather_attention", 6, 29, Rows(low_d_mixed))
    d_attn = d_attn.reshape(count, width)
    owned_down = to_owner(after(near_g_down, d_attn))
    g_out = slot_grad(slot_of, attn_heads, d_attn)
    d_heads = jnp.einsum("td,hd->th", d_attn, w_out, preferred_element_type=jnp.float32).astype(
        jnp.bfloat16
    )
    d_queries, d_low, d_own = attention_call(
        attend_back_kernel,
        "attend_back",
        place,
        [time, begin, queries, lower_kv, own_kv, d_heads],
        [
            jax.ShapeDtypeStruct((count, query_width), jnp.float32),
            jax.ShapeDtypeStruct((count, 2 * key_width), jnp.bfloat16),
            jax.ShapeDtypeStruct((count, 2 * key_width), jnp.float32),
        ],
        5 * score_flops,
    )
    d_low, g_out, *owned_down = lax.optimization_barrier((d_low, g_out, *owned_down))
    near_g_out = to_plane(g_out)
    (from_above,), branch_received = transfer("keys_down", 7, 53, Halves(d_low, 1), Sums(branch))
    d_projected, g_q, g_k = unproject(
        place, d_queries, d_own, from_above, raw, cosine, sine, head_gains
    )
    g_q, g_k = jnp.sum(g_q, axis=0), jnp.sum(g_k, axis=0)
    g_qkv = jnp.einsum("td,tc->dc", full_in, d_projected, preferred_element_type=jnp.float32)
    near_g_qkv = to_plane(g_qkv.astype(jnp.bfloat16).reshape(8, width // 8, -1))
    partial = rows_back("in_rows", d_projected, qkv_blocks)
    received, (owned_gateup,) = transfer("sum_in", 8, 74, Sums(partial), Owners(near_g_gateup))
    near_g_out, near_g_qkv, branch_received, owned_down, received = lax.optimization_barrier(
        (near_g_out, near_g_qkv, branch_received, owned_down, received)
    )
    red_down = both(owned_down)
    result_rows = mixed + summed(branch, branch_received)
    owned_out = to_owner(near_g_out)
    received, owned_out = lax.optimization_barrier((received, owned_out))
    red_gateup = both(owned_gateup)
    red_out, red_qkv = both(owned_out), both(to_owner(near_g_qkv))
    input_grad, in_gain = by_row_tiles(
        in_back_kernel,
        "in_back",
        slot_of,
        [hidden_in, partial, *received, ln_in[None], d_mixed],
        [row, gain_row],
        scratch=True,
        micros=40,
    )
    g_ln_in = jnp.sum(in_gain, axis=0)
    gain_terms = jnp.concatenate([g_ln_in, g_ln_mid, g_q, g_k])
    squares = sum(jnp.sum(red * red) for red in (red_qkv, red_gateup, red_out, red_down))
    totals_here = sum_all(jnp.concatenate([gain_terms, squares[None]]))
    gain_grad, total_squares = totals_here[:-1], totals_here[-1]
    grad_norm = jnp.sqrt(total_squares + jnp.sum(gain_grad * gain_grad))
    factor = jnp.minimum(1.0, CLIP_LIMIT / (grad_norm + 1e-06))
    (
        (qkv_new, qkv_first_new, qkv_second_new),
        (gateup_new, gateup_first_new, gateup_second_new),
        (out_new, out_first_new, out_second_new),
        (down_new, down_first_new, down_second_new),
    ) = adam_all(
        factor,
        [
            (
                LEARN,
                projection_master_weight,
                projection_first_moment,
                projection_second_moment,
                [red_qkv],
            ),
            (LEARN, gateup_weight, gateup_first, gateup_second, [red_gateup]),
            (out_rate, out_weight, out_first, out_second, [red_out]),
            (LEARN, down_weight, down_first, down_second, [red_down]),
        ],
    )
    gains_new, gain_first_new, gain_second_new = adam(
        gains, gain_first, gain_second, gain_grad, factor, GAIN_LEARN, 0.0
    )
    return (
        result_rows.astype(jnp.bfloat16),
        input_grad,
        qkv_new,
        gateup_new,
        out_new,
        down_new,
        qkv_first_new,
        gateup_first_new,
        out_first_new,
        down_first_new,
        qkv_second_new,
        gateup_second_new,
        out_second_new,
        down_second_new,
        gains_new,
        gain_first_new,
        gain_second_new,
        grad_norm,
    )


def paired(mesh):
    return dict(mesh.shape) == {"dp": 8, "mp": 4}


def solution(mesh):
    placed = (
        P(("dp", "mp"), None),
        P(("dp", "mp"), None),
        P("dp", None),
        P(),
        P("dp", "mp"),
        P("dp", "mp"),
        P(("mp", "dp"), None),
        P(("mp", "dp"), None),
        P("dp", "mp"),
        P("dp", "mp"),
        P(("mp", "dp"), None),
        P(("mp", "dp"), None),
        P("dp", "mp"),
        P("dp", "mp"),
        P(("mp", "dp"), None),
        P(("mp", "dp"), None),
        P(),
        P(),
        P(),
    )
    return jax.shard_map(
        shards_paired if paired(mesh) else shards_general,
        mesh=mesh,
        in_specs=placed,
        out_specs=(
            P(("dp", "mp"), None),
            P(("dp", "mp"), None),
            P("dp", "mp"),
            P("dp", "mp"),
            P(("mp", "dp"), None),
            P(("mp", "dp"), None),
            P("dp", "mp"),
            P("dp", "mp"),
            P(("mp", "dp"), None),
            P(("mp", "dp"), None),
            P("dp", "mp"),
            P("dp", "mp"),
            P(("mp", "dp"), None),
            P(("mp", "dp"), None),
            P(),
            P(),
            P(),
            P(),
        ),
        check_vma=False,
    )
```

```python
import jax
import jax.numpy as jnp
from jax import lax
from jax.experimental import pallas as pl
from jax.experimental.pallas import tpu as pltpu
from jax.sharding import PartitionSpec as P

MODEL_WIDTH = 2048
QUERY_HEADS = 16
KEY_VALUE_HEADS = 8
HEAD_SIZE = 128
FF = 6144
STEP = 10


EPS_NORM = 1e-06
THETA = 1000000.0
LEARN = 0.03
GAIN_LEARN = 0.5
FIRST_DECAY = 0.9
SECOND_DECAY = 0.95
ADAM_EPS = 1e-08
WEIGHT_DECAY = 0.1
CLIP_LIMIT = 1.0
MASKED = -1e30


def rms_norm(value_rows, gain):
    return (
        value_rows
        * lax.rsqrt(jnp.mean(value_rows * value_rows, axis=-1, keepdims=True) + EPS_NORM)
        * gain
    )


def norm_back(value_rows, gain, grad):
    score_scale = lax.rsqrt(jnp.mean(value_rows * value_rows, axis=-1, keepdims=True) + EPS_NORM)
    normed_input = value_rows * score_scale
    d_normal = grad * gain
    d_values = score_scale * (
        d_normal - normed_input * jnp.mean(d_normal * normed_input, axis=-1, keepdims=True)
    )
    d_gain = jnp.sum((grad * normed_input).reshape(-1, value_rows.shape[-1]), axis=0)
    return (d_values, d_gain)


def turned(value_rows):
    half = value_rows.shape[-1] // 2
    return jnp.concatenate([-value_rows[..., half:], value_rows[..., :half]], axis=-1)


def rotate(value_rows, cosine, sine):
    return value_rows * cosine + turned(value_rows) * sine


def rotate_back(grad, cosine, sine):
    return grad * cosine - turned(grad * sine)


def rope_tables(lengths, count):
    ends = jnp.cumsum(lengths)
    starts = ends - lengths
    places = jnp.arange(count, dtype=jnp.int32)
    doc_of = jnp.sum((places[:, None] >= ends[None, :]).astype(jnp.int32), axis=1)
    chosen = doc_of[:, None] == jnp.arange(lengths.shape[0], dtype=jnp.int32)[None, :]
    begin = jnp.sum(jnp.where(chosen, starts[None, :], 0), axis=1)
    offset = (places - begin).astype(jnp.float32)
    half = HEAD_SIZE // 2
    freq = THETA ** (-(2.0 * jnp.arange(half, dtype=jnp.float32)) / HEAD_SIZE)
    angle = offset[:, None] * freq[None, :]
    angle = jnp.concatenate([angle, angle], axis=-1)
    return (doc_of, jnp.cos(angle), jnp.sin(angle))


def arrange(gathered, order, blocks_count):
    blocks = gathered.reshape(blocks_count, gathered.shape[0] // blocks_count, gathered.shape[1])
    return jnp.take(blocks, order, axis=0).reshape(gathered.shape)


def fetch_weights(
    projection_master_weight, gateup_weight, out_weight, down_weight, owner, blocks_count
):
    gathered = (
        lax.all_gather(projection_master_weight.astype(jnp.bfloat16), "dp", axis=0, tiled=True),
        lax.all_gather(gateup_weight.astype(jnp.bfloat16), "dp", axis=0, tiled=True),
        lax.all_gather(out_weight.astype(jnp.bfloat16), "dp", axis=0, tiled=True),
        lax.all_gather(down_weight.astype(jnp.bfloat16), "dp", axis=0, tiled=True),
    )
    return tuple((arrange(piece, owner, blocks_count) for piece in gathered))


def fetch_again(
    projection_master_weight, gateup_weight, out_weight, down_weight, owner, blocks_count
):
    gathered = (
        lax.all_gather(projection_master_weight.astype(jnp.bfloat16), "dp", axis=0, tiled=True),
        lax.all_gather(gateup_weight.astype(jnp.bfloat16), "dp", axis=0, tiled=True),
        lax.all_gather(out_weight.astype(jnp.bfloat16), "dp", axis=0, tiled=True),
        lax.all_gather(down_weight.astype(jnp.bfloat16), "dp", axis=0, tiled=True),
    )
    return tuple((arrange(piece, owner, blocks_count) for piece in gathered))


def collect(rows):
    return lax.all_gather(rows, "mp", axis=0, tiled=True)


def collect_back(rows):
    return lax.all_gather(rows, "mp", axis=0, tiled=True)


def spread(operand, weight, rows):

    def term(start, count):
        return jnp.dot(operand, weight, preferred_element_type=jnp.float32)

    return lax.psum_scatter(
        term(jnp.int32(0), rows * lax.axis_size("mp")).astype(jnp.bfloat16),
        "mp",
        scatter_dimension=0,
        tiled=True,
    ).astype(jnp.float32)


def spread_back(operand, weight, rows):

    def term(start, count):
        return jnp.einsum("tc,dc->td", operand, weight, preferred_element_type=jnp.float32)

    return lax.psum_scatter(
        term(jnp.int32(0), rows * lax.axis_size("mp")).astype(jnp.bfloat16),
        "mp",
        scatter_dimension=0,
        tiled=True,
    ).astype(jnp.float32)


def adam(weight, first, second, grad, factor, rate, decay):
    clipped = grad * factor
    first_new = FIRST_DECAY * first + (1.0 - FIRST_DECAY) * clipped
    second_new = SECOND_DECAY * second + (1.0 - SECOND_DECAY) * clipped * clipped
    first_hat = first_new / (1.0 - FIRST_DECAY**STEP)
    second_hat = second_new / (1.0 - SECOND_DECAY**STEP)
    weight_new = weight * (1.0 - rate * decay) - rate * first_hat / (
        jnp.sqrt(second_hat) + ADAM_EPS
    )
    return (weight_new, first_new, second_new)


def shards_general(
    hidden_in,
    cotangent,
    doc_lengths,
    owner,
    projection_master_weight,
    gateup_weight,
    out_weight,
    down_weight,
    projection_first_moment,
    gateup_first,
    out_first,
    down_first,
    projection_second_moment,
    gateup_second,
    out_second,
    down_second,
    gains,
    gain_first,
    gain_second,
):
    total_width = lax.axis_size("mp")
    blocks_count = lax.axis_size("dp")
    heads = QUERY_HEADS // total_width
    key_value_heads = KEY_VALUE_HEADS // total_width
    query_group = heads // key_value_heads
    query_width = heads * HEAD_SIZE
    key_width = key_value_heads * HEAD_SIZE
    units = FF // total_width
    rows_here = hidden_in.shape[0]
    inverse = jnp.argsort(owner)
    out_rate = float(QUERY_HEADS * HEAD_SIZE // 32) ** (-0.5)
    w_qkv, w_gateup, w_out, w_down = fetch_weights(
        projection_master_weight, gateup_weight, out_weight, down_weight, owner, blocks_count
    )
    ln_in = gains[:MODEL_WIDTH]
    ln_mid = gains[MODEL_WIDTH : 2 * MODEL_WIDTH]
    q_gain = gains[2 * MODEL_WIDTH : 2 * MODEL_WIDTH + HEAD_SIZE]
    k_gain = gains[2 * MODEL_WIDTH + HEAD_SIZE :]
    x_rows = hidden_in.astype(jnp.float32)
    full_in = collect(rms_norm(x_rows, ln_in).astype(jnp.bfloat16))
    projected = jnp.dot(full_in, w_qkv, preferred_element_type=jnp.float32)
    count = projected.shape[0]
    doc_of, cosine, sine = rope_tables(doc_lengths[0], count)
    cosine = cosine[:, None, :]
    sine = sine[:, None, :]
    query_raw = projected[:, :query_width].reshape(count, heads, HEAD_SIZE)
    unrotated_key = projected[:, query_width : query_width + key_width].reshape(
        count, key_value_heads, HEAD_SIZE
    )
    projected_value = projected[:, query_width + key_width :].reshape(
        count, key_value_heads, HEAD_SIZE
    )
    query_rows = rotate(rms_norm(query_raw, q_gain), cosine, sine).astype(jnp.bfloat16)
    key_rows = rotate(rms_norm(unrotated_key, k_gain), cosine, sine).astype(jnp.bfloat16)
    value_rows = projected_value.astype(jnp.bfloat16)
    block = min(512, count)
    nblocks = count // block
    score_scale = HEAD_SIZE ** (-0.5)
    places = jnp.arange(count, dtype=jnp.int32)

    def scores_of(start):
        query_block = lax.dynamic_slice_in_dim(query_rows, start, block, 0).reshape(
            block, key_value_heads, query_group, HEAD_SIZE
        )
        raw = (
            jnp.einsum("tlwd,uld->lwtu", query_block, key_rows, preferred_element_type=jnp.float32)
            * score_scale
        )
        row_doc = lax.dynamic_slice_in_dim(doc_of, start, block, 0)
        row_place = start + jnp.arange(block, dtype=jnp.int32)
        allowed = (row_doc[:, None] == doc_of[None, :]) & (places[None, :] <= row_place[:, None])
        return (jnp.where(allowed[None, None], raw, MASKED), query_block)

    def forward_block(index):
        score_matrix, query_block = scores_of(index * block)
        top = jnp.max(score_matrix, axis=-1, keepdims=True)
        total = jnp.log(jnp.sum(jnp.exp(score_matrix - top), axis=-1, keepdims=True)) + top
        probabilities = jnp.exp(score_matrix - total).astype(jnp.bfloat16)
        attention_result = jnp.einsum(
            "cpyx,xca->ycpa", probabilities, value_rows, preferred_element_type=jnp.float32
        )
        return (attention_result.reshape(block, query_width), total)

    outs, totals = lax.map(forward_block, jnp.arange(nblocks, dtype=jnp.int32))
    attn_heads = outs.reshape(count, query_width).astype(jnp.bfloat16)
    attn_rows = spread(attn_heads, w_out, rows_here)
    mixed = x_rows + attn_rows
    full_mid = collect(rms_norm(mixed, ln_mid).astype(jnp.bfloat16))
    gateup = jnp.dot(full_mid, w_gateup, preferred_element_type=jnp.float32)
    gate = gateup[:, :units]
    upper = gateup[:, units:]
    sigma = jax.nn.sigmoid(gate)
    act = (gate * sigma * upper).astype(jnp.bfloat16)
    mlp_rows = spread(act, w_down, rows_here)
    result_rows = mixed + mlp_rows
    w_qkv, w_gateup, w_out, w_down = fetch_again(
        projection_master_weight, gateup_weight, out_weight, down_weight, owner, blocks_count
    )
    grad_out = cotangent.astype(jnp.float32)
    d_branch = collect_back(grad_out.astype(jnp.bfloat16))
    g_down = jnp.einsum("tf,td->fd", act, d_branch, preferred_element_type=jnp.float32)
    d_act = jnp.einsum("td,fd->tf", d_branch, w_down, preferred_element_type=jnp.float32)
    d_upper = d_act * gate * sigma
    d_gate = d_act * upper * sigma * (1.0 + gate * (1.0 - sigma))
    d_gateup = jnp.concatenate([d_gate, d_upper], axis=1).astype(jnp.bfloat16)
    g_gateup = jnp.einsum("td,tf->df", full_mid, d_gateup, preferred_element_type=jnp.float32)
    d_mid_rows = spread_back(d_gateup, w_gateup, rows_here)
    d_mixed, g_ln_mid = norm_back(mixed, ln_mid, d_mid_rows)
    d_mixed = d_mixed + grad_out
    d_attn = collect_back(d_mixed.astype(jnp.bfloat16))
    g_out = jnp.einsum("th,td->hd", attn_heads, d_attn, preferred_element_type=jnp.float32)
    d_heads = jnp.einsum("td,hd->th", d_attn, w_out, preferred_element_type=jnp.float32).astype(
        jnp.bfloat16
    )
    d_heads = d_heads.reshape(count, key_value_heads, query_group, HEAD_SIZE)

    def backward_block(carry, index):
        d_key_sum, d_value_sum = carry
        start = index * block
        score_matrix, query_block = scores_of(start)
        probabilities = jnp.exp(score_matrix - totals[index])
        block_gradient = lax.dynamic_slice_in_dim(d_heads, start, block, 0)
        probability_gradient = jnp.einsum(
            "tlwd,uld->lwtu", block_gradient, value_rows, preferred_element_type=jnp.float32
        )
        d_value_sum = d_value_sum + jnp.einsum(
            "zxrb,rzxd->bzd",
            probabilities.astype(jnp.bfloat16),
            block_gradient,
            preferred_element_type=jnp.float32,
        )
        score_gradient = (
            probabilities
            * (
                probability_gradient
                - jnp.sum(probabilities * probability_gradient, axis=-1, keepdims=True)
            )
        ).astype(jnp.bfloat16)
        d_query = (
            jnp.einsum(
                "cpyx,xca->ycpa", score_gradient, key_rows, preferred_element_type=jnp.float32
            )
            * score_scale
        )
        d_key_sum = (
            d_key_sum
            + jnp.einsum(
                "zxrb,rzxd->bzd", score_gradient, query_block, preferred_element_type=jnp.float32
            )
            * score_scale
        )
        return ((d_key_sum, d_value_sum), d_query.reshape(block, heads, HEAD_SIZE))

    empty = jnp.zeros((count, key_value_heads, HEAD_SIZE), jnp.float32)
    (d_keys, d_values), d_queries = lax.scan(
        backward_block, (empty, empty), jnp.arange(nblocks, dtype=jnp.int32)
    )
    d_queries = d_queries.reshape(count, heads, HEAD_SIZE)
    d_query_raw, g_q = norm_back(query_raw, q_gain, rotate_back(d_queries, cosine, sine))
    d_key_raw, g_k = norm_back(unrotated_key, k_gain, rotate_back(d_keys, cosine, sine))
    d_projected = jnp.concatenate(
        [
            d_query_raw.reshape(count, query_width),
            d_key_raw.reshape(count, key_width),
            d_values.reshape(count, key_width),
        ],
        axis=1,
    ).astype(jnp.bfloat16)
    g_qkv = jnp.einsum("td,tc->dc", full_in, d_projected, preferred_element_type=jnp.float32)
    d_in_rows = spread_back(d_projected, w_qkv, rows_here)
    d_input, g_ln_in = norm_back(x_rows, ln_in, d_in_rows)
    input_grad = d_input + d_mixed
    gain_terms = jnp.concatenate([g_ln_in, g_ln_mid, g_q, g_k])
    red_qkv, red_gateup, red_out, red_down = (
        lax.psum_scatter(
            arrange(g_qkv, inverse, blocks_count).astype(jnp.bfloat16),
            "dp",
            scatter_dimension=0,
            tiled=True,
        ).astype(jnp.float32),
        lax.psum_scatter(
            arrange(g_gateup, inverse, blocks_count).astype(jnp.bfloat16),
            "dp",
            scatter_dimension=0,
            tiled=True,
        ).astype(jnp.float32),
        lax.psum_scatter(
            arrange(g_out, inverse, blocks_count).astype(jnp.bfloat16),
            "dp",
            scatter_dimension=0,
            tiled=True,
        ).astype(jnp.float32),
        lax.psum_scatter(
            arrange(g_down, inverse, blocks_count).astype(jnp.bfloat16),
            "dp",
            scatter_dimension=0,
            tiled=True,
        ).astype(jnp.float32),
    )
    squares = jnp.sum(red_qkv * red_qkv) + jnp.sum(red_gateup * red_gateup)
    squares = squares + jnp.sum(red_out * red_out) + jnp.sum(red_down * red_down)
    total_squares, gain_grad = lax.psum((squares, gain_terms), ("dp", "mp"))
    grad_norm = jnp.sqrt(total_squares + jnp.sum(gain_grad * gain_grad))
    factor = jnp.minimum(1.0, CLIP_LIMIT / (grad_norm + 1e-06))
    qkv_new, qkv_first_new, qkv_second_new = adam(
        projection_master_weight,
        projection_first_moment,
        projection_second_moment,
        red_qkv,
        factor,
        LEARN,
        WEIGHT_DECAY,
    )
    gateup_new, gateup_first_new, gateup_second_new = adam(
        gateup_weight, gateup_first, gateup_second, red_gateup, factor, LEARN, WEIGHT_DECAY
    )
    out_new, out_first_new, out_second_new = adam(
        out_weight, out_first, out_second, red_out, factor, out_rate, WEIGHT_DECAY
    )
    down_new, down_first_new, down_second_new = adam(
        down_weight, down_first, down_second, red_down, factor, LEARN, WEIGHT_DECAY
    )
    gains_new, gain_first_new, gain_second_new = adam(
        gains, gain_first, gain_second, gain_grad, factor, GAIN_LEARN, 0.0
    )
    return (
        result_rows.astype(jnp.bfloat16),
        input_grad,
        qkv_new,
        gateup_new,
        out_new,
        down_new,
        qkv_first_new,
        gateup_first_new,
        out_first_new,
        down_first_new,
        qkv_second_new,
        gateup_second_new,
        out_second_new,
        down_second_new,
        gains_new,
        gain_first_new,
        gain_second_new,
        grad_norm,
    )


def steps(move):
    pairs = []
    for index in range(32):
        y, x, c, zh, zl = (index >> 4) & 1, (index >> 3) & 1, (index >> 2) & 1, (index >> 1) & 1, index & 1
        source = move(y, x, c, zh, zl)
        if source is not None:
            sy, sx, sc, sh, sl = source
            pairs.append(((sy << 4) | (sx << 3) | (sc << 2) | (sh << 1) | sl, index))
    return pairs


OVER_X = steps(lambda y, x, c, h, l: (y, 1 - x, c, h, l))
OVER_Y = steps(lambda y, x, c, h, l: (1 - y, x, c, h, l))
OVER_C = steps(lambda y, x, c, h, l: (y, x, 1 - c, h, l))
OVER_L = steps(lambda y, x, c, h, l: (y, x, c, h, 1 - l))
TO_GROUP = (
    steps(lambda y, x, c, h, l: (y, x, h, c, l)),
    steps(lambda y, x, c, h, l: (y, x, 1 - h, c, l)),
)
FROM_GROUP = tuple([(b, a) for a, b in pairs] for pairs in TO_GROUP)
UPWARD = steps(lambda y, x, c, h, l: (y, x, c, 0, l) if h == 1 else None)
DOWNWARD = steps(lambda y, x, c, h, l: (y, x, c, 1, l) if h == 0 else None)


def move(value, pairs):
    return lax.ppermute(value, ("dp", "mp"), pairs)


def after(value, *others):
    return lax.optimization_barrier((value, *others))[0]


PLANES = [[(block * 2 + c) * 4 + z for block in range(4)] for c in range(2) for z in range(4)]


MESH = pl.DeviceIdType.MESH


class Place:
    def __init__(self):
        dp, mp = lax.axis_index("dp"), lax.axis_index("mp")
        self.y, self.x, self.c = dp // 4, (dp // 2) % 2, dp % 2
        self.h, self.l = mp // 2, mp % 2
        self.block = (dp // 2) * 2

    def at(self, y=None, x=None, c=None, h=None, l=None):
        y, x, c = (o if n is None else n for o, n in ((self.y, y), (self.x, x), (self.c, c)))
        h, l = (o if n is None else n for o, n in ((self.h, h), (self.l, l)))
        return ((y * 2 + x) * 2 + c, h * 2 + l)

    def partners(self):
        return [
            self.at(x=1 - self.x),
            self.at(y=1 - self.y),
            self.at(l=1 - self.l),
            self.at(c=1 - self.c),
            self.at(h=1 - self.h),
            self.at(c=1 - self.c, h=1 - self.h),
        ]


def far_copy(source, target, sems, index, device):
    return pltpu.make_async_remote_copy(
        src_ref=source,
        dst_ref=target,
        send_sem=sems[0].at[index],
        recv_sem=sems[1].at[index],
        device_id=device,
        device_id_type=MESH,
    )


class Swap:
    def __init__(self, place, source, target, sems, index, local_sem):
        self.same = place.c == place.h
        self.far = far_copy(source, target, sems, index, place.at(c=place.h, h=place.c))
        self.near = pltpu.make_async_copy(source, target, local_sem)

    def start(self):
        pl.when(self.same)(self.near.start)
        pl.when(~self.same)(self.far.start)

    def wait_recv(self):
        pl.when(self.same)(self.near.wait)
        pl.when(~self.same)(self.far.wait_recv)

    def wait_send(self):
        pl.when(~self.same)(self.far.wait_send)


class Task:
    copies = 1
    locals = 1
    work = ()

    def __init__(self, *inputs, phase=0):
        self.inputs, self.phase = inputs, phase

    def scratch(self):
        return [
            pltpu.SemaphoreType.DMA((self.copies,)),
            pltpu.SemaphoreType.DMA((self.copies,)),
            pltpu.SemaphoreType.DMA((self.locals,)),
            *self.work,
        ]


class Rows(Task):
    copies = 3

    def outs(self):
        rows = self.inputs[0]
        return [jax.ShapeDtypeStruct((4, *rows.shape), rows.dtype)]

    def steps(self, place, ins, outs, scratch):
        own, full = ins[0], outs[0]
        send, recv, local = scratch[:3]
        keep = pltpu.make_async_copy(own, full.at[0], local.at[0])
        over_z = far_copy(own, full.at[1], (send, recv), 0, place.at(l=1 - place.l))
        over_c = far_copy(own, full.at[2], (send, recv), 1, place.at(c=1 - place.c))
        relay = far_copy(full.at[1], full.at[3], (send, recv), 2, place.at(c=1 - place.c))

        def first():
            over_z.start()
            over_c.start()
            keep.start()

        def second():
            over_z.wait_recv()
            relay.start()

        def last():
            keep.wait()
            over_c.wait()
            over_z.wait_send()
            relay.wait()

        return [first, None, second, last]


class Cores(Task):
    copies = 2
    locals = 2

    def outs(self):
        rows = self.inputs[0]
        return [jax.ShapeDtypeStruct((4, *rows.shape), rows.dtype)]

    def steps(self, place, ins, outs, scratch):
        send, recv, local = scratch[:3]
        full = outs[0]
        core = place.at(c=1 - place.c)
        keeps = [pltpu.make_async_copy(ins[n], full.at[n], local.at[n]) for n in range(2)]
        fars = [far_copy(ins[n], full.at[2 + n], (send, recv), n, core) for n in range(2)]

        def first():
            for copy in (*fars, *keeps):
                copy.start()

        def last():
            for copy in (*keeps, *fars):
                copy.wait()

        return [first, None, None, last]


class Sums(Task):
    copies = 3

    def __init__(self, *inputs, phase=0):
        super().__init__(*inputs, phase=phase)
        block = inputs[0].shape[1:]
        self.work = tuple(pltpu.VMEM(block, jnp.bfloat16) for _ in range(3))

    def outs(self):
        block = jax.ShapeDtypeStruct(self.inputs[0].shape[1:], jnp.bfloat16)
        return [block, block]

    def steps(self, place, ins, outs, scratch):
        partial, (from_c, from_z) = ins[0], outs
        send, recv, local, mine, theirs, total = scratch
        core = place.at(c=1 - place.c)
        load = pltpu.make_async_copy(partial.at[1], mine, local.at[0])
        far = far_copy(partial.at[3], theirs, (send, recv), 0, core)
        near = far_copy(partial.at[2], from_c, (send, recv), 1, core)
        over_z = far_copy(total, from_z, (send, recv), 2, place.at(l=1 - place.l))
        rows = 32

        def first():
            far.start()
            near.start()
            load.start()

        def second():
            load.wait()
            far.wait_recv()

            @pl.loop(0, mine.shape[0] // rows)
            def _(index):
                part = pl.ds(pl.multiple_of(index * rows, rows), rows)
                summed = mine[part, :].astype(jnp.float32) + theirs[part, :].astype(jnp.float32)
                total[part, :] = summed.astype(jnp.bfloat16)

            over_z.start()

        def last():
            far.wait_send()
            near.wait()
            over_z.wait()

        return [first, second, None, last]


class Near(Task):
    copies = 2

    def outs(self):
        shard = self.inputs[0]
        return [jax.ShapeDtypeStruct((2, *shard.shape), shard.dtype)]

    def copies_of(self, place, shard, first, second, scratch):
        send, recv, local = scratch[:3]
        return (
            Swap(place, shard, first, (send, recv), 0, local.at[0]),
            far_copy(shard, second, (send, recv), 1, place.at(c=place.h, h=1 - place.c)),
        )

    def steps(self, place, ins, outs, scratch):
        a, b = self.copies_of(place, ins[0], outs[0].at[0], outs[0].at[1], scratch)

        def first():
            a.start()
            b.start()

        def last():
            a.wait_recv()
            a.wait_send()
            b.wait()

        return [first, None, None, last]


class Planes(Near):
    copies = 8

    def outs(self):
        shard = self.inputs[0]
        return [jax.ShapeDtypeStruct((8, *shard.shape), shard.dtype)]

    def steps(self, place, ins, outs, scratch):
        full = outs[0]
        block = place.block
        a, b = self.copies_of(place, ins[0], full.at[block], full.at[block + 1], scratch)
        over_x, over_y = place.at(x=1 - place.x), place.at(y=1 - place.y)
        x_block = block + 2 - 4 * place.x
        y_block = block + 4 - 8 * place.y

        def pass_on(slot, index, device):
            return far_copy(full.at[slot], full.at[slot], scratch[:2], index, device)

        ax, ay = pass_on(block, 2, over_x), pass_on(block, 3, over_y)
        by, bx = pass_on(block + 1, 4, over_y), pass_on(block + 1, 5, over_x)
        axy = pass_on(x_block, 6, over_y)
        byx = pass_on(y_block + 1, 7, over_x)

        def first():
            a.start()
            b.start()

        def second():
            a.wait_recv()
            ax.start()
            b.wait_recv()
            by.start()
            ay.start()
            bx.start()

        def third():
            ax.wait_recv()
            axy.start()
            by.wait_recv()
            byx.start()

        def last():
            a.wait_send()
            b.wait_send()
            for copy in (ax, by):
                copy.wait_send()
            for copy in (ay, bx, axy, byx):
                copy.wait()

        return [first, second, third, last]


class Owners(Task):
    copies = 2

    def outs(self):
        near = self.inputs[0]
        return [jax.ShapeDtypeStruct(near.shape, near.dtype)]

    def steps(self, place, ins, outs, scratch):
        send, recv, local = scratch[:3]
        near, got = ins[0], outs[0]
        a = Swap(place, near.at[0], got.at[0], (send, recv), 0, local.at[0])
        b = far_copy(near.at[1], got.at[1], (send, recv), 1, place.at(c=1 - place.h, h=place.c))

        def first():
            a.start()
            b.start()

        def last():
            a.wait_recv()
            a.wait_send()
            b.wait()

        return [first, None, None, last]


class Halves(Task):
    def __init__(self, array, sender, phase=0):
        super().__init__(array, phase=phase)
        self.sender = sender

    def outs(self):
        return [jax.ShapeDtypeStruct(self.inputs[0].shape, self.inputs[0].dtype)]

    def steps(self, place, ins, outs, scratch):
        copy = far_copy(ins[0], outs[0], scratch[:2], 0, place.at(h=1 - place.h))
        sends = place.h == self.sender

        def first():
            pl.when(sends)(copy.start)

        def last():
            pl.when(sends)(copy.wait_send)
            pl.when(~sends)(copy.wait_recv)

        return [first, None, None, last]


def transfer(name, number, micros, *tasks, scoped=12):
    outs = [task.outs() for task in tasks]
    scratch = [task.scratch() for task in tasks]

    def kernel(*refs):
        refs = list(refs)

        def take(count):
            taken = refs[:count]
            del refs[:count]
            return taken

        ins_of = [take(len(task.inputs)) for task in tasks]
        outs_of = [take(len(out)) for out in outs]
        scratch_of = [take(len(one)) for one in scratch]
        place = Place()
        barrier = pltpu.get_barrier_semaphore()
        partners = place.partners()
        for partner in partners:
            pl.semaphore_signal(barrier, inc=1, device_id=partner, device_id_type=MESH)
        pl.semaphore_wait(barrier, len(partners))
        plans = [
            task.steps(place, ins_of[n], outs_of[n], scratch_of[n]) for n, task in enumerate(tasks)
        ]
        for phase in range(4):
            for task, plan in zip(tasks, plans):
                steps_now = [plan[phase]] if phase else []
                if phase == task.phase:
                    steps_now.insert(0, plan[0])
                for step in steps_now:
                    if step is not None:
                        step()

    results = pl.pallas_call(
        kernel,
        out_shape=[leaf for out in outs for leaf in out],
        in_specs=[pl.BlockSpec(memory_space=pl.ANY) for task in tasks for _ in task.inputs],
        out_specs=[pl.BlockSpec(memory_space=pl.ANY) for out in outs for _ in out],
        scratch_shapes=[one for part in scratch for one in part],
        compiler_params=pltpu.CompilerParams(
            collective_id=number, has_side_effects=True, vmem_limit_bytes=scoped * 2**20
        ),
        cost_estimate=pl.CostEstimate(
            flops=0, bytes_accessed=micros * 3_300_000, transcendentals=0
        ),
        name=name,
    )(*[leaf for task in tasks for leaf in task.inputs])
    results = list(results)
    grouped = []
    for out in outs:
        grouped.append(results[: len(out)])
        del results[: len(out)]
    return grouped


def to_group(shard):
    return jnp.stack([move(shard, TO_GROUP[0]), move(shard, TO_GROUP[1])])


def to_owner(near):
    return [move(near[0], FROM_GROUP[0]), move(near[1], FROM_GROUP[1])]


def over_plane(near):
    return lax.all_gather(near, ("dp", "mp"), axis=0, tiled=True, axis_index_groups=PLANES)


def to_plane(grads):
    return lax.psum_scatter(
        grads, ("dp", "mp"), scatter_dimension=0, tiled=True, axis_index_groups=PLANES
    )


def both(pair):
    return pair[0].astype(jnp.float32) + pair[1].astype(jnp.float32)


def summed(partial, received):
    return both(received) + partial[0].astype(jnp.float32)


def sum_all_kernel(value, total, by_mp, by_dp, send_sem, recv_sem):
    dp, mp = lax.axis_index("dp"), lax.axis_index("mp")
    over_mp = [(dp, (mp + step) % 4) for step in range(1, 4)]
    over_dp = [((dp + step) % 8, mp) for step in range(1, 8)]
    barrier = pltpu.get_barrier_semaphore()
    for partner in over_mp + over_dp:
        pl.semaphore_signal(
            barrier, inc=1, device_id=partner, device_id_type=pl.DeviceIdType.MESH
        )
    pl.semaphore_wait(barrier, len(over_mp) + len(over_dp))

    def share(table, place, partners, first):
        copies = [
            pltpu.make_async_remote_copy(
                src_ref=table.at[place],
                dst_ref=table.at[place],
                send_sem=send_sem.at[first + step],
                recv_sem=recv_sem.at[first + step],
                device_id=partner,
                device_id_type=pl.DeviceIdType.MESH,
            )
            for step, partner in enumerate(partners)
        ]
        for copy in copies:
            copy.start()
        for copy in copies:
            copy.wait()

    by_mp[mp] = value[...]
    share(by_mp, mp, over_mp, 0)
    by_dp[dp] = (by_mp[0] + by_mp[1]) + (by_mp[2] + by_mp[3])
    share(by_dp, dp, over_dp, 3)
    result = by_dp[0]
    for place in range(1, 8):
        result = result + by_dp[place]
    total[...] = result


def sum_all(vector):
    size = vector.shape[0]
    rows = -(-size // 1024) * 8
    block = jnp.pad(vector, (0, rows * 128 - size)).reshape(rows, 128)
    total = pl.pallas_call(
        sum_all_kernel,
        out_shape=jax.ShapeDtypeStruct((rows, 128), jnp.float32),
        in_specs=[pl.BlockSpec(memory_space=pltpu.VMEM)],
        out_specs=pl.BlockSpec(memory_space=pltpu.VMEM),
        scratch_shapes=[
            pltpu.VMEM((4, rows, 128), jnp.float32),
            pltpu.VMEM((8, rows, 128), jnp.float32),
            pltpu.SemaphoreType.DMA((10,)),
            pltpu.SemaphoreType.DMA((10,)),
        ],
        compiler_params=pltpu.CompilerParams(collective_id=0, has_side_effects=True),
        name="sum_all",
    )(block)
    return total.reshape(-1)[:size]


def column_places(index, high, low, rows):
    chunk = index // rows
    return high * 2 * rows + (low + chunk - 2 * low * chunk) * rows + index - chunk * rows


def project_kernel(rows_ref, weight_ref, cos_ref, sin_ref, gain_ref, raw_ref, query_ref, kv_ref):
    width = rows_ref.shape[1]
    weight = weight_ref[...].reshape(width, weight_ref.shape[2])
    projected = jnp.dot(rows_ref[...], weight, preferred_element_type=jnp.float32)
    query_width, key_width = query_ref.shape[1], kv_ref.shape[1] // 2
    turned_width = query_width + key_width
    raw_ref[...] = projected[:, :turned_width]
    cosine, sine = cos_ref[...], sin_ref[...]
    for start in range(0, turned_width, HEAD_SIZE):
        raw = projected[:, start : start + HEAD_SIZE]
        gain = gain_ref[0:1, :] if start < query_width else gain_ref[1:2, :]
        normed = raw * lax.rsqrt(jnp.mean(raw * raw, axis=1, keepdims=True) + EPS_NORM) * gain
        turned = normed * cosine + pltpu.roll(normed, HEAD_SIZE // 2, 1) * sine
        if start < query_width:
            query_ref[:, start : start + HEAD_SIZE] = turned.astype(jnp.bfloat16)
        else:
            place = start - query_width
            kv_ref[:, place : place + HEAD_SIZE] = turned.astype(jnp.bfloat16)
    kv_ref[:, key_width:] = projected[:, turned_width:].astype(jnp.bfloat16)


def project(rows, blocks, cosine, sine, head_gains, query_width, key_width):
    count, width = rows.shape
    tile = 256
    total = query_width + 2 * key_width
    by_rows = lambda columns: pl.BlockSpec((tile, columns), lambda i: (i, 0))
    return pl.pallas_call(
        project_kernel,
        grid=(count // tile,),
        in_specs=[
            by_rows(width),
            pl.BlockSpec((8, width // 8, total), lambda i: (0, 0, 0)),
            by_rows(HEAD_SIZE),
            by_rows(HEAD_SIZE),
            pl.BlockSpec((2, HEAD_SIZE), lambda i: (0, 0)),
        ],
        out_specs=[by_rows(query_width + key_width), by_rows(query_width), by_rows(2 * key_width)],
        out_shape=[
            jax.ShapeDtypeStruct((count, query_width + key_width), jnp.float32),
            jax.ShapeDtypeStruct((count, query_width), jnp.bfloat16),
            jax.ShapeDtypeStruct((count, 2 * key_width), jnp.bfloat16),
        ],
        compiler_params=pltpu.CompilerParams(vmem_limit_bytes=48 * 2**20),
        cost_estimate=pl.CostEstimate(
            flops=2 * count * width * total, bytes_accessed=16 * 2**20, transcendentals=0
        ),
        name="project",
    )(rows, blocks, cosine, sine, head_gains)


def unproject_kernel(
    place_ref, dq_ref, own_ref, above_ref, raw_ref, cos_ref, sin_ref, gain_ref, out_ref, gq_ref, gk_ref
):
    query_width, key_width = dq_ref.shape[1], own_ref.shape[1] // 2
    turned_width = query_width + key_width
    lower = place_ref[0] == 0
    cosine, sine = cos_ref[...], sin_ref[...]

    @pl.when(pl.program_id(0) == 0)
    def _():
        gq_ref[...] = jnp.zeros_like(gq_ref)
        gk_ref[...] = jnp.zeros_like(gk_ref)

    def with_above(columns):
        above = jnp.where(lower, above_ref[:, columns].astype(jnp.float32), 0.0)
        return own_ref[:, columns] + above

    for start in range(0, turned_width, HEAD_SIZE):
        columns = slice(start, start + HEAD_SIZE)
        if start < query_width:
            grad, gain, gain_sum = dq_ref[:, columns], gain_ref[0:1, :], gq_ref
        else:
            grad = with_above(slice(start - query_width, start - query_width + HEAD_SIZE))
            gain, gain_sum = gain_ref[1:2, :], gk_ref
        grad = grad * cosine - pltpu.roll(grad, HEAD_SIZE // 2, 1) * sine
        raw = raw_ref[:, columns]
        scale = lax.rsqrt(jnp.mean(raw * raw, axis=1, keepdims=True) + EPS_NORM)
        normed = raw * scale
        gain_sum[...] += jnp.sum((grad * normed).reshape(-1, 8, HEAD_SIZE), axis=0)
        d_normal = grad * gain
        value = scale * (d_normal - normed * jnp.mean(d_normal * normed, axis=1, keepdims=True))
        out_ref[:, columns] = value.astype(jnp.bfloat16)
    out_ref[:, turned_width:] = with_above(slice(key_width, 2 * key_width)).astype(jnp.bfloat16)


def unproject(place, d_queries, d_own, above, raw, cosine, sine, head_gains):
    count, query_width = d_queries.shape
    key_width = d_own.shape[1] // 2
    tile = 256
    total = query_width + 2 * key_width
    by_rows = lambda columns: pl.BlockSpec((tile, columns), lambda i, p: (i, 0))
    fixed = lambda rows: pl.BlockSpec((rows, HEAD_SIZE), lambda i, p: (0, 0))
    return pl.pallas_call(
        unproject_kernel,
        grid_spec=pltpu.PrefetchScalarGridSpec(
            num_scalar_prefetch=1,
            grid=(count // tile,),
            in_specs=[
                by_rows(query_width),
                by_rows(2 * key_width),
                by_rows(2 * key_width),
                by_rows(query_width + key_width),
                by_rows(HEAD_SIZE),
                by_rows(HEAD_SIZE),
                fixed(2),
            ],
            out_specs=[by_rows(total), fixed(8), fixed(8)],
        ),
        out_shape=[
            jax.ShapeDtypeStruct((count, total), jnp.bfloat16),
            jax.ShapeDtypeStruct((8, HEAD_SIZE), jnp.float32),
            jax.ShapeDtypeStruct((8, HEAD_SIZE), jnp.float32),
        ],
        compiler_params=pltpu.CompilerParams(vmem_limit_bytes=32 * 2**20),
        cost_estimate=pl.CostEstimate(flops=0, bytes_accessed=2 * 2**20, transcendentals=0),
        name="unproject",
    )(place, d_queries, d_own, above, raw, cosine, sine, head_gains)


def dot_t(left, right):
    return lax.dot_general(
        left, right, (((1,), (1,)), ((), ())), preferred_element_type=jnp.float32
    )


def t_dot(left, right):
    return lax.dot_general(
        left, right, (((0,), (0,)), ((), ())), preferred_element_type=jnp.float32
    )


def exps_of(place_ref, time_ref, begin_ref, rows, query, key_low, key_own):
    high, low = place_ref[0], place_ref[1]
    keys = key_own.shape[0]
    scale = HEAD_SIZE ** (-0.5)
    column = lax.broadcasted_iota(jnp.int32, (rows.size, keys), 1)
    time, begin = time_ref[rows, :], begin_ref[rows, :]
    own_place = column_places(column, high, low, keys // 2)
    low_place = column_places(column, 0, low, keys // 2)
    own_seen = (own_place <= time) & (own_place >= begin)
    low_seen = (low_place >= begin) & (low_place < high * keys)
    own = jnp.where(own_seen, dot_t(query, key_own) * scale, MASKED)
    lower = jnp.where(low_seen, dot_t(query, key_low) * scale, MASKED)
    top = jnp.maximum(
        jnp.max(own, axis=1, keepdims=True), jnp.max(lower, axis=1, keepdims=True)
    )
    own, lower = jnp.exp(own - top), jnp.exp(lower - top)
    total = jnp.sum(own, axis=1, keepdims=True) + jnp.sum(lower, axis=1, keepdims=True)
    return lower, own, 1.0 / total


def attend_kernel(place_ref, time_ref, begin_ref, query_ref, low_ref, own_ref, out_ref):
    half, query_width = query_ref.shape
    key_width = own_ref.shape[1] // 2
    group = query_width // key_width
    size = half // 2
    upper = place_ref[0] == 1
    for kv in range(key_width // HEAD_SIZE):
        key_at = slice(kv * HEAD_SIZE, (kv + 1) * HEAD_SIZE)
        value_at = slice(key_width + kv * HEAD_SIZE, key_width + (kv + 1) * HEAD_SIZE)
        key_low, key_own, value_own = low_ref[:, key_at], own_ref[:, key_at], own_ref[:, value_at]
        value_low = jnp.where(upper, low_ref[:, value_at], jnp.zeros_like(value_own))
        for part in range(2):
            rows = pl.ds(part * size, size)
            for head in range(kv * group, (kv + 1) * group):
                query_at = slice(head * HEAD_SIZE, (head + 1) * HEAD_SIZE)
                lower, own, inverse = exps_of(
                    place_ref, time_ref, begin_ref, rows, query_ref[rows, query_at], key_low, key_own
                )
                result = jnp.dot(
                    lower.astype(jnp.bfloat16), value_low, preferred_element_type=jnp.float32
                ) + jnp.dot(own.astype(jnp.bfloat16), value_own, preferred_element_type=jnp.float32)
                out_ref[rows, query_at] = (result * inverse).astype(jnp.bfloat16)


def attend_back_kernel(
    place_ref, time_ref, begin_ref, query_ref, low_ref, own_ref, grad_ref, dq_ref, dlow_ref, down_ref
):
    half, query_width = query_ref.shape
    key_width = own_ref.shape[1] // 2
    group = query_width // key_width
    size = half // 2
    scale = HEAD_SIZE ** (-0.5)
    upper = place_ref[0] == 1
    for kv in range(key_width // HEAD_SIZE):
        key_at = slice(kv * HEAD_SIZE, (kv + 1) * HEAD_SIZE)
        value_at = slice(key_width + kv * HEAD_SIZE, key_width + (kv + 1) * HEAD_SIZE)
        key_own, value_own = own_ref[:, key_at], own_ref[:, value_at]
        key_low = jnp.where(upper, low_ref[:, key_at], jnp.zeros_like(key_own))
        value_low = jnp.where(upper, low_ref[:, value_at], jnp.zeros_like(value_own))
        dk_low = dk_own = dv_low = dv_own = None
        for part in range(2):
            rows = pl.ds(part * size, size)
            for head in range(kv * group, (kv + 1) * group):
                query_at = slice(head * HEAD_SIZE, (head + 1) * HEAD_SIZE)
                query, grad = query_ref[rows, query_at], grad_ref[rows, query_at]
                lower, own, inverse = exps_of(
                    place_ref, time_ref, begin_ref, rows, query, key_low, key_own
                )
                lower, own = lower * inverse, own * inverse
                g_low, g_own = dot_t(grad, value_low), dot_t(grad, value_own)
                mean = jnp.sum(lower * g_low, axis=1, keepdims=True) + jnp.sum(
                    own * g_own, axis=1, keepdims=True
                )
                s_low = (lower * (g_low - mean)).astype(jnp.bfloat16)
                s_own = (own * (g_own - mean)).astype(jnp.bfloat16)
                dq_ref[rows, query_at] = scale * (
                    jnp.dot(s_low, key_low, preferred_element_type=jnp.float32)
                    + jnp.dot(s_own, key_own, preferred_element_type=jnp.float32)
                )
                terms = (
                    t_dot(s_low, query),
                    t_dot(s_own, query),
                    t_dot(lower.astype(jnp.bfloat16), grad),
                    t_dot(own.astype(jnp.bfloat16), grad),
                )
                if dk_low is None:
                    dk_low, dk_own, dv_low, dv_own = terms
                else:
                    dk_low, dk_own = dk_low + terms[0], dk_own + terms[1]
                    dv_low, dv_own = dv_low + terms[2], dv_own + terms[3]
        dlow_ref[:, key_at] = (dk_low * scale).astype(jnp.bfloat16)
        dlow_ref[:, value_at] = dv_low.astype(jnp.bfloat16)
        down_ref[:, key_at] = dk_own * scale
        down_ref[:, value_at] = dv_own


def attention_call(kernel, name, place, arrays, outs, flops):
    count = arrays[0].shape[0]
    half = count // 2
    spec = lambda leaf: pl.BlockSpec((half, leaf.shape[1]), lambda i, p: (i, 0))
    return pl.pallas_call(
        kernel,
        grid_spec=pltpu.PrefetchScalarGridSpec(
            num_scalar_prefetch=1,
            grid=(2,),
            in_specs=[spec(leaf) for leaf in arrays],
            out_specs=[spec(leaf) for leaf in outs],
        ),
        out_shape=outs,
        compiler_params=pltpu.CompilerParams(vmem_limit_bytes=56 * 2**20),
        cost_estimate=pl.CostEstimate(flops=flops, bytes_accessed=16 * 2**20, transcendentals=0),
        name=name,
    )(place, *arrays)


def scaled(values):
    return values * lax.rsqrt(jnp.mean(values * values, axis=1, keepdims=True) + EPS_NORM)


def three(parts, columns=slice(None)):
    own, from_c, from_z = parts
    return (
        own[0, :, columns].astype(jnp.float32)
        + from_c[:, columns].astype(jnp.float32)
        + from_z[:, columns].astype(jnp.float32)
    )


def slot_columns(slot_ref, index, block):
    return pl.ds(pl.multiple_of(slot_ref[index] * block, block), block)


def store_slots(slot_ref, out_ref, values):
    block = out_ref.shape[1] // 8
    for index in range(8):
        out_ref[:, slot_columns(slot_ref, index, block)] = values[
            :, index * block : (index + 1) * block
        ]


def norm_kernel(slot_ref, x_ref, gain_ref, out_ref):
    x = x_ref[...].astype(jnp.float32)
    store_slots(slot_ref, out_ref, (scaled(x) * gain_ref[...]).astype(jnp.bfloat16))


def mix_kernel(slot_ref, x_ref, own_ref, c_ref, z_ref, gain_ref, mixed_ref, out_ref):
    mixed = x_ref[...].astype(jnp.float32) + three((own_ref, c_ref, z_ref))
    mixed_ref[...] = mixed
    store_slots(slot_ref, out_ref, (scaled(mixed) * gain_ref[...]).astype(jnp.bfloat16))


def norm_back_of(slot_ref, value_ref, parts, gain_ref, sum_ref, grad_ref):
    width = value_ref.shape[1]
    block = width // 8
    for index in range(8):
        grad_ref[:, index * block : (index + 1) * block] = three(
            parts, slot_columns(slot_ref, index, block)
        )
    value, grad = value_ref[...].astype(jnp.float32), grad_ref[...]
    scale = lax.rsqrt(jnp.mean(value * value, axis=1, keepdims=True) + EPS_NORM)
    normed = value * scale

    @pl.when(pl.program_id(0) == 0)
    def _():
        sum_ref[...] = jnp.zeros_like(sum_ref)

    sum_ref[...] += jnp.sum((grad * normed).reshape(-1, 8, width), axis=0)
    d_normal = grad * gain_ref[...]
    return scale * (d_normal - normed * jnp.mean(d_normal * normed, axis=1, keepdims=True))


def mix_back_kernel(
    slot_ref, mixed_ref, own_ref, c_ref, z_ref, gain_ref, cot_ref, d_ref, low_ref, sum_ref, grad_ref
):
    value = norm_back_of(slot_ref, mixed_ref, (own_ref, c_ref, z_ref), gain_ref, sum_ref, grad_ref)
    value = value + cot_ref[...].astype(jnp.float32)
    d_ref[...] = value
    low_ref[...] = value.astype(jnp.bfloat16)


def in_back_kernel(
    slot_ref, x_ref, own_ref, c_ref, z_ref, gain_ref, d_ref, out_ref, sum_ref, grad_ref
):
    value = norm_back_of(slot_ref, x_ref, (own_ref, c_ref, z_ref), gain_ref, sum_ref, grad_ref)
    out_ref[...] = value + d_ref[...]


def by_row_tiles(kernel, name, slot_of, inputs, outs, scratch=False, micros=3):
    rows, width = 128 if scratch else 64, inputs[0].shape[1]
    steps = inputs[0].shape[0] // rows

    def spec(leaf):
        if len(leaf.shape) == 3:
            return pl.BlockSpec((1, rows, width), lambda i, p: (0, i, 0))
        if leaf.shape[0] in (1, 8):
            return pl.BlockSpec(leaf.shape, lambda i, p: (0, 0))
        return pl.BlockSpec((rows, width), lambda i, p: (i, 0))

    return pl.pallas_call(
        kernel,
        grid_spec=pltpu.PrefetchScalarGridSpec(
            num_scalar_prefetch=1,
            grid=(steps,),
            in_specs=[spec(leaf) for leaf in inputs],
            out_specs=[spec(leaf) for leaf in outs],
            scratch_shapes=[pltpu.VMEM((rows, width), jnp.float32)] if scratch else [],
        ),
        out_shape=outs,
        compiler_params=pltpu.CompilerParams(vmem_limit_bytes=(60 if scratch else 24) * 2**20),
        cost_estimate=pl.CostEstimate(flops=0, bytes_accessed=micros * 3_300_000, transcendentals=0),
        name=name,
    )(slot_of, *inputs)


def mlp_front_kernel(rows_ref, gate_ref, up_ref, gate_out, up_out, act_out):
    width = rows_ref.shape[1]
    rows = rows_ref[...]
    gate = jnp.dot(rows, gate_ref[...].reshape(width, -1), preferred_element_type=jnp.float32)
    upper = jnp.dot(rows, up_ref[...].reshape(width, -1), preferred_element_type=jnp.float32)
    gate_out[...] = gate
    up_out[...] = upper
    act_out[...] = (gate * upper / (1.0 + jnp.exp(-gate))).astype(jnp.bfloat16)


def mlp_front(rows, gate_blocks, up_blocks):
    count, width = rows.shape
    units = gate_blocks.shape[2]
    columns = 256
    weight = pl.BlockSpec((8, width // 8, columns), lambda i: (0, 0, i))
    out = pl.BlockSpec((count, columns), lambda i: (0, i))
    return pl.pallas_call(
        mlp_front_kernel,
        grid=(units // columns,),
        in_specs=[pl.BlockSpec((count, width), lambda i: (0, 0)), weight, weight],
        out_specs=[out, out, out],
        out_shape=[
            jax.ShapeDtypeStruct((count, units), jnp.float32),
            jax.ShapeDtypeStruct((count, units), jnp.float32),
            jax.ShapeDtypeStruct((count, units), jnp.bfloat16),
        ],
        compiler_params=pltpu.CompilerParams(vmem_limit_bytes=60 * 2**20),
        cost_estimate=pl.CostEstimate(
            flops=4 * count * units * width, bytes_accessed=32 * 2**20, transcendentals=0
        ),
        name="mlp_front",
    )(rows, gate_blocks, up_blocks)


def mlp_back_kernel(
    slot_ref, dy_ref, gate_ref, up_ref, act_ref, down_ref, dgate_ref, dup_ref, branch_ref, weight_ref
):
    block = down_ref.shape[1]

    @pl.when(pl.program_id(0) == 0)
    def _():
        for index in range(8):
            weight_ref[index * block : (index + 1) * block, :] = down_ref[slot_ref[index]]

    units, step = gate_ref.shape[1], 512
    dy = dy_ref[...]
    total = None
    for start in range(0, units, step):
        columns = slice(start, start + step)
        weight = weight_ref[columns, :]
        gate, upper = gate_ref[:, columns], up_ref[:, columns]
        d_act = dot_t(dy, weight)
        sigma = 1.0 / (1.0 + jnp.exp(-gate))
        dup_ref[:, columns] = (d_act * gate * sigma).astype(jnp.bfloat16)
        d_gate = d_act * upper * sigma * (1.0 + gate * (1.0 - sigma))
        dgate_ref[:, columns] = d_gate.astype(jnp.bfloat16)
        term = jnp.dot(act_ref[:, columns], weight, preferred_element_type=jnp.float32)
        total = term if total is None else total + term
    branch_ref[0] = total.astype(jnp.bfloat16)


def mlp_back(slot_of, d_branch, gate, upper, act, down_blocks):
    count, units = gate.shape
    width = d_branch.shape[1]
    rows = 256
    by_rows = lambda columns: pl.BlockSpec((rows, columns), lambda i, p: (i, 0))
    wide = jax.ShapeDtypeStruct((count, units), jnp.bfloat16)
    return pl.pallas_call(
        mlp_back_kernel,
        grid_spec=pltpu.PrefetchScalarGridSpec(
            num_scalar_prefetch=1,
            grid=(count // rows,),
            in_specs=[
                by_rows(width),
                by_rows(units),
                by_rows(units),
                by_rows(units),
                pl.BlockSpec(down_blocks.shape, lambda i, p: (0, 0, 0)),
            ],
            out_specs=[by_rows(units)] * 2
            + [pl.BlockSpec((1, rows, width), lambda i, p: (i, 0, 0))],
            scratch_shapes=[pltpu.VMEM((units, width), jnp.bfloat16)],
        ),
        out_shape=[
            wide,
            wide,
            jax.ShapeDtypeStruct((count // rows, rows, width), jnp.bfloat16),
        ],
        compiler_params=pltpu.CompilerParams(vmem_limit_bytes=48 * 2**20),
        cost_estimate=pl.CostEstimate(
            flops=4 * count * units * width, bytes_accessed=32 * 2**20, transcendentals=0
        ),
        name="mlp_back",
    )(slot_of, d_branch, gate, upper, act, down_blocks)


def rows_back_kernel(*refs):
    *pairs, out_ref = refs
    total = None
    for grad_ref, weight_ref in zip(pairs[::2], pairs[1::2]):
        term = dot_t(grad_ref[...], weight_ref[0])
        total = term if total is None else total + term
    out_ref[...] = total.astype(jnp.bfloat16).reshape(out_ref.shape)


def rows_back(name, *pairs):
    count = pairs[0].shape[0]
    block = pairs[1].shape[1]
    specs = []
    for grad, weight in zip(pairs[::2], pairs[1::2]):
        specs.append(pl.BlockSpec(grad.shape, lambda i: (0, 0)))
        specs.append(pl.BlockSpec((1, *weight.shape[1:]), lambda i: (i, 0, 0)))
    return pl.pallas_call(
        rows_back_kernel,
        grid=(8,),
        in_specs=specs,
        out_specs=pl.BlockSpec((4, count // 4, block), lambda i: (0, 0, i)),
        out_shape=jax.ShapeDtypeStruct((4, count // 4, 8 * block), jnp.bfloat16),
        compiler_params=pltpu.CompilerParams(vmem_limit_bytes=28 * 2**20),
        cost_estimate=pl.CostEstimate(
            flops=sum(count * w.size for w in pairs[1::2]) // 4,
            bytes_accessed=2 * 2**20,
            transcendentals=0,
        ),
        name=name,
    )(*pairs)


def adam_kernel(factor_ref, *refs, rates):
    factor = factor_ref[0]
    ins, outs = refs[: len(refs) - 3 * len(rates)], refs[len(refs) - 3 * len(rates) :]
    at = 0
    for place, (rate, pieces) in enumerate(rates):
        weight_ref, first_ref, second_ref, *grads = ins[at : at + 3 + pieces]
        at += 3 + pieces
        start = 0
        for grad_ref in grads:
            columns = slice(start, start + grad_ref.shape[1])
            start += grad_ref.shape[1]
            results = adam(
                weight_ref[:, columns],
                first_ref[:, columns],
                second_ref[:, columns],
                grad_ref[...],
                factor,
                rate,
                WEIGHT_DECAY,
            )
            for out_ref, result in zip(outs[3 * place : 3 * place + 3], results):
                out_ref[:, columns] = result


def adam_all(factor, weights):
    steps = 8
    rates = tuple((rate, len(grads)) for rate, *_, grads in weights)
    arrays, outs = [], []
    for _, master, first, second, grads in weights:
        arrays += [master, first, second, *grads]
        outs += [jax.ShapeDtypeStruct(master.shape, jnp.float32)] * 3

    def spec(leaf):
        return pl.BlockSpec((leaf.shape[0] // steps, leaf.shape[1]), lambda i, p: (i, 0))

    results = pl.pallas_call(
        lambda *refs: adam_kernel(*refs, rates=rates),
        grid_spec=pltpu.PrefetchScalarGridSpec(
            num_scalar_prefetch=1,
            grid=(steps,),
            in_specs=[spec(leaf) for leaf in arrays],
            out_specs=[spec(leaf) for leaf in outs],
        ),
        out_shape=outs,
        compiler_params=pltpu.CompilerParams(vmem_limit_bytes=60 * 2**20),
        cost_estimate=pl.CostEstimate(flops=0, bytes_accessed=48 * 2**20, transcendentals=0),
        name="adam_all",
    )(factor[None], *arrays)
    return [results[n : n + 3] for n in range(0, len(results), 3)]


def slot_grad_kernel(slot_ref, left_ref, right_ref, out_ref):
    block = out_ref.shape[1]
    grad = t_dot(left_ref[...], right_ref[...]).astype(jnp.bfloat16)
    for index in range(8):
        out_ref[slot_ref[index]] = grad[index * block : (index + 1) * block, :]


def slot_grad(slot_of, left, right):
    count, rows = left.shape
    width = right.shape[1]
    columns = 512
    return pl.pallas_call(
        slot_grad_kernel,
        grid_spec=pltpu.PrefetchScalarGridSpec(
            num_scalar_prefetch=1,
            grid=(width // columns,),
            in_specs=[
                pl.BlockSpec((count, rows), lambda i, p: (0, 0)),
                pl.BlockSpec((count, columns), lambda i, p: (0, i)),
            ],
            out_specs=pl.BlockSpec((8, rows // 8, columns), lambda i, p: (0, 0, i)),
        ),
        out_shape=jax.ShapeDtypeStruct((8, rows // 8, width), jnp.bfloat16),
        compiler_params=pltpu.CompilerParams(vmem_limit_bytes=48 * 2**20),
        cost_estimate=pl.CostEstimate(
            flops=2 * count * rows * width, bytes_accessed=16 * 2**20, transcendentals=0
        ),
        name="slot_grad",
    )(slot_of, left, right)


class Grads(Task):
    def outs(self):
        rows, left, right = self.inputs
        columns = left.shape[1] + right.shape[1]
        return [jax.ShapeDtypeStruct((8, rows.shape[1] // 8, columns), jnp.bfloat16)]

    def scratch(self):
        return []

    def steps(self, place, ins, outs, scratch):
        count, width = self.inputs[0].shape
        block = width // 8
        columns = self.inputs[1].shape[1]

        def body(rows_ref, left_ref, right_ref, out_ref):
            rows = rows_ref[...]
            out_ref[0, :, :columns] = t_dot(rows, left_ref[...]).astype(jnp.bfloat16)
            out_ref[0, :, columns:] = t_dot(rows, right_ref[...]).astype(jnp.bfloat16)

        def whole(one):
            return pl.BlockSpec((count, one.shape[1]), lambda i: (0, 0))

        run = pltpu.emit_pipeline(
            body,
            grid=(8,),
            in_specs=[
                pl.BlockSpec((count, block), lambda i: (0, i)),
                whole(self.inputs[1]),
                whole(self.inputs[2]),
            ],
            out_specs=[pl.BlockSpec((1, block, 2 * columns), lambda i: (i, 0, 0))],
        )
        return [lambda: None, None, lambda: run(*ins, *outs), None]


def shards_paired(
    hidden_in,
    cotangent,
    doc_lengths,
    owner,
    projection_master_weight,
    gateup_weight,
    out_weight,
    down_weight,
    projection_first_moment,
    gateup_first,
    out_first,
    down_first,
    projection_second_moment,
    gateup_second,
    out_second,
    down_second,
    gains,
    gain_first,
    gain_second,
):
    high, low = lax.axis_index("mp") // 2, lax.axis_index("mp") % 2
    plane = high
    groups = lax.axis_size("mp")
    query_width = QUERY_HEADS // groups * HEAD_SIZE
    key_width = KEY_VALUE_HEADS // groups * HEAD_SIZE
    units = FF // groups
    rows_here = hidden_in.shape[0]
    count = 4 * rows_here
    half = count // 2
    width = hidden_in.shape[1]
    slot_of = (owner ^ plane).astype(jnp.int32)
    out_rate = float(QUERY_HEADS * HEAD_SIZE // 32) ** (-0.5)

    ln_in = gains[:MODEL_WIDTH]
    ln_mid = gains[MODEL_WIDTH : 2 * MODEL_WIDTH]
    q_gain = gains[2 * MODEL_WIDTH : 2 * MODEL_WIDTH + HEAD_SIZE]
    k_gain = gains[2 * MODEL_WIDTH + HEAD_SIZE :]
    low_gateup = gateup_weight.astype(jnp.bfloat16)
    own_in = by_row_tiles(
        norm_kernel,
        "norm_in",
        slot_of,
        [hidden_in, ln_in[None]],
        [jax.ShapeDtypeStruct(hidden_in.shape, jnp.bfloat16)],
    )
    (qkv_blocks,), (out_blocks,), (full_in,), (near_gate,) = transfer(
        "gather_first",
        1,
        75,
        Planes(projection_master_weight.astype(jnp.bfloat16)),
        Planes(out_weight.astype(jnp.bfloat16)),
        Rows(own_in[0]),
        Near(low_gateup[:, :units], phase=1),
    )
    full_in = full_in.reshape(count, width)
    w_out = jnp.take(out_blocks, slot_of, axis=0, mode="clip").reshape(-1, width)
    gate_blocks = over_plane(near_gate)
    near_up = to_group(after(low_gateup[:, units:], full_in))

    lengths = jnp.concatenate([doc_lengths, move(doc_lengths, OVER_C)], axis=0)
    ends = jnp.cumsum(lengths, axis=1)
    spot = jnp.arange(half, dtype=jnp.int32)
    chunk = spot // rows_here
    own_places = high * half + (low ^ chunk) * rows_here + spot % rows_here
    later = own_places[None, :, None] >= ends[:, None, :]
    begin = jnp.max(jnp.where(later, ends[:, None, :], 0), axis=2).reshape(count, 1)
    time = jnp.concatenate([own_places, own_places]).reshape(count, 1)
    freq = THETA ** (-(2.0 * jnp.arange(HEAD_SIZE // 2, dtype=jnp.float32)) / HEAD_SIZE)
    angle = (time - begin).astype(jnp.float32) * freq[None, :]
    cosine, sine = jnp.cos(angle), jnp.sin(angle)
    cosine = jnp.concatenate([cosine, cosine], axis=-1)
    sine = jnp.concatenate([-sine, sine], axis=-1)
    head_gains = jnp.stack([q_gain, k_gain])
    place = jnp.stack([high, low]).astype(jnp.int32)

    raw, queries, own_kv = project(
        full_in, qkv_blocks, cosine, sine, head_gains, query_width, key_width
    )
    low_down = down_weight.astype(jnp.bfloat16)
    own_kv, w_out, low_down = lax.optimization_barrier((own_kv, w_out, low_down))
    near_cotangent = move(after(cotangent, raw), OVER_L)
    ((lower_kv,),) = transfer("keys_up", 2, 40, Halves(own_kv, 0))
    lower_kv, near_up = lax.optimization_barrier((lower_kv, near_up))
    up_blocks = over_plane(near_up)
    score_flops = 2 * count * count * query_width
    (attn_heads,) = attention_call(
        attend_kernel,
        "attend",
        place,
        [time, begin, queries, lower_kv, own_kv],
        [jax.ShapeDtypeStruct((count, query_width), jnp.bfloat16)],
        2 * score_flops,
    )

    def blocks(partial):
        return partial.astype(jnp.bfloat16).reshape(4, rows_here, width)

    partial = blocks(jnp.dot(attn_heads, w_out, preferred_element_type=jnp.float32))
    partial, near_cotangent = lax.optimization_barrier((partial, near_cotangent))
    received, (near_down,) = transfer(
        "sum_attention", 3, 50, Sums(partial), Near(low_down)
    )
    down_blocks = over_plane(near_down)
    row = jax.ShapeDtypeStruct((rows_here, width), jnp.float32)
    low_row = jax.ShapeDtypeStruct((rows_here, width), jnp.bfloat16)
    gain_row = jax.ShapeDtypeStruct((8, width), jnp.float32)
    mixed, own_mid = by_row_tiles(
        mix_kernel, "mix", slot_of, [hidden_in, partial, *received, ln_mid[None]], [row, low_row]
    )
    (full_mid,), (d_branch,) = transfer(
        "gather_mid", 4, 34, Rows(own_mid), Cores(cotangent, near_cotangent)
    )
    d_branch = d_branch.reshape(count, width)
    full_mid = full_mid.reshape(count, width)
    gate, upper, act = mlp_front(full_mid, gate_blocks, up_blocks)
    g_down = slot_grad(slot_of, act, d_branch)
    down_blocks, g_down = lax.optimization_barrier((down_blocks, g_down))
    near_g_down = to_plane(g_down)
    d_gate, d_upper, branch = mlp_back(slot_of, d_branch, gate, upper, act, down_blocks)
    partial = rows_back("mid_rows", d_gate, gate_blocks, d_upper, up_blocks)
    received, (g_gateup,) = transfer(
        "sum_mid", 5, 33, Sums(partial), Grads(full_mid, d_gate, d_upper), scoped=40
    )
    near_g_gateup = to_plane(g_gateup)
    d_mixed, low_d_mixed, mid_gain = by_row_tiles(
        mix_back_kernel,
        "mix_back",
        slot_of,
        [mixed, partial, *received, ln_mid[None], cotangent],
        [row, low_row, gain_row],
        scratch=True,
    )
    g_ln_mid = jnp.sum(mid_gain, axis=0)
    ((d_attn,),) = transfer("gather_attention", 6, 29, Rows(low_d_mixed))
    d_attn = d_attn.reshape(count, width)
    owned_down = to_owner(after(near_g_down, d_attn))
    g_out = slot_grad(slot_of, attn_heads, d_attn)
    d_heads = jnp.einsum("td,hd->th", d_attn, w_out, preferred_element_type=jnp.float32).astype(
        jnp.bfloat16
    )
    d_queries, d_low, d_own = attention_call(
        attend_back_kernel,
        "attend_back",
        place,
        [time, begin, queries, lower_kv, own_kv, d_heads],
        [
            jax.ShapeDtypeStruct((count, query_width), jnp.float32),
            jax.ShapeDtypeStruct((count, 2 * key_width), jnp.bfloat16),
            jax.ShapeDtypeStruct((count, 2 * key_width), jnp.float32),
        ],
        5 * score_flops,
    )
    d_low, g_out, *owned_down = lax.optimization_barrier((d_low, g_out, *owned_down))
    near_g_out = to_plane(g_out)
    (from_above,), branch_received = transfer("keys_down", 7, 53, Halves(d_low, 1), Sums(branch))
    d_projected, g_q, g_k = unproject(
        place, d_queries, d_own, from_above, raw, cosine, sine, head_gains
    )
    g_q, g_k = jnp.sum(g_q, axis=0), jnp.sum(g_k, axis=0)
    g_qkv = jnp.einsum("td,tc->dc", full_in, d_projected, preferred_element_type=jnp.float32)
    near_g_qkv = to_plane(g_qkv.astype(jnp.bfloat16).reshape(8, width // 8, -1))
    partial = rows_back("in_rows", d_projected, qkv_blocks)
    received, (owned_gateup,) = transfer("sum_in", 8, 74, Sums(partial), Owners(near_g_gateup))
    near_g_out, near_g_qkv, branch_received, owned_down, received = lax.optimization_barrier(
        (near_g_out, near_g_qkv, branch_received, owned_down, received)
    )
    red_down = both(owned_down)
    result_rows = mixed + summed(branch, branch_received)
    owned_out = to_owner(near_g_out)
    received, owned_out = lax.optimization_barrier((received, owned_out))
    red_gateup = both(owned_gateup)
    red_out, red_qkv = both(owned_out), both(to_owner(near_g_qkv))
    input_grad, in_gain = by_row_tiles(
        in_back_kernel,
        "in_back",
        slot_of,
        [hidden_in, partial, *received, ln_in[None], d_mixed],
        [row, gain_row],
        scratch=True,
        micros=40,
    )
    g_ln_in = jnp.sum(in_gain, axis=0)
    gain_terms = jnp.concatenate([g_ln_in, g_ln_mid, g_q, g_k])
    squares = sum(jnp.sum(red * red) for red in (red_qkv, red_gateup, red_out, red_down))
    totals_here = sum_all(jnp.concatenate([gain_terms, squares[None]]))
    gain_grad, total_squares = totals_here[:-1], totals_here[-1]
    grad_norm = jnp.sqrt(total_squares + jnp.sum(gain_grad * gain_grad))
    factor = jnp.minimum(1.0, CLIP_LIMIT / (grad_norm + 1e-06))
    (
        (qkv_new, qkv_first_new, qkv_second_new),
        (gateup_new, gateup_first_new, gateup_second_new),
        (out_new, out_first_new, out_second_new),
        (down_new, down_first_new, down_second_new),
    ) = adam_all(
        factor,
        [
            (
                LEARN,
                projection_master_weight,
                projection_first_moment,
                projection_second_moment,
                [red_qkv],
            ),
            (LEARN, gateup_weight, gateup_first, gateup_second, [red_gateup]),
            (out_rate, out_weight, out_first, out_second, [red_out]),
            (LEARN, down_weight, down_first, down_second, [red_down]),
        ],
    )
    gains_new, gain_first_new, gain_second_new = adam(
        gains, gain_first, gain_second, gain_grad, factor, GAIN_LEARN, 0.0
    )
    return (
        result_rows.astype(jnp.bfloat16),
        input_grad,
        qkv_new,
        gateup_new,
        out_new,
        down_new,
        qkv_first_new,
        gateup_first_new,
        out_first_new,
        down_first_new,
        qkv_second_new,
        gateup_second_new,
        out_second_new,
        down_second_new,
        gains_new,
        gain_first_new,
        gain_second_new,
        grad_norm,
    )


def paired(mesh):
    return dict(mesh.shape) == {"dp": 8, "mp": 4}


def solution(mesh):
    placed = (
        P(("dp", "mp"), None),
        P(("dp", "mp"), None),
        P("dp", None),
        P(),
        P("dp", "mp"),
        P("dp", "mp"),
        P(("mp", "dp"), None),
        P(("mp", "dp"), None),
        P("dp", "mp"),
        P("dp", "mp"),
        P(("mp", "dp"), None),
        P(("mp", "dp"), None),
        P("dp", "mp"),
        P("dp", "mp"),
        P(("mp", "dp"), None),
        P(("mp", "dp"), None),
        P(),
        P(),
        P(),
    )
    return jax.shard_map(
        shards_paired if paired(mesh) else shards_general,
        mesh=mesh,
        in_specs=placed,
        out_specs=(
            P(("dp", "mp"), None),
            P(("dp", "mp"), None),
            P("dp", "mp"),
            P("dp", "mp"),
            P(("mp", "dp"), None),
            P(("mp", "dp"), None),
            P("dp", "mp"),
            P("dp", "mp"),
            P(("mp", "dp"), None),
            P(("mp", "dp"), None),
            P("dp", "mp"),
            P("dp", "mp"),
            P(("mp", "dp"), None),
            P(("mp", "dp"), None),
            P(),
            P(),
            P(),
            P(),
        ),
        check_vma=False,
    )
```
